32 devices in a mesh: section: 2 (over x), dp: 4 (over y, core), tensor: 4 (over z).
Axes of the slice: x: 2, y: 2, z: 4, core: 2. Of those that a mesh axis runs over, the one named last changes fastest.
Arguments:
- block_eight_input: bfloat16 [192, 16, 1152], P('tensor', 'dp'), may hold values from -6 to 6
- cond: bfloat16 [16, 3, 1152], P('dp'), may hold values from -6 to 6
- image_slot_index: int32 [16, 192], P('dp'), may hold values from 0 to 2, never falling along the last dimension, each value on 1 to 96 neighbouring positions
- targets: bfloat16 [192, 16, 768], P(None, 'dp', 'tensor'), may hold values from -6 to 6
- cot: bfloat16 [192, 16, 1152], P('tensor', 'dp'), may hold values from -6 to 6
- ada_w: bfloat16 [2, 1152, 6912], P('section', None, 'tensor'), may hold values from -0.1875 to 0.1875
- ada_b: bfloat16 [2, 6912], P('section', 'tensor'), may hold values from -3 to 3
- query_key_value_weight: bfloat16 [2, 1152, 3, 1152], P('section', None, None, 'tensor'), may hold values from -0.1875 to 0.1875
- query_value_bias: bfloat16 [2, 2, 1152], P('section', None, 'tensor'), may hold values from -2 to 2
- attention_output_weight: bfloat16 [2, 1152, 1152], P('section', 'tensor'), may hold values from -1.5 to 1.5
- attention_output_bias: bfloat16 [2, 1152], P('section'), may hold values from -2 to 2
- hidden_weight: bfloat16 [2, 1152, 4608], P('section', None, 'tensor'), may hold values from -0.1875 to 0.1875
- hidden_bias: bfloat16 [2, 4608], P('section', 'tensor'), may hold values from -2 to 2
- output_weight_mlp: bfloat16 [2, 4608, 1152], P('section', 'tensor'), may hold values from -0.09375 to 0.09375
- output_bias_mlp: bfloat16 [2, 1152], P('section'), may hold values from -2 to 2
- p1_w: bfloat16 [1152, 2048], P(None, 'tensor'), may hold values from -0.1875 to 0.1875
- p1_b: bfloat16 [2048], P('tensor'), may hold values from -2 to 2
- p2_w: bfloat16 [2048, 2048], P('tensor'), may hold values from -0.125 to 0.125
- p2_b: bfloat16 [2048], replicated, may hold values from -2 to 2
- p3_w: bfloat16 [2048, 768], P(None, 'tensor'), may hold values from -0.125 to 0.125
- p3_b: bfloat16 [768], P('tensor'), may hold values from -2 to 2
Outputs:
- section_out: bfloat16 [2, 192, 16, 1152], P('section', 'tensor', 'dp')
- section_grad: float32 [2, 192, 16, 1152], P('section', 'tensor', 'dp')
- align_loss: float32 [], replicated
- g_ada_w: float32 [2, 1152, 6912], P('section', 'dp', 'tensor')
- g_ada_b: float32 [2, 6912], P('section', 'tensor')
- g_qkv_w: float32 [2, 1152, 3, 1152], P('section', 'dp', None, 'tensor')
- g_qv_b: float32 [2, 2, 1152], P('section', None, 'tensor')
- g_out_w: float32 [2, 1152, 1152], P('section', 'tensor', 'dp')
- g_out_b: float32 [2, 1152], P('section')
- g_fc1_w: float32 [2, 1152, 4608], P('section', 'dp', 'tensor')
- g_fc1_b: float32 [2, 4608], P('section', 'tensor')
- g_fc2_w: float32 [2, 4608, 1152], P('section', 'tensor', 'dp')
- g_fc2_b: float32 [2, 1152], P('section')
- g_p1_w: float32 [1152, 2048], P(('section', 'dp'), 'tensor')
- g_p1_b: float32 [2048], P('tensor')
- g_p2_w: float32 [2048, 2048], P('tensor', ('section', 'dp'))
- g_p2_b: float32 [2048], replicated
- g_p3_w: float32 [2048, 768], P(('section', 'dp'), 'tensor')
- g_p3_b: float32 [768], P('tensor')
The draws below stay inside these ranges and needn't reach their ends.
Inputs may be any that keep to these rules, and one draw needn't show every extreme that they name: `image_slot_index`: within a row the slot numbers never fall; each slot covers 1 to 96 positions and one covers exactly 96.
All inputs are finite; a program needn't handle non-finite values.
Results may differ from the reference program's by a relative error of at most 0.035.
The reference program's roundings to bfloat16 on the way count: a program that leaves them out, or rounds other values in their place, can miss the bound.
Values may be sent and summed in bfloat16 or wider, within the bound.
A program may use at most 192 MiB of HBM per device.

```python
import math
import jax
import jax.numpy as jnp
import numpy as np
from jax import lax

MODEL_WIDTH = 1152
HEAD_COUNT = 16
HEAD_WIDTH = 72
FF = 4608
PH = 2048
TARGET_WIDTH = 768
ROW_LENGTH = 192
IMAGES_PER_ROW = 3
REPLICA_ROWS = 4
PACKED_ROWS = 16


def block_levels(own_key, dims, cuts, smallest, top_value):
    def one(position, parts):
        heights = jax.random.uniform(jax.random.fold_in(jax.random.fold_in(own_key, 6), position), (parts,), jnp.float32, smallest / len(cuts), top_value / len(cuts))
        return jnp.repeat(jnp.exp(heights), dims[position] // parts).reshape((-1,) + (1,) * (len(dims) - position - 1))

    gain = one(*cuts[0])
    for cut in cuts[1:]:
        gain = gain * one(*cut)
    return gain


def length_profile(amount, total, most, slope):
    weights = [(1 << 20) // math.isqrt(rank ** slope) + 1 for rank in range(2, amount + 1)]
    spare, holding = total - most - (amount - 1), [1] * (amount - 1)
    while spare > 0:
        free = [i for i in range(amount - 1) if holding[i] < most]
        whole, remaining = sum([weights[i] for i in free]), spare
        for i in free:
            addition = min(most - holding[i], max(1, remaining * weights[i] // whole), spare)
            holding[i] = holding[i] + addition
            spare = spare - addition
    return np.array([most] + holding)


def ragged_sizes(key, amount, total, reach, slope):
    if amount == 2:
        one = jax.random.randint(key, (), max(1, total - reach), min(reach, total - 1) + 1)
        return jnp.stack([one, total - one])
    sizes = jnp.asarray(length_profile(amount, total, reach, slope), jnp.int32)
    twos = (amount - 1) // 2
    source_of, taker = sizes[1:1 + 2 * twos:2], sizes[2:2 + 2 * twos:2]
    margin = jnp.minimum(source_of - 1, reach - taker)
    passed = jax.random.randint(jax.random.fold_in(key, 1), (twos,), 0, 1 << 20) % (margin + 1)
    sizes = sizes.at[1:1 + 2 * twos:2].set(source_of - passed).at[2:2 + 2 * twos:2].set(taker + passed)
    return sizes[jax.random.permutation(jax.random.fold_in(key, 2), amount)]


def normal_values(stream_key, shape, spread, reach, cuts=(), held_as=jnp.bfloat16):
    result = spread * jax.random.normal(stream_key, shape, jnp.float32)
    if cuts:
        result = result * block_levels(stream_key, shape, cuts, -0.22, 0.18)
    return jnp.clip(result, -reach, reach).astype(held_as)


def setup_inputs(seed: int = 0) -> dict:
    key_of = jax.random.split(jax.random.key(seed), 22)
    return {
        "block_eight_input": normal_values(key_of[0], (ROW_LENGTH, PACKED_ROWS, MODEL_WIDTH), 1.0, 6.0, ((0, 4), (1, 4))),
        "cond": normal_values(key_of[1], (PACKED_ROWS, IMAGES_PER_ROW, MODEL_WIDTH), 1.0, 6.0, ((0, 4),)),
        "image_slot_index": jax.vmap(lambda own: jnp.searchsorted(jnp.cumsum(ragged_sizes(own, IMAGES_PER_ROW, ROW_LENGTH, ROW_LENGTH // 2, 0)), jnp.arange(ROW_LENGTH), side="right"))(jax.random.split(key_of[2], PACKED_ROWS)).reshape((PACKED_ROWS, ROW_LENGTH)).astype(jnp.int32),
        "targets": normal_values(key_of[3], (ROW_LENGTH, PACKED_ROWS, TARGET_WIDTH), 1.0, 6.0, ((1, 4), (2, 4))),
        "cot": normal_values(key_of[4], (ROW_LENGTH, PACKED_ROWS, MODEL_WIDTH), 1.0, 6.0, ((0, 4), (1, 4))),
        "ada_w": normal_values(key_of[5], (2, MODEL_WIDTH, 6 * MODEL_WIDTH), MODEL_WIDTH ** -0.5, 0.1875, ((0, 2), (2, 4))),
        "ada_b": normal_values(key_of[6], (2, 6 * MODEL_WIDTH), 0.5, 3.0, ((0, 2), (1, 4))),
        "query_key_value_weight": normal_values(key_of[7], (2, MODEL_WIDTH, 3, MODEL_WIDTH), MODEL_WIDTH ** -0.5, 0.1875, ((0, 2), (3, 4))),
        "query_value_bias": normal_values(key_of[8], (2, 2, MODEL_WIDTH), 0.3, 2.0, ((0, 2), (2, 4))),
        "attention_output_weight": normal_values(key_of[9], (2, MODEL_WIDTH, MODEL_WIDTH), (MODEL_WIDTH // 64) ** -0.5, 1.5, ((0, 2), (1, 4))),
        "attention_output_bias": normal_values(key_of[10], (2, MODEL_WIDTH), 0.3, 2.0, ((0, 2),)),
        "hidden_weight": normal_values(key_of[11], (2, MODEL_WIDTH, FF), MODEL_WIDTH ** -0.5, 0.1875, ((0, 2), (2, 4))),
        "hidden_bias": normal_values(key_of[12], (2, FF), 0.3, 2.0, ((0, 2), (1, 4))),
        "output_weight_mlp": normal_values(key_of[13], (2, FF, MODEL_WIDTH), FF ** -0.5, 0.09375, ((0, 2), (1, 4))),
        "output_bias_mlp": normal_values(key_of[14], (2, MODEL_WIDTH), 0.3, 2.0, ((0, 2),)),
        "p1_w": normal_values(key_of[15], (MODEL_WIDTH, PH), MODEL_WIDTH ** -0.5, 0.1875, ((1, 4),)),
        "p1_b": normal_values(key_of[16], (PH,), 0.3, 2.0, ((0, 4),)),
        "p2_w": normal_values(key_of[17], (PH, PH), PH ** -0.5, 0.125, ((0, 4),)),
        "p2_b": normal_values(key_of[18], (PH,), 0.3, 2.0),
        "p3_w": normal_values(key_of[19], (PH, TARGET_WIDTH), PH ** -0.5, 0.125, ((1, 4),)),
        "p3_b": normal_values(key_of[20], (TARGET_WIDTH,), 0.3, 2.0, ((0, 4),)),
    }


highest = lax.Precision.HIGHEST
norm_eps = 1e-06
cosine_eps = 1e-06
masked_score = -1e+30

@jax.custom_vjp
def low(v):
    return lax.optimization_barrier(v.astype(jnp.bfloat16)).astype(jnp.float32)

@jax.custom_vjp
def low_back(v):
    return v

def low_keep(v):
    return (low(v), None)

def low_pass(kept, grad):
    return (grad,)

def back_keep(v):
    return (v, None)

def back_low(kept, grad):
    return (low(grad),)
low.defvjp(low_keep, low_pass)
low_back.defvjp(back_keep, back_low)

def layer_norm(source_rows):
    centred = source_rows - lax.optimization_barrier(jnp.mean(source_rows, axis=-1, keepdims=True))
    return centred * lax.rsqrt(lax.optimization_barrier(jnp.mean(centred * centred, axis=-1, keepdims=True)) + norm_eps)

def row_groups(source_rows):
    moved_rows = jnp.transpose(source_rows.reshape(ROW_LENGTH, PACKED_ROWS, HEAD_COUNT, HEAD_WIDTH), (1, 0, 2, 3))
    return moved_rows.reshape(PACKED_ROWS // REPLICA_ROWS, REPLICA_ROWS, ROW_LENGTH, HEAD_COUNT, HEAD_WIDTH)

def group_attention(items):
    query_rows, key_rows, value_rows, same_image_mask = items
    scores = jnp.einsum('gphd,gqhd->ghpq', query_rows, key_rows, precision=highest) * HEAD_WIDTH ** (-0.5)
    scores = jnp.where(same_image_mask[:, None], low_back(scores), masked_score)
    probs = low(jax.nn.softmax(scores, axis=-1))
    return jnp.einsum('ghpq,gqhd->gphd', probs, value_rows, precision=highest)

def attention(query_rows, key_rows, value_rows, same_image_mask):
    grouped_rows = same_image_mask.reshape(PACKED_ROWS // REPLICA_ROWS, REPLICA_ROWS, ROW_LENGTH, ROW_LENGTH)
    mixed_tokens = lax.map(jax.checkpoint(group_attention), (row_groups(query_rows), row_groups(key_rows), row_groups(value_rows), grouped_rows))
    mixed_tokens = mixed_tokens.reshape(PACKED_ROWS, ROW_LENGTH, HEAD_COUNT * HEAD_WIDTH)
    return jnp.transpose(mixed_tokens, (1, 0, 2))

def gelu_tanh(source_rows):
    return jax.nn.gelu(source_rows, approximate=True)

def transformer_block(block_input, apply_modulation, same_image_mask, layer_step, query_key_value_weight, query_value_bias, attention_output_weight, attention_output_bias, hidden_weight, hidden_bias, output_weight_mlp, output_bias_mlp):
    shift_one, scale_one, gate_one, shift_two, scale_two, gate_two = jnp.split(apply_modulation, 6, axis=-1)
    attn_in = low(layer_norm(block_input) * (1.0 + scale_one) + shift_one)
    projected = jnp.einsum('prd,dkc->prkc', attn_in, query_key_value_weight[layer_step], precision=highest)
    query_rows = low_back(low(projected[:, :, 0] + query_value_bias[layer_step, 0]))
    key_rows = low_back(low(projected[:, :, 1]))
    value_rows = low_back(low(projected[:, :, 2] + query_value_bias[layer_step, 1]))
    mixed_tokens = low_back(low(attention(query_rows, key_rows, value_rows, same_image_mask)))
    branch_one = low_back(jnp.einsum('prc,cd->prd', mixed_tokens, attention_output_weight[layer_step], precision=highest) + attention_output_bias[layer_step])
    middle = block_input + gate_one * branch_one
    mlp_in = low(layer_norm(middle) * (1.0 + scale_two) + shift_two)
    hidden_pre = low_back(jnp.einsum('prd,df->prf', mlp_in, hidden_weight[layer_step], precision=highest) + hidden_bias[layer_step])
    hidden_act = low(gelu_tanh(hidden_pre))
    branch_two = low_back(jnp.einsum('prf,fd->prd', hidden_act, output_weight_mlp[layer_step], precision=highest) + output_bias_mlp[layer_step])
    return middle + gate_two * branch_two

def reference(block_eight_input, cond, image_slot_index, targets, cot, ada_w, ada_b, query_key_value_weight, query_value_bias, attention_output_weight, attention_output_bias, hidden_weight, hidden_bias, output_weight_mlp, output_bias_mlp, p1_w, p1_b, p2_w, p2_b, p3_w, p3_b):
    cond_act = low(jax.nn.silu(cond.astype(jnp.float32)))
    onehot = (image_slot_index[:, :, None] == jnp.arange(IMAGES_PER_ROW, dtype=jnp.int32)).astype(jnp.float32)
    same_image_mask = image_slot_index[:, :, None] == image_slot_index[:, None, :]
    target_rows = targets.astype(jnp.float32)

    def forward(block_input, probe_value, ada_w, ada_b, query_key_value_weight, query_value_bias, attention_output_weight, attention_output_bias, hidden_weight, hidden_bias, output_weight_mlp, output_bias_mlp, p1_w, p1_b, p2_w, p2_b, p3_w, p3_b):

        def modulation_values(layer_step):
            mod_rows = jnp.einsum('rsd,dc->rsc', cond_act, ada_w[layer_step], precision=highest) + ada_b[layer_step]
            return jnp.einsum('rps,rsc->prc', onehot, mod_rows, precision=highest)
        block_weights = (query_key_value_weight, query_value_bias, attention_output_weight, attention_output_bias, hidden_weight, hidden_bias, output_weight_mlp, output_bias_mlp)
        first_block_output = transformer_block(block_input, modulation_values(0), same_image_mask, 0, *block_weights)
        forwarded_rows = low(first_block_output)
        second_block_output = transformer_block(forwarded_rows + probe_value, modulation_values(1), same_image_mask, 1, *block_weights)
        first_pre = low_back(jnp.einsum('prd,de->pre', forwarded_rows, p1_w, precision=highest) + p1_b)
        first_act = low(jax.nn.silu(first_pre))
        second_pre = low_back(jnp.einsum('pre,ef->prf', first_act, p2_w, precision=highest) + p2_b)
        second_act = low(jax.nn.silu(second_pre))
        predicted = low_back(jnp.einsum('prf,fc->prc', second_act, p3_w, precision=highest) + p3_b)
        pred_sq = lax.optimization_barrier(jnp.sum(predicted * predicted, axis=-1))
        cross = lax.optimization_barrier(jnp.sum(predicted * target_rows, axis=-1))
        target_sq = lax.optimization_barrier(jnp.sum(target_rows * target_rows, axis=-1))
        cosine = cross * lax.rsqrt(pred_sq + cosine_eps) * lax.rsqrt(target_sq + cosine_eps)
        align_loss = -0.5 * jnp.mean(cosine)
        return (first_block_output, second_block_output, align_loss)
    primals = [block_eight_input.astype(jnp.float32), jnp.zeros(block_eight_input.shape, jnp.float32)]
    for weight in (ada_w, ada_b, query_key_value_weight, query_value_bias, attention_output_weight, attention_output_bias, hidden_weight, hidden_bias, output_weight_mlp, output_bias_mlp, p1_w, p1_b, p2_w, p2_b, p3_w, p3_b):
        primals.append(weight.astype(jnp.float32))
    outputs, pullback = jax.vjp(forward, *primals)
    first_block_output, second_block_output, align_loss = outputs
    grads = pullback((jnp.zeros_like(first_block_output), cot.astype(jnp.float32), jnp.ones_like(align_loss)))
    section_out = jnp.stack([first_block_output, second_block_output]).astype(jnp.bfloat16)
    section_grad = jnp.stack([grads[0], grads[1]])
    return (section_out, section_grad, align_loss, grads[2], grads[3], grads[4], grads[5], grads[6], grads[7], grads[8], grads[9], grads[10], grads[11], grads[12], grads[13], grads[14], grads[15], grads[16], grads[17])
```

```python
import functools
import math

import jax
import jax.numpy as jnp
from jax import lax
from jax.experimental import pallas as pl
from jax.experimental.pallas import tpu as pltpu
from jax.sharding import PartitionSpec as P

HEAD_WIDTH = 72
HEAD_LANES = 128
IMAGES_PER_ROW = 3
NORM_EPS = 1e-06
COSINE_EPS = 1e-06
MASKED_SCORE = -1e30
HIGHEST = lax.Precision.HIGHEST
MESH = pl.DeviceIdType.MESH
F32 = jnp.float32
BF16 = jnp.bfloat16
NN = (((1,), (0,)), ((), ()))
NT = (((1,), (1,)), ((), ()))
TN = (((0,), (0,)), ((), ()))


def dot(left, right, form=NN):
    return lax.dot_general(left, right, form, preferred_element_type=F32)


def greet(count):
    me = lax.axis_index("tensor")
    barrier = pltpu.get_barrier_semaphore()
    for step in range(1, count):
        pl.semaphore_signal(
            barrier, inc=1, device_id={"tensor": lax.rem(me + step, count)}, device_id_type=MESH
        )
    pl.semaphore_wait(barrier, count - 1)


def own_rows(me, length):
    return pl.ds(pl.multiple_of(me * length, 16), length)


def start_gather(full, length, count, send_sem, recv_sem):
    me = lax.axis_index("tensor")
    copies = []
    for step in range(1, count):
        mine = full.at[:, own_rows(me, length)]
        copy = pltpu.make_async_remote_copy(
            src_ref=mine,
            dst_ref=mine,
            send_sem=send_sem.at[step - 1],
            recv_sem=recv_sem.at[step - 1],
            device_id={"tensor": lax.rem(me + step, count)},
            device_id_type=MESH,
        )
        copy.start()
        copies.append(copy)
    return copies


def wait_all(copies):
    for copy in copies:
        copy.wait()


def scatter_sum(partial, length, count, send_buf, recv_buf, send_sem, recv_sem):
    me = lax.axis_index("tensor")
    copies = []
    for step in range(1, count):
        peer = lax.rem(me + step, count)
        term = partial(own_rows(peer, length))
        send_buf[step - 1] = term.astype(BF16).reshape(send_buf.shape[1:])
        copy = pltpu.make_async_remote_copy(
            src_ref=send_buf.at[step - 1],
            dst_ref=recv_buf.at[step - 1],
            send_sem=send_sem.at[step - 1],
            recv_sem=recv_sem.at[step - 1],
            device_id={"tensor": peer},
            device_id_type=MESH,
        )
        copy.start()
        copies.append(copy)
    total = partial(own_rows(me, length))
    return copies, total


def finish_sum(copies, total, recv_buf):
    wait_all(copies)
    for step in range(recv_buf.shape[0]):
        total = total + recv_buf[step].reshape(total.shape).astype(F32)
    return total


def fetch(block, own_ref, other_ref, target, sem):
    mine = lax.axis_index("section") == block

    @pl.when(mine)
    def own_start():
        pltpu.make_async_copy(own_ref, target, sem).start()

    @pl.when(jnp.logical_not(mine))
    def other_start():
        pltpu.make_async_copy(other_ref, target, sem).start()

    return pltpu.make_async_copy(own_ref, target, sem)


def layer_norm(rows):
    centred = rows - jnp.mean(rows, axis=-1, keepdims=True)
    inverse = lax.rsqrt(jnp.mean(centred * centred, axis=-1, keepdims=True) + NORM_EPS)
    return centred * inverse, inverse


def norm_back(grad, normed, inverse):
    mean_grad = jnp.mean(grad, axis=-1, keepdims=True)
    mean_cross = jnp.mean(grad * normed, axis=-1, keepdims=True)
    return inverse * (grad - mean_grad - normed * mean_cross)


def token_mod(mod_ref, seg_ref, which):
    parts = []
    for row in range(seg_ref.shape[0]):
        seg = seg_ref[row]
        value = mod_ref[which, row, IMAGES_PER_ROW - 1 : IMAGES_PER_ROW, :]
        for slot in range(IMAGES_PER_ROW - 2, -1, -1):
            value = jnp.where(seg == slot, mod_ref[which, row, slot : slot + 1, :], value)
        parts.append(value)
    return jnp.concatenate(parts, axis=0)


def slot_sums(value, seg_ref, out_ref, which):
    length = seg_ref.shape[1]
    for row in range(seg_ref.shape[0]):
        seg = seg_ref[row]
        piece = value[row * length : (row + 1) * length]
        for slot in range(IMAGES_PER_ROW):
            out_ref[which, row, slot : slot + 1, :] = jnp.sum(
                jnp.where(seg == slot, piece, 0.0), axis=0, keepdims=True
            )


def flat(ref):
    return ref[...].reshape(-1, ref.shape[-1])


def spread_matrix(width):
    lanes = width // HEAD_WIDTH * HEAD_LANES
    source = lax.broadcasted_iota(jnp.int32, (width, lanes), 0)
    target = lax.broadcasted_iota(jnp.int32, (width, lanes), 1)
    within = target & (HEAD_LANES - 1)
    head = target >> (HEAD_LANES.bit_length() - 1)
    hit = (within < HEAD_WIDTH) & (source == head * HEAD_WIDTH + within)
    return jnp.where(hit, 1.0, 0.0).astype(BF16)


def gelu_tanh(pre):
    inner = math.sqrt(2.0 / math.pi) * (pre + 0.044715 * (pre * pre * pre))
    return 0.5 * pre * (1.0 + jnp.tanh(inner))


def gelu_slope(pre):
    scale = math.sqrt(2.0 / math.pi)
    square = pre * pre
    tanh = jnp.tanh(scale * (pre + 0.044715 * (pre * square)))
    return 0.5 * (1.0 + tanh) + 0.5 * pre * (1.0 - tanh * tanh) * scale * (
        1.0 + 3 * 0.044715 * square
    )


def attend_kernel(
    count, block,
    u_ref, mod_ref, seg_own, seg_col, seg_row, bias_ref, out_bias_ref, wqkv_own, wqkv_other, wo_own, wo_other,
    middle_ref, branch_ref, full_ref, q_ref, k_ref, v_ref, probs_ref, mixed_ref,
    full, wqkv, wo, mixed_wide, send_buf, recv_buf, w_sem, ag_send, ag_recv, rs_send, rs_recv,
):
    me = lax.axis_index("tensor")
    rows, length, width = u_ref.shape
    heads_width = wo.shape[0]
    heads = heads_width // HEAD_WIDTH
    load_qkv = fetch(block, wqkv_own, wqkv_other, wqkv, w_sem.at[0])
    load_out = fetch(block, wo_own, wo_other, wo, w_sem.at[1])
    u = flat(u_ref).astype(F32)
    normed, unused = layer_norm(u)
    attn_in = normed * (1.0 + token_mod(mod_ref, seg_own, 1)) + token_mod(mod_ref, seg_own, 0)
    full[:, own_rows(me, length), :] = attn_in.astype(BF16).reshape(rows, length, width)
    greet(count)
    gather = start_gather(full, length, count, ag_send, ag_recv)
    spread = spread_matrix(heads_width)
    load_qkv.wait()
    wait_all(gather)
    full_ref[...] = full[...]
    tokens = flat(full)
    for which, target in ((0, q_ref), (1, k_ref), (2, v_ref)):
        projected = dot(tokens, wqkv[which])
        if which != 1:
            projected = projected + bias_ref[which // 2 : which // 2 + 1, :]
        target[...] = dot(projected.astype(BF16), spread).astype(BF16).reshape(target.shape)

    def one_head(index, carry):
        row = index // heads
        head = lax.rem(index, heads)
        lanes = pl.ds(pl.multiple_of(head * HEAD_LANES, HEAD_LANES), HEAD_LANES)
        scores = dot(q_ref[row, :, lanes], k_ref[row, :, lanes], NT) * HEAD_WIDTH ** (-0.5)
        scores = jnp.where(seg_col[row] == seg_row[row], scores, MASKED_SCORE)
        raised = jnp.exp(scores - jnp.max(scores, axis=-1, keepdims=True))
        probs = raised / jnp.sum(raised, axis=-1, keepdims=True)
        probs_ref[index] = probs
        mixed_wide[row, :, lanes] = dot(probs.astype(BF16), v_ref[row, :, lanes]).astype(BF16)
        return carry

    lax.fori_loop(0, rows * heads, one_head, 0)
    mixed_ref[...] = dot(flat(mixed_wide), spread, NT).astype(BF16).reshape(mixed_ref.shape)
    load_out.wait()

    def partial(which_rows):
        return dot(mixed_ref[:, which_rows, :].reshape(rows * length, heads_width), wo[...])

    copies, total = scatter_sum(partial, length, count, send_buf, recv_buf, rs_send, rs_recv)
    branch = finish_sum(copies, total, recv_buf) + out_bias_ref[...]
    branch_ref[...] = branch.reshape(branch_ref.shape)
    middle = flat(u_ref).astype(F32) + token_mod(mod_ref, seg_own, 2) * branch
    middle_ref[...] = middle.reshape(middle_ref.shape)


def mlp_kernel(
    count, block,
    middle_ref, mod_ref, seg_own, hidden_bias_ref, out_bias_ref, w1_own, w1_other, w2_own, w2_other,
    out_ref, branch_ref, full_ref, pre_ref, act_ref,
    full, w1, w2, send_buf, recv_buf, w_sem, ag_send, ag_recv, rs_send, rs_recv,
):
    me = lax.axis_index("tensor")
    rows, length, width = middle_ref.shape
    load_one = fetch(block, w1_own, w1_other, w1, w_sem.at[0])
    load_two = fetch(block, w2_own, w2_other, w2, w_sem.at[1])
    normed, unused = layer_norm(flat(middle_ref))
    mlp_in = normed * (1.0 + token_mod(mod_ref, seg_own, 4)) + token_mod(mod_ref, seg_own, 3)
    full[:, own_rows(me, length), :] = mlp_in.astype(BF16).reshape(rows, length, width)
    greet(count)
    gather = start_gather(full, length, count, ag_send, ag_recv)
    load_one.wait()
    wait_all(gather)
    full_ref[...] = full[...]
    pre = dot(flat(full), w1[...]) + hidden_bias_ref[...]
    pre_ref[...] = pre.reshape(pre_ref.shape)
    act_ref[...] = gelu_tanh(pre).astype(BF16).reshape(act_ref.shape)
    load_two.wait()

    def partial(which_rows):
        return dot(act_ref[:, which_rows, :].reshape(rows * length, -1), w2[...])

    copies, total = scatter_sum(partial, length, count, send_buf, recv_buf, rs_send, rs_recv)
    branch = finish_sum(copies, total, recv_buf) + out_bias_ref[...]
    branch_ref[...] = branch.reshape(branch_ref.shape)
    out = flat(middle_ref) + token_mod(mod_ref, seg_own, 5) * branch
    out_ref[...] = out.astype(BF16).reshape(out_ref.shape)


def mlp_back_kernel(
    count, block,
    g_ref, middle_ref, branch_ref, mod_ref, seg_own, full_ref, pre_ref, act_ref, w1_own, w1_other, w2_own, w2_other,
    d_middle_ref, d_mod_ref, d_w1_ref, d_w2_ref, d_b1_ref, d_b2_ref,
    full, d_pre, w1, w2, send_buf, recv_buf, w_sem, ag_send, ag_recv, rs_send, rs_recv,
):
    me = lax.axis_index("tensor")
    rows, length, width = middle_ref.shape
    load_one = fetch(block, w1_own, w1_other, w1, w_sem.at[0])
    load_two = fetch(block, w2_own, w2_other, w2, w_sem.at[1])
    g = flat(g_ref).astype(F32)
    d_branch = (g * token_mod(mod_ref, seg_own, 5)).astype(BF16)
    full[:, own_rows(me, length), :] = d_branch.reshape(rows, length, width)
    greet(count)
    gather = start_gather(full, length, count, ag_send, ag_recv)
    slot_sums(g * flat(branch_ref), seg_own, d_mod_ref, 2)
    load_two.wait()
    wait_all(gather)
    d_act = dot(flat(full), w2[...], NT)
    d_pre[...] = (d_act * gelu_slope(flat(pre_ref))).astype(BF16).reshape(d_pre.shape)
    load_one.wait()

    def partial(which_rows):
        return dot(d_pre[:, which_rows, :].reshape(rows * length, -1), w1[...], NT)

    copies, total = scatter_sum(partial, length, count, send_buf, recv_buf, rs_send, rs_recv)
    d_b2_ref[...] = jnp.sum(flat(full).astype(F32), axis=0, keepdims=True)
    d_b1_ref[...] = jnp.sum(flat(d_pre).astype(F32), axis=0, keepdims=True)
    d_w2_ref[...] = dot(flat(full), flat(act_ref), TN).astype(BF16)
    d_w1_ref[...] = dot(flat(full_ref), flat(d_pre), TN).astype(BF16)
    d_in = finish_sum(copies, total, recv_buf)
    normed, inverse = layer_norm(flat(middle_ref))
    d_middle = flat(g_ref).astype(F32) + norm_back(
        d_in * (1.0 + token_mod(mod_ref, seg_own, 4)), normed, inverse
    )
    d_middle_ref[...] = d_middle.reshape(d_middle_ref.shape)
    slot_sums(d_in, seg_own, d_mod_ref, 0)
    slot_sums(d_in * normed, seg_own, d_mod_ref, 1)


def attend_back_kernel(
    count, block,
    d_middle_ref, u_ref, branch_ref, mod_ref, seg_own, full_ref, q_ref, k_ref, v_ref, probs_ref, mixed_ref,
    wqkv_own, wqkv_other, wo_own, wo_other,
    d_in_ref, d_mod_ref, d_wqkv_ref, d_wo_ref, d_bqv_ref, d_bo_ref,
    full, wide, narrow, wqkv, wo, send_buf, recv_buf, w_sem, ag_send, ag_recv, rs_send, rs_recv,
):
    me = lax.axis_index("tensor")
    rows, length, width = u_ref.shape
    heads_width = wo.shape[0]
    heads = heads_width // HEAD_WIDTH
    load_qkv = fetch(block, wqkv_own, wqkv_other, wqkv, w_sem.at[0])
    load_out = fetch(block, wo_own, wo_other, wo, w_sem.at[1])
    d_middle = flat(d_middle_ref)
    d_branch = (d_middle * token_mod(mod_ref, seg_own, 2)).astype(BF16)
    full[:, own_rows(me, length), :] = d_branch.reshape(rows, length, width)
    greet(count)
    gather = start_gather(full, length, count, ag_send, ag_recv)
    slot_sums(d_middle * flat(branch_ref), seg_own, d_mod_ref, 2)
    spread = spread_matrix(heads_width)
    load_out.wait()
    wait_all(gather)
    d_mixed = dot(flat(full), wo[...], NT).astype(BF16)
    wide[3] = dot(d_mixed, spread).astype(BF16).reshape(wide.shape[1:])

    def one_head(index, carry):
        row = index // heads
        head = lax.rem(index, heads)
        lanes = pl.ds(pl.multiple_of(head * HEAD_LANES, HEAD_LANES), HEAD_LANES)
        grad = wide[3, row, :, lanes]
        probs = probs_ref[index]
        d_probs = dot(grad, v_ref[row, :, lanes], NT)
        d_scores = (
            probs * (d_probs - jnp.sum(d_probs * probs, axis=-1, keepdims=True))
        ).astype(BF16)
        scale = HEAD_WIDTH ** (-0.5)
        wide[0, row, :, lanes] = (dot(d_scores, k_ref[row, :, lanes]) * scale).astype(BF16)
        wide[1, row, :, lanes] = (dot(d_scores, q_ref[row, :, lanes], TN) * scale).astype(BF16)
        wide[2, row, :, lanes] = dot(probs.astype(BF16), grad, TN).astype(BF16)
        return carry

    lax.fori_loop(0, rows * heads, one_head, 0)
    for which in range(3):
        narrow[which] = (
            dot(flat(wide.at[which]), spread, NT).astype(BF16).reshape(narrow.shape[1:])
        )
    load_qkv.wait()

    def partial(which_rows):
        total = dot(narrow[0, :, which_rows, :].reshape(rows * length, heads_width), wqkv[0], NT)
        for which in (1, 2):
            total = total + dot(
                narrow[which, :, which_rows, :].reshape(rows * length, heads_width), wqkv[which], NT
            )
        return total

    copies, total = scatter_sum(partial, length, count, send_buf, recv_buf, rs_send, rs_recv)
    d_bo_ref[...] = jnp.sum(flat(full).astype(F32), axis=0, keepdims=True)
    d_bqv_ref[0:1, :] = jnp.sum(flat(narrow.at[0]).astype(F32), axis=0, keepdims=True)
    d_bqv_ref[1:2, :] = jnp.sum(flat(narrow.at[2]).astype(F32), axis=0, keepdims=True)
    d_wo_ref[...] = dot(flat(full), flat(mixed_ref), TN).astype(BF16)
    for which in range(3):
        d_wqkv_ref[which] = dot(flat(full_ref), flat(narrow.at[which]), TN).astype(BF16)
    d_attn_in = finish_sum(copies, total, recv_buf)
    normed, inverse = layer_norm(flat(u_ref).astype(F32))
    d_in = flat(d_middle_ref) + norm_back(
        d_attn_in * (1.0 + token_mod(mod_ref, seg_own, 1)), normed, inverse
    )
    d_in_ref[...] = d_in.reshape(d_in_ref.shape)
    slot_sums(d_attn_in, seg_own, d_mod_ref, 0)
    slot_sums(d_attn_in * normed, seg_own, d_mod_ref, 1)


VMEM = pl.BlockSpec(memory_space=pltpu.VMEM)
ANY = pl.BlockSpec(memory_space=pl.ANY)


def call(kernel, number, inputs, specs, outs, scratch, flops):
    moved = sum(math.prod(one.shape) * one.dtype.itemsize for one in inputs)
    return pl.pallas_call(
        kernel,
        out_shape=[jax.ShapeDtypeStruct(shape, dtype) for shape, dtype in outs],
        in_specs=specs,
        out_specs=[VMEM] * len(outs),
        scratch_shapes=scratch,
        compiler_params=pltpu.CompilerParams(
            collective_id=number, has_side_effects=True, vmem_limit_bytes=52 * 2**20
        ),
        cost_estimate=pl.CostEstimate(flops=flops, bytes_accessed=moved, transcendentals=0),
    )(*inputs)


def exchange_scratch(count, rows, length, width):
    return [
        pltpu.VMEM((count - 1, rows, length, width), BF16),
        pltpu.VMEM((count - 1, rows, length, width), BF16),
    ]


def semaphores(count):
    return [pltpu.SemaphoreType.DMA((2,))] + [pltpu.SemaphoreType.DMA((count - 1,))] * 4


class Block:
    def __init__(self, number, count, mod, segs, biases, own, other):
        self.number, self.count, self.mod = number, count, mod
        self.seg_own, self.seg_col, self.seg_row = segs
        self.bias_qv, self.bias_out, self.bias_one, self.bias_two = biases
        self.own, self.other = own, other

    def pair(self, which):
        return [self.own[which], self.other[which]]

    def forward(self, u):
        rows, length, width = u.shape
        count = self.count
        positions = length * count
        heads_width = self.own["out"].shape[0]
        hidden = self.own["one"].shape[1]
        heads = heads_width // HEAD_WIDTH
        wide = (rows, positions, heads * HEAD_LANES)
        local, full = (rows, length, width), (rows, positions, width)
        tokens = rows * positions
        self.u = u
        inputs = [u, self.mod, self.seg_own, self.seg_col, self.seg_row, self.bias_qv, self.bias_out]
        inputs += self.pair("qkv") + self.pair("out")
        (
            self.middle, self.branch_one, self.attn_full, self.q, self.k, self.v, self.probs, self.mixed
        ) = call(
            functools.partial(attend_kernel, count, self.number),
            self.number * 4,
            inputs,
            [VMEM] * 7 + [ANY] * 4,
            [
                (local, F32), (local, F32), (full, BF16), (wide, BF16), (wide, BF16), (wide, BF16),
                ((rows * heads, positions, positions), F32), ((rows, positions, heads_width), BF16),
            ],
            [
                pltpu.VMEM(full, BF16),
                pltpu.VMEM(self.own["qkv"].shape, BF16),
                pltpu.VMEM(self.own["out"].shape, BF16),
                pltpu.VMEM(wide, BF16),
            ] + exchange_scratch(count, *local) + semaphores(count),
            2 * tokens * width * heads_width * 4,
        )
        inputs = [self.middle, self.mod, self.seg_own, self.bias_one, self.bias_two]
        inputs += self.pair("one") + self.pair("two")
        out, self.branch_two, self.mlp_full, self.pre, self.act = call(
            functools.partial(mlp_kernel, count, self.number),
            self.number * 4 + 1,
            inputs,
            [VMEM] * 5 + [ANY] * 4,
            [
                (local, BF16), (local, F32), (full, BF16),
                ((rows, positions, hidden), F32), ((rows, positions, hidden), BF16),
            ],
            [
                pltpu.VMEM(full, BF16),
                pltpu.VMEM(self.own["one"].shape, BF16),
                pltpu.VMEM(self.own["two"].shape, BF16),
            ] + exchange_scratch(count, *local) + semaphores(count),
            2 * tokens * width * hidden * 2,
        )
        return out

    def backward_mlp(self, g):
        rows, length, width = g.shape
        count = self.count
        positions = length * count
        hidden = self.own["one"].shape[1]
        local, full = (rows, length, width), (rows, positions, width)
        inputs = [
            g, self.middle, self.branch_two, self.mod, self.seg_own, self.mlp_full, self.pre, self.act
        ] + self.pair("one") + self.pair("two")
        return call(
            functools.partial(mlp_back_kernel, count, self.number),
            self.number * 4 + 2,
            inputs,
            [VMEM] * 8 + [ANY] * 4,
            [
                (local, F32), ((3, rows, IMAGES_PER_ROW, width), F32),
                ((width, hidden), BF16), ((width, hidden), BF16),
                ((1, hidden), F32), ((1, width), F32),
            ],
            [
                pltpu.VMEM(full, BF16),
                pltpu.VMEM((rows, positions, hidden), BF16),
                pltpu.VMEM(self.own["one"].shape, BF16),
                pltpu.VMEM(self.own["two"].shape, BF16),
            ] + exchange_scratch(count, *local) + semaphores(count),
            2 * rows * positions * width * hidden * 4,
        )

    def backward_attend(self, d_middle):
        rows, length, width = d_middle.shape
        count = self.count
        positions = length * count
        heads_width = self.own["out"].shape[0]
        heads = heads_width // HEAD_WIDTH
        local, full = (rows, length, width), (rows, positions, width)
        inputs = [
            d_middle, self.u, self.branch_one, self.mod, self.seg_own, self.attn_full,
            self.q, self.k, self.v, self.probs, self.mixed,
        ] + self.pair("qkv") + self.pair("out")
        return call(
            functools.partial(attend_back_kernel, count, self.number),
            self.number * 4 + 3,
            inputs,
            [VMEM] * 11 + [ANY] * 4,
            [
                (local, F32), ((3, rows, IMAGES_PER_ROW, width), F32),
                ((3, width, heads_width), BF16), ((width, heads_width), BF16),
                ((2, heads_width), F32), ((1, width), F32),
            ],
            [
                pltpu.VMEM(full, BF16),
                pltpu.VMEM((4, rows, positions, heads * HEAD_LANES), BF16),
                pltpu.VMEM((3, rows, positions, heads_width), BF16),
                pltpu.VMEM(self.own["qkv"].shape, BF16),
                pltpu.VMEM(self.own["out"].shape, BF16),
            ] + exchange_scratch(count, *local) + semaphores(count),
            2 * rows * positions * width * heads_width * 8,
        )


def act_grad(function, source_rows, upstream):
    unused_value, pullback = jax.vjp(function, source_rows)
    return pullback(upstream)[0]


def gather_rows(source_rows):
    return lax.all_gather(source_rows, "tensor", axis=0, tiled=True)


def scatter_rows(terms):
    return lax.psum_scatter(
        terms.astype(BF16), "tensor", scatter_dimension=0, tiled=True
    ).astype(F32)


def align_pass(sent_rows, target_cols, proj_weights, total_token_count):
    p1_w, p1_b, p2_w, p2_b, p3_w, p3_b = proj_weights
    input_full = gather_rows(sent_rows)
    first_pre = dot(input_full, p1_w) + p1_b.astype(F32)
    first_act = jax.nn.silu(first_pre).astype(BF16)
    second_pre = scatter_rows(dot(first_act, p2_w)) + p2_b.astype(F32)
    second_act = jax.nn.silu(second_pre).astype(BF16)
    second_full = gather_rows(second_act)
    predicted = dot(second_full, p3_w) + p3_b.astype(F32)
    pred_sq, cross, target_sq = lax.psum(
        jnp.stack(
            [
                jnp.sum(predicted * predicted, axis=1),
                jnp.sum(predicted * target_cols, axis=1),
                jnp.sum(target_cols * target_cols, axis=1),
            ]
        ),
        "tensor",
    )
    inv_pred = lax.rsqrt(pred_sq + COSINE_EPS)
    inv_target = lax.rsqrt(target_sq + COSINE_EPS)
    cosine = cross * inv_pred * inv_target
    loss_local = jnp.sum(cosine)
    factor = -0.5 / total_token_count
    grad_pred = (
        (factor * inv_pred * inv_target)[:, None] * target_cols
        - (factor * cosine * inv_pred * inv_pred)[:, None] * predicted
    ).astype(BF16)
    grad_p3_b = jnp.sum(grad_pred.astype(F32), axis=0)
    grad_p3_w = dot(second_full, grad_pred, TN)
    grad_second_act = scatter_rows(dot(grad_pred, p3_w, NT))
    grad_second_pre = act_grad(jax.nn.silu, second_pre, grad_second_act).astype(BF16)
    grad_second_full = gather_rows(grad_second_pre)
    grad_p2_b = jnp.sum(grad_second_full.astype(F32), axis=0)
    grad_p2_w = dot(grad_second_full, first_act, TN)
    grad_first_act = dot(grad_second_full, p2_w, NT)
    grad_first_pre = act_grad(jax.nn.silu, first_pre, grad_first_act).astype(BF16)
    grad_p1_b = jnp.sum(grad_first_pre.astype(F32), axis=0)
    grad_p1_w = dot(input_full, grad_first_pre, TN)
    grad_sent = scatter_rows(dot(grad_first_pre, p1_w, NT))
    return (
        loss_local,
        grad_sent,
        (grad_p1_w, grad_p2_w, grad_p3_w),
        (grad_p1_b, grad_p2_b, grad_p3_b),
    )


def swap(value, axis, bit):
    size = lax.axis_size(axis)
    return lax.ppermute(value, axis, [(i, i ^ bit) for i in range(size)])


def halve(value, axis, bit, position):
    mine = (lax.axis_index(axis) & bit) // bit
    keep = lax.dynamic_index_in_dim(value, mine, position, keepdims=False)
    give = lax.dynamic_index_in_dim(value, 1 - mine, position, keepdims=False)
    got = swap(give, axis, bit)
    return (keep.astype(F32) + got.astype(F32)).astype(BF16)


def sum_over_dp(value):
    size = lax.axis_size("dp")
    bits = size.bit_length() - 1
    value = value.reshape((2,) * bits + (value.shape[0] // size, value.shape[1]))
    for bit in range(bits):
        value = halve(value, "dp", 1 << bit, bits - 1 - bit)
    return value


def send_to(value, owner):
    return lax.ppermute(value, "section", [(1 - owner, owner)])


def from_other(weight):
    share = weight.shape[0] // lax.axis_size("dp")
    part = lax.dynamic_slice_in_dim(weight, lax.axis_index("dp") * share, share, 0)
    return lax.all_gather(swap(part, "section", 1), "dp", axis=0, tiled=True)


def per_device(
    block_eight_input,
    cond,
    image_slot_index,
    targets,
    cot,
    ada_w,
    ada_b,
    query_key_value_weight,
    query_value_bias,
    attention_output_weight,
    attention_output_bias,
    hidden_weight,
    hidden_bias,
    output_weight_mlp,
    output_bias_mlp,
    p1_w,
    p1_b,
    p2_w,
    p2_b,
    p3_w,
    p3_b,
):
    section = lax.axis_index("section")
    tensor = lax.axis_index("tensor")
    is_first = section == 0
    count = lax.axis_size("tensor")
    sections = lax.axis_size("section")
    length, replica_rows, width = block_eight_input.shape
    positions = length * count
    rows = replica_rows // sections
    total_token_count = positions * replica_rows * lax.axis_size("dp")
    heads_width = attention_output_weight.shape[1]

    def my_rows(value, axis):
        return lax.dynamic_slice_in_dim(value, section * rows, rows, axis)

    def to_rows(value):
        return jnp.transpose(my_rows(value, 1), (1, 0, 2))

    own = {
        "qkv": jnp.transpose(query_key_value_weight[0], (1, 0, 2)),
        "out": attention_output_weight[0],
        "one": hidden_weight[0],
        "two": output_weight_mlp[0],
    }
    other = {}
    for name in ("qkv", "out", "one", "two"):
        shard = own[name]
        other[name] = from_other(shard.reshape(-1, shard.shape[-1])).reshape(shard.shape)

    cond_act = jax.nn.silu(cond.astype(F32)).astype(BF16)
    mod_local = jnp.einsum(
        "rsd,dc->rsc", cond_act, ada_w[0], preferred_element_type=F32
    ) + ada_b[0].astype(F32)
    mod_all = lax.all_gather(mod_local, ("section", "tensor"), axis=0, tiled=False)
    mod_all = mod_all.reshape(sections, count, replica_rows, IMAGES_PER_ROW, -1)
    mod_all = jnp.transpose(my_rows(mod_all, 2), (0, 2, 3, 1, 4))
    mod_all = mod_all.reshape(sections, rows, IMAGES_PER_ROW, 6, width)
    mod_all = jnp.transpose(mod_all, (0, 3, 1, 2, 4))
    biases = jnp.concatenate(
        [
            query_value_bias.reshape(-1),
            attention_output_bias.reshape(-1),
            hidden_bias.reshape(-1),
            output_bias_mlp.reshape(-1),
        ]
    ).astype(F32)
    other_biases = swap(biases, "section", 1)

    segs_full = my_rows(image_slot_index, 0)
    seg_own = lax.dynamic_slice_in_dim(segs_full, tensor * length, length, 1)
    segs = (seg_own[:, :, None], segs_full[:, :, None], segs_full[:, None, :])

    def make_block(number):
        values = jnp.where(section == number, biases, other_biases)
        cuts = [2 * heads_width, width, hidden_weight.shape[2], width]
        starts = [sum(cuts[:i]) for i in range(4)]
        pieces = [values[start : start + cut] for start, cut in zip(starts, cuts)]
        shaped = [pieces[0].reshape(2, heads_width)] + [piece[None] for piece in pieces[1:]]
        return Block(number, count, mod_all[number], segs, shaped, own, other)

    first, second = make_block(0), make_block(1)
    first_out = first.forward(to_rows(block_eight_input))
    second_out = second.forward(first_out)

    target_cols = my_rows(targets, 1).reshape(count, length, rows, -1)
    target_cols = jnp.transpose(target_cols, (0, 2, 1, 3)).reshape(rows * positions, -1)
    loss_local, grad_sent, proj_grads, proj_bias_grads = align_pass(
        first_out.reshape(rows * length, width),
        target_cols.astype(F32),
        (p1_w, p1_b, p2_w, p2_b, p3_w, p3_b),
        total_token_count,
    )

    sums = {}
    mods = {}
    bias_grads = {}

    def run_back(block, g):
        d_middle, mod_mlp, d_w1, d_w2, d_b1, d_b2 = block.backward_mlp(g)
        d_in, mod_attend, d_wqkv, d_wo, d_bqv, d_bo = block.backward_attend(d_middle)
        reduced = []
        for value in (d_w1, d_w2, d_wo):
            value = sum_over_dp(value)
            reduced.append((value, send_to(value, block.number)))
        parts = sum_over_dp(jnp.transpose(d_wqkv, (1, 0, 2)).reshape(width, 3 * heads_width))
        reduced.append((parts, send_to(parts, block.number)))
        sums[block.number] = [mine.astype(F32) + got.astype(F32) for mine, got in reduced]
        mods[block.number] = jnp.concatenate([mod_attend, mod_mlp], axis=0)
        bias_grads[block.number] = jnp.concatenate(
            [d_bqv.reshape(-1), d_bo[0], d_b1[0], d_b2[0]]
        )
        return d_in

    second_grad = run_back(second, to_rows(cot))
    first_grad = run_back(first, second_grad + grad_sent.reshape(rows, length, width))

    red_fc1, red_fc2, red_out, red_qkv = [
        jnp.where(is_first, one, two) for one, two in zip(sums[0], sums[1])
    ]

    mod_grad = jnp.stack([mods[0], mods[1]])
    mod_grad = jnp.transpose(mod_grad, (0, 2, 3, 1, 4)).reshape(
        sections, rows * IMAGES_PER_ROW, 6 * width
    )
    mod_grad = lax.psum_scatter(mod_grad, "tensor", scatter_dimension=2, tiled=True)
    mod_grad = lax.all_gather(mod_grad, ("dp", "section"), axis=0, tiled=False)
    mod_grad = lax.dynamic_index_in_dim(mod_grad, section, 1, keepdims=False)
    mod_grad = mod_grad.reshape(-1, mod_grad.shape[-1])
    cond_all = lax.all_gather(cond_act, "dp", axis=0, tiled=True).reshape(-1, width)
    share = width // lax.axis_size("dp")
    cond_cols = lax.dynamic_slice_in_dim(cond_all, lax.axis_index("dp") * share, share, 1)
    grad_ada_w = lax.dot_general(cond_cols.astype(F32), mod_grad, TN, precision=HIGHEST)
    grad_ada_b = jnp.sum(mod_grad, axis=0)

    small = jnp.stack([bias_grads[0], bias_grads[1]])
    small, loss_total, red_p1_b, red_p2_b, red_p3_b = lax.psum(
        (small, loss_local) + proj_bias_grads, ("section", "dp")
    )
    small = lax.dynamic_index_in_dim(small, section, 0, keepdims=False)
    align_loss = -0.5 * loss_total / total_token_count
    hidden = hidden_weight.shape[2]
    cut_one = 2 * heads_width
    red_qv_b = small[:cut_one].reshape(2, heads_width)
    red_out_b = small[cut_one : cut_one + width]
    red_fc1_b = small[cut_one + width : cut_one + width + hidden]
    red_fc2_b = small[cut_one + width + hidden :]

    grad_p1_w, grad_p2_w, grad_p3_w = proj_grads
    red_p1_w, red_p2_w, red_p3_w = [
        lax.psum_scatter(value.astype(BF16), ("section", "dp"), scatter_dimension=0, tiled=True)
        for value in (grad_p1_w, grad_p2_w, grad_p3_w)
    ]

    def place(one, two):
        got = swap(jnp.where(is_first, two, one), "section", 1).astype(one.dtype)
        keep = jnp.where(is_first, one, two)
        both = jnp.where(
            is_first, jnp.concatenate([keep, got], axis=0), jnp.concatenate([got, keep], axis=0)
        )
        return jnp.transpose(both, (1, 0, 2))[None]

    section_out = place(first_out, second_out)
    section_grad = place(first_grad.astype(BF16), second_grad.astype(BF16)).astype(F32)
    return (
        section_out,
        section_grad,
        align_loss,
        grad_ada_w[None],
        grad_ada_b[None],
        red_qkv.reshape(1, -1, 3, heads_width),
        red_qv_b[None],
        red_out.T[None],
        red_out_b[None],
        red_fc1[None],
        red_fc1_b[None],
        red_fc2.T[None],
        red_fc2_b[None],
        red_p1_w.astype(F32),
        red_p1_b,
        red_p2_w.T.astype(F32),
        red_p2_b,
        red_p3_w.astype(F32),
        red_p3_b,
    )


def solution(mesh):
    in_specs = (
        P("tensor", "dp", None),
        P("dp", None, None),
        P("dp", None),
        P(None, "dp", "tensor"),
        P("tensor", "dp", None),
        P("section", None, "tensor"),
        P("section", "tensor"),
        P("section", None, None, "tensor"),
        P("section", None, "tensor"),
        P("section", "tensor", None),
        P("section", None),
        P("section", None, "tensor"),
        P("section", "tensor"),
        P("section", "tensor", None),
        P("section", None),
        P(None, "tensor"),
        P("tensor"),
        P("tensor", None),
        P(),
        P(None, "tensor"),
        P("tensor"),
    )
    out_specs = (
        P("section", "tensor", "dp", None),
        P("section", "tensor", "dp", None),
        P(),
        P("section", "dp", "tensor"),
        P("section", "tensor"),
        P("section", "dp", None, "tensor"),
        P("section", None, "tensor"),
        P("section", "tensor", "dp"),
        P("section", None),
        P("section", "dp", "tensor"),
        P("section", "tensor"),
        P("section", "tensor", "dp"),
        P("section", None),
        P(("section", "dp"), "tensor"),
        P("tensor"),
        P("tensor", ("section", "dp")),
        P(),
        P(("section", "dp"), "tensor"),
        P("tensor"),
    )
    return jax.shard_map(
        per_device, mesh=mesh, in_specs=in_specs, out_specs=out_specs, check_vma=False
    )
```

```python
import functools
import math

import jax
import jax.numpy as jnp
from jax import lax
from jax.experimental import pallas as pl
from jax.experimental.pallas import tpu as pltpu
from jax.sharding import PartitionSpec as P

HEAD_WIDTH = 72
HEAD_LANES = 128
IMAGES_PER_ROW = 3
NORM_EPS = 1e-06
COSINE_EPS = 1e-06
MASKED_SCORE = -1e30
HIGHEST = lax.Precision.HIGHEST
MESH = pl.DeviceIdType.MESH
F32 = jnp.float32
BF16 = jnp.bfloat16
NN = (((1,), (0,)), ((), ()))
NT = (((1,), (1,)), ((), ()))
TN = (((0,), (0,)), ((), ()))


def dot(left, right, form=NN):
    return lax.dot_general(left, right, form, preferred_element_type=F32)


def z_peers(count):
    me = lax.axis_index("tensor")
    return [{"tensor": lax.rem(me + step, count)} for step in range(1, count)]


def x_peer():
    return {"section": 1 - lax.axis_index("section")}


def core_bit():
    return lax.rem(lax.axis_index("dp"), 2)


def y_bit():
    return lax.rem(lax.axis_index("dp") // 2, 2)


def core_peer():
    return {"dp": lax.axis_index("dp") + 1 - 2 * core_bit()}


def y_peer():
    return {"dp": lax.axis_index("dp") + 2 - 4 * y_bit()}


def greet(peers):
    barrier = pltpu.get_barrier_semaphore()
    for peer in peers:
        pl.semaphore_signal(barrier, inc=1, device_id=peer, device_id_type=MESH)
    pl.semaphore_wait(barrier, len(peers))


def remote(source, target, send_sem, recv_sem, peer):
    copy = pltpu.make_async_remote_copy(
        src_ref=source,
        dst_ref=target,
        send_sem=send_sem,
        recv_sem=recv_sem,
        device_id=peer,
        device_id_type=MESH,
    )
    copy.start()
    return copy


def local(source, target, sem):
    copy = pltpu.make_async_copy(source, target, sem)
    copy.start()
    return copy


def own_rows(me, length):
    return pl.ds(pl.multiple_of(me * length, 16), length)


def start_gather(full, length, count, sems):
    mine = full.at[:, own_rows(lax.axis_index("tensor"), length)]
    return [
        remote(mine, mine, sems[0].at[step], sems[1].at[step], peer)
        for step, peer in enumerate(z_peers(count))
    ]


def wait_all(copies):
    for copy in copies:
        copy.wait()


def scatter_sum(partial, length, count, buffers, sems):
    send_buf, recv_buf = buffers
    copies = []
    for step, peer in enumerate(z_peers(count)):
        term = partial(own_rows(peer["tensor"], length))
        send_buf[step] = term.astype(BF16).reshape(send_buf.shape[1:])
        copies.append(
            remote(send_buf.at[step], recv_buf.at[step], sems[2].at[step], sems[3].at[step], peer)
        )
    return copies, partial(own_rows(lax.axis_index("tensor"), length))


def finish_sum(copies, total, buffers):
    wait_all(copies)
    recv_buf = buffers[1]
    for step in range(recv_buf.shape[0]):
        total = total + recv_buf[step].reshape(total.shape).astype(F32)
    return total


def fetch(block, own_ref, other_ref, target, sem):
    mine = lax.axis_index("section") == block

    @pl.when(mine)
    def own_start():
        pltpu.make_async_copy(own_ref, target, sem).start()

    @pl.when(jnp.logical_not(mine))
    def other_start():
        pltpu.make_async_copy(other_ref, target, sem).start()

    return pltpu.make_async_copy(own_ref, target, sem)


def layer_norm(rows):
    centred = rows - jnp.mean(rows, axis=-1, keepdims=True)
    inverse = lax.rsqrt(jnp.mean(centred * centred, axis=-1, keepdims=True) + NORM_EPS)
    return centred * inverse, inverse


def norm_back(grad, normed, inverse):
    mean_grad = jnp.mean(grad, axis=-1, keepdims=True)
    mean_cross = jnp.mean(grad * normed, axis=-1, keepdims=True)
    return inverse * (grad - mean_grad - normed * mean_cross)


def token_mod(mod_ref, seg_ref, which):
    parts = []
    for row in range(seg_ref.shape[0]):
        seg = seg_ref[row]
        line = [
            mod_ref[which, pl.ds(row * IMAGES_PER_ROW + slot, 1), :]
            for slot in range(IMAGES_PER_ROW)
        ]
        value = line[-1]
        for slot in range(IMAGES_PER_ROW - 2, -1, -1):
            value = jnp.where(seg == slot, line[slot], value)
        parts.append(value)
    return jnp.concatenate(parts, axis=0)


def slot_sums(value, seg_ref, out_ref, which):
    length = seg_ref.shape[1]
    lines = []
    for row in range(seg_ref.shape[0]):
        seg = seg_ref[row]
        piece = value[row * length : (row + 1) * length]
        for slot in range(IMAGES_PER_ROW):
            lines.append(jnp.sum(jnp.where(seg == slot, piece, 0.0), axis=0, keepdims=True))
    spare = out_ref.shape[1] - len(lines)
    lines.append(jnp.zeros((spare, value.shape[1]), F32))
    out_ref[which] = jnp.concatenate(lines, axis=0)


def flat(ref):
    return ref[...].reshape(-1, ref.shape[-1])


def spread_matrix(width):
    lanes = width // HEAD_WIDTH * HEAD_LANES
    source = lax.broadcasted_iota(jnp.int32, (width, lanes), 0)
    target = lax.broadcasted_iota(jnp.int32, (width, lanes), 1)
    within = target & (HEAD_LANES - 1)
    head = target >> (HEAD_LANES.bit_length() - 1)
    hit = (within < HEAD_WIDTH) & (source == head * HEAD_WIDTH + within)
    return jnp.where(hit, 1.0, 0.0).astype(BF16)


def gelu_tanh(pre):
    inner = math.sqrt(2.0 / math.pi) * (pre + 0.044715 * (pre * pre * pre))
    return 0.5 * pre * (1.0 + jnp.tanh(inner))


def gelu_slope(pre):
    scale = math.sqrt(2.0 / math.pi)
    square = pre * pre
    tanh = jnp.tanh(scale * (pre + 0.044715 * (pre * square)))
    return 0.5 * (1.0 + tanh) + 0.5 * pre * (1.0 - tanh * tanh) * scale * (
        1.0 + 3 * 0.044715 * square
    )


def silu(value):
    return value / (1.0 + jnp.exp(-value))


class Share:
    def __init__(self, own, other, parts, sems):
        self.own, self.other, self.parts = own, other, parts
        self.send, self.recv = sems
        self.size = own.shape[0] // parts
        self.copies = []

    def rows(self, core, y):
        part = core if self.parts == 2 else core + 2 * y
        return pl.ds(pl.multiple_of(part * self.size, 16), self.size)

    def begin(self):
        rows = self.rows(core_bit(), y_bit())
        self.first = remote(
            self.own.at[rows], self.other.at[rows], self.send.at[0], self.recv.at[0], x_peer()
        )

    def forward(self):
        self.first.wait()
        mine = self.other.at[self.rows(core_bit(), y_bit())]
        self.copies.append(remote(mine, mine, self.send.at[1], self.recv.at[1], core_peer()))
        if self.parts == 4:
            self.second = remote(mine, mine, self.send.at[2], self.recv.at[2], y_peer())

    def forward_again(self):
        if self.parts == 4:
            self.second.wait()
            got = self.other.at[self.rows(core_bit(), 1 - y_bit())]
            self.copies.append(remote(got, got, self.send.at[3], self.recv.at[3], core_peer()))

    def finish(self):
        wait_all(self.copies)


class Courier:
    def __init__(self, grad, out, scratch):
        self.grad, self.out = grad, out
        self.keep, self.from_core, self.from_y, self.part, self.from_x, self.sems = scratch
        self.size = grad.shape[-2] // 4

    def rows(self, core, y):
        part = pl.ds(pl.multiple_of((core + 2 * y) * self.size, 16), self.size)
        return self.grad.at[:, part] if len(self.grad.shape) == 3 else self.grad.at[part]

    def begin(self):
        core, self.copies = core_bit(), []
        for y in range(2):
            self.copies.append(
                remote(
                    self.rows(1 - core, y), self.from_core.at[y],
                    self.sems.at[0, y], self.sems.at[1, y], core_peer(),
                )
            )
            self.copies.append(local(self.rows(core, y), self.keep.at[y], self.sems.at[2, y]))

    def to_y(self):
        wait_all(self.copies)
        for y in range(2):
            self.keep[y] = (self.keep[y].astype(F32) + self.from_core[y].astype(F32)).astype(BF16)
        self.copies = [
            remote(
                self.keep.at[1 - y_bit()], self.from_y,
                self.sems.at[0, 2], self.sems.at[1, 2], y_peer(),
            )
        ]

    def to_x(self):
        wait_all(self.copies)
        mine = self.keep[y_bit()].astype(F32) + self.from_y[...].astype(F32)
        self.part[...] = mine.astype(BF16)
        self.copies = [
            remote(self.part, self.from_x, self.sems.at[0, 3], self.sems.at[1, 3], x_peer())
        ]

    def finish(self):
        wait_all(self.copies)
        self.out[...] = self.part[...].astype(F32) + self.from_x[...].astype(F32)


COURIER_REFS = 6


def quarter(shape):
    return shape[:-2] + (shape[-2] // 4, shape[-1])


def courier_scratch(shape):
    part = quarter(shape)
    return [
        pltpu.VMEM((2,) + part, BF16),
        pltpu.VMEM((2,) + part, BF16),
        pltpu.VMEM(part, BF16),
        pltpu.VMEM(part, BF16),
        pltpu.VMEM(part, BF16),
        pltpu.SemaphoreType.DMA((3, 4)),
    ]


def make_couriers(grads, outs, scratch):
    return [
        Courier(grad, out, scratch[COURIER_REFS * i : COURIER_REFS * (i + 1)])
        for i, (grad, out) in enumerate(zip(grads, outs))
    ]


def courier_peers(couriers):
    return [core_peer(), y_peer(), x_peer()] if couriers else []


def attend_body(
    count, peers, u_ref, mods, segs, biases, outs, scratch, sems, need_qkv, need_out, steps
):
    middle_ref, branch_ref, full_ref, q_ref, k_ref, v_ref, probs_ref, mixed_ref = outs
    full, wqkv, wo, mixed_wide = scratch[:4]
    buffers = scratch[4:6]
    seg_own, seg_col, seg_row = segs
    mod_ref = mods()
    me = lax.axis_index("tensor")
    rows, length, width = u_ref.shape
    heads_width = wo.shape[0]
    heads = heads_width // HEAD_WIDTH
    u = flat(u_ref).astype(F32)
    normed, unused = layer_norm(u)
    attn_in = normed * (1.0 + token_mod(mod_ref, seg_own, 1)) + token_mod(mod_ref, seg_own, 0)
    full[:, own_rows(me, length), :] = attn_in.astype(BF16).reshape(rows, length, width)
    if peers is not None:
        greet(peers)
    gather = start_gather(full, length, count, sems)
    steps[0]()
    spread = spread_matrix(heads_width)
    need_qkv()
    wait_all(gather)
    full_ref[...] = full[...]
    tokens = flat(full)
    bias = biases()
    for which, target in ((0, q_ref), (1, k_ref), (2, v_ref)):
        projected = dot(tokens, wqkv[pl.ds(which * width, width), :])
        if which != 1:
            projected = projected + bias[which // 2 : which // 2 + 1, :heads_width]
        target[...] = dot(projected.astype(BF16), spread).astype(BF16).reshape(target.shape)

    def one_head(index, carry):
        row = index // heads
        head = lax.rem(index, heads)
        lanes = pl.ds(pl.multiple_of(head * HEAD_LANES, HEAD_LANES), HEAD_LANES)
        scores = dot(q_ref[row, :, lanes], k_ref[row, :, lanes], NT) * HEAD_WIDTH ** (-0.5)
        scores = jnp.where(seg_col[row] == seg_row[row], scores, MASKED_SCORE)
        raised = jnp.exp(scores - jnp.max(scores, axis=-1, keepdims=True))
        probs = raised / jnp.sum(raised, axis=-1, keepdims=True)
        probs_ref[index] = probs
        mixed_wide[row, :, lanes] = dot(probs.astype(BF16), v_ref[row, :, lanes]).astype(BF16)
        return carry

    lax.fori_loop(0, rows * heads, one_head, 0)
    mixed_ref[...] = dot(flat(mixed_wide), spread, NT).astype(BF16).reshape(mixed_ref.shape)
    need_out()

    def partial(which_rows):
        return dot(mixed_ref[:, which_rows, :].reshape(rows * length, heads_width), wo[...])

    copies, total = scatter_sum(partial, length, count, buffers, sems)
    steps[1]()
    branch = finish_sum(copies, total, buffers) + bias[2:3, :]
    branch_ref[...] = branch.reshape(branch_ref.shape)
    middle = flat(u_ref).astype(F32) + token_mod(mod_ref, seg_own, 2) * branch
    middle_ref[...] = middle.reshape(middle_ref.shape)


def nothing():
    pass


def open_kernel(count, sections, *refs):
    u_ref, cond_ref, ada_b_ref, biases_ref, seg_own, seg_col, seg_row = refs[:7]
    ada_w, own_qkv, own_out, own_one, own_two = refs[7:12]
    mods_ref, bias_ref, other_qkv, other_out, other_one, other_two = refs[12:18]
    outs = refs[18:26]
    scratch = refs[26:32]
    ada, mod_src, mod_buf, bias_buf, w_sem, ag_send, ag_recv, rs_send, rs_recv = refs[32:41]
    mod_send, mod_recv, share_send, share_recv, ada_sem = refs[41:]
    wqkv, wo = scratch[1:3]
    section, tensor = lax.axis_index("section"), lax.axis_index("tensor")
    load_ada = local(ada_w, ada, ada_sem)
    shares = [
        Share(own, other, parts, (share_send.at[i], share_recv.at[i]))
        for i, (own, other, parts) in enumerate(
            (
                (own_qkv, other_qkv, 4), (own_out, other_out, 2),
                (own_one, other_one, 4), (own_two, other_two, 4),
            )
        )
    ]
    plane = [
        {"section": lax.rem(section + a, sections), "tensor": lax.rem(tensor + b, count)}
        for a in range(sections)
        for b in range(count)
        if a or b
    ]
    greet(plane + [core_peer(), y_peer()])
    for share in shares:
        share.begin()
    bias_buf[section] = biases_ref[...]
    bias_copy = remote(
        biases_ref, bias_buf.at[section],
        mod_send.at[len(plane)], mod_recv.at[len(plane)], x_peer(),
    )
    cond_act = silu(cond_ref[...].astype(F32)).astype(BF16)
    load_ada.wait()
    mod = dot(cond_act, ada[...]) + ada_b_ref[...].astype(F32)
    mod_src[...] = mod.reshape(mod_src.shape)
    mod_buf[section, tensor] = mod_src[section]
    copies = [
        remote(
            mod_src.at[peer["section"]], mod_buf.at[section, tensor],
            mod_send.at[i], mod_recv.at[i], peer,
        )
        for i, peer in enumerate(plane)
    ]

    def mods():
        wait_all(copies)
        width, piece = mods_ref.shape[-1], mod_buf.shape[-1]
        for block in range(sections):
            for which in range(6):
                parts, at = [], which * width
                while at < (which + 1) * width:
                    end = min((at // piece + 1) * piece, (which + 1) * width)
                    start = at - at // piece * piece
                    parts.append(mod_buf[block, at // piece][:, start : start + end - at])
                    at = end
                mods_ref[block, which] = (
                    jnp.concatenate(parts, axis=1) if len(parts) > 1 else parts[0]
                )
        return mods_ref.at[0]

    def biases():
        bias_copy.wait()
        bias_ref[...] = bias_buf[...]
        return bias_buf[0]

    def need_qkv():
        fetch(0, own_qkv, other_qkv, wqkv, w_sem.at[0]).wait()

    def need_out():
        fetch(0, own_out, other_out, wo, w_sem.at[1]).wait()

    def after_gather():
        shares[0].forward()
        shares[1].forward()
        shares[0].forward_again()
        shares[2].forward()
        shares[0].finish()
        shares[1].finish()

    def after_scatter():
        shares[2].forward_again()
        shares[3].forward()
        shares[3].forward_again()

    attend_body(
        count, None, u_ref, mods, (seg_own, seg_col, seg_row), biases, outs, scratch,
        (ag_send, ag_recv, rs_send, rs_recv), need_qkv, need_out, (after_gather, after_scatter),
    )
    shares[2].finish()
    shares[3].finish()


def attend_kernel(count, block, *refs):
    u_ref, mods_ref, bias_ref, seg_own, seg_col, seg_row = refs[:6]
    own_qkv, other_qkv, own_out, other_out = refs[6:10]
    outs, scratch, w_sem = refs[10:18], refs[18:24], refs[24]
    load_qkv = fetch(block, own_qkv, other_qkv, scratch[1], w_sem.at[0])
    load_out = fetch(block, own_out, other_out, scratch[2], w_sem.at[1])
    attend_body(
        count, z_peers(count), u_ref, lambda: mods_ref.at[block], (seg_own, seg_col, seg_row),
        lambda: bias_ref[block], outs, scratch, refs[25:29],
        load_qkv.wait, load_out.wait, (nothing, nothing),
    )


def mlp_kernel(
    count, block,
    middle_ref, mods_ref, bias_ref, seg_own, w1_own, w1_other, w2_own, w2_other,
    out_ref, branch_ref, full_ref, pre_ref, act_ref,
    full, w1, w2, send_buf, recv_buf, w_sem, *sems,
):
    me = lax.axis_index("tensor")
    rows, length, width = middle_ref.shape
    mod_ref = mods_ref.at[block]
    load_one = fetch(block, w1_own, w1_other, w1, w_sem.at[0])
    load_two = fetch(block, w2_own, w2_other, w2, w_sem.at[1])
    normed, unused = layer_norm(flat(middle_ref))
    mlp_in = normed * (1.0 + token_mod(mod_ref, seg_own, 4)) + token_mod(mod_ref, seg_own, 3)
    full[:, own_rows(me, length), :] = mlp_in.astype(BF16).reshape(rows, length, width)
    greet(z_peers(count))
    gather = start_gather(full, length, count, sems)
    load_one.wait()
    wait_all(gather)
    full_ref[...] = full[...]
    pre = dot(flat(full), w1[...]) + bias_ref[block, 3:4, : w1.shape[1]]
    pre_ref[...] = pre.reshape(pre_ref.shape)
    act_ref[...] = gelu_tanh(pre).astype(BF16).reshape(act_ref.shape)
    load_two.wait()

    def partial(which_rows):
        return dot(act_ref[:, which_rows, :].reshape(rows * length, -1), w2[...])

    buffers = (send_buf, recv_buf)
    copies, total = scatter_sum(partial, length, count, buffers, sems)
    branch = finish_sum(copies, total, buffers) + bias_ref[block, 4:5, :]
    branch_ref[...] = branch.reshape(branch_ref.shape)
    out = flat(middle_ref) + token_mod(mod_ref, seg_own, 5) * branch
    out_ref[...] = out.astype(BF16).reshape(out_ref.shape)


def mlp_back_kernel(count, block, loads, *refs):
    g_ref, middle_ref, branch_ref, mods_ref, seg_own, full_ref, pre_ref, act_ref = refs[:8]
    w1_own, w1_other, w2_own, w2_other = refs[8:12]
    grads, refs = refs[12 : 12 + loads], refs[12 + loads :]
    d_middle_ref, d_mod_ref, d_w1_ref, d_w2_ref, d_b1_ref, d_b2_ref = refs[:6]
    sums, refs = refs[6 : 6 + loads], refs[6 + loads :]
    full, d_pre, w1, w2, send_buf, recv_buf, w_sem = refs[:7]
    sems, couriers = refs[7:11], make_couriers(grads, sums, refs[11:])
    me = lax.axis_index("tensor")
    rows, length, width = middle_ref.shape
    mod_ref = mods_ref.at[block]
    load_one = fetch(block, w1_own, w1_other, w1, w_sem.at[0])
    load_two = fetch(block, w2_own, w2_other, w2, w_sem.at[1])
    g = flat(g_ref).astype(F32)
    d_branch = (g * token_mod(mod_ref, seg_own, 5)).astype(BF16)
    full[:, own_rows(me, length), :] = d_branch.reshape(rows, length, width)
    greet(z_peers(count) + courier_peers(couriers))
    gather = start_gather(full, length, count, sems)
    for courier in couriers:
        courier.begin()
    slot_sums(g * flat(branch_ref), seg_own, d_mod_ref, 2)
    for courier in couriers:
        courier.to_y()
    load_two.wait()
    wait_all(gather)
    d_act = dot(flat(full), w2[...], NT)
    d_pre[...] = (d_act * gelu_slope(flat(pre_ref))).astype(BF16).reshape(d_pre.shape)
    load_one.wait()

    def partial(which_rows):
        return dot(d_pre[:, which_rows, :].reshape(rows * length, -1), w1[...], NT)

    buffers = (send_buf, recv_buf)
    copies, total = scatter_sum(partial, length, count, buffers, sems)
    for courier in couriers:
        courier.to_x()
    d_b2_ref[...] = jnp.sum(flat(full).astype(F32), axis=0, keepdims=True)
    d_b1_ref[...] = jnp.sum(flat(d_pre).astype(F32), axis=0, keepdims=True)
    d_w2_ref[...] = dot(flat(full), flat(act_ref), TN).astype(BF16)
    d_w1_ref[...] = dot(flat(full_ref), flat(d_pre), TN).astype(BF16)
    d_in = finish_sum(copies, total, buffers)
    normed, inverse = layer_norm(flat(middle_ref))
    d_middle = flat(g_ref).astype(F32) + norm_back(
        d_in * (1.0 + token_mod(mod_ref, seg_own, 4)), normed, inverse
    )
    d_middle_ref[...] = d_middle.reshape(d_middle_ref.shape)
    slot_sums(d_in, seg_own, d_mod_ref, 0)
    slot_sums(d_in * normed, seg_own, d_mod_ref, 1)
    for courier in couriers:
        courier.finish()


def attend_back_kernel(count, block, loads, *refs):
    d_middle_ref, u_ref, branch_ref, mods_ref, seg_own, full_ref = refs[:6]
    q_ref, k_ref, v_ref, probs_ref, mixed_ref = refs[6:11]
    wqkv_own, wqkv_other, wo_own, wo_other = refs[11:15]
    grads, refs = refs[15 : 15 + loads], refs[15 + loads :]
    d_in_ref, d_mod_ref, d_wqkv_ref, d_wo_ref, d_bqv_ref, d_bo_ref = refs[:6]
    sums, refs = refs[6 : 6 + loads], refs[6 + loads :]
    full, wide, narrow, wqkv, wo, send_buf, recv_buf, w_sem = refs[:8]
    sems, couriers = refs[8:12], make_couriers(grads, sums, refs[12:])
    me = lax.axis_index("tensor")
    rows, length, width = u_ref.shape
    heads_width = wo.shape[0]
    heads = heads_width // HEAD_WIDTH
    mod_ref = mods_ref.at[block]
    load_qkv = fetch(block, wqkv_own, wqkv_other, wqkv, w_sem.at[0])
    load_out = fetch(block, wo_own, wo_other, wo, w_sem.at[1])
    d_middle = flat(d_middle_ref)
    d_branch = (d_middle * token_mod(mod_ref, seg_own, 2)).astype(BF16)
    full[:, own_rows(me, length), :] = d_branch.reshape(rows, length, width)
    greet(z_peers(count) + courier_peers(couriers))
    gather = start_gather(full, length, count, sems)
    for courier in couriers:
        courier.begin()
    slot_sums(d_middle * flat(branch_ref), seg_own, d_mod_ref, 2)
    spread = spread_matrix(heads_width)
    for courier in couriers:
        courier.to_y()
    load_out.wait()
    wait_all(gather)
    d_mixed = dot(flat(full), wo[...], NT).astype(BF16)
    wide[3] = dot(d_mixed, spread).astype(BF16).reshape(wide.shape[1:])

    def one_head(index, carry):
        row = index // heads
        head = lax.rem(index, heads)
        lanes = pl.ds(pl.multiple_of(head * HEAD_LANES, HEAD_LANES), HEAD_LANES)
        grad = wide[3, row, :, lanes]
        probs = probs_ref[index]
        d_probs = dot(grad, v_ref[row, :, lanes], NT)
        d_scores = (
            probs * (d_probs - jnp.sum(d_probs * probs, axis=-1, keepdims=True))
        ).astype(BF16)
        scale = HEAD_WIDTH ** (-0.5)
        wide[0, row, :, lanes] = (dot(d_scores, k_ref[row, :, lanes]) * scale).astype(BF16)
        wide[1, row, :, lanes] = (dot(d_scores, q_ref[row, :, lanes], TN) * scale).astype(BF16)
        wide[2, row, :, lanes] = dot(probs.astype(BF16), grad, TN).astype(BF16)
        return carry

    lax.fori_loop(0, rows * heads, one_head, 0)
    for which in range(3):
        narrow[which] = (
            dot(flat(wide.at[which]), spread, NT).astype(BF16).reshape(narrow.shape[1:])
        )
    load_qkv.wait()

    def partial(which_rows):
        total = 0.0
        for which in range(3):
            total = total + dot(
                narrow[which, :, which_rows, :].reshape(rows * length, heads_width),
                wqkv[pl.ds(which * width, width), :],
                NT,
            )
        return total

    buffers = (send_buf, recv_buf)
    copies, total = scatter_sum(partial, length, count, buffers, sems)
    for courier in couriers:
        courier.to_x()
    d_bo_ref[...] = jnp.sum(flat(full).astype(F32), axis=0, keepdims=True)
    d_bqv_ref[0:1, :] = jnp.sum(flat(narrow.at[0]).astype(F32), axis=0, keepdims=True)
    d_bqv_ref[1:2, :] = jnp.sum(flat(narrow.at[2]).astype(F32), axis=0, keepdims=True)
    d_wo_ref[...] = dot(flat(full), flat(mixed_ref), TN).astype(BF16)
    for which in range(3):
        d_wqkv_ref[which] = dot(flat(full_ref), flat(narrow.at[which]), TN).astype(BF16)
    d_attn_in = finish_sum(copies, total, buffers)
    normed, inverse = layer_norm(flat(u_ref).astype(F32))
    d_in = flat(d_middle_ref) + norm_back(
        d_attn_in * (1.0 + token_mod(mod_ref, seg_own, 1)), normed, inverse
    )
    d_in_ref[...] = d_in.reshape(d_in_ref.shape)
    slot_sums(d_attn_in, seg_own, d_mod_ref, 0)
    slot_sums(d_attn_in * normed, seg_own, d_mod_ref, 1)
    for courier in couriers:
        courier.finish()


def close_kernel(count, sections, replicas, *refs):
    outs_ref, grads_ref, mod_refs, small_refs = refs[:2], refs[2:4], refs[4:8], refs[8:17]
    cond_ref, wqkv_grad, wo_grad = refs[17:20]
    out_ref, grad_ref, ada_w_ref, ada_b_ref, small_ref, qkv_sum, wo_sum = refs[20:27]
    z_src, z_buf, mod_src, mod_buf, small_src, small_buf, cond_buf = refs[27:34]
    place_src, place_buf = refs[34:36]
    sems = refs[36:38]
    couriers = make_couriers((wqkv_grad, wo_grad), (qkv_sum, wo_sum), refs[38:])
    section, tensor, replica = (lax.axis_index(name) for name in ("section", "tensor", "dp"))
    send, recv = sems
    others = [
        {"section": lax.rem(section + a, sections), "dp": lax.rem(replica + b, replicas)}
        for a in range(sections)
        for b in range(replicas)
        if a or b
    ]
    greet(z_peers(count) + others)
    for courier in couriers:
        courier.begin()
    piece = z_src.shape[-1]
    for block in range(sections):
        attend_mod, mlp_mod = mod_refs[2 * block : 2 * block + 2]
        width = attend_mod.shape[-1]
        for part in range(count):
            at, end, cuts = part * piece, (part + 1) * piece, []
            while at < end:
                which = at // width
                stop = min((which + 1) * width, end)
                ref = attend_mod if which < 3 else mlp_mod
                cuts.append(ref[which % 3][:, at - which * width : stop - which * width])
                at = stop
            z_src[part, block] = jnp.concatenate(cuts, axis=1) if len(cuts) > 1 else cuts[0]
    z_copies = [
        remote(z_src.at[peer["tensor"]], z_buf.at[i], send.at[i], recv.at[i], peer)
        for i, peer in enumerate(z_peers(count))
    ]
    at = count - 1
    @pl.when(section == 0)
    def first_place():
        place_src[0] = outs_ref[1][...]
        place_src[1] = grads_ref[1][...].astype(BF16)

    @pl.when(section != 0)
    def second_place():
        place_src[0] = outs_ref[0][...]
        place_src[1] = grads_ref[0][...].astype(BF16)

    place_copy = remote(place_src, place_buf, send.at[at], recv.at[at], x_peer())
    at = at + 1
    heads_width = small_refs[0].shape[-1]
    small_src[...] = jnp.zeros_like(small_src)
    for block in range(sections):
        d_bqv, d_bo, d_b1, d_b2 = small_refs[4 * block : 4 * block + 4]
        small_src[block, 0:2, :heads_width] = d_bqv[...]
        small_src[block, 2:3, :] = d_bo[...]
        small_src[block, 3:4, : d_b1.shape[1]] = d_b1[...]
        small_src[block, 4:5, :] = d_b2[...]
        small_src[block, 5:8, :] = small_refs[8][...]
    small_buf[section, replica] = small_src[section]
    cond_buf[section, replica] = cond_ref[replica]
    copies = []
    for peer in others:
        copies.append(
            remote(
                small_src.at[peer["section"]], small_buf.at[section, replica],
                send.at[at], recv.at[at], peer,
            )
        )
        copies.append(
            remote(
                cond_ref.at[peer["dp"]], cond_buf.at[section, replica],
                send.at[at + 1], recv.at[at + 1], peer,
            )
        )
        at = at + 2
    for courier in couriers:
        courier.to_y()
    wait_all(z_copies)
    mine = z_src[tensor]
    for step in range(count - 1):
        mine = mine + z_buf[step]
    mod_src[...] = mine
    mod_buf[section, replica] = mod_src[section]
    for peer in others:
        copies.append(
            remote(
                mod_src.at[peer["section"]], mod_buf.at[section, replica],
                send.at[at], recv.at[at], peer,
            )
        )
        at = at + 1
    for courier in couriers:
        courier.to_x()
    place_copy.wait()
    rows = place_buf.shape[1]

    @pl.when(section == 0)
    def first_out():
        out_ref[:rows] = outs_ref[0][...]
        grad_ref[:rows] = grads_ref[0][...]
        out_ref[rows:] = place_buf[0]
        grad_ref[rows:] = place_buf[1].astype(F32)

    @pl.when(section != 0)
    def second_out():
        out_ref[rows:] = outs_ref[1][...]
        grad_ref[rows:] = grads_ref[1][...]
        out_ref[:rows] = place_buf[0]
        grad_ref[:rows] = place_buf[1].astype(F32)

    wait_all(copies)
    small = small_buf[0, 0]
    for a in range(sections):
        for b in range(replicas):
            if a or b:
                small = small + small_buf[a, b]
    small_ref[...] = small
    mod_all = flat(mod_buf)
    ada_b_ref[...] = jnp.sum(mod_all, axis=0, keepdims=True)
    ada_w_ref[...] = lax.dot_general(
        flat(cond_buf), mod_all, TN, precision=HIGHEST, preferred_element_type=F32
    )
    for courier in couriers:
        courier.finish()


VMEM = pl.BlockSpec(memory_space=pltpu.VMEM)
ANY = pl.BlockSpec(memory_space=pl.ANY)
MOD_ROWS = 8


def call(kernel, number, inputs, in_any, outs, out_any, scratch, flops):
    moved = sum(math.prod(one.shape) * one.dtype.itemsize for one in inputs)
    return pl.pallas_call(
        kernel,
        out_shape=[jax.ShapeDtypeStruct(shape, dtype) for shape, dtype in outs],
        in_specs=[VMEM] * (len(inputs) - in_any) + [ANY] * in_any,
        out_specs=[ANY if i in out_any else VMEM for i in range(len(outs))],
        scratch_shapes=scratch,
        compiler_params=pltpu.CompilerParams(
            collective_id=number, has_side_effects=True, vmem_limit_bytes=56 * 2**20
        ),
        cost_estimate=pl.CostEstimate(flops=flops, bytes_accessed=moved, transcendentals=0),
    )(*inputs)


def exchange_scratch(count, rows, length, width):
    return [
        pltpu.VMEM((count - 1, rows, length, width), BF16),
        pltpu.VMEM((count - 1, rows, length, width), BF16),
    ]


def semaphores(count):
    return [pltpu.SemaphoreType.DMA((2,))] + [pltpu.SemaphoreType.DMA((count - 1,))] * 4


class Shapes:
    def __init__(self, u, own, count):
        self.rows, self.length, self.width = u.shape
        self.count = count
        self.positions = self.length * count
        self.tokens = self.rows * self.positions
        self.heads_width = own["out"].shape[0]
        self.hidden = own["one"].shape[1]
        self.heads = self.heads_width // HEAD_WIDTH
        self.local = (self.rows, self.length, self.width)
        self.full = (self.rows, self.positions, self.width)
        self.wide = (self.rows, self.positions, self.heads * HEAD_LANES)
        self.own = own
        self.attend_outs = [
            (self.local, F32), (self.local, F32), (self.full, BF16),
            (self.wide, BF16), (self.wide, BF16), (self.wide, BF16),
            ((self.rows * self.heads, self.positions, self.positions), F32),
            ((self.rows, self.positions, self.heads_width), BF16),
        ]
        self.attend_scratch = [
            pltpu.VMEM(self.full, BF16),
            pltpu.VMEM(own["qkv"].shape, BF16),
            pltpu.VMEM(own["out"].shape, BF16),
            pltpu.VMEM(self.wide, BF16),
        ] + exchange_scratch(count, *self.local)
        self.mods = (3, MOD_ROWS, self.width)


def pairs(own, other, names):
    out = []
    for name in names:
        out += [own[name], other[name]]
    return out


def open_forward(sizes, u, cond, ada_w, ada_b, biases, segs, own, sections):
    count, width = sizes.count, sizes.width
    piece = ada_w.shape[1]
    inputs = [u, cond, ada_b, biases, *segs, ada_w] + [own[n] for n in ("qkv", "out", "one", "two")]
    plane = sections * count - 1
    results = call(
        functools.partial(open_kernel, count, sections),
        0,
        inputs,
        5,
        [((sections, 6, MOD_ROWS, width), F32), ((sections,) + biases.shape, F32)]
        + [(own[n].shape, BF16) for n in ("qkv", "out", "one", "two")]
        + sizes.attend_outs,
        (2, 3, 4, 5),
        sizes.attend_scratch
        + [
            pltpu.VMEM(ada_w.shape, BF16),
            pltpu.VMEM((sections, MOD_ROWS, piece), F32),
            pltpu.VMEM((sections, count, MOD_ROWS, piece), F32),
            pltpu.VMEM((sections,) + biases.shape, F32),
        ]
        + semaphores(count)
        + [
            pltpu.SemaphoreType.DMA((plane + 1,)),
            pltpu.SemaphoreType.DMA((plane + 1,)),
            pltpu.SemaphoreType.DMA((4, 4)),
            pltpu.SemaphoreType.DMA((4, 4)),
            pltpu.SemaphoreType.DMA,
        ],
        2 * sizes.tokens * width * sizes.heads_width * 4,
    )
    other = dict(zip(("qkv", "out", "one", "two"), results[2:6]))
    return results[0], results[1], other, results[6:]


def attend_forward(sizes, block, u, mods, biases, segs, own, other):
    inputs = [u, mods, biases, *segs] + pairs(own, other, ("qkv", "out"))
    return call(
        functools.partial(attend_kernel, sizes.count, block),
        1,
        inputs,
        4,
        sizes.attend_outs,
        (),
        sizes.attend_scratch + semaphores(sizes.count),
        2 * sizes.tokens * sizes.width * sizes.heads_width * 4,
    )


def mlp_forward(sizes, block, middle, mods, biases, segs, own, other):
    inputs = [middle, mods, biases, segs[0]] + pairs(own, other, ("one", "two"))
    hidden = (sizes.rows, sizes.positions, sizes.hidden)
    return call(
        functools.partial(mlp_kernel, sizes.count, block),
        2 + block,
        inputs,
        4,
        [
            (sizes.local, BF16), (sizes.local, F32), (sizes.full, BF16),
            (hidden, F32), (hidden, BF16),
        ],
        (),
        [
            pltpu.VMEM(sizes.full, BF16),
            pltpu.VMEM(own["one"].shape, BF16),
            pltpu.VMEM(own["two"].shape, BF16),
        ]
        + exchange_scratch(sizes.count, *sizes.local)
        + semaphores(sizes.count),
        2 * sizes.tokens * sizes.width * sizes.hidden * 2,
    )


def mlp_backward(sizes, block, g, attend, mlp, mods, segs, own, other, loads):
    out, branch, full, pre, act = mlp
    inputs = [g, attend[0], branch, mods, segs[0], full, pre, act]
    inputs += pairs(own, other, ("one", "two")) + list(loads)
    carried = [scratch for load in loads for scratch in courier_scratch(load.shape)]
    return call(
        functools.partial(mlp_back_kernel, sizes.count, block, len(loads)),
        4 + block,
        inputs,
        4 + len(loads),
        [
            (sizes.local, F32), (sizes.mods, F32),
            ((sizes.width, sizes.hidden), BF16), ((sizes.width, sizes.hidden), BF16),
            ((1, sizes.hidden), F32), ((1, sizes.width), F32),
        ]
        + [(quarter(load.shape), F32) for load in loads],
        (),
        [
            pltpu.VMEM(sizes.full, BF16),
            pltpu.VMEM((sizes.rows, sizes.positions, sizes.hidden), BF16),
            pltpu.VMEM(own["one"].shape, BF16),
            pltpu.VMEM(own["two"].shape, BF16),
        ]
        + exchange_scratch(sizes.count, *sizes.local)
        + semaphores(sizes.count)
        + carried,
        2 * sizes.tokens * sizes.width * sizes.hidden * 4,
    )


def attend_backward(sizes, block, d_middle, u, attend, mods, segs, own, other, loads):
    middle, branch, full, q, k, v, probs, mixed = attend
    inputs = [d_middle, u, branch, mods, segs[0], full, q, k, v, probs, mixed]
    inputs += pairs(own, other, ("qkv", "out")) + list(loads)
    carried = [scratch for load in loads for scratch in courier_scratch(load.shape)]
    return call(
        functools.partial(attend_back_kernel, sizes.count, block, len(loads)),
        6 + block,
        inputs,
        4 + len(loads),
        [
            (sizes.local, F32), (sizes.mods, F32),
            ((3, sizes.width, sizes.heads_width), BF16), ((sizes.width, sizes.heads_width), BF16),
            ((2, sizes.heads_width), F32), ((1, sizes.width), F32),
        ]
        + [(quarter(load.shape), F32) for load in loads],
        (),
        [
            pltpu.VMEM(sizes.full, BF16),
            pltpu.VMEM((4,) + sizes.wide, BF16),
            pltpu.VMEM((3, sizes.rows, sizes.positions, sizes.heads_width), BF16),
            pltpu.VMEM(own["qkv"].shape, BF16),
            pltpu.VMEM(own["out"].shape, BF16),
        ]
        + exchange_scratch(sizes.count, *sizes.local)
        + semaphores(sizes.count)
        + carried,
        2 * sizes.tokens * sizes.width * sizes.heads_width * 8,
    )


def close_backward(sizes, outs, grads, mod_grads, small, proj_small, cond, loads, sections, replicas):
    count, width = sizes.count, sizes.width
    piece = 6 * width // count
    share = width // replicas
    inputs = [*outs, *grads, *mod_grads, *small, proj_small, cond, *loads]
    copies = count + 3 * (sections * replicas - 1)
    carried = [scratch for load in loads for scratch in courier_scratch(load.shape)]
    both = (sections * sizes.rows,) + sizes.local[1:]
    return call(
        functools.partial(close_kernel, count, sections, replicas),
        8,
        inputs,
        len(loads),
        [
            (both, BF16), (both, F32), ((share, piece), F32), ((1, piece), F32),
            ((MOD_ROWS, width), F32),
        ]
        + [(quarter(load.shape), F32) for load in loads],
        (),
        [
            pltpu.VMEM((count, sections, MOD_ROWS, piece), F32),
            pltpu.VMEM((count - 1, sections, MOD_ROWS, piece), F32),
            pltpu.VMEM((sections, MOD_ROWS, piece), F32),
            pltpu.VMEM((sections, replicas, MOD_ROWS, piece), F32),
            pltpu.VMEM((sections, MOD_ROWS, width), F32),
            pltpu.VMEM((sections, replicas, MOD_ROWS, width), F32),
            pltpu.VMEM((sections, replicas, MOD_ROWS, share), F32),
            pltpu.VMEM((2,) + sizes.local, BF16),
            pltpu.VMEM((2,) + sizes.local, BF16),
            pltpu.SemaphoreType.DMA((copies,)),
            pltpu.SemaphoreType.DMA((copies,)),
        ]
        + carried,
        2 * sections * replicas * MOD_ROWS * share * piece,
    )


def act_grad(function, source_rows, upstream):
    unused_value, pullback = jax.vjp(function, source_rows)
    return pullback(upstream)[0]


def gather_rows(source_rows):
    return lax.all_gather(source_rows, "tensor", axis=0, tiled=True)


def scatter_rows(terms):
    return lax.psum_scatter(
        terms.astype(BF16), "tensor", scatter_dimension=0, tiled=True
    ).astype(F32)


def align_pass(sent_rows, target_cols, proj_weights, total_token_count):
    p1_w, p1_b, p2_w, p2_b, p3_w, p3_b = proj_weights
    input_full = gather_rows(sent_rows)
    first_pre = dot(input_full, p1_w) + p1_b.astype(F32)
    first_act = jax.nn.silu(first_pre).astype(BF16)
    second_pre = scatter_rows(dot(first_act, p2_w)) + p2_b.astype(F32)
    second_act = jax.nn.silu(second_pre).astype(BF16)
    second_full = gather_rows(second_act)
    predicted = dot(second_full, p3_w) + p3_b.astype(F32)
    pred_sq, cross, target_sq = lax.psum(
        jnp.stack(
            [
                jnp.sum(predicted * predicted, axis=1),
                jnp.sum(predicted * target_cols, axis=1),
                jnp.sum(target_cols * target_cols, axis=1),
            ]
        ),
        "tensor",
    )
    inv_pred = lax.rsqrt(pred_sq + COSINE_EPS)
    inv_target = lax.rsqrt(target_sq + COSINE_EPS)
    cosine = cross * inv_pred * inv_target
    loss_local = jnp.sum(cosine)
    factor = -0.5 / total_token_count
    grad_pred = (
        (factor * inv_pred * inv_target)[:, None] * target_cols
        - (factor * cosine * inv_pred * inv_pred)[:, None] * predicted
    ).astype(BF16)
    grad_p3_b = jnp.sum(grad_pred.astype(F32), axis=0)
    grad_p3_w = dot(second_full, grad_pred, TN)
    grad_second_act = scatter_rows(dot(grad_pred, p3_w, NT))
    grad_second_pre = act_grad(jax.nn.silu, second_pre, grad_second_act).astype(BF16)
    grad_second_full = gather_rows(grad_second_pre)
    grad_p2_b = jnp.sum(grad_second_full.astype(F32), axis=0)
    grad_p2_w = dot(grad_second_full, first_act, TN)
    grad_first_act = dot(grad_second_full, p2_w, NT)
    grad_first_pre = act_grad(jax.nn.silu, first_pre, grad_first_act).astype(BF16)
    grad_p1_b = jnp.sum(grad_first_pre.astype(F32), axis=0)
    grad_p1_w = dot(input_full, grad_first_pre, TN)
    grad_sent = scatter_rows(dot(grad_first_pre, p1_w, NT))
    return (
        loss_local,
        grad_sent,
        (grad_p1_w, grad_p2_w, grad_p3_w),
        (grad_p1_b, grad_p2_b, grad_p3_b),
    )


def halve(value, axis, bit, position):
    size = lax.axis_size(axis)
    mine = (lax.axis_index(axis) & bit) // bit
    keep = lax.dynamic_index_in_dim(value, mine, position, keepdims=False)
    give = lax.dynamic_index_in_dim(value, 1 - mine, position, keepdims=False)
    return keep + lax.ppermute(give, axis, [(i, i ^ bit) for i in range(size)])


def sum_beyond_quads(value):
    size = lax.axis_size("dp")
    if size == 4:
        return value
    quads = size // 4
    bits = quads.bit_length() - 1
    lead = value.ndim - 2
    shape = value.shape
    value = value.reshape(shape[:lead] + (2,) * bits + (shape[-2] // quads, shape[-1]))
    for bit in range(bits):
        value = halve(value, "dp", 4 << bit, lead + bits - 1 - bit)
    route = [(high * 4 + low, low * quads + high) for high in range(quads) for low in range(4)]
    return lax.ppermute(value, "dp", route)


def per_device(
    block_eight_input,
    cond,
    image_slot_index,
    targets,
    cot,
    ada_w,
    ada_b,
    query_key_value_weight,
    query_value_bias,
    attention_output_weight,
    attention_output_bias,
    hidden_weight,
    hidden_bias,
    output_weight_mlp,
    output_bias_mlp,
    p1_w,
    p1_b,
    p2_w,
    p2_b,
    p3_w,
    p3_b,
):
    section = lax.axis_index("section")
    tensor = lax.axis_index("tensor")
    is_first = section == 0
    count = lax.axis_size("tensor")
    sections = lax.axis_size("section")
    replicas = lax.axis_size("dp")
    length, replica_rows, width = block_eight_input.shape
    positions = length * count
    rows = replica_rows // sections
    total_token_count = positions * replica_rows * replicas
    heads_width = attention_output_weight.shape[1]
    hidden = hidden_weight.shape[2]

    def my_rows(value, axis):
        return lax.dynamic_slice_in_dim(value, section * rows, rows, axis)

    def to_rows(value):
        return jnp.transpose(my_rows(value, 1), (1, 0, 2))

    own = {
        "qkv": jnp.transpose(query_key_value_weight[0], (1, 0, 2)).reshape(3 * width, heads_width),
        "out": attention_output_weight[0],
        "one": hidden_weight[0],
        "two": output_weight_mlp[0],
    }

    def padded(value):
        return jnp.pad(value.astype(F32), ((0, 0), (0, width - value.shape[-1])))

    biases = jnp.concatenate(
        [
            padded(query_value_bias[0]), padded(attention_output_bias), padded(hidden_bias),
            padded(output_bias_mlp), jnp.zeros((MOD_ROWS - 5, width), F32),
        ],
        axis=0,
    )
    used = rows * IMAGES_PER_ROW
    cond_pad = jnp.pad(
        cond.reshape(sections, used, width), ((0, 0), (0, MOD_ROWS - used), (0, 0))
    )
    segs_full = my_rows(image_slot_index, 0)
    seg_own = lax.dynamic_slice_in_dim(segs_full, tensor * length, length, 1)
    segs = (seg_own[:, :, None], segs_full[:, :, None], segs_full[:, None, :])

    u = to_rows(block_eight_input)
    sizes = Shapes(u, own, count)
    mods, bias_all, other, attend_one = open_forward(
        sizes, u, cond_pad.reshape(-1, width), ada_w[0], ada_b, biases, segs, own, sections
    )
    mlp_one = mlp_forward(sizes, 0, attend_one[0], mods, bias_all, segs, own, other)
    first_out = mlp_one[0]
    attend_two = attend_forward(sizes, 1, first_out, mods, bias_all, segs, own, other)
    mlp_two = mlp_forward(sizes, 1, attend_two[0], mods, bias_all, segs, own, other)
    second_out = mlp_two[0]

    target_cols = my_rows(targets, 1).reshape(count, length, rows, -1)
    target_cols = jnp.transpose(target_cols, (0, 2, 1, 3)).reshape(rows * positions, -1)
    loss_local, grad_sent, proj_grads, proj_bias_grads = align_pass(
        first_out.reshape(rows * length, width),
        target_cols.astype(F32),
        (p1_w, p1_b, p2_w, p2_b, p3_w, p3_b),
        total_token_count,
    )

    back = (mods, segs, own, other)
    d_middle_two, mod_mlp_two, *mlp_grads_two = mlp_backward(
        sizes, 1, to_rows(cot), attend_two, mlp_two, *back, ()
    )
    second_grad, mod_attend_two, *attend_grads_two = attend_backward(
        sizes, 1, d_middle_two, first_out, attend_two, *back, mlp_grads_two[:2]
    )
    sums_mlp_two = attend_grads_two[4:]
    d_middle_one, mod_mlp_one, *mlp_grads_one = mlp_backward(
        sizes, 0, second_grad + grad_sent.reshape(rows, length, width), attend_one, mlp_one, *back,
        attend_grads_two[:2],
    )
    sums_attend_two = mlp_grads_one[4:]
    first_grad, mod_attend_one, *attend_grads_one = attend_backward(
        sizes, 0, d_middle_one, u, attend_one, *back, mlp_grads_one[:2]
    )
    sums_mlp_one = attend_grads_one[4:]

    p1_len, p2_len, p3_len = p1_b.shape[0], p2_b.shape[0], p3_b.shape[0]
    d_p1_b, d_p2_b, d_p3_b = proj_bias_grads
    flat_small = jnp.concatenate([d_p2_b, d_p1_b, d_p3_b, loss_local[None]])
    proj_small = jnp.pad(flat_small, (0, 3 * width - flat_small.shape[0])).reshape(3, width)
    cond_act = silu(my_rows(cond, 0).astype(F32)).astype(BF16).astype(F32)
    share = width // replicas
    cond_cols = jnp.pad(cond_act.reshape(used, width), ((0, MOD_ROWS - used), (0, 0)))
    cond_cols = jnp.transpose(cond_cols.reshape(MOD_ROWS, replicas, share), (1, 0, 2))
    small = [
        attend_grads_one[2], attend_grads_one[3], mlp_grads_one[2], mlp_grads_one[3],
        attend_grads_two[2], attend_grads_two[3], mlp_grads_two[2], mlp_grads_two[3],
    ]
    section_out, section_grad, grad_ada_w, grad_ada_b, small, *sums_attend_one = close_backward(
        sizes, (first_out, second_out), (first_grad, second_grad),
        (mod_attend_one, mod_mlp_one, mod_attend_two, mod_mlp_two),
        small, proj_small, cond_cols, attend_grads_one[:2], sections, replicas,
    )

    red_fc1, red_fc2, red_qkv, red_out = [
        sum_beyond_quads(jnp.where(is_first, one, two))
        for one, two in zip(
            list(sums_mlp_one) + list(sums_attend_one), list(sums_mlp_two) + list(sums_attend_two)
        )
    ]
    flat_small = small[5:8].reshape(-1)
    red_p2_b = flat_small[:p2_len]
    red_p1_b = flat_small[p2_len : p2_len + p1_len]
    red_p3_b = flat_small[p2_len + p1_len : p2_len + p1_len + p3_len]
    loss_total = flat_small[p2_len + p1_len + p3_len]
    align_loss = -0.5 * loss_total / total_token_count

    grad_p1_w, grad_p2_w, grad_p3_w = proj_grads
    red_p1_w, red_p2_w, red_p3_w = [
        lax.psum_scatter(value.astype(BF16), ("section", "dp"), scatter_dimension=0, tiled=True)
        for value in (grad_p1_w, grad_p2_w, grad_p3_w)
    ]
    return (
        jnp.transpose(section_out, (1, 0, 2))[None],
        jnp.transpose(section_grad, (1, 0, 2))[None],
        align_loss,
        grad_ada_w[None],
        grad_ada_b,
        jnp.transpose(red_qkv, (1, 0, 2))[None],
        small[0:2, :heads_width][None],
        red_out.T[None],
        small[2:3],
        red_fc1[None],
        small[3:4, :hidden],
        red_fc2.T[None],
        small[4:5],
        red_p1_w.astype(F32),
        red_p1_b,
        red_p2_w.T.astype(F32),
        red_p2_b,
        red_p3_w.astype(F32),
        red_p3_b,
    )


def solution(mesh):
    in_specs = (
        P("tensor", "dp", None),
        P("dp", None, None),
        P("dp", None),
        P(None, "dp", "tensor"),
        P("tensor", "dp", None),
        P("section", None, "tensor"),
        P("section", "tensor"),
        P("section", None, None, "tensor"),
        P("section", None, "tensor"),
        P("section", "tensor", None),
        P("section", None),
        P("section", None, "tensor"),
        P("section", "tensor"),
        P("section", "tensor", None),
        P("section", None),
        P(None, "tensor"),
        P("tensor"),
        P("tensor", None),
        P(),
        P(None, "tensor"),
        P("tensor"),
    )
    out_specs = (
        P("section", "tensor", "dp", None),
        P("section", "tensor", "dp", None),
        P(),
        P("section", "dp", "tensor"),
        P("section", "tensor"),
        P("section", "dp", None, "tensor"),
        P("section", None, "tensor"),
        P("section", "tensor", "dp"),
        P("section", None),
        P("section", "dp", "tensor"),
        P("section", "tensor"),
        P("section", "tensor", "dp"),
        P("section", None),
        P(("section", "dp"), "tensor"),
        P("tensor"),
        P("tensor", ("section", "dp")),
        P(),
        P(("section", "dp"), "tensor"),
        P("tensor"),
    )
    return jax.shard_map(
        per_device, mesh=mesh, in_specs=in_specs, out_specs=out_specs, check_vma=False
    )
```

```python
import functools
import math

import jax
import jax.numpy as jnp
from jax import lax
from jax.experimental import pallas as pl
from jax.experimental.pallas import tpu as pltpu
from jax.sharding import PartitionSpec as P

HEAD_WIDTH = 72
HEAD_LANES = 128
IMAGES_PER_ROW = 3
NORM_EPS = 1e-06
COSINE_EPS = 1e-06
MASKED_SCORE = -1e30
HIGHEST = lax.Precision.HIGHEST
MESH = pl.DeviceIdType.MESH
F32 = jnp.float32
BF16 = jnp.bfloat16
NN = (((1,), (0,)), ((), ()))
NT = (((1,), (1,)), ((), ()))
TN = (((0,), (0,)), ((), ()))


def dot(left, right, form=NN):
    return lax.dot_general(left, right, form, preferred_element_type=F32)


def z_peers(count):
    me = lax.axis_index("tensor")
    return [{"tensor": lax.rem(me + step, count)} for step in range(1, count)]


def x_peer():
    return {"section": 1 - lax.axis_index("section")}


def core_bit():
    return lax.rem(lax.axis_index("dp"), 2)


def y_bit():
    return lax.rem(lax.axis_index("dp") // 2, 2)


def core_peer():
    return {"dp": lax.axis_index("dp") + 1 - 2 * core_bit()}


def y_peer():
    return {"dp": lax.axis_index("dp") + 2 - 4 * y_bit()}


def greet(peers):
    barrier = pltpu.get_barrier_semaphore()
    for peer in peers:
        pl.semaphore_signal(barrier, inc=1, device_id=peer, device_id_type=MESH)
    pl.semaphore_wait(barrier, len(peers))


def remote(source, target, send_sem, recv_sem, peer):
    copy = describe(source, target, send_sem, recv_sem, peer)
    copy.start()
    return copy


def local(source, target, sem):
    copy = pltpu.make_async_copy(source, target, sem)
    copy.start()
    return copy


def own_rows(me, length):
    return pl.ds(pl.multiple_of(me * length, 16), length)


def describe(source, target, send_sem, recv_sem, peer):
    return pltpu.make_async_remote_copy(
        src_ref=source,
        dst_ref=target,
        send_sem=send_sem,
        recv_sem=recv_sem,
        device_id=peer,
        device_id_type=MESH,
    )


def wait_all(copies):
    for copy in copies:
        copy.wait()


class Line:
    def __init__(self, length, sems):
        self.length, (self.ag_send, self.ag_recv, self.rs_send, self.rs_recv) = length, sems
        self.me = lax.axis_index("tensor")
        self.mirror = 3 - self.me
        self.near = self.me + 1 - 2 * lax.rem(self.me, 2)
        self.opposite = lax.rem(self.me + 2, 4)
        self.is_end = jnp.logical_or(self.me == 0, self.me == 3)
        self.is_middle = jnp.logical_not(self.is_end)

    def block(self, full, place, which, peer):
        part = full.at[:, own_rows(place, self.length)]
        return describe(
            part, part, self.ag_send.at[which], self.ag_recv.at[place], {"tensor": peer}
        )

    def start_gather(self, full):
        self.block(full, self.me, 0, self.opposite).start()
        self.block(full, self.me, 1, self.near).start()

        @pl.when(self.is_middle)
        def to_mirror():
            self.block(full, self.me, 2, self.mirror).start()

    def relay(self, full):
        self.block(full, self.opposite, 2, self.mirror).wait_recv()

        @pl.when(self.is_middle)
        def pass_on():
            self.block(full, self.opposite, 3, 3 - self.opposite).start()

    def finish_gather(self, full):
        self.block(full, self.near, 1, self.near).wait_recv()
        self.block(full, self.mirror, 1, self.near).wait_recv()
        self.block(full, self.me, 0, self.opposite).wait_send()
        self.block(full, self.me, 1, self.near).wait_send()

        @pl.when(self.is_middle)
        def sent():
            self.block(full, self.me, 2, self.mirror).wait_send()
            self.block(full, self.opposite, 3, 3 - self.opposite).wait_send()

    def scatter_sum(self, partial, buffers):
        send_buf, recv_buf, relay_buf = buffers
        me, relay_sem = self.me, 4

        def term(peer):
            return partial(own_rows(peer, self.length))

        def keep(which, value):
            send_buf[which] = value.astype(BF16).reshape(send_buf.shape[1:])

        self.to_mirror = describe(
            send_buf.at[0], recv_buf.at[me], self.rs_send.at[0], self.rs_recv.at[me],
            {"tensor": self.mirror},
        )
        self.to_relay = describe(
            send_buf.at[0], relay_buf, self.rs_send.at[0], self.rs_recv.at[relay_sem],
            {"tensor": self.near},
        )
        self.to_near = describe(
            send_buf.at[1], recv_buf.at[me], self.rs_send.at[1], self.rs_recv.at[me],
            {"tensor": self.near},
        )
        self.to_opposite = describe(
            send_buf.at[2], recv_buf.at[me], self.rs_send.at[2], self.rs_recv.at[me],
            {"tensor": self.opposite},
        )
        keep(0, term(self.mirror))

        @pl.when(self.is_end)
        def first_end():
            self.to_relay.start()
            relay_buf[...] = jnp.zeros_like(relay_buf)
            recv_buf[self.mirror] = jnp.zeros(recv_buf.shape[1:], BF16)

        @pl.when(self.is_middle)
        def first_middle():
            self.to_mirror.start()

        keep(1, term(self.near))
        self.to_near.start()
        last = term(self.opposite)

        @pl.when(self.is_middle)
        def relayed():
            self.to_relay.wait_recv()

        keep(2, last + relay_buf[...].reshape(last.shape).astype(F32))
        self.to_opposite.start()
        return term(me)

    def finish_sum(self, total, buffers):
        send_buf, recv_buf, relay_buf = buffers

        def got(source):
            describe(
                send_buf.at[1], recv_buf.at[source], self.rs_send.at[1], self.rs_recv.at[source],
                {"tensor": self.near},
            ).wait_recv()

        got(self.near)
        got(self.opposite)

        @pl.when(self.is_middle)
        def third():
            got(self.mirror)

        self.to_near.wait_send()
        self.to_opposite.wait_send()
        self.to_mirror.wait_send()
        for source in (self.near, self.opposite, self.mirror):
            total = total + recv_buf[source].reshape(total.shape).astype(F32)
        return total


def fetch(block, own_ref, other_ref, target, sem):
    mine = lax.axis_index("section") == block

    @pl.when(mine)
    def own_start():
        pltpu.make_async_copy(own_ref, target, sem).start()

    @pl.when(jnp.logical_not(mine))
    def other_start():
        pltpu.make_async_copy(other_ref, target, sem).start()

    return pltpu.make_async_copy(own_ref, target, sem)


def layer_norm(rows):
    centred = rows - jnp.mean(rows, axis=-1, keepdims=True)
    inverse = lax.rsqrt(jnp.mean(centred * centred, axis=-1, keepdims=True) + NORM_EPS)
    return centred * inverse, inverse


def norm_back(grad, normed, inverse):
    mean_grad = jnp.mean(grad, axis=-1, keepdims=True)
    mean_cross = jnp.mean(grad * normed, axis=-1, keepdims=True)
    return inverse * (grad - mean_grad - normed * mean_cross)


def token_mod(mod_ref, seg_ref, which):
    parts = []
    for row in range(seg_ref.shape[0]):
        seg = seg_ref[row]
        line = [
            mod_ref[which, pl.ds(row * IMAGES_PER_ROW + slot, 1), :]
            for slot in range(IMAGES_PER_ROW)
        ]
        value = line[-1]
        for slot in range(IMAGES_PER_ROW - 2, -1, -1):
            value = jnp.where(seg == slot, line[slot], value)
        parts.append(value)
    return jnp.concatenate(parts, axis=0)


def slot_sums(value, seg_ref, out_ref, which):
    length = seg_ref.shape[1]
    lines = []
    for row in range(seg_ref.shape[0]):
        seg = seg_ref[row]
        piece = value[row * length : (row + 1) * length]
        for slot in range(IMAGES_PER_ROW):
            lines.append(jnp.sum(jnp.where(seg == slot, piece, 0.0), axis=0, keepdims=True))
    spare = out_ref.shape[1] - len(lines)
    lines.append(jnp.zeros((spare, value.shape[1]), F32))
    out_ref[which] = jnp.concatenate(lines, axis=0)


def flat(ref):
    return ref[...].reshape(-1, ref.shape[-1])


def spread_matrix(width):
    lanes = width // HEAD_WIDTH * HEAD_LANES
    source = lax.broadcasted_iota(jnp.int32, (width, lanes), 0)
    target = lax.broadcasted_iota(jnp.int32, (width, lanes), 1)
    within = target & (HEAD_LANES - 1)
    head = target >> (HEAD_LANES.bit_length() - 1)
    hit = (within < HEAD_WIDTH) & (source == head * HEAD_WIDTH + within)
    return jnp.where(hit, 1.0, 0.0).astype(BF16)


def gelu_tanh(pre):
    inner = math.sqrt(2.0 / math.pi) * (pre + 0.044715 * (pre * pre * pre))
    return 0.5 * pre * (1.0 + jnp.tanh(inner))


def gelu_slope(pre):
    scale = math.sqrt(2.0 / math.pi)
    square = pre * pre
    tanh = jnp.tanh(scale * (pre + 0.044715 * (pre * square)))
    return 0.5 * (1.0 + tanh) + 0.5 * pre * (1.0 - tanh * tanh) * scale * (
        1.0 + 3 * 0.044715 * square
    )


def silu(value):
    return value / (1.0 + jnp.exp(-value))


class Share:
    def __init__(self, own, other, parts, sems):
        self.own, self.other, self.parts = own, other, parts
        self.send, self.recv = sems
        self.size = own.shape[0] // parts
        self.copies = []

    def rows(self, core, y):
        part = core if self.parts == 2 else core + 2 * y
        return pl.ds(pl.multiple_of(part * self.size, 16), self.size)

    def begin(self):
        rows = self.rows(core_bit(), y_bit())
        self.first = remote(
            self.own.at[rows], self.other.at[rows], self.send.at[0], self.recv.at[0], x_peer()
        )

    def forward(self, first):
        if first is not None:
            first.wait()
        mine = self.other.at[self.rows(core_bit(), y_bit())]
        self.copies.append(remote(mine, mine, self.send.at[1], self.recv.at[1], core_peer()))
        if self.parts == 4:
            self.second = remote(mine, mine, self.send.at[2], self.recv.at[2], y_peer())

    def forward_again(self):
        if self.parts == 4:
            self.second.wait()
            got = self.other.at[self.rows(core_bit(), 1 - y_bit())]
            self.copies.append(remote(got, got, self.send.at[3], self.recv.at[3], core_peer()))

    def finish(self):
        wait_all(self.copies)


class Cargo:
    inputs, outs, scratch, aliases, any_outs = (), (), (), {}, False

    def bind(self, inputs, outs, scratch):
        self.ins, self.out_refs, self.held = inputs, outs, scratch

    def peers(self):
        return []

    def begin(self):
        pass

    def middle(self):
        pass

    def end(self):
        pass


def quarter(shape):
    return shape[:-2] + (shape[-2] // 4, shape[-1])


class QuadSum(Cargo):
    def __init__(self, grad):
        part = quarter(grad.shape)
        self.inputs = (grad,)
        self.outs = ((part, BF16),)
        self.size = grad.shape[-2] // 4
        self.scratch = (
            pltpu.VMEM((2,) + part, BF16),
            pltpu.VMEM((2,) + part, BF16),
            pltpu.VMEM(part, BF16),
            pltpu.SemaphoreType.DMA((3, 3)),
        )

    def peers(self):
        return ["core", "y"]

    def rows(self, core, y):
        grad = self.ins[0]
        part = pl.ds(pl.multiple_of((core + 2 * y) * self.size, 16), self.size)
        return grad.at[:, part] if len(grad.shape) == 3 else grad.at[part]

    def begin(self):
        keep, from_core, from_y, sems = self.held
        core, self.copies = core_bit(), []
        for y in range(2):
            self.copies.append(
                remote(
                    self.rows(1 - core, y), from_core.at[y], sems.at[0, y], sems.at[1, y], core_peer()
                )
            )
            self.copies.append(local(self.rows(core, y), keep.at[y], sems.at[2, y]))

    def middle(self):
        keep, from_core, from_y, sems = self.held
        wait_all(self.copies)
        for y in range(2):
            keep[y] = (keep[y].astype(F32) + from_core[y].astype(F32)).astype(BF16)
        self.copies = [
            remote(keep.at[1 - y_bit()], from_y, sems.at[0, 2], sems.at[1, 2], y_peer())
        ]

    def end(self):
        keep, from_core, from_y, sems = self.held
        wait_all(self.copies)
        self.out_refs[0][...] = (
            keep[y_bit()].astype(F32) + from_y[...].astype(F32)
        ).astype(BF16)


class SectionSum(Cargo):
    def __init__(self, part):
        self.inputs = (part,)
        self.outs = ((part.shape, F32),)
        self.scratch = (
            pltpu.VMEM(part.shape, BF16),
            pltpu.VMEM(part.shape, BF16),
            pltpu.SemaphoreType.DMA((3,)),
        )

    def peers(self):
        return ["x"]

    def begin(self):
        mine, other, sems = self.held
        self.copies = [
            local(self.ins[0], mine, sems.at[2]),
            remote(self.ins[0], other, sems.at[0], sems.at[1], x_peer()),
        ]

    def end(self):
        mine, other, sems = self.held
        wait_all(self.copies)
        self.out_refs[0][...] = mine[...].astype(F32) + other[...].astype(F32)


class LastSum(QuadSum):
    def __init__(self, grad):
        super().__init__(grad)
        part = quarter(grad.shape)
        self.outs = ((part, F32),)
        self.scratch = self.scratch + (
            pltpu.VMEM(part, BF16),
            pltpu.VMEM(part, BF16),
            pltpu.SemaphoreType.DMA((2,)),
        )

    def peers(self):
        return ["core", "y", "x"]

    def begin(self):
        self.all_held = self.held
        self.held, self.last = self.held[:4], self.held[4:]
        super().begin()

    def to_x(self):
        keep, from_core, from_y, sems = self.held
        mine, other, last_sems = self.last
        wait_all(self.copies)
        mine[...] = (keep[y_bit()].astype(F32) + from_y[...].astype(F32)).astype(BF16)
        self.copies = [remote(mine, other, last_sems.at[0], last_sems.at[1], x_peer())]

    def end(self):
        mine, other, last_sems = self.last
        wait_all(self.copies)
        self.out_refs[0][...] = mine[...].astype(F32) + other[...].astype(F32)


class LateShare(Cargo):
    any_outs = True

    def __init__(self, other):
        self.inputs = (other,)
        self.outs = ((other.shape, BF16),)
        self.aliases = {0: 0}
        self.scratch = (pltpu.SemaphoreType.DMA((4,)), pltpu.SemaphoreType.DMA((4,)))

    def peers(self):
        return ["core", "y"]

    def begin(self):
        out = self.out_refs[0]
        self.share = Share(out, out, 4, self.held)
        self.share.forward(None)

    def middle(self):
        self.share.forward_again()
        self.share.finish()


class Bundle:
    def __init__(self, cargos):
        self.cargos = cargos

    def peers(self):
        names = [name for cargo in self.cargos for name in cargo.peers()]
        known = {"core": core_peer, "y": y_peer, "x": x_peer}
        return [make() for name, make in known.items() if name in names]

    def begin(self):
        for cargo in self.cargos:
            cargo.begin()

    def middle(self):
        for cargo in self.cargos:
            cargo.middle()

    def end(self):
        for cargo in self.cargos:
            cargo.end()


def attend_body(
    count, peers, u_ref, mods, segs, biases, outs, scratch, sems, need_qkv, need_out, steps
):
    middle_ref, branch_ref, full_ref, q_ref, k_ref, v_ref, probs_ref, mixed_ref = outs
    full, wqkv, wo, mixed_wide = scratch[:4]
    buffers = scratch[4:7]
    seg_own, seg_col, seg_row = segs
    mod_ref = mods()
    me = lax.axis_index("tensor")
    rows, length, width = u_ref.shape
    heads_width = wo.shape[0]
    heads = heads_width // HEAD_WIDTH
    u = flat(u_ref).astype(F32)
    normed, unused = layer_norm(u)
    attn_in = normed * (1.0 + token_mod(mod_ref, seg_own, 1)) + token_mod(mod_ref, seg_own, 0)
    full[:, own_rows(me, length), :] = attn_in.astype(BF16).reshape(rows, length, width)
    if peers is not None:
        greet(peers)
    line = Line(length, sems)
    line.start_gather(full)
    spread = spread_matrix(heads_width)
    line.relay(full)
    steps[0]()
    need_qkv()
    line.finish_gather(full)
    full_ref[...] = full[...]
    tokens = flat(full)
    bias = biases()
    for which, target in ((0, q_ref), (1, k_ref), (2, v_ref)):
        projected = dot(tokens, wqkv[pl.ds(which * width, width), :])
        if which != 1:
            projected = projected + bias[which // 2 : which // 2 + 1, :heads_width]
        target[...] = dot(projected.astype(BF16), spread).astype(BF16).reshape(target.shape)

    def one_head(index, carry):
        row = index // heads
        head = lax.rem(index, heads)
        lanes = pl.ds(pl.multiple_of(head * HEAD_LANES, HEAD_LANES), HEAD_LANES)
        scores = dot(q_ref[row, :, lanes], k_ref[row, :, lanes], NT) * HEAD_WIDTH ** (-0.5)
        scores = jnp.where(seg_col[row] == seg_row[row], scores, MASKED_SCORE)
        raised = jnp.exp(scores - jnp.max(scores, axis=-1, keepdims=True))
        probs = raised / jnp.sum(raised, axis=-1, keepdims=True)
        probs_ref[index] = probs
        mixed_wide[row, :, lanes] = dot(probs.astype(BF16), v_ref[row, :, lanes]).astype(BF16)
        return carry

    lax.fori_loop(0, rows * heads, one_head, 0)
    mixed_ref[...] = dot(flat(mixed_wide), spread, NT).astype(BF16).reshape(mixed_ref.shape)
    need_out()

    def partial(which_rows):
        return dot(mixed_ref[:, which_rows, :].reshape(rows * length, heads_width), wo[...])

    total = line.scatter_sum(partial, buffers)
    steps[1]()
    branch = line.finish_sum(total, buffers) + bias[2:3, :]
    branch_ref[...] = branch.reshape(branch_ref.shape)
    middle = flat(u_ref).astype(F32) + token_mod(mod_ref, seg_own, 2) * branch
    middle_ref[...] = middle.reshape(middle_ref.shape)


def open_kernel(count, sections, *refs, cargo):
    u_ref, cond_ref, ada_b_ref, biases_ref, seg_own, seg_col, seg_row = refs[:7]
    ada_w, own_qkv, own_out, own_one, own_two = refs[7:12]
    mods_ref, bias_ref, other_qkv, other_out, other_one, other_two = refs[12:18]
    outs = refs[18:26]
    scratch = refs[26:33]
    ada, mod_src, mod_buf, bias_buf, w_sem, ag_send, ag_recv, rs_send, rs_recv = refs[33:42]
    mod_send, mod_recv, share_send, share_recv, ada_sem = refs[42:]
    wqkv, wo = scratch[1:3]
    section, tensor = lax.axis_index("section"), lax.axis_index("tensor")
    load_ada = local(ada_w, ada, ada_sem)
    shares = [
        Share(own, other, parts, (share_send.at[i], share_recv.at[i]))
        for i, (own, other, parts) in enumerate(
            (
                (own_qkv, other_qkv, 4), (own_out, other_out, 2),
                (own_one, other_one, 4), (own_two, other_two, 4),
            )
        )
    ]
    plane = [
        {"section": lax.rem(section + a, sections), "tensor": lax.rem(tensor + b, count)}
        for a in range(sections)
        for b in range(count)
        if a or b
    ]
    greet(plane + [core_peer(), y_peer()])
    cargo.begin()
    shares[0].begin()
    cond_act = silu(cond_ref[...].astype(F32)).astype(BF16)
    load_ada.wait()
    mod = dot(cond_act, ada[...]) + ada_b_ref[...].astype(F32)
    mod_src[...] = mod.reshape(mod_src.shape)
    mod_buf[section, tensor] = mod_src[section]
    copies = [
        remote(
            mod_src.at[peer["section"]], mod_buf.at[section, tensor],
            mod_send.at[i], mod_recv.at[i], peer,
        )
        for i, peer in enumerate(plane)
    ]
    bias_buf[section] = biases_ref[...]
    bias_copy = remote(
        biases_ref, bias_buf.at[section],
        mod_send.at[len(plane)], mod_recv.at[len(plane)], x_peer(),
    )
    for share in shares[1:]:
        share.begin()

    def mods():
        wait_all(copies)
        width, piece = mods_ref.shape[-1], mod_buf.shape[-1]
        for block in range(sections):
            for which in range(6):
                parts, at = [], which * width
                while at < (which + 1) * width:
                    end = min((at // piece + 1) * piece, (which + 1) * width)
                    start = at - at // piece * piece
                    parts.append(mod_buf[block, at // piece][:, start : start + end - at])
                    at = end
                mods_ref[block, which] = (
                    jnp.concatenate(parts, axis=1) if len(parts) > 1 else parts[0]
                )
        return mods_ref.at[0]

    def biases():
        bias_copy.wait()
        bias_ref[...] = bias_buf[...]
        return bias_buf[0]

    def need_qkv():
        fetch(0, own_qkv, other_qkv, wqkv, w_sem.at[0]).wait()

    def need_out():
        shares[1].finish()
        fetch(0, own_out, other_out, wo, w_sem.at[1]).wait()

    def after_gather():
        shares[0].forward(shares[0].first)
        shares[1].forward(shares[1].first)
        shares[0].forward_again()
        shares[0].finish()

    def after_scatter():
        shares[2].forward(shares[2].first)
        shares[2].forward_again()

    attend_body(
        count, None, u_ref, mods, (seg_own, seg_col, seg_row), biases, outs, scratch,
        (ag_send, ag_recv, rs_send, rs_recv), need_qkv, need_out, (after_gather, after_scatter),
    )
    cargo.end()
    shares[2].finish()
    shares[3].first.wait()


def attend_kernel(count, block, *refs, cargo):
    u_ref, mods_ref, bias_ref, seg_own, seg_col, seg_row = refs[:6]
    own_qkv, other_qkv, own_out, other_out = refs[6:10]
    outs, scratch, w_sem = refs[10:18], refs[18:25], refs[25]
    load_qkv = fetch(block, own_qkv, other_qkv, scratch[1], w_sem.at[0])
    load_out = fetch(block, own_out, other_out, scratch[2], w_sem.at[1])
    attend_body(
        count, z_peers(count) + cargo.peers(), u_ref, lambda: mods_ref.at[block],
        (seg_own, seg_col, seg_row), lambda: bias_ref[block], outs, scratch, refs[26:30],
        load_qkv.wait, load_out.wait, (cargo.begin, cargo.middle),
    )
    cargo.end()


def mlp_kernel(
    count, block,
    middle_ref, mods_ref, bias_ref, seg_own, w1_own, w1_other, w2_own, w2_other,
    out_ref, branch_ref, full_ref, pre_ref, act_ref,
    full, w1, w2, send_buf, recv_buf, relay_buf, w_sem, *sems, cargo, late,
):
    me = lax.axis_index("tensor")
    rows, length, width = middle_ref.shape
    mod_ref = mods_ref.at[block]
    load_one = fetch(block, w1_own, w1_other, w1, w_sem.at[0])
    normed, unused = layer_norm(flat(middle_ref))
    mlp_in = normed * (1.0 + token_mod(mod_ref, seg_own, 4)) + token_mod(mod_ref, seg_own, 3)
    full[:, own_rows(me, length), :] = mlp_in.astype(BF16).reshape(rows, length, width)
    greet(z_peers(count) + cargo.peers())
    line = Line(length, sems)
    line.start_gather(full)
    cargo.begin()
    line.relay(full)
    load_one.wait()
    line.finish_gather(full)
    full_ref[...] = full[...]
    pre = dot(flat(full), w1[...]) + bias_ref[block, 3:4, : w1.shape[1]]
    pre_ref[...] = pre.reshape(pre_ref.shape)
    cargo.middle()
    if late:
        w2_other = cargo.cargos[0].out_refs[0]
    load_two = fetch(block, w2_own, w2_other, w2, w_sem.at[1])
    act_ref[...] = gelu_tanh(pre).astype(BF16).reshape(act_ref.shape)
    load_two.wait()

    def partial(which_rows):
        return dot(act_ref[:, which_rows, :].reshape(rows * length, -1), w2[...])

    buffers = (send_buf, recv_buf, relay_buf)
    total = line.scatter_sum(partial, buffers)
    branch = line.finish_sum(total, buffers) + bias_ref[block, 4:5, :]
    cargo.end()
    branch_ref[...] = branch.reshape(branch_ref.shape)
    out = flat(middle_ref) + token_mod(mod_ref, seg_own, 5) * branch
    out_ref[...] = out.astype(BF16).reshape(out_ref.shape)


def mlp_back_kernel(count, block, *refs, cargo):
    g_ref, middle_ref, branch_ref, mods_ref, seg_own, full_ref, pre_ref, act_ref = refs[:8]
    w1_own, w1_other, w2_own, w2_other = refs[8:12]
    d_middle_ref, d_mod_ref, d_w1_ref, d_w2_ref, d_b1_ref, d_b2_ref = refs[12:18]
    full, d_pre, w1, w2, *buffers, w_sem = refs[18:26]
    sems = refs[26:]
    me = lax.axis_index("tensor")
    rows, length, width = middle_ref.shape
    mod_ref = mods_ref.at[block]
    load_one = fetch(block, w1_own, w1_other, w1, w_sem.at[0])
    load_two = fetch(block, w2_own, w2_other, w2, w_sem.at[1])
    g = flat(g_ref).astype(F32)
    d_branch = (g * token_mod(mod_ref, seg_own, 5)).astype(BF16)
    full[:, own_rows(me, length), :] = d_branch.reshape(rows, length, width)
    greet(z_peers(count) + cargo.peers())
    line = Line(length, sems)
    line.start_gather(full)
    cargo.begin()
    slot_sums(g * flat(branch_ref), seg_own, d_mod_ref, 2)
    line.relay(full)
    cargo.middle()
    load_two.wait()
    line.finish_gather(full)
    d_act = dot(flat(full), w2[...], NT)
    d_pre[...] = (d_act * gelu_slope(flat(pre_ref))).astype(BF16).reshape(d_pre.shape)
    load_one.wait()

    def partial(which_rows):
        return dot(d_pre[:, which_rows, :].reshape(rows * length, -1), w1[...], NT)

    total = line.scatter_sum(partial, buffers)
    d_b2_ref[...] = jnp.sum(flat(full).astype(F32), axis=0, keepdims=True)
    d_b1_ref[...] = jnp.sum(flat(d_pre).astype(F32), axis=0, keepdims=True)
    d_w2_ref[...] = dot(flat(full), flat(act_ref), TN).astype(BF16)
    d_w1_ref[...] = dot(flat(full_ref), flat(d_pre), TN).astype(BF16)
    d_in = line.finish_sum(total, buffers)
    normed, inverse = layer_norm(flat(middle_ref))
    d_middle = flat(g_ref).astype(F32) + norm_back(
        d_in * (1.0 + token_mod(mod_ref, seg_own, 4)), normed, inverse
    )
    d_middle_ref[...] = d_middle.reshape(d_middle_ref.shape)
    slot_sums(d_in, seg_own, d_mod_ref, 0)
    slot_sums(d_in * normed, seg_own, d_mod_ref, 1)
    cargo.end()


def attend_back_kernel(count, block, *refs, cargo):
    d_middle_ref, u_ref, branch_ref, mods_ref, seg_own, full_ref = refs[:6]
    q_ref, k_ref, v_ref, probs_ref, mixed_ref = refs[6:11]
    wqkv_own, wqkv_other, wo_own, wo_other = refs[11:15]
    d_in_ref, d_mod_ref, d_wqkv_ref, d_wo_ref, d_bqv_ref, d_bo_ref = refs[15:21]
    full, wide, narrow, wqkv, wo, *buffers, w_sem = refs[21:30]
    sems = refs[30:]
    me = lax.axis_index("tensor")
    rows, length, width = u_ref.shape
    heads_width = wo.shape[0]
    heads = heads_width // HEAD_WIDTH
    mod_ref = mods_ref.at[block]
    load_qkv = fetch(block, wqkv_own, wqkv_other, wqkv, w_sem.at[0])
    load_out = fetch(block, wo_own, wo_other, wo, w_sem.at[1])
    d_middle = flat(d_middle_ref)
    d_branch = (d_middle * token_mod(mod_ref, seg_own, 2)).astype(BF16)
    full[:, own_rows(me, length), :] = d_branch.reshape(rows, length, width)
    greet(z_peers(count) + cargo.peers())
    line = Line(length, sems)
    line.start_gather(full)
    cargo.begin()
    slot_sums(d_middle * flat(branch_ref), seg_own, d_mod_ref, 2)
    spread = spread_matrix(heads_width)
    line.relay(full)
    cargo.middle()
    load_out.wait()
    line.finish_gather(full)
    d_mixed = dot(flat(full), wo[...], NT).astype(BF16)
    wide[3] = dot(d_mixed, spread).astype(BF16).reshape(wide.shape[1:])

    def one_head(index, carry):
        row = index // heads
        head = lax.rem(index, heads)
        lanes = pl.ds(pl.multiple_of(head * HEAD_LANES, HEAD_LANES), HEAD_LANES)
        grad = wide[3, row, :, lanes]
        probs = probs_ref[index]
        d_probs = dot(grad, v_ref[row, :, lanes], NT)
        d_scores = (
            probs * (d_probs - jnp.sum(d_probs * probs, axis=-1, keepdims=True))
        ).astype(BF16)
        scale = HEAD_WIDTH ** (-0.5)
        wide[0, row, :, lanes] = (dot(d_scores, k_ref[row, :, lanes]) * scale).astype(BF16)
        wide[1, row, :, lanes] = (dot(d_scores, q_ref[row, :, lanes], TN) * scale).astype(BF16)
        wide[2, row, :, lanes] = dot(probs.astype(BF16), grad, TN).astype(BF16)
        return carry

    lax.fori_loop(0, rows * heads, one_head, 0)
    for which in range(3):
        narrow[which] = (
            dot(flat(wide.at[which]), spread, NT).astype(BF16).reshape(narrow.shape[1:])
        )
    load_qkv.wait()

    def partial(which_rows):
        total = 0.0
        for which in range(3):
            total = total + dot(
                narrow[which, :, which_rows, :].reshape(rows * length, heads_width),
                wqkv[pl.ds(which * width, width), :],
                NT,
            )
        return total

    total = line.scatter_sum(partial, buffers)
    d_bo_ref[...] = jnp.sum(flat(full).astype(F32), axis=0, keepdims=True)
    d_bqv_ref[0:1, :] = jnp.sum(flat(narrow.at[0]).astype(F32), axis=0, keepdims=True)
    d_bqv_ref[1:2, :] = jnp.sum(flat(narrow.at[2]).astype(F32), axis=0, keepdims=True)
    d_wo_ref[...] = dot(flat(full), flat(mixed_ref), TN).astype(BF16)
    for which in range(3):
        d_wqkv_ref[which] = dot(flat(full_ref), flat(narrow.at[which]), TN).astype(BF16)
    d_attn_in = line.finish_sum(total, buffers)
    normed, inverse = layer_norm(flat(u_ref).astype(F32))
    d_in = flat(d_middle_ref) + norm_back(
        d_attn_in * (1.0 + token_mod(mod_ref, seg_own, 1)), normed, inverse
    )
    d_in_ref[...] = d_in.reshape(d_in_ref.shape)
    slot_sums(d_attn_in, seg_own, d_mod_ref, 0)
    slot_sums(d_attn_in * normed, seg_own, d_mod_ref, 1)
    cargo.end()


def close_kernel(count, sections, replicas, *refs, cargo):
    outs_ref, grads_ref, mod_refs, small_refs = refs[:2], refs[2:4], refs[4:8], refs[8:17]
    cond_ref = refs[17]
    out_ref, grad_ref, ada_w_ref, ada_b_ref, small_ref = refs[18:23]
    z_src, z_buf, mod_src, mod_buf, small_src, small_buf, cond_buf = refs[23:30]
    place_src, place_buf = refs[30:32]
    sems = refs[32:34]
    section, tensor, replica = (lax.axis_index(name) for name in ("section", "tensor", "dp"))
    send, recv = sems
    others = [
        {"section": lax.rem(section + a, sections), "dp": lax.rem(replica + b, replicas)}
        for a in range(sections)
        for b in range(replicas)
        if a or b
    ]
    greet(z_peers(count) + others)
    cargo.begin()
    piece = z_src.shape[-1]
    for block in range(sections):
        attend_mod, mlp_mod = mod_refs[2 * block : 2 * block + 2]
        width = attend_mod.shape[-1]
        for part in range(count):
            at, end, cuts = part * piece, (part + 1) * piece, []
            while at < end:
                which = at // width
                stop = min((which + 1) * width, end)
                ref = attend_mod if which < 3 else mlp_mod
                cuts.append(ref[which % 3][:, at - which * width : stop - which * width])
                at = stop
            z_src[part, block] = jnp.concatenate(cuts, axis=1) if len(cuts) > 1 else cuts[0]
    z_copies = [
        remote(z_src.at[peer["tensor"]], z_buf.at[i], send.at[i], recv.at[i], peer)
        for i, peer in enumerate(z_peers(count))
    ]
    at = count - 1
    @pl.when(section == 0)
    def first_place():
        place_src[0] = outs_ref[1][...]
        place_src[1] = grads_ref[1][...].astype(BF16)

    @pl.when(section != 0)
    def second_place():
        place_src[0] = outs_ref[0][...]
        place_src[1] = grads_ref[0][...].astype(BF16)

    place_copy = remote(place_src, place_buf, send.at[at], recv.at[at], x_peer())
    at = at + 1
    heads_width = small_refs[0].shape[-1]
    small_src[...] = jnp.zeros_like(small_src)
    for block in range(sections):
        d_bqv, d_bo, d_b1, d_b2 = small_refs[4 * block : 4 * block + 4]
        small_src[block, 0:2, :heads_width] = d_bqv[...]
        small_src[block, 2:3, :] = d_bo[...]
        small_src[block, 3:4, : d_b1.shape[1]] = d_b1[...]
        small_src[block, 4:5, :] = d_b2[...]
        small_src[block, 5:8, :] = small_refs[8][...]
    small_buf[section, replica] = small_src[section]
    cond_buf[section, replica] = cond_ref[replica]
    copies = []
    for peer in others:
        copies.append(
            remote(
                small_src.at[peer["section"]], small_buf.at[section, replica],
                send.at[at], recv.at[at], peer,
            )
        )
        copies.append(
            remote(
                cond_ref.at[peer["dp"]], cond_buf.at[section, replica],
                send.at[at + 1], recv.at[at + 1], peer,
            )
        )
        at = at + 2
    cargo.middle()
    wait_all(z_copies)
    mine = z_src[tensor]
    for step in range(count - 1):
        mine = mine + z_buf[step]
    mod_src[...] = mine
    mod_buf[section, replica] = mod_src[section]
    for peer in others:
        copies.append(
            remote(
                mod_src.at[peer["section"]], mod_buf.at[section, replica],
                send.at[at], recv.at[at], peer,
            )
        )
        at = at + 1
    for one in cargo.cargos:
        if isinstance(one, LastSum):
            one.to_x()
    place_copy.wait()
    rows = place_buf.shape[1]

    @pl.when(section == 0)
    def first_out():
        out_ref[:rows] = outs_ref[0][...]
        grad_ref[:rows] = grads_ref[0][...]
        out_ref[rows:] = place_buf[0]
        grad_ref[rows:] = place_buf[1].astype(F32)

    @pl.when(section != 0)
    def second_out():
        out_ref[rows:] = outs_ref[1][...]
        grad_ref[rows:] = grads_ref[1][...]
        out_ref[:rows] = place_buf[0]
        grad_ref[:rows] = place_buf[1].astype(F32)

    wait_all(copies)
    small = small_buf[0, 0]
    for a in range(sections):
        for b in range(replicas):
            if a or b:
                small = small + small_buf[a, b]
    small_ref[...] = small
    mod_all = flat(mod_buf)
    ada_b_ref[...] = jnp.sum(mod_all, axis=0, keepdims=True)
    ada_w_ref[...] = lax.dot_general(
        flat(cond_buf), mod_all, TN, precision=HIGHEST, preferred_element_type=F32
    )
    cargo.end()


VMEM = pl.BlockSpec(memory_space=pltpu.VMEM)
ANY = pl.BlockSpec(memory_space=pl.ANY)
MOD_ROWS = 8


def call(kernel, number, inputs, in_any, outs, out_any, scratch, flops, cargos=()):
    own_in, own_out, own_scratch = len(inputs), len(outs), len(scratch)
    specs = [VMEM] * (own_in - in_any) + [ANY] * in_any
    out_specs = [ANY if i in out_any else VMEM for i in range(own_out)]
    inputs, outs, scratch, aliases = list(inputs), list(outs), list(scratch), {}
    for cargo in cargos:
        for source, target in cargo.aliases.items():
            aliases[len(inputs) + source] = len(outs) + target
        inputs += cargo.inputs
        outs += cargo.outs
        scratch += cargo.scratch
        specs += [ANY] * len(cargo.inputs)
        out_specs += [ANY if cargo.any_outs else VMEM] * len(cargo.outs)

    def body(*refs):
        parts = [list(refs[: len(inputs)])]
        parts.append(list(refs[len(inputs) : len(inputs) + len(outs)]))
        parts.append(list(refs[len(inputs) + len(outs) :]))
        base = parts[0][:own_in] + parts[1][:own_out] + parts[2][:own_scratch]
        at = [own_in, own_out, own_scratch]
        for cargo in cargos:
            held = []
            for i, items in enumerate((cargo.inputs, cargo.outs, cargo.scratch)):
                held.append(parts[i][at[i] : at[i] + len(items)])
                at[i] += len(items)
            cargo.bind(*held)
        kernel(*base, cargo=Bundle(cargos))

    moved = sum(math.prod(one.shape) * one.dtype.itemsize for one in inputs)
    results = pl.pallas_call(
        body,
        out_shape=[jax.ShapeDtypeStruct(shape, dtype) for shape, dtype in outs],
        in_specs=specs,
        out_specs=out_specs,
        scratch_shapes=scratch,
        input_output_aliases=aliases,
        compiler_params=pltpu.CompilerParams(
            collective_id=number, has_side_effects=True, vmem_limit_bytes=56 * 2**20
        ),
        cost_estimate=pl.CostEstimate(flops=flops, bytes_accessed=moved, transcendentals=0),
    )(*inputs)
    at, carried = own_out, []
    for cargo in cargos:
        carried.append(results[at : at + len(cargo.outs)])
        at += len(cargo.outs)
    return results[:own_out], carried


def exchange_scratch(count, rows, length, width):
    return [
        pltpu.VMEM((count - 1, rows, length, width), BF16),
        pltpu.VMEM((count, rows, length, width), BF16),
        pltpu.VMEM((rows, length, width), BF16),
    ]


def semaphores(count):
    return [pltpu.SemaphoreType.DMA((2,))] + [
        pltpu.SemaphoreType.DMA((size,)) for size in (count, count, count - 1, count + 1)
    ]


class Shapes:
    def __init__(self, u, own, count):
        self.rows, self.length, self.width = u.shape
        self.count = count
        self.positions = self.length * count
        self.tokens = self.rows * self.positions
        self.heads_width = own["out"].shape[0]
        self.hidden = own["one"].shape[1]
        self.heads = self.heads_width // HEAD_WIDTH
        self.local = (self.rows, self.length, self.width)
        self.full = (self.rows, self.positions, self.width)
        self.wide = (self.rows, self.positions, self.heads * HEAD_LANES)
        self.own = own
        self.attend_outs = [
            (self.local, F32), (self.local, F32), (self.full, BF16),
            (self.wide, BF16), (self.wide, BF16), (self.wide, BF16),
            ((self.rows * self.heads, self.positions, self.positions), F32),
            ((self.rows, self.positions, self.heads_width), BF16),
        ]
        self.attend_scratch = [
            pltpu.VMEM(self.full, BF16),
            pltpu.VMEM(own["qkv"].shape, BF16),
            pltpu.VMEM(own["out"].shape, BF16),
            pltpu.VMEM(self.wide, BF16),
        ] + exchange_scratch(count, *self.local)
        self.mods = (3, MOD_ROWS, self.width)


def pairs(own, other, names):
    out = []
    for name in names:
        out += [own[name], other[name]]
    return out


def open_forward(sizes, u, cond, ada_w, ada_b, biases, segs, own, sections, cargos):
    count, width = sizes.count, sizes.width
    piece = ada_w.shape[1]
    inputs = [u, cond, ada_b, biases, *segs, ada_w] + [own[n] for n in ("qkv", "out", "one", "two")]
    plane = sections * count - 1
    results, carried = call(
        functools.partial(open_kernel, count, sections),
        0,
        inputs,
        5,
        [((sections, 6, MOD_ROWS, width), F32), ((sections,) + biases.shape, F32)]
        + [(own[n].shape, BF16) for n in ("qkv", "out", "one", "two")]
        + sizes.attend_outs,
        (2, 3, 4, 5),
        sizes.attend_scratch
        + [
            pltpu.VMEM(ada_w.shape, BF16),
            pltpu.VMEM((sections, MOD_ROWS, piece), F32),
            pltpu.VMEM((sections, count, MOD_ROWS, piece), F32),
            pltpu.VMEM((sections,) + biases.shape, F32),
        ]
        + semaphores(count)
        + [
            pltpu.SemaphoreType.DMA((plane + 1,)),
            pltpu.SemaphoreType.DMA((plane + 1,)),
            pltpu.SemaphoreType.DMA((4, 4)),
            pltpu.SemaphoreType.DMA((4, 4)),
            pltpu.SemaphoreType.DMA,
        ],
        2 * sizes.tokens * width * sizes.heads_width * 4,
        cargos,
    )
    other = dict(zip(("qkv", "out", "one", "two"), results[2:6]))
    return results[0], results[1], other, results[6:], carried


def attend_forward(sizes, block, u, mods, biases, segs, own, other, cargos):
    inputs = [u, mods, biases, *segs] + pairs(own, other, ("qkv", "out"))
    return call(
        functools.partial(attend_kernel, sizes.count, block),
        1,
        inputs,
        4,
        sizes.attend_outs,
        (),
        sizes.attend_scratch + semaphores(sizes.count),
        2 * sizes.tokens * sizes.width * sizes.heads_width * 4,
        cargos,
    )


def mlp_forward(sizes, block, middle, mods, biases, segs, own, other, late, cargos):
    inputs = [middle, mods, biases, segs[0]] + pairs(own, other, ("one", "two"))
    hidden = (sizes.rows, sizes.positions, sizes.hidden)
    return call(
        functools.partial(mlp_kernel, sizes.count, block, late=late),
        2 + block,
        inputs,
        4,
        [
            (sizes.local, BF16), (sizes.local, F32), (sizes.full, BF16),
            (hidden, F32), (hidden, BF16),
        ],
        (),
        [
            pltpu.VMEM(sizes.full, BF16),
            pltpu.VMEM(own["one"].shape, BF16),
            pltpu.VMEM(own["two"].shape, BF16),
        ]
        + exchange_scratch(sizes.count, *sizes.local)
        + semaphores(sizes.count),
        2 * sizes.tokens * sizes.width * sizes.hidden * 2,
        cargos,
    )


def mlp_backward(sizes, block, g, attend, mlp, mods, segs, own, other, cargos):
    out, branch, full, pre, act = mlp
    inputs = [g, attend[0], branch, mods, segs[0], full, pre, act]
    inputs += pairs(own, other, ("one", "two"))
    return call(
        functools.partial(mlp_back_kernel, sizes.count, block),
        4 + block,
        inputs,
        4,
        [
            (sizes.local, F32), (sizes.mods, F32),
            ((sizes.width, sizes.hidden), BF16), ((sizes.width, sizes.hidden), BF16),
            ((1, sizes.hidden), F32), ((1, sizes.width), F32),
        ],
        (),
        [
            pltpu.VMEM(sizes.full, BF16),
            pltpu.VMEM((sizes.rows, sizes.positions, sizes.hidden), BF16),
            pltpu.VMEM(own["one"].shape, BF16),
            pltpu.VMEM(own["two"].shape, BF16),
        ]
        + exchange_scratch(sizes.count, *sizes.local)
        + semaphores(sizes.count),
        2 * sizes.tokens * sizes.width * sizes.hidden * 4,
        cargos,
    )


def attend_backward(sizes, block, d_middle, u, attend, mods, segs, own, other, cargos):
    middle, branch, full, q, k, v, probs, mixed = attend
    inputs = [d_middle, u, branch, mods, segs[0], full, q, k, v, probs, mixed]
    inputs += pairs(own, other, ("qkv", "out"))
    return call(
        functools.partial(attend_back_kernel, sizes.count, block),
        6 + block,
        inputs,
        4,
        [
            (sizes.local, F32), (sizes.mods, F32),
            ((3, sizes.width, sizes.heads_width), BF16), ((sizes.width, sizes.heads_width), BF16),
            ((2, sizes.heads_width), F32), ((1, sizes.width), F32),
        ],
        (),
        [
            pltpu.VMEM(sizes.full, BF16),
            pltpu.VMEM((4,) + sizes.wide, BF16),
            pltpu.VMEM((3, sizes.rows, sizes.positions, sizes.heads_width), BF16),
            pltpu.VMEM(own["qkv"].shape, BF16),
            pltpu.VMEM(own["out"].shape, BF16),
        ]
        + exchange_scratch(sizes.count, *sizes.local)
        + semaphores(sizes.count),
        2 * sizes.tokens * sizes.width * sizes.heads_width * 8,
        cargos,
    )


def close_backward(sizes, outs, grads, mod_grads, small, proj_small, cond, sections, replicas, cargos):
    count, width = sizes.count, sizes.width
    piece = 6 * width // count
    share = width // replicas
    inputs = [*outs, *grads, *mod_grads, *small, proj_small, cond]
    copies = count + 3 * (sections * replicas - 1)
    both = (sections * sizes.rows,) + sizes.local[1:]
    return call(
        functools.partial(close_kernel, count, sections, replicas),
        8,
        inputs,
        0,
        [
            (both, BF16), (both, F32), ((share, piece), F32), ((1, piece), F32),
            ((MOD_ROWS, width), F32),
        ],
        (),
        [
            pltpu.VMEM((count, sections, MOD_ROWS, piece), F32),
            pltpu.VMEM((count - 1, sections, MOD_ROWS, piece), F32),
            pltpu.VMEM((sections, MOD_ROWS, piece), F32),
            pltpu.VMEM((sections, replicas, MOD_ROWS, piece), F32),
            pltpu.VMEM((sections, MOD_ROWS, width), F32),
            pltpu.VMEM((sections, replicas, MOD_ROWS, width), F32),
            pltpu.VMEM((sections, replicas, MOD_ROWS, share), F32),
            pltpu.VMEM((2,) + sizes.local, BF16),
            pltpu.VMEM((2,) + sizes.local, BF16),
            pltpu.SemaphoreType.DMA((copies,)),
            pltpu.SemaphoreType.DMA((copies,)),
        ],
        2 * sections * replicas * MOD_ROWS * share * piece,
        cargos,
    )


def act_grad(function, source_rows, upstream):
    unused_value, pullback = jax.vjp(function, source_rows)
    return pullback(upstream)[0]


def gather_rows(source_rows):
    return lax.all_gather(source_rows, "tensor", axis=0, tiled=True)


def scatter_rows(terms):
    return lax.psum_scatter(
        terms.astype(BF16), "tensor", scatter_dimension=0, tiled=True
    ).astype(F32)


def align_pass(sent_rows, target_cols, proj_weights, total_token_count):
    p1_w, p1_b, p2_w, p2_b, p3_w, p3_b = proj_weights
    input_full = gather_rows(sent_rows)
    first_pre = dot(input_full, p1_w) + p1_b.astype(F32)
    first_act = jax.nn.silu(first_pre).astype(BF16)
    second_pre = scatter_rows(dot(first_act, p2_w)) + p2_b.astype(F32)
    second_act = jax.nn.silu(second_pre).astype(BF16)
    second_full = gather_rows(second_act)
    predicted = dot(second_full, p3_w) + p3_b.astype(F32)
    pred_sq, cross, target_sq = lax.psum(
        jnp.stack(
            [
                jnp.sum(predicted * predicted, axis=1),
                jnp.sum(predicted * target_cols, axis=1),
                jnp.sum(target_cols * target_cols, axis=1),
            ]
        ),
        "tensor",
    )
    inv_pred = lax.rsqrt(pred_sq + COSINE_EPS)
    inv_target = lax.rsqrt(target_sq + COSINE_EPS)
    cosine = cross * inv_pred * inv_target
    loss_local = jnp.sum(cosine)
    factor = -0.5 / total_token_count
    grad_pred = (
        (factor * inv_pred * inv_target)[:, None] * target_cols
        - (factor * cosine * inv_pred * inv_pred)[:, None] * predicted
    ).astype(BF16)
    grad_p3_b = jnp.sum(grad_pred.astype(F32), axis=0)
    grad_p3_w = dot(second_full, grad_pred, TN)
    grad_second_act = scatter_rows(dot(grad_pred, p3_w, NT))
    grad_second_pre = act_grad(jax.nn.silu, second_pre, grad_second_act).astype(BF16)
    grad_second_full = gather_rows(grad_second_pre)
    grad_p2_b = jnp.sum(grad_second_full.astype(F32), axis=0)
    grad_p2_w = dot(grad_second_full, first_act, TN)
    grad_first_act = dot(grad_second_full, p2_w, NT)
    grad_first_pre = act_grad(jax.nn.silu, first_pre, grad_first_act).astype(BF16)
    grad_p1_b = jnp.sum(grad_first_pre.astype(F32), axis=0)
    grad_p1_w = dot(input_full, grad_first_pre, TN)
    grad_sent = scatter_rows(dot(grad_first_pre, p1_w, NT))
    return (
        loss_local,
        grad_sent,
        (grad_p1_w, grad_p2_w, grad_p3_w),
        (grad_p1_b, grad_p2_b, grad_p3_b),
    )


def halve(value, axis, bit, position):
    size = lax.axis_size(axis)
    mine = (lax.axis_index(axis) & bit) // bit
    keep = lax.dynamic_index_in_dim(value, mine, position, keepdims=False)
    give = lax.dynamic_index_in_dim(value, 1 - mine, position, keepdims=False)
    return keep + lax.ppermute(give, axis, [(i, i ^ bit) for i in range(size)])


def sum_beyond_quads(value):
    size = lax.axis_size("dp")
    if size == 4:
        return value
    quads = size // 4
    bits = quads.bit_length() - 1
    lead = value.ndim - 2
    shape = value.shape
    value = value.reshape(shape[:lead] + (2,) * bits + (shape[-2] // quads, shape[-1]))
    for bit in range(bits):
        value = halve(value, "dp", 4 << bit, lead + bits - 1 - bit)
    route = [(high * 4 + low, low * quads + high) for high in range(quads) for low in range(4)]
    return lax.ppermute(value, "dp", route)


def per_device(
    block_eight_input,
    cond,
    image_slot_index,
    targets,
    cot,
    ada_w,
    ada_b,
    query_key_value_weight,
    query_value_bias,
    attention_output_weight,
    attention_output_bias,
    hidden_weight,
    hidden_bias,
    output_weight_mlp,
    output_bias_mlp,
    p1_w,
    p1_b,
    p2_w,
    p2_b,
    p3_w,
    p3_b,
):
    section = lax.axis_index("section")
    tensor = lax.axis_index("tensor")
    is_first = section == 0
    count = lax.axis_size("tensor")
    sections = lax.axis_size("section")
    replicas = lax.axis_size("dp")
    length, replica_rows, width = block_eight_input.shape
    positions = length * count
    rows = replica_rows // sections
    total_token_count = positions * replica_rows * replicas
    heads_width = attention_output_weight.shape[1]
    hidden = hidden_weight.shape[2]

    def my_rows(value, axis):
        return lax.dynamic_slice_in_dim(value, section * rows, rows, axis)

    def to_rows(value):
        return jnp.transpose(my_rows(value, 1), (1, 0, 2))

    own = {
        "qkv": jnp.transpose(query_key_value_weight[0], (1, 0, 2)).reshape(3 * width, heads_width),
        "out": attention_output_weight[0],
        "one": hidden_weight[0],
        "two": output_weight_mlp[0],
    }

    def padded(value):
        return jnp.pad(value.astype(F32), ((0, 0), (0, width - value.shape[-1])))

    biases = jnp.concatenate(
        [
            padded(query_value_bias[0]), padded(attention_output_bias), padded(hidden_bias),
            padded(output_bias_mlp), jnp.zeros((MOD_ROWS - 5, width), F32),
        ],
        axis=0,
    )
    used = rows * IMAGES_PER_ROW
    cond_pad = jnp.pad(
        cond.reshape(sections, used, width), ((0, 0), (0, MOD_ROWS - used), (0, 0))
    )
    segs_full = my_rows(image_slot_index, 0)
    seg_own = lax.dynamic_slice_in_dim(segs_full, tensor * length, length, 1)
    segs = (seg_own[:, :, None], segs_full[:, :, None], segs_full[:, None, :])

    u = to_rows(block_eight_input)
    sizes = Shapes(u, own, count)
    mods, bias_all, other, attend_one, unused = open_forward(
        sizes, u, cond_pad.reshape(-1, width), ada_w[0], ada_b, biases, segs, own, sections, ()
    )
    mlp_one, carried = mlp_forward(
        sizes, 0, attend_one[0], mods, bias_all, segs, own, other, True, (LateShare(other["two"]),)
    )
    other["two"] = carried[0][0]
    first_out = mlp_one[0]
    attend_two, carried = attend_forward(
        sizes, 1, first_out, mods, bias_all, segs, own, other, ()
    )
    mlp_two, carried = mlp_forward(
        sizes, 1, attend_two[0], mods, bias_all, segs, own, other, False, ()
    )
    second_out = mlp_two[0]

    target_cols = my_rows(targets, 1).reshape(count, length, rows, -1)
    target_cols = jnp.transpose(target_cols, (0, 2, 1, 3)).reshape(rows * positions, -1)
    loss_local, grad_sent, proj_grads, proj_bias_grads = align_pass(
        first_out.reshape(rows * length, width),
        target_cols.astype(F32),
        (p1_w, p1_b, p2_w, p2_b, p3_w, p3_b),
        total_token_count,
    )

    back = (mods, segs, own, other)
    (d_middle_two, mod_mlp_two, *mlp_grads_two), unused = mlp_backward(
        sizes, 1, to_rows(cot), attend_two, mlp_two, *back, ()
    )
    (second_grad, mod_attend_two, *attend_grads_two), mlp_parts_two = attend_backward(
        sizes, 1, d_middle_two, first_out, attend_two, *back,
        [QuadSum(grad) for grad in mlp_grads_two[:2]],
    )
    (d_middle_one, mod_mlp_one, *mlp_grads_one), carried = mlp_backward(
        sizes, 0, second_grad + grad_sent.reshape(rows, length, width), attend_one, mlp_one, *back,
        [QuadSum(grad) for grad in attend_grads_two[:2]]
        + [SectionSum(part) for part, in mlp_parts_two],
    )
    attend_parts_two, sums_mlp_two = carried[:2], carried[2:]
    (first_grad, mod_attend_one, *attend_grads_one), carried = attend_backward(
        sizes, 0, d_middle_one, u, attend_one, *back,
        [QuadSum(grad) for grad in mlp_grads_one[:2]]
        + [SectionSum(part) for part, in attend_parts_two],
    )
    mlp_parts_one, sums_attend_two = carried[:2], carried[2:]

    p1_len, p2_len, p3_len = p1_b.shape[0], p2_b.shape[0], p3_b.shape[0]
    d_p1_b, d_p2_b, d_p3_b = proj_bias_grads
    flat_small = jnp.concatenate([d_p2_b, d_p1_b, d_p3_b, loss_local[None]])
    proj_small = jnp.pad(flat_small, (0, 3 * width - flat_small.shape[0])).reshape(3, width)
    cond_act = silu(my_rows(cond, 0).astype(F32)).astype(BF16).astype(F32)
    share = width // replicas
    cond_cols = jnp.pad(cond_act.reshape(used, width), ((0, MOD_ROWS - used), (0, 0)))
    cond_cols = jnp.transpose(cond_cols.reshape(MOD_ROWS, replicas, share), (1, 0, 2))
    small = [
        attend_grads_one[2], attend_grads_one[3], mlp_grads_one[2], mlp_grads_one[3],
        attend_grads_two[2], attend_grads_two[3], mlp_grads_two[2], mlp_grads_two[3],
    ]
    (section_out, section_grad, grad_ada_w, grad_ada_b, small), carried = close_backward(
        sizes, (first_out, second_out), (first_grad, second_grad),
        (mod_attend_one, mod_mlp_one, mod_attend_two, mod_mlp_two),
        small, proj_small, cond_cols, sections, replicas,
        [LastSum(grad) for grad in attend_grads_one[:2]]
        + [SectionSum(part) for part, in mlp_parts_one],
    )
    sums_attend_one, sums_mlp_one = carried[:2], carried[2:]

    red_fc1, red_fc2, red_qkv, red_out = [
        sum_beyond_quads(jnp.where(is_first, one[0], two[0]))
        for one, two in zip(
            list(sums_mlp_one) + list(sums_attend_one), list(sums_mlp_two) + list(sums_attend_two)
        )
    ]
    flat_small = small[5:8].reshape(-1)
    red_p2_b = flat_small[:p2_len]
    red_p1_b = flat_small[p2_len : p2_len + p1_len]
    red_p3_b = flat_small[p2_len + p1_len : p2_len + p1_len + p3_len]
    loss_total = flat_small[p2_len + p1_len + p3_len]
    align_loss = -0.5 * loss_total / total_token_count

    grad_p1_w, grad_p2_w, grad_p3_w = proj_grads
    red_p1_w, red_p2_w, red_p3_w = [
        lax.psum_scatter(value.astype(BF16), ("section", "dp"), scatter_dimension=0, tiled=True)
        for value in (grad_p1_w, grad_p2_w, grad_p3_w)
    ]
    return (
        jnp.transpose(section_out, (1, 0, 2))[None],
        jnp.transpose(section_grad, (1, 0, 2))[None],
        align_loss,
        grad_ada_w[None],
        grad_ada_b,
        jnp.transpose(red_qkv, (1, 0, 2))[None],
        small[0:2, :heads_width][None],
        red_out.T[None],
        small[2:3],
        red_fc1[None],
        small[3:4, :hidden],
        red_fc2.T[None],
        small[4:5],
        red_p1_w.astype(F32),
        red_p1_b,
        red_p2_w.T.astype(F32),
        red_p2_b,
        red_p3_w.astype(F32),
        red_p3_b,
    )


def solution(mesh):
    in_specs = (
        P("tensor", "dp", None),
        P("dp", None, None),
        P("dp", None),
        P(None, "dp", "tensor"),
        P("tensor", "dp", None),
        P("section", None, "tensor"),
        P("section", "tensor"),
        P("section", None, None, "tensor"),
        P("section", None, "tensor"),
        P("section", "tensor", None),
        P("section", None),
        P("section", None, "tensor"),
        P("section", "tensor"),
        P("section", "tensor", None),
        P("section", None),
        P(None, "tensor"),
        P("tensor"),
        P("tensor", None),
        P(),
        P(None, "tensor"),
        P("tensor"),
    )
    out_specs = (
        P("section", "tensor", "dp", None),
        P("section", "tensor", "dp", None),
        P(),
        P("section", "dp", "tensor"),
        P("section", "tensor"),
        P("section", "dp", None, "tensor"),
        P("section", None, "tensor"),
        P("section", "tensor", "dp"),
        P("section", None),
        P("section", "dp", "tensor"),
        P("section", "tensor"),
        P("section", "tensor", "dp"),
        P("section", None),
        P(("section", "dp"), "tensor"),
        P("tensor"),
        P("tensor", ("section", "dp")),
        P(),
        P(("section", "dp"), "tensor"),
        P("tensor"),
    )
    return jax.shard_map(
        per_device, mesh=mesh, in_specs=in_specs, out_specs=out_specs, check_vma=False
    )
```

```python
import functools
import math

import jax
import jax.numpy as jnp
from jax import lax
from jax.experimental import pallas as pl
from jax.experimental.pallas import tpu as pltpu
from jax.sharding import PartitionSpec as P

HEAD_WIDTH = 72
HEAD_LANES = 128
IMAGES_PER_ROW = 3
NORM_EPS = 1e-06
COSINE_EPS = 1e-06
MASKED_SCORE = -1e30
HIGHEST = lax.Precision.HIGHEST
MESH = pl.DeviceIdType.MESH
F32 = jnp.float32
BF16 = jnp.bfloat16
NN = (((1,), (0,)), ((), ()))
NT = (((1,), (1,)), ((), ()))
TN = (((0,), (0,)), ((), ()))


def dot(left, right, form=NN):
    return lax.dot_general(left, right, form, preferred_element_type=F32)


def z_peers(count):
    me = lax.axis_index("tensor")
    return [{"tensor": lax.rem(me + step, count)} for step in range(1, count)]


def x_peer():
    return {"section": 1 - lax.axis_index("section")}


def core_bit():
    return lax.rem(lax.axis_index("dp"), 2)


def y_bit():
    return lax.rem(lax.axis_index("dp") // 2, 2)


def core_peer():
    return {"dp": lax.axis_index("dp") + 1 - 2 * core_bit()}


def y_peer():
    return {"dp": lax.axis_index("dp") + 2 - 4 * y_bit()}


def greet(peers):
    barrier = pltpu.get_barrier_semaphore()
    for peer in peers:
        pl.semaphore_signal(barrier, inc=1, device_id=peer, device_id_type=MESH)
    pl.semaphore_wait(barrier, len(peers))


def remote(source, target, send_sem, recv_sem, peer):
    copy = describe(source, target, send_sem, recv_sem, peer)
    copy.start()
    return copy


def local(source, target, sem):
    copy = pltpu.make_async_copy(source, target, sem)
    copy.start()
    return copy


def own_rows(me, length):
    return pl.ds(pl.multiple_of(me * length, 16), length)


def describe(source, target, send_sem, recv_sem, peer):
    return pltpu.make_async_remote_copy(
        src_ref=source,
        dst_ref=target,
        send_sem=send_sem,
        recv_sem=recv_sem,
        device_id=peer,
        device_id_type=MESH,
    )


def wait_all(copies):
    for copy in copies:
        copy.wait()


class Line:
    def __init__(self, length, sems):
        self.length, (self.ag_send, self.ag_recv, self.rs_send, self.rs_recv) = length, sems
        self.me = lax.axis_index("tensor")
        self.mirror = 3 - self.me
        self.near = self.me + 1 - 2 * lax.rem(self.me, 2)
        self.opposite = lax.rem(self.me + 2, 4)
        self.is_end = jnp.logical_or(self.me == 0, self.me == 3)
        self.is_middle = jnp.logical_not(self.is_end)

    def block(self, full, place, which, peer):
        part = full.at[:, own_rows(place, self.length)]
        return describe(
            part, part, self.ag_send.at[which], self.ag_recv.at[place], {"tensor": peer}
        )

    def start_gather(self, full):
        self.block(full, self.me, 0, self.opposite).start()
        self.block(full, self.me, 1, self.near).start()

        @pl.when(self.is_middle)
        def to_mirror():
            self.block(full, self.me, 2, self.mirror).start()

    def relay(self, full):
        self.block(full, self.opposite, 2, self.mirror).wait_recv()

        @pl.when(self.is_middle)
        def pass_on():
            self.block(full, self.opposite, 3, 3 - self.opposite).start()

    def finish_gather(self, full):
        self.block(full, self.near, 1, self.near).wait_recv()
        self.block(full, self.mirror, 1, self.near).wait_recv()
        self.block(full, self.me, 0, self.opposite).wait_send()
        self.block(full, self.me, 1, self.near).wait_send()

        @pl.when(self.is_middle)
        def sent():
            self.block(full, self.me, 2, self.mirror).wait_send()
            self.block(full, self.opposite, 3, 3 - self.opposite).wait_send()

    def scatter_sum(self, partial, buffers):
        send_buf, recv_buf, relay_buf = buffers
        me, relay_sem = self.me, 4

        def term(peer):
            return partial(own_rows(peer, self.length))

        def keep(which, value):
            send_buf[which] = value.astype(BF16).reshape(send_buf.shape[1:])

        self.to_mirror = describe(
            send_buf.at[0], recv_buf.at[me], self.rs_send.at[0], self.rs_recv.at[me],
            {"tensor": self.mirror},
        )
        self.to_relay = describe(
            send_buf.at[0], relay_buf, self.rs_send.at[0], self.rs_recv.at[relay_sem],
            {"tensor": self.near},
        )
        self.to_near = describe(
            send_buf.at[1], recv_buf.at[me], self.rs_send.at[1], self.rs_recv.at[me],
            {"tensor": self.near},
        )
        self.to_opposite = describe(
            send_buf.at[2], recv_buf.at[me], self.rs_send.at[2], self.rs_recv.at[me],
            {"tensor": self.opposite},
        )
        keep(0, term(self.mirror))

        @pl.when(self.is_end)
        def first_end():
            self.to_relay.start()
            relay_buf[...] = jnp.zeros_like(relay_buf)
            recv_buf[self.mirror] = jnp.zeros(recv_buf.shape[1:], BF16)

        @pl.when(self.is_middle)
        def first_middle():
            self.to_mirror.start()

        keep(1, term(self.near))
        self.to_near.start()
        last = term(self.opposite)

        @pl.when(self.is_middle)
        def relayed():
            self.to_relay.wait_recv()

        keep(2, last + relay_buf[...].reshape(last.shape).astype(F32))
        self.to_opposite.start()
        return term(me)

    def finish_sum(self, total, buffers):
        send_buf, recv_buf, relay_buf = buffers

        def got(source):
            describe(
                send_buf.at[1], recv_buf.at[source], self.rs_send.at[1], self.rs_recv.at[source],
                {"tensor": self.near},
            ).wait_recv()

        got(self.near)
        got(self.opposite)

        @pl.when(self.is_middle)
        def third():
            got(self.mirror)

        self.to_near.wait_send()
        self.to_opposite.wait_send()
        self.to_mirror.wait_send()
        for source in (self.near, self.opposite, self.mirror):
            total = total + recv_buf[source].reshape(total.shape).astype(F32)
        return total


def fetch(block, own_ref, other_ref, target, sem):
    mine = lax.axis_index("section") == block

    @pl.when(mine)
    def own_start():
        pltpu.make_async_copy(own_ref, target, sem).start()

    @pl.when(jnp.logical_not(mine))
    def other_start():
        pltpu.make_async_copy(other_ref, target, sem).start()

    return pltpu.make_async_copy(own_ref, target, sem)


def layer_norm(rows):
    centred = rows - jnp.mean(rows, axis=-1, keepdims=True)
    inverse = lax.rsqrt(jnp.mean(centred * centred, axis=-1, keepdims=True) + NORM_EPS)
    return centred * inverse, inverse


def norm_back(grad, normed, inverse):
    mean_grad = jnp.mean(grad, axis=-1, keepdims=True)
    mean_cross = jnp.mean(grad * normed, axis=-1, keepdims=True)
    return inverse * (grad - mean_grad - normed * mean_cross)


def token_mod(mod_ref, seg_ref, which):
    parts = []
    for row in range(seg_ref.shape[0]):
        seg = seg_ref[row]
        line = [
            mod_ref[which, pl.ds(row * IMAGES_PER_ROW + slot, 1), :]
            for slot in range(IMAGES_PER_ROW)
        ]
        value = line[-1]
        for slot in range(IMAGES_PER_ROW - 2, -1, -1):
            value = jnp.where(seg == slot, line[slot], value)
        parts.append(value)
    return jnp.concatenate(parts, axis=0)


def slot_sums(value, seg_ref, out_ref, which):
    length = seg_ref.shape[1]
    lines = []
    for row in range(seg_ref.shape[0]):
        seg = seg_ref[row]
        piece = value[row * length : (row + 1) * length]
        for slot in range(IMAGES_PER_ROW):
            lines.append(jnp.sum(jnp.where(seg == slot, piece, 0.0), axis=0, keepdims=True))
    spare = out_ref.shape[1] - len(lines)
    lines.append(jnp.zeros((spare, value.shape[1]), F32))
    out_ref[which] = jnp.concatenate(lines, axis=0)


def flat(ref):
    return ref[...].reshape(-1, ref.shape[-1])


def spread_matrix(width):
    lanes = width // HEAD_WIDTH * HEAD_LANES
    source = lax.broadcasted_iota(jnp.int32, (width, lanes), 0)
    target = lax.broadcasted_iota(jnp.int32, (width, lanes), 1)
    within = target & (HEAD_LANES - 1)
    head = target >> (HEAD_LANES.bit_length() - 1)
    hit = (within < HEAD_WIDTH) & (source == head * HEAD_WIDTH + within)
    return jnp.where(hit, 1.0, 0.0).astype(BF16)


def gelu_tanh(pre):
    inner = math.sqrt(2.0 / math.pi) * (pre + 0.044715 * (pre * pre * pre))
    return 0.5 * pre * (1.0 + jnp.tanh(inner))


def gelu_slope(pre):
    scale = math.sqrt(2.0 / math.pi)
    square = pre * pre
    tanh = jnp.tanh(scale * (pre + 0.044715 * (pre * square)))
    return 0.5 * (1.0 + tanh) + 0.5 * pre * (1.0 - tanh * tanh) * scale * (
        1.0 + 3 * 0.044715 * square
    )


def silu(value):
    return value / (1.0 + jnp.exp(-value))


class Share:
    def __init__(self, own, other, parts, sems):
        self.own, self.other, self.parts = own, other, parts
        self.send, self.recv = sems
        self.size = own.shape[0] // parts
        self.copies = []

    def rows(self, core, y):
        part = core if self.parts == 2 else core + 2 * y
        return pl.ds(pl.multiple_of(part * self.size, 16), self.size)

    def begin(self):
        rows = self.rows(core_bit(), y_bit())
        self.first = remote(
            self.own.at[rows], self.other.at[rows], self.send.at[0], self.recv.at[0], x_peer()
        )

    def forward(self, first):
        if first is not None:
            first.wait()
        mine = self.other.at[self.rows(core_bit(), y_bit())]
        self.copies.append(remote(mine, mine, self.send.at[1], self.recv.at[1], core_peer()))
        if self.parts == 4:
            self.second = remote(mine, mine, self.send.at[2], self.recv.at[2], y_peer())

    def forward_again(self):
        if self.parts == 4:
            self.second.wait()
            got = self.other.at[self.rows(core_bit(), 1 - y_bit())]
            self.copies.append(remote(got, got, self.send.at[3], self.recv.at[3], core_peer()))

    def finish(self):
        wait_all(self.copies)


class Cargo:
    inputs, outs, scratch, aliases, any_outs = (), (), (), {}, False

    def bind(self, inputs, outs, scratch):
        self.ins, self.out_refs, self.held = inputs, outs, scratch

    def peers(self):
        return []

    def begin(self):
        pass

    def middle(self):
        pass

    def end(self):
        pass


def quarter(shape):
    return shape[:-2] + (shape[-2] // 4, shape[-1])


class QuadSum(Cargo):
    def __init__(self, grad):
        part = quarter(grad.shape)
        self.inputs = (grad,)
        self.outs = ((part, BF16),)
        self.size = grad.shape[-2] // 4
        self.scratch = (
            pltpu.VMEM((2,) + part, BF16),
            pltpu.VMEM((2,) + part, BF16),
            pltpu.VMEM(part, BF16),
            pltpu.SemaphoreType.DMA((3, 3)),
        )

    def peers(self):
        return ["core", "y"]

    def rows(self, core, y):
        grad = self.ins[0]
        part = pl.ds(pl.multiple_of((core + 2 * y) * self.size, 16), self.size)
        return grad.at[:, part] if len(grad.shape) == 3 else grad.at[part]

    def begin(self):
        keep, from_core, from_y, sems = self.held
        core, self.copies = core_bit(), []
        for y in range(2):
            self.copies.append(
                remote(
                    self.rows(1 - core, y), from_core.at[y], sems.at[0, y], sems.at[1, y], core_peer()
                )
            )
            self.copies.append(local(self.rows(core, y), keep.at[y], sems.at[2, y]))

    def middle(self):
        keep, from_core, from_y, sems = self.held
        wait_all(self.copies)
        for y in range(2):
            keep[y] = (keep[y].astype(F32) + from_core[y].astype(F32)).astype(BF16)
        self.copies = [
            remote(keep.at[1 - y_bit()], from_y, sems.at[0, 2], sems.at[1, 2], y_peer())
        ]

    def end(self):
        keep, from_core, from_y, sems = self.held
        wait_all(self.copies)
        self.out_refs[0][...] = (
            keep[y_bit()].astype(F32) + from_y[...].astype(F32)
        ).astype(BF16)


class SectionSum(Cargo):
    def __init__(self, part):
        self.inputs = (part,)
        self.outs = ((part.shape, F32),)
        self.scratch = (
            pltpu.VMEM(part.shape, BF16),
            pltpu.VMEM(part.shape, BF16),
            pltpu.SemaphoreType.DMA((3,)),
        )

    def peers(self):
        return ["x"]

    def begin(self):
        mine, other, sems = self.held
        self.copies = [
            local(self.ins[0], mine, sems.at[2]),
            remote(self.ins[0], other, sems.at[0], sems.at[1], x_peer()),
        ]

    def end(self):
        mine, other, sems = self.held
        wait_all(self.copies)
        self.out_refs[0][...] = mine[...].astype(F32) + other[...].astype(F32)


class LastSum(QuadSum):
    def __init__(self, grad):
        super().__init__(grad)
        part = quarter(grad.shape)
        self.outs = ((part, F32),)
        self.scratch = self.scratch + (
            pltpu.VMEM(part, BF16),
            pltpu.VMEM(part, BF16),
            pltpu.SemaphoreType.DMA((2,)),
        )

    def peers(self):
        return ["core", "y", "x"]

    def begin(self):
        self.all_held = self.held
        self.held, self.last = self.held[:4], self.held[4:]
        super().begin()

    def to_x(self):
        keep, from_core, from_y, sems = self.held
        mine, other, last_sems = self.last
        wait_all(self.copies)
        mine[...] = (keep[y_bit()].astype(F32) + from_y[...].astype(F32)).astype(BF16)
        self.copies = [remote(mine, other, last_sems.at[0], last_sems.at[1], x_peer())]

    def end(self):
        mine, other, last_sems = self.last
        wait_all(self.copies)
        self.out_refs[0][...] = mine[...].astype(F32) + other[...].astype(F32)


class LateShare(Cargo):
    any_outs = True

    def __init__(self, other):
        self.inputs = (other,)
        self.outs = ((other.shape, BF16),)
        self.aliases = {0: 0}
        self.scratch = (pltpu.SemaphoreType.DMA((4,)), pltpu.SemaphoreType.DMA((4,)))

    def peers(self):
        return ["core", "y"]

    def begin(self):
        out = self.out_refs[0]
        self.share = Share(out, out, 4, self.held)
        self.share.forward(None)

    def middle(self):
        self.share.forward_again()
        self.share.finish()


class QuadSumX(Cargo):
    def __init__(self, grad):
        part = (2,) + quarter(grad.shape)
        self.inputs = (grad,)
        self.outs = ((part, BF16),)
        self.size = grad.shape[-2] // 4
        self.scratch = (
            pltpu.VMEM(part, BF16),
            pltpu.VMEM(part, BF16),
            pltpu.VMEM(part, BF16),
            pltpu.SemaphoreType.DMA((3, 3)),
        )

    def peers(self):
        return ["core", "x"]

    rows = QuadSum.rows

    def begin(self):
        QuadSum.begin(self)

    def middle(self):
        keep, from_core, from_x, sems = self.held
        wait_all(self.copies)
        for y in range(2):
            keep[y] = (keep[y].astype(F32) + from_core[y].astype(F32)).astype(BF16)
        self.copies = [remote(keep, from_x, sems.at[0, 2], sems.at[1, 2], x_peer())]

    def end(self):
        keep, from_core, from_x, sems = self.held
        wait_all(self.copies)
        self.out_refs[0][...] = (keep[...].astype(F32) + from_x[...].astype(F32)).astype(BF16)


class LastY(Cargo):
    def __init__(self, parts):
        part = parts.shape[1:]
        self.inputs = (parts,)
        self.outs = ((part, F32),)
        self.scratch = (
            pltpu.VMEM(part, BF16),
            pltpu.VMEM(part, BF16),
            pltpu.SemaphoreType.DMA((3,)),
        )

    def peers(self):
        return ["y"]

    def begin(self):
        mine, other, sems = self.held
        self.copies = [
            local(self.ins[0].at[y_bit()], mine, sems.at[2]),
            remote(self.ins[0].at[1 - y_bit()], other, sems.at[0], sems.at[1], y_peer()),
        ]

    end = SectionSum.end


class Swap(Cargo):
    def __init__(self, one, two):
        self.inputs = (one, two)
        self.outs = ((one.shape, one.dtype),)
        self.scratch = (pltpu.VMEM(one.shape, one.dtype), pltpu.SemaphoreType.DMA((2,)))

    def peers(self):
        return ["x"]

    def begin(self):
        got, sems = self.held
        one, two = self.ins
        self.copy = describe(two, got, sems.at[0], sems.at[1], x_peer())
        is_first = lax.axis_index("section") == 0

        @pl.when(is_first)
        def give_two():
            self.copy.start()

        @pl.when(jnp.logical_not(is_first))
        def give_one():
            describe(one, got, sems.at[0], sems.at[1], x_peer()).start()

    def end(self):
        self.copy.wait()
        self.out_refs[0][...] = self.held[0][...]


def span(ref, axis, start, size):
    part = pl.ds(pl.multiple_of(start, 128 if axis == 1 else 16), size)
    lead = (slice(None),) * (len(ref.shape) - 2)
    return ref.at[lead + ((slice(None), part) if axis == 1 else (part, slice(None)))]


def cut(shape, axis, by):
    shape = list(shape)
    shape[axis - 2] //= by
    return tuple(shape)


class HalfSum(Cargo):
    def __init__(self, grad, axis, name):
        part = cut(grad.shape, axis, 2)
        self.axis, self.name, self.size = axis, name, part[axis - 2]
        self.inputs = (grad,)
        self.outs = ((part, BF16),)
        self.scratch = (
            pltpu.VMEM(part, BF16),
            pltpu.VMEM(part, BF16),
            pltpu.SemaphoreType.DMA((3,)),
        )

    def peers(self):
        return [self.name]

    def begin(self):
        mine, other, sems = self.held
        if self.name == "x":
            bit, peer = lax.axis_index("section"), x_peer()
        else:
            bit, peer = y_bit(), y_peer()
        grad = self.ins[0]
        self.copies = [
            remote(
                span(grad, self.axis, (1 - bit) * self.size, self.size), other,
                sems.at[0], sems.at[1], peer,
            ),
            local(span(grad, self.axis, bit * self.size, self.size), mine, sems.at[2]),
        ]

    def end(self):
        mine, other, sems = self.held
        wait_all(self.copies)
        self.out_refs[0][...] = (mine[...].astype(F32) + other[...].astype(F32)).astype(BF16)


class ColumnGather(Cargo):
    any_outs = True

    def __init__(self, weights, targets, biases, sections):
        self.inputs = (*weights, targets, biases)
        self.outs = tuple(((2,) + one.shape, BF16) for one in weights) + (
            ((2, 2) + targets.shape[1:], BF16),
            ((2, 2) + biases.shape, F32),
        )
        self.scratch = (
            pltpu.SemaphoreType.DMA((5, 4)),
            pltpu.SemaphoreType.DMA((5, 2, 2)),
            pltpu.SemaphoreType.DMA((5,)),
        )

    def peers(self):
        return ["core", "cross"]

    def pieces(self, target):
        tensor, core = lax.axis_index("tensor"), core_bit()
        eighth = lax.axis_index("section") * 4 + y_bit() * 2 + core
        slot, out = lax.rem(tensor, 2), []
        for source, place in zip(self.ins[:3], self.out_refs[:3]):
            size = source.shape[0] // 8
            rows = pl.ds(pl.multiple_of(eighth * size, 16), size)
            out.append((source.at[rows], place.at[slot, rows]))
        out.append((self.ins[3].at[target], self.out_refs[3].at[slot, core]))
        out.append((self.ins[4], self.out_refs[4].at[slot, core]))
        return out

    def copies(self, step):
        tensor, core = lax.axis_index("tensor"), core_bit()
        send, recv, own = self.held
        target = lax.rem(tensor + step, 4)
        peer = {"tensor": target, "dp": lax.axis_index("dp") - core + tensor // 2}
        return [
            describe(source, place, send.at[i, step], recv.at[i, lax.rem(tensor, 2), core], peer)
            for i, (source, place) in enumerate(self.pieces(target))
        ]

    def stays(self):
        return core_bit() == lax.axis_index("tensor") // 2

    def own_copies(self):
        own = self.held[2]
        return [
            pltpu.make_async_copy(source, place, own.at[i])
            for i, (source, place) in enumerate(self.pieces(lax.axis_index("tensor")))
        ]

    def begin(self):
        for step in range(1, 4):
            for copy in self.copies(step):
                copy.start()

        @pl.when(self.stays())
        def keep():
            for copy in self.own_copies():
                copy.start()

        @pl.when(jnp.logical_not(self.stays()))
        def give():
            for copy in self.copies(0):
                copy.start()

    def end(self):
        send, recv, own = self.held
        tensor, core = lax.axis_index("tensor"), core_bit()
        for step in range(1, 4):
            for copy in self.copies(step):
                copy.wait_send()

        @pl.when(self.stays())
        def kept():
            for copy in self.own_copies():
                copy.wait()

        @pl.when(jnp.logical_not(self.stays()))
        def given():
            for copy in self.copies(0):
                copy.wait_send()

        for slot in range(2):
            for other in range(2):
                mine = jnp.logical_and(2 * core + slot == tensor, core == other)

                @pl.when(jnp.logical_not(mine))
                def arrived(slot=slot, other=other):
                    peer = {"tensor": lax.rem(tensor + 1, 4)}
                    for i, (source, place) in enumerate(self.pieces(tensor)):
                        describe(
                            source, place, send.at[i, 1], recv.at[i, slot, other], peer
                        ).wait_recv()


class ShareAlong(Cargo):
    any_outs = True

    def __init__(self, weights, second):
        self.inputs = tuple(weights)
        self.outs = tuple((one.shape, BF16) for one in weights)
        self.aliases = {0: 0, 1: 1, 2: 2}
        self.second = second
        self.scratch = (pltpu.SemaphoreType.DMA((4,)), pltpu.SemaphoreType.DMA((4,)))

    def peers(self):
        return ["x", "y"]

    def begin(self):
        send, recv = self.held
        section, y, self.copies = lax.axis_index("section"), y_bit(), []

        def give(which, start, parts, peer):
            ref = self.out_refs[which]
            size = ref.shape[1] // 4
            part = ref.at[:, pl.ds(pl.multiple_of(start * size, 16), parts * size)]
            i = len(self.copies)
            self.copies.append(remote(part, part, send.at[i], recv.at[i], peer))

        if not self.second:
            give(1, 2 * section + y, 1, x_peer())
            give(0, 2 * section + y, 1, y_peer())
            give(2, 2 * section + y, 1, y_peer())
        else:
            give(0, 2 * section, 2, x_peer())
            give(2, 2 * section, 2, x_peer())
            give(1, y, 1, y_peer())
            give(1, 2 + y, 1, y_peer())

    def end(self):
        wait_all(self.copies)


class ColumnSum(Cargo):
    def __init__(self, grad, axis):
        self.axis = axis
        self.part = cut(grad.shape[1:], axis, 2)
        self.inputs = (grad,)
        self.outs = ((self.part, F32),)
        self.scratch = (
            pltpu.VMEM((4,) + self.part, BF16),
            pltpu.SemaphoreType.DMA((4,)),
            pltpu.SemaphoreType.DMA((4,)),
            pltpu.SemaphoreType.DMA,
        )

    def peers(self):
        return ["core", "cross"]

    def copy(self, slot, other):
        got, send, recv, own = self.held
        tensor, core = lax.axis_index("tensor"), core_bit()
        size = self.part[self.axis]
        source = span(self.ins[0].at[slot], self.axis, other * size, size)
        peer = {"tensor": 2 * core + slot, "dp": lax.axis_index("dp") - core + other}
        mine = jnp.logical_and(2 * core + slot == tensor, core == other)
        away = describe(source, got.at[tensor], send.at[2 * slot + other], recv.at[tensor], peer)
        return mine, away, pltpu.make_async_copy(source, got.at[tensor], own)

    def each(self, act_away, act_own):
        for slot in range(2):
            for other in range(2):
                mine, away, own = self.copy(slot, other)

                @pl.when(mine)
                def stay(own=own):
                    act_own(own)

                @pl.when(jnp.logical_not(mine))
                def leave(away=away):
                    act_away(away)

    def begin(self):
        self.each(lambda copy: copy.start(), lambda copy: copy.start())

    def end(self):
        got, send, recv, own = self.held
        tensor, core = lax.axis_index("tensor"), core_bit()
        self.each(lambda copy: copy.wait_send(), lambda copy: copy.wait())
        for source in range(4):
            mine = jnp.logical_and(tensor == source, core == tensor // 2)

            @pl.when(jnp.logical_not(mine))
            def arrived(source=source):
                describe(
                    got.at[source], got.at[source], send.at[0], recv.at[source],
                    {"tensor": lax.rem(tensor + 1, 4)},
                ).wait_recv()

        total = got[0].astype(F32)
        for source in range(1, 4):
            total = total + got[source].astype(F32)
        self.out_refs[0][...] = total


def cross_peers():
    tensor, dp = lax.axis_index("tensor"), core_peer()["dp"]
    return [{"tensor": lax.rem(tensor + step, 4), "dp": dp} for step in range(1, 4)]


class Bundle:
    def __init__(self, cargos):
        self.cargos = cargos

    def peers(self):
        names = [name for cargo in self.cargos for name in cargo.peers()]
        known = {"core": core_peer, "y": y_peer, "x": x_peer}
        cross = cross_peers() if "cross" in names else []
        return [make() for name, make in known.items() if name in names] + cross

    def begin(self):
        for cargo in self.cargos:
            cargo.begin()

    def middle(self):
        for cargo in self.cargos:
            cargo.middle()

    def end(self):
        for cargo in self.cargos:
            cargo.end()


def attend_body(
    count, peers, u_ref, mods, segs, biases, outs, scratch, sems, need_qkv, need_out, steps
):
    middle_ref, branch_ref, full_ref, q_ref, k_ref, v_ref, probs_ref, mixed_ref = outs
    full, wqkv, wo, mixed_wide = scratch[:4]
    buffers = scratch[4:7]
    seg_own, seg_col, seg_row = segs
    mod_ref = mods()
    me = lax.axis_index("tensor")
    rows, length, width = u_ref.shape
    heads_width = wo.shape[0]
    heads = heads_width // HEAD_WIDTH
    u = flat(u_ref).astype(F32)
    normed, unused = layer_norm(u)
    attn_in = normed * (1.0 + token_mod(mod_ref, seg_own, 1)) + token_mod(mod_ref, seg_own, 0)
    full[:, own_rows(me, length), :] = attn_in.astype(BF16).reshape(rows, length, width)
    if peers is not None:
        greet(peers)
    line = Line(length, sems)
    line.start_gather(full)
    spread = spread_matrix(heads_width)
    line.relay(full)
    steps[0]()
    need_qkv()
    line.finish_gather(full)
    full_ref[...] = full[...]
    tokens = flat(full)
    bias = biases()
    for which, target in ((0, q_ref), (1, k_ref), (2, v_ref)):
        projected = dot(tokens, wqkv[pl.ds(which * width, width), :])
        if which != 1:
            projected = projected + bias[which // 2 : which // 2 + 1, :heads_width]
        target[...] = dot(projected.astype(BF16), spread).astype(BF16).reshape(target.shape)

    def one_head(index, carry):
        row = index // heads
        head = lax.rem(index, heads)
        lanes = pl.ds(pl.multiple_of(head * HEAD_LANES, HEAD_LANES), HEAD_LANES)
        scores = dot(q_ref[row, :, lanes], k_ref[row, :, lanes], NT) * HEAD_WIDTH ** (-0.5)
        scores = jnp.where(seg_col[row] == seg_row[row], scores, MASKED_SCORE)
        raised = jnp.exp(scores - jnp.max(scores, axis=-1, keepdims=True))
        probs = raised / jnp.sum(raised, axis=-1, keepdims=True)
        probs_ref[index] = probs
        mixed_wide[row, :, lanes] = dot(probs.astype(BF16), v_ref[row, :, lanes]).astype(BF16)
        return carry

    lax.fori_loop(0, rows * heads, one_head, 0)
    mixed_ref[...] = dot(flat(mixed_wide), spread, NT).astype(BF16).reshape(mixed_ref.shape)
    need_out()

    def partial(which_rows):
        return dot(mixed_ref[:, which_rows, :].reshape(rows * length, heads_width), wo[...])

    total = line.scatter_sum(partial, buffers)
    steps[1]()
    branch = line.finish_sum(total, buffers) + bias[2:3, :]
    branch_ref[...] = branch.reshape(branch_ref.shape)
    middle = flat(u_ref).astype(F32) + token_mod(mod_ref, seg_own, 2) * branch
    middle_ref[...] = middle.reshape(middle_ref.shape)


def open_kernel(count, sections, *refs, cargo):
    u_ref, cond_ref, ada_b_ref, biases_ref, seg_own, seg_col, seg_row = refs[:7]
    ada_w, own_qkv, own_out, own_one, own_two = refs[7:12]
    mods_ref, bias_ref, other_qkv, other_out, other_one, other_two = refs[12:18]
    outs = refs[18:26]
    scratch = refs[26:33]
    ada, mod_src, mod_buf, bias_buf, w_sem, ag_send, ag_recv, rs_send, rs_recv = refs[33:42]
    mod_send, mod_recv, share_send, share_recv, ada_sem = refs[42:]
    wqkv, wo = scratch[1:3]
    section, tensor = lax.axis_index("section"), lax.axis_index("tensor")
    load_ada = local(ada_w, ada, ada_sem)
    shares = [
        Share(own, other, parts, (share_send.at[i], share_recv.at[i]))
        for i, (own, other, parts) in enumerate(
            (
                (own_qkv, other_qkv, 4), (own_out, other_out, 2),
                (own_one, other_one, 4), (own_two, other_two, 4),
            )
        )
    ]
    plane = [
        {"section": lax.rem(section + a, sections), "tensor": lax.rem(tensor + b, count)}
        for a in range(sections)
        for b in range(count)
        if a or b
    ]
    greet(plane + [core_peer(), y_peer()] + cross_peers())
    shares[0].begin()
    cond_act = silu(cond_ref[...].astype(F32)).astype(BF16)
    load_ada.wait()
    mod = dot(cond_act, ada[...]) + ada_b_ref[...].astype(F32)
    mod_src[...] = mod.reshape(mod_src.shape)
    mod_buf[section, tensor] = mod_src[section]
    copies = [
        remote(
            mod_src.at[peer["section"]], mod_buf.at[section, tensor],
            mod_send.at[i], mod_recv.at[i], peer,
        )
        for i, peer in enumerate(plane)
    ]
    bias_buf[section] = biases_ref[...]
    bias_copy = remote(
        biases_ref, bias_buf.at[section],
        mod_send.at[len(plane)], mod_recv.at[len(plane)], x_peer(),
    )
    for share in shares[1:]:
        share.begin()
    cargo.begin()

    def mods():
        wait_all(copies)
        width, piece = mods_ref.shape[-1], mod_buf.shape[-1]
        for block in range(sections):
            for which in range(6):
                parts, at = [], which * width
                while at < (which + 1) * width:
                    end = min((at // piece + 1) * piece, (which + 1) * width)
                    start = at - at // piece * piece
                    parts.append(mod_buf[block, at // piece][:, start : start + end - at])
                    at = end
                mods_ref[block, which] = (
                    jnp.concatenate(parts, axis=1) if len(parts) > 1 else parts[0]
                )
        return mods_ref.at[0]

    def biases():
        bias_copy.wait()
        bias_ref[...] = bias_buf[...]
        return bias_buf[0]

    def need_qkv():
        fetch(0, own_qkv, other_qkv, wqkv, w_sem.at[0]).wait()

    def need_out():
        shares[1].finish()
        fetch(0, own_out, other_out, wo, w_sem.at[1]).wait()

    def after_gather():
        shares[0].forward(shares[0].first)
        shares[1].forward(shares[1].first)
        shares[0].forward_again()
        shares[0].finish()

    def after_scatter():
        shares[2].forward(shares[2].first)
        shares[2].forward_again()

    attend_body(
        count, None, u_ref, mods, (seg_own, seg_col, seg_row), biases, outs, scratch,
        (ag_send, ag_recv, rs_send, rs_recv), need_qkv, need_out, (after_gather, after_scatter),
    )
    cargo.end()
    shares[2].finish()
    shares[3].first.wait()


def attend_kernel(count, block, *refs, cargo):
    u_ref, mods_ref, bias_ref, seg_own, seg_col, seg_row = refs[:6]
    own_qkv, other_qkv, own_out, other_out = refs[6:10]
    outs, scratch, w_sem = refs[10:18], refs[18:25], refs[25]
    load_qkv = fetch(block, own_qkv, other_qkv, scratch[1], w_sem.at[0])
    load_out = fetch(block, own_out, other_out, scratch[2], w_sem.at[1])
    attend_body(
        count, z_peers(count) + cargo.peers(), u_ref, lambda: mods_ref.at[block],
        (seg_own, seg_col, seg_row), lambda: bias_ref[block], outs, scratch, refs[26:30],
        load_qkv.wait, load_out.wait, (cargo.begin, cargo.middle),
    )
    cargo.end()


def mlp_kernel(
    count, block,
    middle_ref, mods_ref, bias_ref, seg_own, w1_own, w1_other, w2_own, w2_other,
    out_ref, branch_ref, full_ref, pre_ref, act_ref,
    full, w1, w2, send_buf, recv_buf, relay_buf, w_sem, *sems, cargo, late,
):
    me = lax.axis_index("tensor")
    rows, length, width = middle_ref.shape
    mod_ref = mods_ref.at[block]
    load_one = fetch(block, w1_own, w1_other, w1, w_sem.at[0])
    normed, unused = layer_norm(flat(middle_ref))
    mlp_in = normed * (1.0 + token_mod(mod_ref, seg_own, 4)) + token_mod(mod_ref, seg_own, 3)
    full[:, own_rows(me, length), :] = mlp_in.astype(BF16).reshape(rows, length, width)
    greet(z_peers(count) + cargo.peers())
    line = Line(length, sems)
    line.start_gather(full)
    cargo.begin()
    line.relay(full)
    load_one.wait()
    line.finish_gather(full)
    full_ref[...] = full[...]
    pre = dot(flat(full), w1[...]) + bias_ref[block, 3:4, : w1.shape[1]]
    pre_ref[...] = pre.reshape(pre_ref.shape)
    cargo.middle()
    if late:
        w2_other = cargo.cargos[0].out_refs[0]
    load_two = fetch(block, w2_own, w2_other, w2, w_sem.at[1])
    act_ref[...] = gelu_tanh(pre).astype(BF16).reshape(act_ref.shape)
    load_two.wait()

    def partial(which_rows):
        return dot(act_ref[:, which_rows, :].reshape(rows * length, -1), w2[...])

    buffers = (send_buf, recv_buf, relay_buf)
    total = line.scatter_sum(partial, buffers)
    branch = line.finish_sum(total, buffers) + bias_ref[block, 4:5, :]
    cargo.end()
    branch_ref[...] = branch.reshape(branch_ref.shape)
    out = flat(middle_ref) + token_mod(mod_ref, seg_own, 5) * branch
    out_ref[...] = out.astype(BF16).reshape(out_ref.shape)


def mlp_back_kernel(count, block, *refs, cargo):
    g_ref, middle_ref, branch_ref, mods_ref, seg_own, full_ref, pre_ref, act_ref = refs[:8]
    w1_own, w1_other, w2_own, w2_other = refs[8:12]
    d_middle_ref, d_mod_ref, d_w1_ref, d_w2_ref, d_b1_ref, d_b2_ref = refs[12:18]
    full, d_pre, w1, w2, *buffers, w_sem = refs[18:26]
    sems = refs[26:]
    me = lax.axis_index("tensor")
    rows, length, width = middle_ref.shape
    mod_ref = mods_ref.at[block]
    load_one = fetch(block, w1_own, w1_other, w1, w_sem.at[0])
    load_two = fetch(block, w2_own, w2_other, w2, w_sem.at[1])
    g = flat(g_ref).astype(F32)
    d_branch = (g * token_mod(mod_ref, seg_own, 5)).astype(BF16)
    full[:, own_rows(me, length), :] = d_branch.reshape(rows, length, width)
    greet(z_peers(count) + cargo.peers())
    line = Line(length, sems)
    line.start_gather(full)
    cargo.begin()
    slot_sums(g * flat(branch_ref), seg_own, d_mod_ref, 2)
    line.relay(full)
    cargo.middle()
    load_two.wait()
    line.finish_gather(full)
    d_act = dot(flat(full), w2[...], NT)
    d_pre[...] = (d_act * gelu_slope(flat(pre_ref))).astype(BF16).reshape(d_pre.shape)
    load_one.wait()

    def partial(which_rows):
        return dot(d_pre[:, which_rows, :].reshape(rows * length, -1), w1[...], NT)

    total = line.scatter_sum(partial, buffers)
    d_b2_ref[...] = jnp.sum(flat(full).astype(F32), axis=0, keepdims=True)
    d_b1_ref[...] = jnp.sum(flat(d_pre).astype(F32), axis=0, keepdims=True)
    d_w2_ref[...] = dot(flat(full), flat(act_ref), TN).astype(BF16)
    d_w1_ref[...] = dot(flat(full_ref), flat(d_pre), TN).astype(BF16)
    d_in = line.finish_sum(total, buffers)
    normed, inverse = layer_norm(flat(middle_ref))
    d_middle = flat(g_ref).astype(F32) + norm_back(
        d_in * (1.0 + token_mod(mod_ref, seg_own, 4)), normed, inverse
    )
    d_middle_ref[...] = d_middle.reshape(d_middle_ref.shape)
    slot_sums(d_in, seg_own, d_mod_ref, 0)
    slot_sums(d_in * normed, seg_own, d_mod_ref, 1)
    cargo.end()


def attend_back_kernel(count, block, *refs, cargo):
    d_middle_ref, u_ref, branch_ref, mods_ref, seg_own, full_ref = refs[:6]
    q_ref, k_ref, v_ref, probs_ref, mixed_ref = refs[6:11]
    wqkv_own, wqkv_other, wo_own, wo_other = refs[11:15]
    d_in_ref, d_mod_ref, d_wqkv_ref, d_wo_ref, d_bqv_ref, d_bo_ref = refs[15:21]
    full, wide, narrow, wqkv, wo, *buffers, w_sem = refs[21:30]
    sems = refs[30:]
    me = lax.axis_index("tensor")
    rows, length, width = u_ref.shape
    heads_width = wo.shape[0]
    heads = heads_width // HEAD_WIDTH
    mod_ref = mods_ref.at[block]
    load_qkv = fetch(block, wqkv_own, wqkv_other, wqkv, w_sem.at[0])
    load_out = fetch(block, wo_own, wo_other, wo, w_sem.at[1])
    d_middle = flat(d_middle_ref)
    d_branch = (d_middle * token_mod(mod_ref, seg_own, 2)).astype(BF16)
    full[:, own_rows(me, length), :] = d_branch.reshape(rows, length, width)
    greet(z_peers(count) + cargo.peers())
    line = Line(length, sems)
    line.start_gather(full)
    cargo.begin()
    slot_sums(d_middle * flat(branch_ref), seg_own, d_mod_ref, 2)
    spread = spread_matrix(heads_width)
    line.relay(full)
    cargo.middle()
    load_out.wait()
    line.finish_gather(full)
    d_mixed = dot(flat(full), wo[...], NT).astype(BF16)
    wide[3] = dot(d_mixed, spread).astype(BF16).reshape(wide.shape[1:])

    def one_head(index, carry):
        row = index // heads
        head = lax.rem(index, heads)
        lanes = pl.ds(pl.multiple_of(head * HEAD_LANES, HEAD_LANES), HEAD_LANES)
        grad = wide[3, row, :, lanes]
        probs = probs_ref[index]
        d_probs = dot(grad, v_ref[row, :, lanes], NT)
        d_scores = (
            probs * (d_probs - jnp.sum(d_probs * probs, axis=-1, keepdims=True))
        ).astype(BF16)
        scale = HEAD_WIDTH ** (-0.5)
        wide[0, row, :, lanes] = (dot(d_scores, k_ref[row, :, lanes]) * scale).astype(BF16)
        wide[1, row, :, lanes] = (dot(d_scores, q_ref[row, :, lanes], TN) * scale).astype(BF16)
        wide[2, row, :, lanes] = dot(probs.astype(BF16), grad, TN).astype(BF16)
        return carry

    lax.fori_loop(0, rows * heads, one_head, 0)
    for which in range(3):
        narrow[which] = (
            dot(flat(wide.at[which]), spread, NT).astype(BF16).reshape(narrow.shape[1:])
        )
    load_qkv.wait()

    def partial(which_rows):
        total = 0.0
        for which in range(3):
            total = total + dot(
                narrow[which, :, which_rows, :].reshape(rows * length, heads_width),
                wqkv[pl.ds(which * width, width), :],
                NT,
            )
        return total

    total = line.scatter_sum(partial, buffers)
    d_bo_ref[...] = jnp.sum(flat(full).astype(F32), axis=0, keepdims=True)
    d_bqv_ref[0:1, :] = jnp.sum(flat(narrow.at[0]).astype(F32), axis=0, keepdims=True)
    d_bqv_ref[1:2, :] = jnp.sum(flat(narrow.at[2]).astype(F32), axis=0, keepdims=True)
    d_wo_ref[...] = dot(flat(full), flat(mixed_ref), TN).astype(BF16)
    for which in range(3):
        d_wqkv_ref[which] = dot(flat(full_ref), flat(narrow.at[which]), TN).astype(BF16)
    d_attn_in = line.finish_sum(total, buffers)
    normed, inverse = layer_norm(flat(u_ref).astype(F32))
    d_in = flat(d_middle_ref) + norm_back(
        d_attn_in * (1.0 + token_mod(mod_ref, seg_own, 1)), normed, inverse
    )
    d_in_ref[...] = d_in.reshape(d_in_ref.shape)
    slot_sums(d_attn_in, seg_own, d_mod_ref, 0)
    slot_sums(d_attn_in * normed, seg_own, d_mod_ref, 1)
    cargo.end()


def silu_slope(value):
    gate = 1.0 / (1.0 + jnp.exp(-value))
    return gate * (1.0 + value * (1.0 - gate))


def project_kernel(token_count, *refs, cargo):
    sent_ref, targets_ref, biases_ref, p2_b_ref, p1_any, p2_any, p3_any = refs[:7]
    d_sent_ref, d_p1_ref, d_p2_ref, d_p3_ref, small_ref = refs[7:12]
    p1, p2, p3, tokens, first_pre, first, second_pre, second, d_second, norms = refs[12:22]
    buf_a, buf_b, buf_c, d_first, load_sem, send, recv = refs[22:]
    core, peer = core_bit(), core_peer()
    loads = [
        local(source, place, load_sem.at[i])
        for i, (source, place) in enumerate(((p1_any, p1), (p2_any, p2), (p3_any, p3)))
    ]
    count = tokens.shape[1]
    tokens[core] = flat(sent_ref)
    greet([peer])

    def trade(ref, which):
        return remote(ref.at[core], ref.at[core], send.at[which], recv.at[which], peer)

    def give(buffer, value, which):
        buffer[0] = value.astype(BF16)
        return remote(buffer.at[0], buffer.at[1], send.at[which], recv.at[which], peer)

    def block(ref, side):
        return ref[side]

    copy = trade(tokens, 0)
    target = [
        targets_ref[slot].reshape(2 * count, targets_ref.shape[-1]).astype(F32) for slot in range(2)
    ]
    target_sq = sum(jnp.sum(one * one, axis=1, keepdims=True) for one in target)
    loads[0].wait()
    copy.wait()
    all_tokens = flat(tokens)
    for slot in range(2):
        pre = dot(all_tokens, p1[slot]) + biases_ref[slot, 0, 0:1, :]
        first_pre[slot] = pre
        first[slot] = silu(pre).astype(BF16)
    loads[1].wait()

    def second_term(side):
        rows = pl.ds(pl.multiple_of(side * count, 16), count)
        return dot(first[0, rows, :], p2[0]) + dot(first[1, rows, :], p2[1])

    copy = give(buf_a, second_term(1 - core), 1)
    pre = second_term(core)
    copy.wait()
    pre = pre + buf_a[1].astype(F32) + p2_b_ref[...].astype(F32)
    second_pre[...] = pre
    second[core] = silu(pre).astype(BF16)
    copy = trade(second, 2)
    loads[2].wait()
    copy.wait()
    all_second = flat(second)
    width = target[0].shape[1]
    predicted = [
        dot(all_second, p3[slot]) + biases_ref[slot, 0, 1:2, :width] for slot in range(2)
    ]
    pred_sq = sum(jnp.sum(one * one, axis=1, keepdims=True) for one in predicted)
    cross = sum(
        jnp.sum(one * two, axis=1, keepdims=True) for one, two in zip(predicted, target)
    )
    lanes = lax.broadcasted_iota(jnp.int32, norms.shape[1:], 1)
    norms[core] = jnp.where(lanes == 0, pred_sq, jnp.where(lanes == 1, cross, target_sq))
    copy = trade(norms, 3)
    copy.wait()
    total = norms[0] + norms[1]
    inv_pred = lax.rsqrt(total[:, 0:1] + COSINE_EPS)
    inv_target = lax.rsqrt(total[:, 2:3] + COSINE_EPS)
    cosine = total[:, 1:2] * inv_pred * inv_target
    side = lax.broadcasted_iota(jnp.int32, cosine.shape, 0)
    own = jnp.logical_and(side >= core * count, side < (core + 1) * count)
    loss = jnp.sum(jnp.where(own, cosine, 0.0), axis=0, keepdims=True)
    factor = -0.5 / token_count
    one_scale = factor * inv_pred * inv_target
    two_scale = factor * cosine * inv_pred * inv_pred
    d_pred = [
        (one_scale * two - two_scale * one).astype(BF16) for one, two in zip(predicted, target)
    ]
    small_ref[...] = jnp.zeros_like(small_ref)
    for slot in range(2):
        small_ref[2 * core + slot, 1:2, :width] = jnp.sum(
            d_pred[slot].astype(F32), axis=0, keepdims=True
        )

    def d_second_term(side):
        terms = 0.0
        for slot in range(2):
            mine = jnp.where(
                side == 0, d_pred[slot][:count].astype(F32), d_pred[slot][count:].astype(F32)
            )
            terms = terms + dot(mine.astype(BF16), p3[slot], NT)
        return terms

    copy = give(buf_b, d_second_term(1 - core), 4)
    grad = d_second_term(core)
    for slot in range(2):
        d_p3_ref[slot] = dot(all_second, d_pred[slot], TN).astype(BF16)
    copy.wait()
    grad = ((grad + buf_b[1].astype(F32)) * silu_slope(second_pre[...])).astype(BF16)
    d_second[core] = grad
    copy = trade(d_second, 5)
    d_p2_b = jnp.sum(grad.astype(F32), axis=0, keepdims=True)
    lane = small_ref.shape[2]
    loss_row = jnp.where(lax.broadcasted_iota(jnp.int32, (1, lane), 1) == 0, loss, 0.0)
    for part in range(4):
        for row in range(d_p2_b.shape[1] // lane):
            small_ref[part, 2 + row : 3 + row, :] = d_p2_b[:, row * lane : (row + 1) * lane]
        small_ref[part, 6:7, :] = loss_row
    copy.wait()
    all_d_second = flat(d_second)
    for slot in range(2):
        back = dot(all_d_second, p2[slot], NT) * silu_slope(first_pre[slot])
        d_first[slot] = back.astype(BF16)
        small_ref[2 * core + slot, 0:1, :] = jnp.sum(
            d_first[slot].astype(F32), axis=0, keepdims=True
        )

    def d_sent_term(side):
        rows = pl.ds(pl.multiple_of(side * count, 16), count)
        return dot(d_first[0, rows, :], p1[0], NT) + dot(d_first[1, rows, :], p1[1], NT)

    copy = give(buf_c, d_sent_term(1 - core), 6)
    grad = d_sent_term(core)
    for slot in range(2):
        d_p2_ref[slot] = dot(first[slot], all_d_second, TN).astype(BF16)
        d_p1_ref[slot] = dot(all_tokens, d_first[slot], TN).astype(BF16)
    copy.wait()
    d_sent_ref[...] = (grad + buf_c[1].astype(F32)).reshape(d_sent_ref.shape)


def close_kernel(count, sections, replicas, *refs, cargo):
    grads_ref, mod_refs, small_refs, proj_ref, cond_ref = (
        refs[:2], refs[2:6], refs[6:14], refs[14], refs[15]
    )
    grad_ref, ada_w_ref, ada_b_ref, small_ref, proj_sum_ref = refs[16:21]
    z_src, z_buf, mod_src, mod_buf, small_src, small_buf, cond_buf = refs[21:28]
    place_src, place_buf, proj_got, proj_src, proj_buf = refs[28:33]
    sems = refs[33:35]
    section, tensor, replica = (lax.axis_index(name) for name in ("section", "tensor", "dp"))
    send, recv = sems
    others = [
        {"section": lax.rem(section + a, sections), "dp": lax.rem(replica + b, replicas)}
        for a in range(sections)
        for b in range(replicas)
        if a or b
    ]
    greet(z_peers(count) + others + cross_peers())
    for one in cargo.cargos:
        if isinstance(one, LastSum):
            one.begin()
    piece = z_src.shape[-1]
    for block in range(sections):
        attend_mod, mlp_mod = mod_refs[2 * block : 2 * block + 2]
        width = attend_mod.shape[-1]
        for part in range(count):
            at, end, cuts = part * piece, (part + 1) * piece, []
            while at < end:
                which = at // width
                stop = min((which + 1) * width, end)
                ref = attend_mod if which < 3 else mlp_mod
                cuts.append(ref[which % 3][:, at - which * width : stop - which * width])
                at = stop
            z_src[part, block] = jnp.concatenate(cuts, axis=1) if len(cuts) > 1 else cuts[0]
    z_copies = [
        remote(z_src.at[peer["tensor"]], z_buf.at[i], send.at[i], recv.at[i], peer)
        for i, peer in enumerate(z_peers(count))
    ]
    at = count - 1
    z_copies += [
        remote(proj_ref.at[peer["tensor"]], proj_got.at[i], send.at[at + i], recv.at[at + i], peer)
        for i, peer in enumerate(z_peers(count))
    ]
    at = at + count - 1

    @pl.when(section == 0)
    def first_place():
        place_src[...] = grads_ref[1][...].astype(BF16)

    @pl.when(section != 0)
    def second_place():
        place_src[...] = grads_ref[0][...].astype(BF16)

    place_copy = remote(place_src, place_buf, send.at[at], recv.at[at], x_peer())
    at = at + 1
    heads_width = small_refs[0].shape[-1]
    small_src[...] = jnp.zeros_like(small_src)
    for block in range(sections):
        d_bqv, d_bo, d_b1, d_b2 = small_refs[4 * block : 4 * block + 4]
        small_src[block, 0:2, :heads_width] = d_bqv[...]
        small_src[block, 2:3, :] = d_bo[...]
        small_src[block, 3:4, : d_b1.shape[1]] = d_b1[...]
        small_src[block, 4:5, :] = d_b2[...]
    small_buf[section, replica] = small_src[section]
    cond_buf[section, replica] = cond_ref[replica]
    copies = []
    for peer in others:
        copies.append(
            remote(
                small_src.at[peer["section"]], small_buf.at[section, replica],
                send.at[at], recv.at[at], peer,
            )
        )
        copies.append(
            remote(
                cond_ref.at[peer["dp"]], cond_buf.at[section, replica],
                send.at[at + 1], recv.at[at + 1], peer,
            )
        )
        at = at + 2
    cargo.middle()
    wait_all(z_copies)
    mine, mine_proj = z_src[tensor], proj_ref[tensor]
    for step in range(count - 1):
        mine = mine + z_buf[step]
        mine_proj = mine_proj + proj_got[step]
    mod_src[...] = mine
    mod_buf[section, replica] = mod_src[section]
    proj_src[...] = mine_proj
    proj_buf[section, replica] = mine_proj
    for peer in others:
        copies.append(
            remote(
                mod_src.at[peer["section"]], mod_buf.at[section, replica],
                send.at[at], recv.at[at], peer,
            )
        )
        copies.append(
            remote(
                proj_src, proj_buf.at[section, replica], send.at[at + 1], recv.at[at + 1], peer
            )
        )
        at = at + 2
    for one in cargo.cargos:
        if not isinstance(one, LastSum):
            one.begin()
    for one in cargo.cargos:
        if isinstance(one, LastSum):
            one.to_x()
    place_copy.wait()
    rows = place_buf.shape[0]

    @pl.when(section == 0)
    def first_out():
        grad_ref[:rows] = grads_ref[0][...]
        grad_ref[rows:] = place_buf[...].astype(F32)

    @pl.when(section != 0)
    def second_out():
        grad_ref[rows:] = grads_ref[1][...]
        grad_ref[:rows] = place_buf[...].astype(F32)

    wait_all(copies)
    small, proj_sum = small_buf[0, 0], proj_buf[0, 0]
    for a in range(sections):
        for b in range(replicas):
            if a or b:
                small = small + small_buf[a, b]
                proj_sum = proj_sum + proj_buf[a, b]
    small_ref[...] = small
    proj_sum_ref[...] = proj_sum
    mod_all = flat(mod_buf)
    ada_b_ref[...] = jnp.sum(mod_all, axis=0, keepdims=True)
    ada_w_ref[...] = lax.dot_general(
        flat(cond_buf), mod_all, TN, precision=HIGHEST, preferred_element_type=F32
    )
    cargo.end()


VMEM = pl.BlockSpec(memory_space=pltpu.VMEM)
ANY = pl.BlockSpec(memory_space=pl.ANY)
MOD_ROWS = 8


def call(kernel, number, inputs, in_any, outs, out_any, scratch, flops, cargos=()):
    own_in, own_out, own_scratch = len(inputs), len(outs), len(scratch)
    specs = [VMEM] * (own_in - in_any) + [ANY] * in_any
    out_specs = [ANY if i in out_any else VMEM for i in range(own_out)]
    inputs, outs, scratch, aliases = list(inputs), list(outs), list(scratch), {}
    for cargo in cargos:
        for source, target in cargo.aliases.items():
            aliases[len(inputs) + source] = len(outs) + target
        inputs += cargo.inputs
        outs += cargo.outs
        scratch += cargo.scratch
        specs += [ANY] * len(cargo.inputs)
        out_specs += [ANY if cargo.any_outs else VMEM] * len(cargo.outs)

    def body(*refs):
        parts = [list(refs[: len(inputs)])]
        parts.append(list(refs[len(inputs) : len(inputs) + len(outs)]))
        parts.append(list(refs[len(inputs) + len(outs) :]))
        base = parts[0][:own_in] + parts[1][:own_out] + parts[2][:own_scratch]
        at = [own_in, own_out, own_scratch]
        for cargo in cargos:
            held = []
            for i, items in enumerate((cargo.inputs, cargo.outs, cargo.scratch)):
                held.append(parts[i][at[i] : at[i] + len(items)])
                at[i] += len(items)
            cargo.bind(*held)
        kernel(*base, cargo=Bundle(cargos))

    moved = sum(math.prod(one.shape) * one.dtype.itemsize for one in inputs)
    results = pl.pallas_call(
        body,
        out_shape=[jax.ShapeDtypeStruct(shape, dtype) for shape, dtype in outs],
        in_specs=specs,
        out_specs=out_specs,
        scratch_shapes=scratch,
        input_output_aliases=aliases,
        compiler_params=pltpu.CompilerParams(
            collective_id=number, has_side_effects=True, vmem_limit_bytes=56 * 2**20
        ),
        cost_estimate=pl.CostEstimate(flops=flops, bytes_accessed=moved, transcendentals=0),
    )(*inputs)
    at, carried = own_out, []
    for cargo in cargos:
        carried.append(results[at : at + len(cargo.outs)])
        at += len(cargo.outs)
    return results[:own_out], carried


def exchange_scratch(count, rows, length, width):
    return [
        pltpu.VMEM((count - 1, rows, length, width), BF16),
        pltpu.VMEM((count, rows, length, width), BF16),
        pltpu.VMEM((rows, length, width), BF16),
    ]


def semaphores(count):
    return [pltpu.SemaphoreType.DMA((2,))] + [
        pltpu.SemaphoreType.DMA((size,)) for size in (count, count, count - 1, count + 1)
    ]


class Shapes:
    def __init__(self, u, own, count):
        self.rows, self.length, self.width = u.shape
        self.count = count
        self.positions = self.length * count
        self.tokens = self.rows * self.positions
        self.heads_width = own["out"].shape[0]
        self.hidden = own["one"].shape[1]
        self.heads = self.heads_width // HEAD_WIDTH
        self.local = (self.rows, self.length, self.width)
        self.full = (self.rows, self.positions, self.width)
        self.wide = (self.rows, self.positions, self.heads * HEAD_LANES)
        self.own = own
        self.attend_outs = [
            (self.local, F32), (self.local, F32), (self.full, BF16),
            (self.wide, BF16), (self.wide, BF16), (self.wide, BF16),
            ((self.rows * self.heads, self.positions, self.positions), F32),
            ((self.rows, self.positions, self.heads_width), BF16),
        ]
        self.attend_scratch = [
            pltpu.VMEM(self.full, BF16),
            pltpu.VMEM(own["qkv"].shape, BF16),
            pltpu.VMEM(own["out"].shape, BF16),
            pltpu.VMEM(self.wide, BF16),
        ] + exchange_scratch(count, *self.local)
        self.mods = (3, MOD_ROWS, self.width)


def pairs(own, other, names):
    out = []
    for name in names:
        out += [own[name], other[name]]
    return out


def open_forward(sizes, u, cond, ada_w, ada_b, biases, segs, own, sections, cargos):
    count, width = sizes.count, sizes.width
    piece = ada_w.shape[1]
    inputs = [u, cond, ada_b, biases, *segs, ada_w] + [own[n] for n in ("qkv", "out", "one", "two")]
    plane = sections * count - 1
    results, carried = call(
        functools.partial(open_kernel, count, sections),
        0,
        inputs,
        5,
        [((sections, 6, MOD_ROWS, width), F32), ((sections,) + biases.shape, F32)]
        + [(own[n].shape, BF16) for n in ("qkv", "out", "one", "two")]
        + sizes.attend_outs,
        (2, 3, 4, 5),
        sizes.attend_scratch
        + [
            pltpu.VMEM(ada_w.shape, BF16),
            pltpu.VMEM((sections, MOD_ROWS, piece), F32),
            pltpu.VMEM((sections, count, MOD_ROWS, piece), F32),
            pltpu.VMEM((sections,) + biases.shape, F32),
        ]
        + semaphores(count)
        + [
            pltpu.SemaphoreType.DMA((plane + 1,)),
            pltpu.SemaphoreType.DMA((plane + 1,)),
            pltpu.SemaphoreType.DMA((4, 4)),
            pltpu.SemaphoreType.DMA((4, 4)),
            pltpu.SemaphoreType.DMA,
        ],
        2 * sizes.tokens * width * sizes.heads_width * 4,
        cargos,
    )
    other = dict(zip(("qkv", "out", "one", "two"), results[2:6]))
    return results[0], results[1], other, results[6:], carried


def attend_forward(sizes, block, u, mods, biases, segs, own, other, cargos):
    inputs = [u, mods, biases, *segs] + pairs(own, other, ("qkv", "out"))
    return call(
        functools.partial(attend_kernel, sizes.count, block),
        1,
        inputs,
        4,
        sizes.attend_outs,
        (),
        sizes.attend_scratch + semaphores(sizes.count),
        2 * sizes.tokens * sizes.width * sizes.heads_width * 4,
        cargos,
    )


def mlp_forward(sizes, block, middle, mods, biases, segs, own, other, late, cargos):
    inputs = [middle, mods, biases, segs[0]] + pairs(own, other, ("one", "two"))
    hidden = (sizes.rows, sizes.positions, sizes.hidden)
    return call(
        functools.partial(mlp_kernel, sizes.count, block, late=late),
        2 + block,
        inputs,
        4,
        [
            (sizes.local, BF16), (sizes.local, F32), (sizes.full, BF16),
            (hidden, F32), (hidden, BF16),
        ],
        (),
        [
            pltpu.VMEM(sizes.full, BF16),
            pltpu.VMEM(own["one"].shape, BF16),
            pltpu.VMEM(own["two"].shape, BF16),
        ]
        + exchange_scratch(sizes.count, *sizes.local)
        + semaphores(sizes.count),
        2 * sizes.tokens * sizes.width * sizes.hidden * 2,
        cargos,
    )


def mlp_backward(sizes, block, g, attend, mlp, mods, segs, own, other, cargos):
    out, branch, full, pre, act = mlp
    inputs = [g, attend[0], branch, mods, segs[0], full, pre, act]
    inputs += pairs(own, other, ("one", "two"))
    return call(
        functools.partial(mlp_back_kernel, sizes.count, block),
        4 + block,
        inputs,
        4,
        [
            (sizes.local, F32), (sizes.mods, F32),
            ((sizes.width, sizes.hidden), BF16), ((sizes.width, sizes.hidden), BF16),
            ((1, sizes.hidden), F32), ((1, sizes.width), F32),
        ],
        (),
        [
            pltpu.VMEM(sizes.full, BF16),
            pltpu.VMEM((sizes.rows, sizes.positions, sizes.hidden), BF16),
            pltpu.VMEM(own["one"].shape, BF16),
            pltpu.VMEM(own["two"].shape, BF16),
        ]
        + exchange_scratch(sizes.count, *sizes.local)
        + semaphores(sizes.count),
        2 * sizes.tokens * sizes.width * sizes.hidden * 4,
        cargos,
    )


def attend_backward(sizes, block, d_middle, u, attend, mods, segs, own, other, cargos):
    middle, branch, full, q, k, v, probs, mixed = attend
    inputs = [d_middle, u, branch, mods, segs[0], full, q, k, v, probs, mixed]
    inputs += pairs(own, other, ("qkv", "out"))
    return call(
        functools.partial(attend_back_kernel, sizes.count, block),
        6 + block,
        inputs,
        4,
        [
            (sizes.local, F32), (sizes.mods, F32),
            ((3, sizes.width, sizes.heads_width), BF16), ((sizes.width, sizes.heads_width), BF16),
            ((2, sizes.heads_width), F32), ((1, sizes.width), F32),
        ],
        (),
        [
            pltpu.VMEM(sizes.full, BF16),
            pltpu.VMEM((4,) + sizes.wide, BF16),
            pltpu.VMEM((3, sizes.rows, sizes.positions, sizes.heads_width), BF16),
            pltpu.VMEM(own["qkv"].shape, BF16),
            pltpu.VMEM(own["out"].shape, BF16),
        ]
        + exchange_scratch(sizes.count, *sizes.local)
        + semaphores(sizes.count),
        2 * sizes.tokens * sizes.width * sizes.heads_width * 8,
        cargos,
    )


def project(sizes, sent, weights, targets, biases, p2_b, token_count):
    tokens = sizes.rows * sizes.length
    p1, p2, p3 = weights
    lane, hidden = p1.shape[2], p2.shape[2]
    inputs = [sent, targets, biases, p2_b, p1, p2, p3]
    results, unused = call(
        functools.partial(project_kernel, token_count),
        9,
        inputs,
        3,
        [
            (sizes.local, F32), (p1.shape, BF16), (p2.shape, BF16), (p3.shape, BF16),
            ((sizes.count, MOD_ROWS, lane), F32),
        ],
        (),
        [
            pltpu.VMEM(p1.shape, BF16),
            pltpu.VMEM(p2.shape, BF16),
            pltpu.VMEM(p3.shape, BF16),
            pltpu.VMEM((2, tokens, sizes.width), BF16),
            pltpu.VMEM((2, 2 * tokens, lane), F32),
            pltpu.VMEM((2, 2 * tokens, lane), BF16),
            pltpu.VMEM((tokens, hidden), F32),
            pltpu.VMEM((2, tokens, hidden), BF16),
            pltpu.VMEM((2, tokens, hidden), BF16),
            pltpu.VMEM((2, 2 * tokens, HEAD_LANES), F32),
            pltpu.VMEM((2, tokens, hidden), BF16),
            pltpu.VMEM((2, tokens, hidden), BF16),
            pltpu.VMEM((2, tokens, sizes.width), BF16),
            pltpu.VMEM((2, 2 * tokens, lane), BF16),
            pltpu.SemaphoreType.DMA((3,)),
            pltpu.SemaphoreType.DMA((7,)),
            pltpu.SemaphoreType.DMA((7,)),
        ],
        12 * tokens * sum(math.prod(one.shape) for one in weights),
    )
    return results


def close_backward(sizes, grads, mod_grads, small, proj_small, cond, sections, replicas, cargos):
    count, width = sizes.count, sizes.width
    piece = 6 * width // count
    share = width // replicas
    inputs = [*grads, *mod_grads, *small, proj_small, cond]
    copies = 2 * count + 4 * (sections * replicas - 1)
    both = (sections * sizes.rows,) + sizes.local[1:]
    return call(
        functools.partial(close_kernel, count, sections, replicas),
        8,
        inputs,
        0,
        [
            (both, F32), ((share, piece), F32), ((1, piece), F32),
            ((MOD_ROWS, width), F32), (proj_small.shape[1:], F32),
        ],
        (),
        [
            pltpu.VMEM((count, sections, MOD_ROWS, piece), F32),
            pltpu.VMEM((count - 1, sections, MOD_ROWS, piece), F32),
            pltpu.VMEM((sections, MOD_ROWS, piece), F32),
            pltpu.VMEM((sections, replicas, MOD_ROWS, piece), F32),
            pltpu.VMEM((sections, MOD_ROWS, width), F32),
            pltpu.VMEM((sections, replicas, MOD_ROWS, width), F32),
            pltpu.VMEM((sections, replicas, MOD_ROWS, share), F32),
            pltpu.VMEM(sizes.local, BF16),
            pltpu.VMEM(sizes.local, BF16),
            pltpu.VMEM((count - 1,) + proj_small.shape[1:], F32),
            pltpu.VMEM(proj_small.shape[1:], F32),
            pltpu.VMEM((sections, replicas) + proj_small.shape[1:], F32),
            pltpu.SemaphoreType.DMA((copies,)),
            pltpu.SemaphoreType.DMA((copies,)),
        ],
        2 * sections * replicas * MOD_ROWS * share * piece,
        cargos,
    )


def halve(value, axis, bit, position):
    size = lax.axis_size(axis)
    mine = (lax.axis_index(axis) & bit) // bit
    keep = lax.dynamic_index_in_dim(value, mine, position, keepdims=False)
    give = lax.dynamic_index_in_dim(value, 1 - mine, position, keepdims=False)
    return keep + lax.ppermute(give, axis, [(i, i ^ bit) for i in range(size)])


def sum_beyond_quads(value):
    size = lax.axis_size("dp")
    if size == 4:
        return value
    quads = size // 4
    bits = quads.bit_length() - 1
    lead = value.ndim - 2
    shape = value.shape
    value = value.reshape(shape[:lead] + (2,) * bits + (shape[-2] // quads, shape[-1]))
    for bit in range(bits):
        value = halve(value, "dp", 4 << bit, lead + bits - 1 - bit)
    route = [(high * 4 + low, low * quads + high) for high in range(quads) for low in range(4)]
    return lax.ppermute(value, "dp", route)


def per_device(
    block_eight_input,
    cond,
    image_slot_index,
    targets,
    cot,
    ada_w,
    ada_b,
    query_key_value_weight,
    query_value_bias,
    attention_output_weight,
    attention_output_bias,
    hidden_weight,
    hidden_bias,
    output_weight_mlp,
    output_bias_mlp,
    p1_w,
    p1_b,
    p2_w,
    p2_b,
    p3_w,
    p3_b,
):
    section = lax.axis_index("section")
    tensor = lax.axis_index("tensor")
    is_first = section == 0
    count = lax.axis_size("tensor")
    sections = lax.axis_size("section")
    replicas = lax.axis_size("dp")
    length, replica_rows, width = block_eight_input.shape
    positions = length * count
    rows = replica_rows // sections
    total_token_count = positions * replica_rows * replicas
    heads_width = attention_output_weight.shape[1]
    hidden = hidden_weight.shape[2]

    def my_rows(value, axis):
        return lax.dynamic_slice_in_dim(value, section * rows, rows, axis)

    def to_rows(value):
        return jnp.transpose(my_rows(value, 1), (1, 0, 2))

    own = {
        "qkv": jnp.transpose(query_key_value_weight[0], (1, 0, 2)).reshape(3 * width, heads_width),
        "out": attention_output_weight[0],
        "one": hidden_weight[0],
        "two": output_weight_mlp[0],
    }

    def padded(value):
        return jnp.pad(value.astype(F32), ((0, 0), (0, width - value.shape[-1])))

    biases = jnp.concatenate(
        [
            padded(query_value_bias[0]), padded(attention_output_bias), padded(hidden_bias),
            padded(output_bias_mlp), jnp.zeros((MOD_ROWS - 5, width), F32),
        ],
        axis=0,
    )
    used = rows * IMAGES_PER_ROW
    cond_pad = jnp.pad(
        cond.reshape(sections, used, width), ((0, 0), (0, MOD_ROWS - used), (0, 0))
    )
    segs_full = my_rows(image_slot_index, 0)
    seg_own = lax.dynamic_slice_in_dim(segs_full, tensor * length, length, 1)
    segs = (seg_own[:, :, None], segs_full[:, :, None], segs_full[:, None, :])

    target_parts = my_rows(targets, 1).reshape(count, length, rows, targets.shape[2])
    target_parts = jnp.transpose(target_parts, (0, 2, 1, 3))
    lane = p1_b.shape[0]
    proj_biases = jnp.concatenate(
        [
            p1_b.astype(F32)[None],
            jnp.pad(p3_b.astype(F32), (0, lane - p3_b.shape[0]))[None],
            jnp.zeros((MOD_ROWS - 2, lane), F32),
        ],
        axis=0,
    )
    gather = ColumnGather((p1_w, p2_w, p3_w), target_parts, proj_biases, sections)

    u = to_rows(block_eight_input)
    sizes = Shapes(u, own, count)
    mods, bias_all, other, attend_one, carried = open_forward(
        sizes, u, cond_pad.reshape(-1, width), ada_w[0], ada_b, biases, segs, own, sections,
        (gather,),
    )
    *proj_weights, target_all, proj_bias_all = carried[0]
    mlp_one, carried = mlp_forward(
        sizes, 0, attend_one[0], mods, bias_all, segs, own, other, True,
        (LateShare(other["two"]), ShareAlong(proj_weights, False)),
    )
    other["two"] = carried[0][0]
    proj_weights = carried[1]
    first_out = mlp_one[0]
    attend_two, carried = attend_forward(
        sizes, 1, first_out, mods, bias_all, segs, own, other, (ShareAlong(proj_weights, True),)
    )
    proj_weights = carried[0]
    mlp_two, carried = mlp_forward(
        sizes, 1, attend_two[0], mods, bias_all, segs, own, other, False, ()
    )
    second_out = mlp_two[0]

    grad_sent, grad_p1, grad_p2, grad_p3, proj_small = project(
        sizes, first_out, proj_weights, target_all, proj_bias_all, p2_b[None], total_token_count
    )

    back = (mods, segs, own, other)
    (d_middle_two, mod_mlp_two, *mlp_grads_two), carried = mlp_backward(
        sizes, 1, to_rows(cot), attend_two, mlp_two, *back,
        [HalfSum(grad_p2, 1, "x"), Swap(first_out, second_out)],
    )
    (grad_p2,), (other_out,) = carried
    (second_grad, mod_attend_two, *attend_grads_two), carried = attend_backward(
        sizes, 1, d_middle_two, first_out, attend_two, *back,
        [QuadSum(grad) for grad in mlp_grads_two[:2]]
        + [HalfSum(grad_p1, 0, "x"), HalfSum(grad_p3, 0, "x")],
    )
    mlp_parts_two, ((grad_p1,), (grad_p3,)) = carried[:2], carried[2:]
    (d_middle_one, mod_mlp_one, *mlp_grads_one), carried = mlp_backward(
        sizes, 0, second_grad + grad_sent, attend_one, mlp_one, *back,
        [QuadSum(grad) for grad in attend_grads_two[:2]]
        + [SectionSum(part) for part, in mlp_parts_two]
        + [HalfSum(grad_p2, 1, "y")],
    )
    attend_parts_two, sums_mlp_two, ((grad_p2,),) = carried[:2], carried[2:4], carried[4:]
    (first_grad, mod_attend_one, *attend_grads_one), carried = attend_backward(
        sizes, 0, d_middle_one, u, attend_one, *back,
        [QuadSum(mlp_grads_one[0]), QuadSumX(mlp_grads_one[1])]
        + [SectionSum(part) for part, in attend_parts_two]
        + [HalfSum(grad_p1, 0, "y"), HalfSum(grad_p3, 0, "y"), ColumnSum(grad_p2, 1)],
    )
    ((mlp_part_one,), (mlp_part_two,)), sums_attend_two = carried[:2], carried[2:4]
    (grad_p1,), (grad_p3,), (red_p2_w,) = carried[4:]

    cond_act = silu(my_rows(cond, 0).astype(F32)).astype(BF16).astype(F32)
    share = width // replicas
    cond_cols = jnp.pad(cond_act.reshape(used, width), ((0, MOD_ROWS - used), (0, 0)))
    cond_cols = jnp.transpose(cond_cols.reshape(MOD_ROWS, replicas, share), (1, 0, 2))
    small = [
        attend_grads_one[2], attend_grads_one[3], mlp_grads_one[2], mlp_grads_one[3],
        attend_grads_two[2], attend_grads_two[3], mlp_grads_two[2], mlp_grads_two[3],
    ]
    (section_grad, grad_ada_w, grad_ada_b, small, proj_small), carried = close_backward(
        sizes, (first_grad, second_grad),
        (mod_attend_one, mod_mlp_one, mod_attend_two, mod_mlp_two),
        small, proj_small, cond_cols, sections, replicas,
        [LastSum(grad) for grad in attend_grads_one[:2]]
        + [SectionSum(mlp_part_one), LastY(mlp_part_two)]
        + [ColumnSum(grad_p1, 0), ColumnSum(grad_p3, 0)],
    )
    sums_attend_one, sums_mlp_one, ((red_p1_w,), (red_p3_w,)) = carried[:2], carried[2:4], carried[4:]

    red_fc1, red_fc2, red_qkv, red_out = [
        sum_beyond_quads(jnp.where(is_first, one[0], two[0]))
        for one, two in zip(
            list(sums_mlp_one) + list(sums_attend_one), list(sums_mlp_two) + list(sums_attend_two)
        )
    ]
    red_p1_w, red_p3_w = sum_beyond_quads(red_p1_w), sum_beyond_quads(red_p3_w)
    if replicas > 4:
        red_p2_w = sum_beyond_quads(red_p2_w.T).T
    align_loss = -0.5 * proj_small[6, 0] / total_token_count
    own_out = jnp.where(is_first, first_out, second_out)
    section_out = jnp.where(
        is_first,
        jnp.concatenate([own_out, other_out], axis=0),
        jnp.concatenate([other_out, own_out], axis=0),
    )
    return (
        jnp.transpose(section_out, (1, 0, 2))[None],
        jnp.transpose(section_grad, (1, 0, 2))[None],
        align_loss,
        grad_ada_w[None],
        grad_ada_b,
        jnp.transpose(red_qkv, (1, 0, 2))[None],
        small[0:2, :heads_width][None],
        red_out.T[None],
        small[2:3],
        red_fc1[None],
        small[3:4, :hidden],
        red_fc2.T[None],
        small[4:5],
        red_p1_w,
        proj_small[0],
        red_p2_w,
        proj_small[2:6].reshape(-1)[: p2_b.shape[0]],
        red_p3_w,
        proj_small[1, : p3_b.shape[0]],
    )


def solution(mesh):
    in_specs = (
        P("tensor", "dp", None),
        P("dp", None, None),
        P("dp", None),
        P(None, "dp", "tensor"),
        P("tensor", "dp", None),
        P("section", None, "tensor"),
        P("section", "tensor"),
        P("section", None, None, "tensor"),
        P("section", None, "tensor"),
        P("section", "tensor", None),
        P("section", None),
        P("section", None, "tensor"),
        P("section", "tensor"),
        P("section", "tensor", None),
        P("section", None),
        P(None, "tensor"),
        P("tensor"),
        P("tensor", None),
        P(),
        P(None, "tensor"),
        P("tensor"),
    )
    out_specs = (
        P("section", "tensor", "dp", None),
        P("section", "tensor", "dp", None),
        P(),
        P("section", "dp", "tensor"),
        P("section", "tensor"),
        P("section", "dp", None, "tensor"),
        P("section", None, "tensor"),
        P("section", "tensor", "dp"),
        P("section", None),
        P("section", "dp", "tensor"),
        P("section", "tensor"),
        P("section", "tensor", "dp"),
        P("section", None),
        P(("section", "dp"), "tensor"),
        P("tensor"),
        P("tensor", ("section", "dp")),
        P(),
        P(("section", "dp"), "tensor"),
        P("tensor"),
    )
    return jax.shard_map(
        per_device, mesh=mesh, in_specs=in_specs, out_specs=out_specs, check_vma=False
    )
```

```python
import functools
import math

import jax
import jax.numpy as jnp
from jax import lax
from jax.experimental import pallas as pl
from jax.experimental.pallas import tpu as pltpu
from jax.sharding import PartitionSpec as P

HEAD_WIDTH = 72
HEAD_LANES = 128
IMAGES_PER_ROW = 3
NORM_EPS = 1e-06
COSINE_EPS = 1e-06
MASKED_SCORE = -1e30
HIGHEST = lax.Precision.HIGHEST
MESH = pl.DeviceIdType.MESH
F32 = jnp.float32
BF16 = jnp.bfloat16
NN = (((1,), (0,)), ((), ()))
NT = (((1,), (1,)), ((), ()))
TN = (((0,), (0,)), ((), ()))


def dot(left, right, form=NN):
    return lax.dot_general(left, right, form, preferred_element_type=F32)


def z_peers(count):
    me = lax.axis_index("tensor")
    return [{"tensor": lax.rem(me + step, count)} for step in range(1, count)]


def x_peer():
    return {"section": 1 - lax.axis_index("section")}


def core_bit():
    return lax.rem(lax.axis_index("dp"), 2)


def y_bit():
    return lax.rem(lax.axis_index("dp") // 2, 2)


def core_peer():
    return {"dp": lax.axis_index("dp") + 1 - 2 * core_bit()}


def y_peer():
    return {"dp": lax.axis_index("dp") + 2 - 4 * y_bit()}


def greet(peers):
    barrier = pltpu.get_barrier_semaphore()
    for peer in peers:
        pl.semaphore_signal(barrier, inc=1, device_id=peer, device_id_type=MESH)
    pl.semaphore_wait(barrier, len(peers))


def remote(source, target, send_sem, recv_sem, peer):
    copy = describe(source, target, send_sem, recv_sem, peer)
    copy.start()
    return copy


def local(source, target, sem):
    copy = pltpu.make_async_copy(source, target, sem)
    copy.start()
    return copy


def own_rows(me, length):
    return pl.ds(pl.multiple_of(me * length, 16), length)


def describe(source, target, send_sem, recv_sem, peer):
    return pltpu.make_async_remote_copy(
        src_ref=source,
        dst_ref=target,
        send_sem=send_sem,
        recv_sem=recv_sem,
        device_id=peer,
        device_id_type=MESH,
    )


def wait_all(copies):
    for copy in copies:
        copy.wait()


class Line:
    def __init__(self, length, sems):
        self.length, (self.ag_send, self.ag_recv, self.rs_send, self.rs_recv) = length, sems
        self.me = lax.axis_index("tensor")
        self.mirror = 3 - self.me
        self.near = self.me + 1 - 2 * lax.rem(self.me, 2)
        self.opposite = lax.rem(self.me + 2, 4)
        self.is_end = jnp.logical_or(self.me == 0, self.me == 3)
        self.is_middle = jnp.logical_not(self.is_end)

    def block(self, full, place, which, peer):
        part = full.at[:, own_rows(place, self.length)]
        return describe(
            part, part, self.ag_send.at[which], self.ag_recv.at[place], {"tensor": peer}
        )

    def start_gather(self, full):
        self.block(full, self.me, 0, self.opposite).start()
        self.block(full, self.me, 1, self.near).start()

        @pl.when(self.is_middle)
        def to_mirror():
            self.block(full, self.me, 2, self.mirror).start()

    def relay(self, full):
        self.block(full, self.opposite, 2, self.mirror).wait_recv()

        @pl.when(self.is_middle)
        def pass_on():
            self.block(full, self.opposite, 3, 3 - self.opposite).start()

    def finish_gather(self, full):
        self.block(full, self.near, 1, self.near).wait_recv()
        self.block(full, self.mirror, 1, self.near).wait_recv()
        self.block(full, self.me, 0, self.opposite).wait_send()
        self.block(full, self.me, 1, self.near).wait_send()

        @pl.when(self.is_middle)
        def sent():
            self.block(full, self.me, 2, self.mirror).wait_send()
            self.block(full, self.opposite, 3, 3 - self.opposite).wait_send()

    def scatter_sum(self, partial, buffers):
        send_buf, recv_buf, relay_buf = buffers
        me, relay_sem = self.me, 4

        def term(peer):
            return partial(own_rows(peer, self.length))

        def keep(which, value):
            send_buf[which] = value.astype(BF16).reshape(send_buf.shape[1:])

        self.to_mirror = describe(
            send_buf.at[0], recv_buf.at[me], self.rs_send.at[0], self.rs_recv.at[me],
            {"tensor": self.mirror},
        )
        self.to_relay = describe(
            send_buf.at[0], relay_buf, self.rs_send.at[0], self.rs_recv.at[relay_sem],
            {"tensor": self.near},
        )
        self.to_near = describe(
            send_buf.at[1], recv_buf.at[me], self.rs_send.at[1], self.rs_recv.at[me],
            {"tensor": self.near},
        )
        self.to_opposite = describe(
            send_buf.at[2], recv_buf.at[me], self.rs_send.at[2], self.rs_recv.at[me],
            {"tensor": self.opposite},
        )
        keep(0, term(self.mirror))

        @pl.when(self.is_end)
        def first_end():
            self.to_relay.start()
            relay_buf[...] = jnp.zeros_like(relay_buf)
            recv_buf[self.mirror] = jnp.zeros(recv_buf.shape[1:], BF16)

        @pl.when(self.is_middle)
        def first_middle():
            self.to_mirror.start()

        keep(1, term(self.near))
        self.to_near.start()
        last = term(self.opposite)

        @pl.when(self.is_middle)
        def relayed():
            self.to_relay.wait_recv()

        keep(2, last + relay_buf[...].reshape(last.shape).astype(F32))
        self.to_opposite.start()
        return term(me)

    def finish_sum(self, total, buffers):
        send_buf, recv_buf, relay_buf = buffers

        def got(source):
            describe(
                send_buf.at[1], recv_buf.at[source], self.rs_send.at[1], self.rs_recv.at[source],
                {"tensor": self.near},
            ).wait_recv()

        got(self.near)
        got(self.opposite)

        @pl.when(self.is_middle)
        def third():
            got(self.mirror)

        self.to_near.wait_send()
        self.to_opposite.wait_send()
        self.to_mirror.wait_send()
        for source in (self.near, self.opposite, self.mirror):
            total = total + recv_buf[source].reshape(total.shape).astype(F32)
        return total


def fetch(block, own_ref, other_ref, target, sem):
    mine = lax.axis_index("section") == block

    @pl.when(mine)
    def own_start():
        pltpu.make_async_copy(own_ref, target, sem).start()

    @pl.when(jnp.logical_not(mine))
    def other_start():
        pltpu.make_async_copy(other_ref, target, sem).start()

    return pltpu.make_async_copy(own_ref, target, sem)


def layer_norm(rows):
    centred = rows - jnp.mean(rows, axis=-1, keepdims=True)
    inverse = lax.rsqrt(jnp.mean(centred * centred, axis=-1, keepdims=True) + NORM_EPS)
    return centred * inverse, inverse


def norm_back(grad, normed, inverse):
    mean_grad = jnp.mean(grad, axis=-1, keepdims=True)
    mean_cross = jnp.mean(grad * normed, axis=-1, keepdims=True)
    return inverse * (grad - mean_grad - normed * mean_cross)


def token_mod(mod_ref, seg_ref, which):
    parts = []
    for row in range(seg_ref.shape[0]):
        seg = seg_ref[row]
        line = [
            mod_ref[which, pl.ds(row * IMAGES_PER_ROW + slot, 1), :]
            for slot in range(IMAGES_PER_ROW)
        ]
        value = line[-1]
        for slot in range(IMAGES_PER_ROW - 2, -1, -1):
            value = jnp.where(seg == slot, line[slot], value)
        parts.append(value)
    return jnp.concatenate(parts, axis=0)


def slot_sums(value, seg_ref, out_ref, which):
    length = seg_ref.shape[1]
    lines = []
    for row in range(seg_ref.shape[0]):
        seg = seg_ref[row]
        piece = value[row * length : (row + 1) * length]
        for slot in range(IMAGES_PER_ROW):
            lines.append(jnp.sum(jnp.where(seg == slot, piece, 0.0), axis=0, keepdims=True))
    spare = out_ref.shape[1] - len(lines)
    lines.append(jnp.zeros((spare, value.shape[1]), F32))
    out_ref[which] = jnp.concatenate(lines, axis=0)


def flat(ref):
    return ref[...].reshape(-1, ref.shape[-1])


def spread_matrix(width):
    lanes = width // HEAD_WIDTH * HEAD_LANES
    source = lax.broadcasted_iota(jnp.int32, (width, lanes), 0)
    target = lax.broadcasted_iota(jnp.int32, (width, lanes), 1)
    within = target & (HEAD_LANES - 1)
    head = target >> (HEAD_LANES.bit_length() - 1)
    hit = (within < HEAD_WIDTH) & (source == head * HEAD_WIDTH + within)
    return jnp.where(hit, 1.0, 0.0).astype(BF16)


def gelu_tanh(pre):
    inner = math.sqrt(2.0 / math.pi) * (pre + 0.044715 * (pre * pre * pre))
    return 0.5 * pre * (1.0 + jnp.tanh(inner))


def gelu_slope(pre):
    scale = math.sqrt(2.0 / math.pi)
    square = pre * pre
    tanh = jnp.tanh(scale * (pre + 0.044715 * (pre * square)))
    return 0.5 * (1.0 + tanh) + 0.5 * pre * (1.0 - tanh * tanh) * scale * (
        1.0 + 3 * 0.044715 * square
    )


def silu(value):
    return value / (1.0 + jnp.exp(-value))


class Share:
    def __init__(self, own, other, parts, sems):
        self.own, self.other, self.parts = own, other, parts
        self.send, self.recv = sems
        self.size = own.shape[0] // parts
        self.copies = []

    def rows(self, core, y):
        part = core if self.parts == 2 else core + 2 * y
        return pl.ds(pl.multiple_of(part * self.size, 16), self.size)

    def begin(self):
        rows = self.rows(core_bit(), y_bit())
        self.first = remote(
            self.own.at[rows], self.other.at[rows], self.send.at[0], self.recv.at[0], x_peer()
        )

    def forward(self, first):
        if first is not None:
            first.wait()
        mine = self.other.at[self.rows(core_bit(), y_bit())]
        self.copies.append(remote(mine, mine, self.send.at[1], self.recv.at[1], core_peer()))
        if self.parts == 4:
            self.second = remote(mine, mine, self.send.at[2], self.recv.at[2], y_peer())

    def forward_again(self):
        if self.parts == 4:
            self.second.wait()
            got = self.other.at[self.rows(core_bit(), 1 - y_bit())]
            self.copies.append(remote(got, got, self.send.at[3], self.recv.at[3], core_peer()))

    def finish(self):
        wait_all(self.copies)


class Cargo:
    inputs, outs, scratch, aliases, any_outs = (), (), (), {}, False

    def bind(self, inputs, outs, scratch):
        self.ins, self.out_refs, self.held = inputs, outs, scratch

    def peers(self):
        return []

    def begin(self):
        pass

    def middle(self):
        pass

    def late(self):
        pass

    def end(self):
        pass


def quarter(shape):
    return shape[:-2] + (shape[-2] // 4, shape[-1])


class CoreSum:
    def __init__(self, whole, got, out, sems):
        self.whole, self.got, self.out, self.sems = whole, got, out, sems
        self.size = whole.shape[-2] // 4

    def rows(self, core, y):
        part = pl.ds(pl.multiple_of((core + 2 * y) * self.size, 16), self.size)
        whole = self.whole
        return whole.at[:, part] if len(whole.shape) == 3 else whole.at[part]

    def begin(self):
        self.copies = [
            remote(
                self.rows(1 - core_bit(), y), self.got.at[y],
                self.sems.at[0, y], self.sems.at[1, y], core_peer(),
            )
            for y in range(2)
        ]

    def end(self):
        wait_all(self.copies)
        for y in range(2):
            mine = self.rows(core_bit(), y)[...]
            self.out[y] = (mine.astype(F32) + self.got[y].astype(F32)).astype(BF16)


def core_sum_scratch(shape):
    return [
        pltpu.VMEM(shape, BF16),
        pltpu.VMEM((2,) + quarter(shape), BF16),
        pltpu.SemaphoreType.DMA((2, 2)),
    ]


class YSum(Cargo):
    def __init__(self, parts, dtype):
        part = parts.shape[1:]
        self.inputs = (parts,)
        self.outs = ((part, dtype),)
        self.scratch = (
            pltpu.VMEM(part, BF16),
            pltpu.VMEM(part, BF16),
            pltpu.SemaphoreType.DMA((3,)),
        )

    def peers(self):
        return ["y"]

    def begin(self):
        mine, other, sems = self.held
        self.copies = [
            remote(self.ins[0].at[1 - y_bit()], other, sems.at[0], sems.at[1], y_peer()),
            local(self.ins[0].at[y_bit()], mine, sems.at[2]),
        ]

    def end(self):
        mine, other, sems = self.held
        out = self.out_refs[0]
        wait_all(self.copies)
        out[...] = (mine[...].astype(F32) + other[...].astype(F32)).astype(out.dtype)


class SectionSum(Cargo):
    def __init__(self, part, owner, dtype=F32):
        self.owner = owner
        self.inputs = (part,)
        self.outs = ((part.shape, dtype),)
        self.scratch = (
            pltpu.VMEM(part.shape, BF16),
            pltpu.VMEM(part.shape, BF16),
            pltpu.SemaphoreType.DMA((3,)),
        )

    def peers(self):
        return ["x"]

    def source(self):
        return self.ins[0]

    def begin(self):
        mine, other, sems = self.held
        self.copy = describe(self.source(), other, sems.at[0], sems.at[1], x_peer())
        self.load = pltpu.make_async_copy(self.source(), mine, sems.at[2])
        is_owner = lax.axis_index("section") == self.owner

        @pl.when(is_owner)
        def take():
            self.load.start()

        @pl.when(jnp.logical_not(is_owner))
        def give():
            self.copy.start()

    def end(self):
        mine, other, sems = self.held
        is_owner = lax.axis_index("section") == self.owner

        @pl.when(is_owner)
        def add():
            self.load.wait()
            self.copy.wait_recv()
            out = self.out_refs[0]
            out[...] = (mine[...].astype(F32) + other[...].astype(F32)).astype(out.dtype)

        @pl.when(jnp.logical_not(is_owner))
        def given():
            self.copy.wait_send()
            self.out_refs[0][...] = jnp.zeros_like(self.out_refs[0])


class LastSum(YSum):
    def __init__(self, parts, owner):
        super().__init__(parts, F32)
        part = parts.shape[1:]
        self.owner = owner
        self.scratch = self.scratch + (
            pltpu.VMEM(part, BF16),
            pltpu.VMEM(part, BF16),
            pltpu.SemaphoreType.DMA((2,)),
        )

    def peers(self):
        return ["y", "x"]

    def begin(self):
        self.held, self.last = self.held[:3], self.held[3:]
        super().begin()

    def to_x(self):
        mine, other, sems = self.held
        total, got, last_sems = self.last
        wait_all(self.copies)
        total[...] = (mine[...].astype(F32) + other[...].astype(F32)).astype(BF16)
        self.copy = describe(total, got, last_sems.at[0], last_sems.at[1], x_peer())

        @pl.when(lax.axis_index("section") != self.owner)
        def give():
            self.copy.start()

    def end(self):
        total, got, last_sems = self.last
        is_owner = lax.axis_index("section") == self.owner

        @pl.when(is_owner)
        def add():
            self.copy.wait_recv()
            self.out_refs[0][...] = total[...].astype(F32) + got[...].astype(F32)

        @pl.when(jnp.logical_not(is_owner))
        def given():
            self.copy.wait_send()
            self.out_refs[0][...] = jnp.zeros_like(self.out_refs[0])


class LateShare(Cargo):
    any_outs = True

    def __init__(self, other):
        self.inputs = (other,)
        self.outs = ((other.shape, BF16),)
        self.aliases = {0: 0}
        self.scratch = (pltpu.SemaphoreType.DMA((4,)), pltpu.SemaphoreType.DMA((4,)))

    def peers(self):
        return ["core", "y"]

    def begin(self):
        out = self.out_refs[0]
        self.share = Share(out, out, 4, self.held)
        self.share.forward(None)

    def middle(self):
        self.share.forward_again()

    def late(self):
        self.share.finish()


class Swap(Cargo):
    def __init__(self, one, two):
        self.inputs = (one, two)
        self.outs = ((one.shape, one.dtype),)
        self.scratch = (pltpu.VMEM(one.shape, one.dtype), pltpu.SemaphoreType.DMA((2,)))

    def peers(self):
        return ["x"]

    def begin(self):
        got, sems = self.held
        one, two = self.ins
        self.copy = describe(two, got, sems.at[0], sems.at[1], x_peer())
        is_first = lax.axis_index("section") == 0

        @pl.when(is_first)
        def give_two():
            self.copy.start()

        @pl.when(jnp.logical_not(is_first))
        def give_one():
            describe(one, got, sems.at[0], sems.at[1], x_peer()).start()

    def end(self):
        self.copy.wait()
        self.out_refs[0][...] = self.held[0][...]


def span(ref, axis, start, size):
    part = pl.ds(pl.multiple_of(start, 128 if axis == 1 else 16), size)
    lead = (slice(None),) * (len(ref.shape) - 2)
    return ref.at[lead + ((slice(None), part) if axis == 1 else (part, slice(None)))]


def cut(shape, axis, by):
    shape = list(shape)
    shape[axis - 2] //= by
    return tuple(shape)


class HalfSum(Cargo):
    def __init__(self, grad, axis, name, slots=None):
        self.slots = slots if slots is not None else (0, grad.shape[0])
        part = cut((self.slots[1],) + grad.shape[1:], axis, 2)
        self.axis, self.name, self.size = axis, name, part[axis - 2]
        self.inputs = (grad,)
        self.outs = ((part, BF16),)
        self.scratch = (
            pltpu.VMEM(part, BF16),
            pltpu.VMEM(part, BF16),
            pltpu.SemaphoreType.DMA((3,)),
        )

    def peers(self):
        return [self.name]

    def begin(self):
        mine, other, sems = self.held
        if self.name == "x":
            bit, peer = lax.axis_index("section"), x_peer()
        else:
            bit, peer = y_bit(), y_peer()
        grad = self.ins[0].at[pl.ds(*self.slots)]
        self.copies = [
            remote(
                span(grad, self.axis, (1 - bit) * self.size, self.size), other,
                sems.at[0], sems.at[1], peer,
            ),
            local(span(grad, self.axis, bit * self.size, self.size), mine, sems.at[2]),
        ]

    def end(self):
        mine, other, sems = self.held
        wait_all(self.copies)
        self.out_refs[0][...] = (mine[...].astype(F32) + other[...].astype(F32)).astype(BF16)


class ColumnGather(Cargo):
    any_outs = True

    def __init__(self, weights, targets, biases, sections):
        self.inputs = (*weights, targets, biases)
        self.outs = tuple(((2,) + one.shape, BF16) for one in weights) + (
            ((2, 2) + targets.shape[1:], BF16),
            ((2, 2) + biases.shape, F32),
        )
        self.scratch = (
            pltpu.SemaphoreType.DMA((5, 6)),
            pltpu.SemaphoreType.DMA((5, 2, 2)),
            pltpu.SemaphoreType.DMA((5,)),
        )

    def peers(self):
        return ["core", "cross"]

    def pieces(self, target):
        tensor, core = lax.axis_index("tensor"), core_bit()
        eighth = lax.axis_index("section") * 4 + y_bit() * 2 + core
        slot, out = lax.rem(tensor, 2), []
        for source, place in zip(self.ins[:3], self.out_refs[:3]):
            size = source.shape[0] // 8
            rows = pl.ds(pl.multiple_of(eighth * size, 16), size)
            out.append((source.at[rows], place.at[slot, rows]))
        out.append((self.ins[3].at[target], self.out_refs[3].at[slot, core]))
        out.append((self.ins[4], self.out_refs[4].at[slot, core]))
        return out

    def copies(self, step):
        tensor, core = lax.axis_index("tensor"), core_bit()
        send, recv, own = self.held
        target = lax.rem(tensor + step, 4)
        peer = {"tensor": target, "dp": lax.axis_index("dp") - core + tensor // 2}
        return [
            describe(source, place, send.at[i, step], recv.at[i, lax.rem(tensor, 2), core], peer)
            for i, (source, place) in enumerate(self.pieces(target))
        ]

    def stays(self):
        return core_bit() == lax.axis_index("tensor") // 2

    def own_copies(self):
        own = self.held[2]
        return [
            pltpu.make_async_copy(source, place, own.at[i])
            for i, (source, place) in enumerate(self.pieces(lax.axis_index("tensor")))
        ]

    def direct(self, step, i):
        if step == 2 or i > 2:
            return None
        return lax.axis_index("tensor") != (3 if step == 1 else 0)

    def each(self, which, act):
        for step in range(1, 4):
            for i, copy in enumerate(self.copies(step)):
                if i in which:
                    allowed = self.direct(step, i)
                    if allowed is None:
                        act(copy)
                    else:

                        @pl.when(allowed)
                        def go(copy=copy):
                            act(copy)

    def start(self, which):
        self.each(which, lambda copy: copy.start())

        @pl.when(self.stays())
        def keep():
            for i, copy in enumerate(self.own_copies()):
                if i in which:
                    copy.start()

        @pl.when(jnp.logical_not(self.stays()))
        def give():
            for i, copy in enumerate(self.copies(0)):
                if i in which:
                    copy.start()

    def passes_on(self):
        tensor, core = lax.axis_index("tensor"), core_bit()
        return jnp.logical_or(
            jnp.logical_and(tensor == 2, core == 0), jnp.logical_and(tensor == 1, core == 1)
        )

    def passed(self, i, other):
        send, recv, own = self.held
        tensor, slot = lax.axis_index("tensor"), core_bit()
        place = self.out_refs[i]
        size = self.ins[i].shape[0] // 8
        eighth = lax.axis_index("section") * 4 + y_bit() * 2 + other
        part = place.at[slot, pl.ds(pl.multiple_of(eighth * size, 16), size)]
        return describe(
            part, part, send.at[i, 4 + other], recv.at[i, slot, other], {"tensor": 3 * (tensor - 1)}
        )

    def relay(self, which):
        @pl.when(self.passes_on())
        def pass_on():
            for i in which:
                for other in range(2):
                    copy = self.passed(i, other)
                    copy.wait_recv()
                    copy.start()

    def begin(self):
        self.start((2, 3, 4))

    def middle(self):
        self.relay((2,))
        self.start((0,))

    def late(self):
        self.relay((0,))
        self.start((1,))

    def end(self):
        send, recv, own = self.held
        tensor, core = lax.axis_index("tensor"), core_bit()
        self.relay((1,))
        self.each(range(5), lambda copy: copy.wait_send())

        @pl.when(self.stays())
        def kept():
            for copy in self.own_copies():
                copy.wait()

        @pl.when(jnp.logical_not(self.stays()))
        def given():
            for copy in self.copies(0):
                copy.wait_send()

        @pl.when(self.passes_on())
        def passed_on():
            for i in range(3):
                for other in range(2):
                    self.passed(i, other).wait_send()

        for slot in range(2):
            for other in range(2):
                mine = jnp.logical_and(2 * core + slot == tensor, core == other)
                relayed = jnp.logical_and(self.passes_on(), core == slot)
                peer = {"tensor": lax.rem(tensor + 1, 4)}
                waits = [
                    describe(source, place, send.at[i, 1], recv.at[i, slot, other], peer)
                    for i, (source, place) in enumerate(self.pieces(tensor))
                ]

                @pl.when(jnp.logical_not(mine))
                def arrived(waits=waits):
                    for copy in waits[3:]:
                        copy.wait_recv()

                @pl.when(jnp.logical_not(jnp.logical_or(mine, relayed)))
                def weights_arrived(waits=waits):
                    for copy in waits[:3]:
                        copy.wait_recv()


class ShareAlong(Cargo):
    any_outs = True

    def __init__(self, weights, stage):
        self.inputs = tuple(weights)
        self.outs = tuple((one.shape, BF16) for one in weights)
        self.aliases = {0: 0, 1: 1, 2: 2}
        self.stage = stage
        self.scratch = (pltpu.SemaphoreType.DMA((4,)), pltpu.SemaphoreType.DMA((4,)))

    def peers(self):
        return ["x", "y"]

    def begin(self):
        send, recv = self.held
        section, y, self.copies = lax.axis_index("section"), y_bit(), []

        def give(which, start, parts, peer):
            ref = self.out_refs[which]
            size = ref.shape[1] // 4
            part = ref.at[:, pl.ds(pl.multiple_of(start * size, 16), parts * size)]
            i = len(self.copies)
            self.copies.append(remote(part, part, send.at[i], recv.at[i], peer))

        if self.stage == 0:
            give(1, 2 * section + y, 1, x_peer())
            give(0, 2 * section + y, 1, y_peer())
            give(2, 2 * section + y, 1, y_peer())
        elif self.stage == 1:
            give(0, 2 * section, 2, x_peer())
            give(1, y, 1, y_peer())
        else:
            give(2, 2 * section, 2, x_peer())
            give(1, 2 + y, 1, y_peer())

    def end(self):
        wait_all(self.copies)


class ColumnSum(Cargo):
    def __init__(self, grads, axis):
        self.axis = axis
        self.part = cut(grads[0].shape[1:], axis, 2)
        self.inputs = tuple(grads)
        self.outs = ((self.part, F32),)
        self.scratch = (
            pltpu.VMEM((4,) + self.part, BF16),
            pltpu.SemaphoreType.DMA((4,)),
            pltpu.SemaphoreType.DMA((4,)),
            pltpu.SemaphoreType.DMA,
        )

    def peers(self):
        return ["core", "cross"]

    def copy(self, slot, other):
        got, send, recv, own = self.held
        tensor, core = lax.axis_index("tensor"), core_bit()
        size = self.part[self.axis]
        ref = self.ins[0].at[slot] if len(self.ins) == 1 else self.ins[slot].at[0]
        source = span(ref, self.axis, other * size, size)
        peer = {"tensor": 2 * core + slot, "dp": lax.axis_index("dp") - core + other}
        mine = jnp.logical_and(2 * core + slot == tensor, core == other)
        away = describe(source, got.at[tensor], send.at[2 * slot + other], recv.at[tensor], peer)
        return mine, away, pltpu.make_async_copy(source, got.at[tensor], own)

    def each(self, act_away, act_own):
        for slot in range(2):
            for other in range(2):
                mine, away, own = self.copy(slot, other)

                @pl.when(mine)
                def stay(own=own):
                    act_own(own)

                @pl.when(jnp.logical_not(mine))
                def leave(away=away):
                    act_away(away)

    def begin(self):
        self.each(lambda copy: copy.start(), lambda copy: copy.start())

    def end(self):
        got, send, recv, own = self.held
        tensor, core = lax.axis_index("tensor"), core_bit()
        self.each(lambda copy: copy.wait_send(), lambda copy: copy.wait())
        for source in range(4):
            mine = jnp.logical_and(tensor == source, core == tensor // 2)

            @pl.when(jnp.logical_not(mine))
            def arrived(source=source):
                describe(
                    got.at[source], got.at[source], send.at[0], recv.at[source],
                    {"tensor": lax.rem(tensor + 1, 4)},
                ).wait_recv()

        total = got[0].astype(F32)
        for source in range(1, 4):
            total = total + got[source].astype(F32)
        self.out_refs[0][...] = total


def cross_peers():
    tensor, dp = lax.axis_index("tensor"), core_peer()["dp"]
    return [{"tensor": lax.rem(tensor + step, 4), "dp": dp} for step in range(1, 4)]


class Bundle:
    def __init__(self, cargos):
        self.cargos = cargos

    def peers(self, names=()):
        names = list(names) + [name for cargo in self.cargos for name in cargo.peers()]
        known = {"core": core_peer, "y": y_peer, "x": x_peer}
        cross = cross_peers() if "cross" in names else []
        return [make() for name, make in known.items() if name in names] + cross

    def begin(self):
        for cargo in self.cargos:
            cargo.begin()

    def middle(self):
        for cargo in self.cargos:
            cargo.middle()

    def late(self):
        for cargo in self.cargos:
            cargo.late()

    def end(self):
        for cargo in self.cargos:
            cargo.end()


def attend_body(
    count, peers, u_ref, mods, segs, biases, outs, scratch, sems, need_qkv, need_out, steps
):
    middle_ref, branch_ref, full_ref, q_ref, k_ref, v_ref, probs_ref, mixed_ref = outs
    full, wqkv, wo, mixed_wide = scratch[:4]
    buffers = scratch[4:7]
    seg_own, seg_col, seg_row = segs
    mod_ref = mods()
    me = lax.axis_index("tensor")
    rows, length, width = u_ref.shape
    heads_width = wo.shape[0]
    heads = heads_width // HEAD_WIDTH
    u = flat(u_ref).astype(F32)
    normed, unused = layer_norm(u)
    attn_in = normed * (1.0 + token_mod(mod_ref, seg_own, 1)) + token_mod(mod_ref, seg_own, 0)
    full[:, own_rows(me, length), :] = attn_in.astype(BF16).reshape(rows, length, width)
    if peers is not None:
        greet(peers)
    line = Line(length, sems)
    line.start_gather(full)
    spread = spread_matrix(heads_width)
    line.relay(full)
    steps[0]()
    need_qkv()
    line.finish_gather(full)
    full_ref[...] = full[...]
    tokens = flat(full)
    bias = biases()
    for which, target in ((0, q_ref), (1, k_ref), (2, v_ref)):
        projected = dot(tokens, wqkv[pl.ds(which * width, width), :])
        if which != 1:
            projected = projected + bias[which // 2 : which // 2 + 1, :heads_width]
        target[...] = dot(projected.astype(BF16), spread).astype(BF16).reshape(target.shape)

    def one_head(index, carry):
        row = index // heads
        head = lax.rem(index, heads)
        lanes = pl.ds(pl.multiple_of(head * HEAD_LANES, HEAD_LANES), HEAD_LANES)
        scores = dot(q_ref[row, :, lanes], k_ref[row, :, lanes], NT) * HEAD_WIDTH ** (-0.5)
        scores = jnp.where(seg_col[row] == seg_row[row], scores, MASKED_SCORE)
        raised = jnp.exp(scores - jnp.max(scores, axis=-1, keepdims=True))
        probs = raised / jnp.sum(raised, axis=-1, keepdims=True)
        probs_ref[index] = probs
        mixed_wide[row, :, lanes] = dot(probs.astype(BF16), v_ref[row, :, lanes]).astype(BF16)
        return carry

    steps[1]()
    lax.fori_loop(0, rows * heads, one_head, 0)
    mixed_ref[...] = dot(flat(mixed_wide), spread, NT).astype(BF16).reshape(mixed_ref.shape)
    need_out()

    def partial(which_rows):
        return dot(mixed_ref[:, which_rows, :].reshape(rows * length, heads_width), wo[...])

    total = line.scatter_sum(partial, buffers)
    steps[2]()
    branch = line.finish_sum(total, buffers) + bias[2:3, :]
    branch_ref[...] = branch.reshape(branch_ref.shape)
    middle = flat(u_ref).astype(F32) + token_mod(mod_ref, seg_own, 2) * branch
    middle_ref[...] = middle.reshape(middle_ref.shape)


def open_kernel(count, sections, *refs, cargo):
    u_ref, cond_ref, ada_b_ref, biases_ref, seg_own, seg_col, seg_row = refs[:7]
    ada_w, own_qkv, own_out, own_one, own_two = refs[7:12]
    mods_ref, bias_ref, other_qkv, other_out, other_one, other_two = refs[12:18]
    outs = refs[18:26]
    scratch = refs[26:33]
    ada, mod_src, mod_buf, bias_buf, w_sem, ag_send, ag_recv, rs_send, rs_recv = refs[33:42]
    mod_send, mod_recv, share_send, share_recv, ada_sem = refs[42:]
    wqkv, wo = scratch[1:3]
    section, tensor = lax.axis_index("section"), lax.axis_index("tensor")
    load_ada = local(ada_w, ada, ada_sem)
    shares = [
        Share(own, other, parts, (share_send.at[i], share_recv.at[i]))
        for i, (own, other, parts) in enumerate(
            (
                (own_qkv, other_qkv, 4), (own_out, other_out, 2),
                (own_one, other_one, 4), (own_two, other_two, 4),
            )
        )
    ]
    plane = [
        {"section": lax.rem(section + a, sections), "tensor": lax.rem(tensor + b, count)}
        for a in range(sections)
        for b in range(count)
        if a or b
    ]
    greet(plane + [core_peer(), y_peer()] + cross_peers())
    shares[0].begin()
    cargo.begin()
    cond_act = silu(cond_ref[...].astype(F32)).astype(BF16)
    load_ada.wait()
    mod = dot(cond_act, ada[...]) + ada_b_ref[...].astype(F32)
    mod_src[...] = mod.reshape(mod_src.shape)
    mod_buf[section, tensor] = mod_src[section]
    copies = [
        remote(
            mod_src.at[peer["section"]], mod_buf.at[section, tensor],
            mod_send.at[i], mod_recv.at[i], peer,
        )
        for i, peer in enumerate(plane)
    ]
    bias_buf[section] = biases_ref[...]
    bias_copy = remote(
        biases_ref, bias_buf.at[section],
        mod_send.at[len(plane)], mod_recv.at[len(plane)], x_peer(),
    )
    for share in shares[1:]:
        share.begin()

    def mods():
        wait_all(copies)
        width, piece = mods_ref.shape[-1], mod_buf.shape[-1]
        for block in range(sections):
            for which in range(6):
                parts, at = [], which * width
                while at < (which + 1) * width:
                    end = min((at // piece + 1) * piece, (which + 1) * width)
                    start = at - at // piece * piece
                    parts.append(mod_buf[block, at // piece][:, start : start + end - at])
                    at = end
                mods_ref[block, which] = (
                    jnp.concatenate(parts, axis=1) if len(parts) > 1 else parts[0]
                )
        return mods_ref.at[0]

    def biases():
        bias_copy.wait()
        bias_ref[...] = bias_buf[...]
        return bias_buf[0]

    def need_qkv():
        fetch(0, own_qkv, other_qkv, wqkv, w_sem.at[0]).wait()

    def need_out():
        shares[1].finish()
        fetch(0, own_out, other_out, wo, w_sem.at[1]).wait()

    def after_gather():
        shares[0].forward(shares[0].first)
        cargo.middle()
        shares[1].forward(shares[1].first)
        shares[0].forward_again()
        shares[0].finish()

    def before_heads():
        shares[2].forward(shares[2].first)

    def after_scatter():
        cargo.late()
        shares[2].forward_again()
        shares[2].finish()

    attend_body(
        count, None, u_ref, mods, (seg_own, seg_col, seg_row), biases, outs, scratch,
        (ag_send, ag_recv, rs_send, rs_recv), need_qkv, need_out,
        (after_gather, before_heads, after_scatter),
    )
    shares[3].first.wait()
    cargo.end()


def attend_kernel(count, block, *refs, cargo):
    u_ref, mods_ref, bias_ref, seg_own, seg_col, seg_row = refs[:6]
    own_qkv, other_qkv, own_out, other_out = refs[6:10]
    outs, scratch, w_sem = refs[10:18], refs[18:25], refs[25]
    load_qkv = fetch(block, own_qkv, other_qkv, scratch[1], w_sem.at[0])
    load_out = fetch(block, own_out, other_out, scratch[2], w_sem.at[1])
    attend_body(
        count, z_peers(count) + cargo.peers(), u_ref, lambda: mods_ref.at[block],
        (seg_own, seg_col, seg_row), lambda: bias_ref[block], outs, scratch, refs[26:30],
        load_qkv.wait, load_out.wait, (cargo.begin, cargo.middle, cargo.late),
    )
    cargo.end()


def mlp_kernel(
    count, block,
    middle_ref, mods_ref, bias_ref, seg_own, w1_own, w1_other, w2_own, w2_other,
    out_ref, branch_ref, full_ref, pre_ref, act_ref,
    full, w1, w2, send_buf, recv_buf, relay_buf, w_sem, *sems, cargo,
):
    me = lax.axis_index("tensor")
    rows, length, width = middle_ref.shape
    mod_ref = mods_ref.at[block]
    load_one = fetch(block, w1_own, w1_other, w1, w_sem.at[0])
    late = [one for one in cargo.cargos if isinstance(one, LateShare)]
    if not late:
        load_two = fetch(block, w2_own, w2_other, w2, w_sem.at[1])
    normed, unused = layer_norm(flat(middle_ref))
    mlp_in = normed * (1.0 + token_mod(mod_ref, seg_own, 4)) + token_mod(mod_ref, seg_own, 3)
    full[:, own_rows(me, length), :] = mlp_in.astype(BF16).reshape(rows, length, width)
    greet(z_peers(count) + cargo.peers())
    line = Line(length, sems)
    line.start_gather(full)
    cargo.begin()
    line.relay(full)
    load_one.wait()
    line.finish_gather(full)
    full_ref[...] = full[...]
    pre = dot(flat(full), w1[...]) + bias_ref[block, 3:4, : w1.shape[1]]
    pre_ref[...] = pre.reshape(pre_ref.shape)
    cargo.middle()
    act_ref[...] = gelu_tanh(pre).astype(BF16).reshape(act_ref.shape)
    cargo.late()
    if late:
        load_two = fetch(block, w2_own, late[0].out_refs[0], w2, w_sem.at[1])
    load_two.wait()

    def partial(which_rows):
        return dot(act_ref[:, which_rows, :].reshape(rows * length, -1), w2[...])

    buffers = (send_buf, recv_buf, relay_buf)
    total = line.scatter_sum(partial, buffers)
    branch = line.finish_sum(total, buffers) + bias_ref[block, 4:5, :]
    cargo.end()
    branch_ref[...] = branch.reshape(branch_ref.shape)
    out = flat(middle_ref) + token_mod(mod_ref, seg_own, 5) * branch
    out_ref[...] = out.astype(BF16).reshape(out_ref.shape)


def mlp_back_kernel(count, block, *refs, cargo):
    g_ref, middle_ref, branch_ref, mods_ref, seg_own, full_ref, pre_ref, act_ref = refs[:8]
    w1_own, w1_other, w2_own, w2_other = refs[8:12]
    d_middle_ref, d_mod_ref, d_w1_ref, d_w2_ref, d_b1_ref, d_b2_ref = refs[12:18]
    full, d_pre, w1, w2, *buffers, w_sem = refs[18:26]
    sems = refs[26:30]
    w1_whole, w1_got, w1_sems, w2_whole, w2_got, w2_sems = refs[30:]
    w1_sum = CoreSum(w1_whole, w1_got, d_w1_ref, w1_sems)
    w2_sum = CoreSum(w2_whole, w2_got, d_w2_ref, w2_sems)
    me = lax.axis_index("tensor")
    rows, length, width = middle_ref.shape
    mod_ref = mods_ref.at[block]
    load_one = fetch(block, w1_own, w1_other, w1, w_sem.at[0])
    load_two = fetch(block, w2_own, w2_other, w2, w_sem.at[1])
    g = flat(g_ref).astype(F32)
    d_branch = (g * token_mod(mod_ref, seg_own, 5)).astype(BF16)
    full[:, own_rows(me, length), :] = d_branch.reshape(rows, length, width)
    greet(z_peers(count) + cargo.peers(["core"]))
    line = Line(length, sems)
    line.start_gather(full)
    cargo.begin()
    slot_sums(g * flat(branch_ref), seg_own, d_mod_ref, 2)
    line.relay(full)
    cargo.middle()
    load_two.wait()
    line.finish_gather(full)
    d_act = dot(flat(full), w2[...], NT)
    d_pre[...] = (d_act * gelu_slope(flat(pre_ref))).astype(BF16).reshape(d_pre.shape)
    load_one.wait()

    def partial(which_rows):
        return dot(d_pre[:, which_rows, :].reshape(rows * length, -1), w1[...], NT)

    total = line.scatter_sum(partial, buffers)
    w2_whole[...] = dot(flat(full), flat(act_ref), TN).astype(BF16)
    w2_sum.begin()
    w1_whole[...] = dot(flat(full_ref), flat(d_pre), TN).astype(BF16)
    w1_sum.begin()
    d_b2_ref[...] = jnp.sum(flat(full).astype(F32), axis=0, keepdims=True)
    d_b1_ref[...] = jnp.sum(flat(d_pre).astype(F32), axis=0, keepdims=True)
    d_in = line.finish_sum(total, buffers)
    normed, inverse = layer_norm(flat(middle_ref))
    d_middle = flat(g_ref).astype(F32) + norm_back(
        d_in * (1.0 + token_mod(mod_ref, seg_own, 4)), normed, inverse
    )
    d_middle_ref[...] = d_middle.reshape(d_middle_ref.shape)
    slot_sums(d_in, seg_own, d_mod_ref, 0)
    slot_sums(d_in * normed, seg_own, d_mod_ref, 1)
    w2_sum.end()
    w1_sum.end()
    cargo.end()


def attend_back_kernel(count, block, *refs, cargo):
    d_middle_ref, u_ref, branch_ref, mods_ref, seg_own, full_ref = refs[:6]
    q_ref, k_ref, v_ref, probs_ref, mixed_ref = refs[6:11]
    wqkv_own, wqkv_other, wo_own, wo_other = refs[11:15]
    d_in_ref, d_mod_ref, d_wqkv_ref, d_wo_ref, d_bqv_ref, d_bo_ref = refs[15:21]
    full, wide, narrow, wqkv, wo, *buffers, w_sem = refs[21:30]
    sems = refs[30:34]
    qkv_whole, qkv_got, qkv_sems, wo_whole, wo_got, wo_sems = refs[34:]
    qkv_sum = CoreSum(qkv_whole, qkv_got, d_wqkv_ref, qkv_sems)
    wo_sum = CoreSum(wo_whole, wo_got, d_wo_ref, wo_sems)
    me = lax.axis_index("tensor")
    rows, length, width = u_ref.shape
    heads_width = wo.shape[0]
    heads = heads_width // HEAD_WIDTH
    mod_ref = mods_ref.at[block]
    load_qkv = fetch(block, wqkv_own, wqkv_other, wqkv, w_sem.at[0])
    load_out = fetch(block, wo_own, wo_other, wo, w_sem.at[1])
    d_middle = flat(d_middle_ref)
    d_branch = (d_middle * token_mod(mod_ref, seg_own, 2)).astype(BF16)
    full[:, own_rows(me, length), :] = d_branch.reshape(rows, length, width)
    greet(z_peers(count) + cargo.peers(["core"]))
    line = Line(length, sems)
    line.start_gather(full)
    cargo.begin()
    slot_sums(d_middle * flat(branch_ref), seg_own, d_mod_ref, 2)
    spread = spread_matrix(heads_width)
    line.relay(full)
    cargo.middle()
    load_out.wait()
    line.finish_gather(full)
    d_mixed = dot(flat(full), wo[...], NT).astype(BF16)
    wide[3] = dot(d_mixed, spread).astype(BF16).reshape(wide.shape[1:])

    def one_head(index, carry):
        row = index // heads
        head = lax.rem(index, heads)
        lanes = pl.ds(pl.multiple_of(head * HEAD_LANES, HEAD_LANES), HEAD_LANES)
        grad = wide[3, row, :, lanes]
        probs = probs_ref[index]
        d_probs = dot(grad, v_ref[row, :, lanes], NT)
        d_scores = (
            probs * (d_probs - jnp.sum(d_probs * probs, axis=-1, keepdims=True))
        ).astype(BF16)
        scale = HEAD_WIDTH ** (-0.5)
        wide[0, row, :, lanes] = (dot(d_scores, k_ref[row, :, lanes]) * scale).astype(BF16)
        wide[1, row, :, lanes] = (dot(d_scores, q_ref[row, :, lanes], TN) * scale).astype(BF16)
        wide[2, row, :, lanes] = dot(probs.astype(BF16), grad, TN).astype(BF16)
        return carry

    lax.fori_loop(0, rows * heads, one_head, 0)
    for which in range(3):
        narrow[which] = (
            dot(flat(wide.at[which]), spread, NT).astype(BF16).reshape(narrow.shape[1:])
        )
    load_qkv.wait()

    def partial(which_rows):
        total = 0.0
        for which in range(3):
            total = total + dot(
                narrow[which, :, which_rows, :].reshape(rows * length, heads_width),
                wqkv[pl.ds(which * width, width), :],
                NT,
            )
        return total

    total = line.scatter_sum(partial, buffers)
    d_bo_ref[...] = jnp.sum(flat(full).astype(F32), axis=0, keepdims=True)
    d_bqv_ref[0:1, :] = jnp.sum(flat(narrow.at[0]).astype(F32), axis=0, keepdims=True)
    d_bqv_ref[1:2, :] = jnp.sum(flat(narrow.at[2]).astype(F32), axis=0, keepdims=True)
    wo_whole[...] = dot(flat(full), flat(mixed_ref), TN).astype(BF16)
    wo_sum.begin()
    for which in range(3):
        qkv_whole[which] = dot(flat(full_ref), flat(narrow.at[which]), TN).astype(BF16)
    qkv_sum.begin()
    d_attn_in = line.finish_sum(total, buffers)
    normed, inverse = layer_norm(flat(u_ref).astype(F32))
    d_in = flat(d_middle_ref) + norm_back(
        d_attn_in * (1.0 + token_mod(mod_ref, seg_own, 1)), normed, inverse
    )
    d_in_ref[...] = d_in.reshape(d_in_ref.shape)
    slot_sums(d_attn_in, seg_own, d_mod_ref, 0)
    slot_sums(d_attn_in * normed, seg_own, d_mod_ref, 1)
    wo_sum.end()
    qkv_sum.end()
    cargo.end()


def silu_slope(value):
    gate = 1.0 / (1.0 + jnp.exp(-value))
    return gate * (1.0 + value * (1.0 - gate))


def project_kernel(token_count, *refs, cargo):
    sent_ref, targets_ref, biases_ref, p2_b_ref, p1_any, p2_any, p3_any = refs[:7]
    d_sent_ref, d_p1_ref, d_p2_ref, d_p3_ref, small_ref = refs[7:12]
    p1, p2, p3, tokens, first_pre, first, second_pre, second, d_second, norms = refs[12:22]
    buf_a, buf_b, buf_c, d_first, load_sem, send, recv = refs[22:]
    core, peer = core_bit(), core_peer()
    loads = [
        local(source, place, load_sem.at[i])
        for i, (source, place) in enumerate(((p1_any, p1), (p2_any, p2), (p3_any, p3)))
    ]
    count = tokens.shape[1]
    tokens[core] = flat(sent_ref)
    greet([peer])

    def trade(ref, which):
        return remote(ref.at[core], ref.at[core], send.at[which], recv.at[which], peer)

    def give(buffer, value, which):
        buffer[0] = value.astype(BF16)
        return remote(buffer.at[0], buffer.at[1], send.at[which], recv.at[which], peer)

    def block(ref, side):
        return ref[side]

    copy = trade(tokens, 0)
    target = [
        targets_ref[slot].reshape(2 * count, targets_ref.shape[-1]).astype(F32) for slot in range(2)
    ]
    target_sq = sum(jnp.sum(one * one, axis=1, keepdims=True) for one in target)
    loads[0].wait()
    copy.wait()
    all_tokens = flat(tokens)
    for slot in range(2):
        pre = dot(all_tokens, p1[slot]) + biases_ref[slot, 0, 0:1, :]
        first_pre[slot] = pre
        first[slot] = silu(pre).astype(BF16)
    loads[1].wait()

    def second_term(side):
        rows = pl.ds(pl.multiple_of(side * count, 16), count)
        return dot(first[0, rows, :], p2[0]) + dot(first[1, rows, :], p2[1])

    copy = give(buf_a, second_term(1 - core), 1)
    pre = second_term(core)
    copy.wait()
    pre = pre + buf_a[1].astype(F32) + p2_b_ref[...].astype(F32)
    second_pre[...] = pre
    second[core] = silu(pre).astype(BF16)
    copy = trade(second, 2)
    loads[2].wait()
    copy.wait()
    all_second = flat(second)
    width = target[0].shape[1]
    predicted = [
        dot(all_second, p3[slot]) + biases_ref[slot, 0, 1:2, :width] for slot in range(2)
    ]
    pred_sq = sum(jnp.sum(one * one, axis=1, keepdims=True) for one in predicted)
    cross = sum(
        jnp.sum(one * two, axis=1, keepdims=True) for one, two in zip(predicted, target)
    )
    lanes = lax.broadcasted_iota(jnp.int32, norms.shape[1:], 1)
    norms[core] = jnp.where(lanes == 0, pred_sq, jnp.where(lanes == 1, cross, target_sq))
    copy = trade(norms, 3)
    copy.wait()
    total = norms[0] + norms[1]
    inv_pred = lax.rsqrt(total[:, 0:1] + COSINE_EPS)
    inv_target = lax.rsqrt(total[:, 2:3] + COSINE_EPS)
    cosine = total[:, 1:2] * inv_pred * inv_target
    side = lax.broadcasted_iota(jnp.int32, cosine.shape, 0)
    own = jnp.logical_and(side >= core * count, side < (core + 1) * count)
    loss = jnp.sum(jnp.where(own, cosine, 0.0), axis=0, keepdims=True)
    factor = -0.5 / token_count
    one_scale = factor * inv_pred * inv_target
    two_scale = factor * cosine * inv_pred * inv_pred
    d_pred = [
        (one_scale * two - two_scale * one).astype(BF16) for one, two in zip(predicted, target)
    ]
    small_ref[...] = jnp.zeros_like(small_ref)
    for slot in range(2):
        small_ref[2 * core + slot, 1:2, :width] = jnp.sum(
            d_pred[slot].astype(F32), axis=0, keepdims=True
        )

    def d_second_term(side):
        terms = 0.0
        for slot in range(2):
            mine = jnp.where(
                side == 0, d_pred[slot][:count].astype(F32), d_pred[slot][count:].astype(F32)
            )
            terms = terms + dot(mine.astype(BF16), p3[slot], NT)
        return terms

    copy = give(buf_b, d_second_term(1 - core), 4)
    grad = d_second_term(core)
    for slot in range(2):
        d_p3_ref[slot] = dot(all_second, d_pred[slot], TN).astype(BF16)
    copy.wait()
    grad = ((grad + buf_b[1].astype(F32)) * silu_slope(second_pre[...])).astype(BF16)
    d_second[core] = grad
    copy = trade(d_second, 5)
    d_p2_b = jnp.sum(grad.astype(F32), axis=0, keepdims=True)
    lane = small_ref.shape[2]
    loss_row = jnp.where(lax.broadcasted_iota(jnp.int32, (1, lane), 1) == 0, loss, 0.0)
    for part in range(4):
        for row in range(d_p2_b.shape[1] // lane):
            small_ref[part, 2 + row : 3 + row, :] = d_p2_b[:, row * lane : (row + 1) * lane]
        small_ref[part, 6:7, :] = loss_row
    copy.wait()
    all_d_second = flat(d_second)
    for slot in range(2):
        back = dot(all_d_second, p2[slot], NT) * silu_slope(first_pre[slot])
        d_first[slot] = back.astype(BF16)
        small_ref[2 * core + slot, 0:1, :] = jnp.sum(
            d_first[slot].astype(F32), axis=0, keepdims=True
        )

    def d_sent_term(side):
        rows = pl.ds(pl.multiple_of(side * count, 16), count)
        return dot(d_first[0, rows, :], p1[0], NT) + dot(d_first[1, rows, :], p1[1], NT)

    copy = give(buf_c, d_sent_term(1 - core), 6)
    grad = d_sent_term(core)
    for slot in range(2):
        d_p2_ref[slot] = dot(first[slot], all_d_second, TN).astype(BF16)
        d_p1_ref[slot] = dot(all_tokens, d_first[slot], TN).astype(BF16)
    copy.wait()
    d_sent_ref[...] = (grad + buf_c[1].astype(F32)).reshape(d_sent_ref.shape)


def close_kernel(count, sections, replicas, *refs, cargo):
    grads_ref, mod_refs, small_refs, proj_ref, cond_ref = (
        refs[:2], refs[2:6], refs[6:14], refs[14], refs[15]
    )
    grad_ref, ada_w_ref, ada_b_ref, small_ref, proj_sum_ref = refs[16:21]
    z_src, z_buf, mod_src, mod_buf, small_src, small_buf, cond_buf = refs[21:28]
    place_src, place_buf, proj_got, proj_src, proj_buf = refs[28:33]
    sems = refs[33:35]
    section, tensor, replica = (lax.axis_index(name) for name in ("section", "tensor", "dp"))
    send, recv = sems
    others = [
        {"section": lax.rem(section + a, sections), "dp": lax.rem(replica + b, replicas)}
        for a in range(sections)
        for b in range(replicas)
        if a or b
    ]
    greet(z_peers(count) + others + cross_peers())
    for one in cargo.cargos:
        if isinstance(one, YSum):
            one.begin()
    piece = z_src.shape[-1]
    for block in range(sections):
        attend_mod, mlp_mod = mod_refs[2 * block : 2 * block + 2]
        width = attend_mod.shape[-1]
        for part in range(count):
            at, end, cuts = part * piece, (part + 1) * piece, []
            while at < end:
                which = at // width
                stop = min((which + 1) * width, end)
                ref = attend_mod if which < 3 else mlp_mod
                cuts.append(ref[which % 3][:, at - which * width : stop - which * width])
                at = stop
            z_src[part, block] = jnp.concatenate(cuts, axis=1) if len(cuts) > 1 else cuts[0]
    z_copies = [
        remote(z_src.at[peer["tensor"]], z_buf.at[i], send.at[i], recv.at[i], peer)
        for i, peer in enumerate(z_peers(count))
    ]
    at = count - 1
    z_copies += [
        remote(proj_ref.at[peer["tensor"]], proj_got.at[i], send.at[at + i], recv.at[at + i], peer)
        for i, peer in enumerate(z_peers(count))
    ]
    at = at + count - 1

    @pl.when(section == 0)
    def first_place():
        place_src[...] = grads_ref[1][...].astype(BF16)

    @pl.when(section != 0)
    def second_place():
        place_src[...] = grads_ref[0][...].astype(BF16)

    place_copy = remote(place_src, place_buf, send.at[at], recv.at[at], x_peer())
    at = at + 1
    heads_width = small_refs[0].shape[-1]
    small_src[...] = jnp.zeros_like(small_src)
    for block in range(sections):
        d_bqv, d_bo, d_b1, d_b2 = small_refs[4 * block : 4 * block + 4]
        small_src[block, 0:2, :heads_width] = d_bqv[...]
        small_src[block, 2:3, :] = d_bo[...]
        small_src[block, 3:4, : d_b1.shape[1]] = d_b1[...]
        small_src[block, 4:5, :] = d_b2[...]
    small_buf[section, replica] = small_src[section]
    cond_buf[section, replica] = cond_ref[replica]
    copies = []
    for peer in others:
        copies.append(
            remote(
                small_src.at[peer["section"]], small_buf.at[section, replica],
                send.at[at], recv.at[at], peer,
            )
        )
        copies.append(
            remote(
                cond_ref.at[peer["dp"]], cond_buf.at[section, replica],
                send.at[at + 1], recv.at[at + 1], peer,
            )
        )
        at = at + 2
    for one in cargo.cargos:
        if not isinstance(one, YSum):
            one.begin()
    wait_all(z_copies)
    mine, mine_proj = z_src[tensor], proj_ref[tensor]
    for step in range(count - 1):
        mine = mine + z_buf[step]
        mine_proj = mine_proj + proj_got[step]
    mod_src[...] = mine
    mod_buf[section, replica] = mod_src[section]
    proj_src[...] = mine_proj
    proj_buf[section, replica] = mine_proj
    for peer in others:
        copies.append(
            remote(
                mod_src.at[peer["section"]], mod_buf.at[section, replica],
                send.at[at], recv.at[at], peer,
            )
        )
        copies.append(
            remote(
                proj_src, proj_buf.at[section, replica], send.at[at + 1], recv.at[at + 1], peer
            )
        )
        at = at + 2
    for one in cargo.cargos:
        if isinstance(one, LastSum):
            one.to_x()
    place_copy.wait()
    rows = place_buf.shape[0]

    @pl.when(section == 0)
    def first_out():
        grad_ref[:rows] = grads_ref[0][...]
        grad_ref[rows:] = place_buf[...].astype(F32)

    @pl.when(section != 0)
    def second_out():
        grad_ref[rows:] = grads_ref[1][...]
        grad_ref[:rows] = place_buf[...].astype(F32)

    wait_all(copies)
    small, proj_sum = small_buf[0, 0], proj_buf[0, 0]
    for a in range(sections):
        for b in range(replicas):
            if a or b:
                small = small + small_buf[a, b]
                proj_sum = proj_sum + proj_buf[a, b]
    small_ref[...] = small
    proj_sum_ref[...] = proj_sum
    mod_all = flat(mod_buf)
    ada_b_ref[...] = jnp.sum(mod_all, axis=0, keepdims=True)
    ada_w_ref[...] = lax.dot_general(
        flat(cond_buf), mod_all, TN, precision=HIGHEST, preferred_element_type=F32
    )
    cargo.end()


VMEM = pl.BlockSpec(memory_space=pltpu.VMEM)
ANY = pl.BlockSpec(memory_space=pl.ANY)
MOD_ROWS = 8


def call(kernel, number, inputs, in_any, outs, out_any, scratch, flops, cargos=()):
    own_in, own_out, own_scratch = len(inputs), len(outs), len(scratch)
    specs = [VMEM] * (own_in - in_any) + [ANY] * in_any
    out_specs = [ANY if i in out_any else VMEM for i in range(own_out)]
    inputs, outs, scratch, aliases = list(inputs), list(outs), list(scratch), {}
    for cargo in cargos:
        for source, target in cargo.aliases.items():
            aliases[len(inputs) + source] = len(outs) + target
        inputs += cargo.inputs
        outs += cargo.outs
        scratch += cargo.scratch
        specs += [ANY] * len(cargo.inputs)
        out_specs += [ANY if cargo.any_outs else VMEM] * len(cargo.outs)

    def body(*refs):
        parts = [list(refs[: len(inputs)])]
        parts.append(list(refs[len(inputs) : len(inputs) + len(outs)]))
        parts.append(list(refs[len(inputs) + len(outs) :]))
        base = parts[0][:own_in] + parts[1][:own_out] + parts[2][:own_scratch]
        at = [own_in, own_out, own_scratch]
        for cargo in cargos:
            held = []
            for i, items in enumerate((cargo.inputs, cargo.outs, cargo.scratch)):
                held.append(parts[i][at[i] : at[i] + len(items)])
                at[i] += len(items)
            cargo.bind(*held)
        kernel(*base, cargo=Bundle(cargos))

    moved = sum(math.prod(one.shape) * one.dtype.itemsize for one in inputs)
    results = pl.pallas_call(
        body,
        out_shape=[jax.ShapeDtypeStruct(shape, dtype) for shape, dtype in outs],
        in_specs=specs,
        out_specs=out_specs,
        scratch_shapes=scratch,
        input_output_aliases=aliases,
        compiler_params=pltpu.CompilerParams(
            collective_id=number, has_side_effects=True, vmem_limit_bytes=56 * 2**20
        ),
        cost_estimate=pl.CostEstimate(flops=flops, bytes_accessed=moved, transcendentals=0),
    )(*inputs)
    at, carried = own_out, []
    for cargo in cargos:
        carried.append(results[at : at + len(cargo.outs)])
        at += len(cargo.outs)
    return results[:own_out], carried


def exchange_scratch(count, rows, length, width):
    return [
        pltpu.VMEM((count - 1, rows, length, width), BF16),
        pltpu.VMEM((count, rows, length, width), BF16),
        pltpu.VMEM((rows, length, width), BF16),
    ]


def semaphores(count):
    return [pltpu.SemaphoreType.DMA((2,))] + [
        pltpu.SemaphoreType.DMA((size,)) for size in (count, count, count - 1, count + 1)
    ]


class Shapes:
    def __init__(self, u, own, count):
        self.rows, self.length, self.width = u.shape
        self.count = count
        self.positions = self.length * count
        self.tokens = self.rows * self.positions
        self.heads_width = own["out"].shape[0]
        self.hidden = own["one"].shape[1]
        self.heads = self.heads_width // HEAD_WIDTH
        self.local = (self.rows, self.length, self.width)
        self.full = (self.rows, self.positions, self.width)
        self.wide = (self.rows, self.positions, self.heads * HEAD_LANES)
        self.own = own
        self.attend_outs = [
            (self.local, F32), (self.local, F32), (self.full, BF16),
            (self.wide, BF16), (self.wide, BF16), (self.wide, BF16),
            ((self.rows * self.heads, self.positions, self.positions), F32),
            ((self.rows, self.positions, self.heads_width), BF16),
        ]
        self.attend_scratch = [
            pltpu.VMEM(self.full, BF16),
            pltpu.VMEM(own["qkv"].shape, BF16),
            pltpu.VMEM(own["out"].shape, BF16),
            pltpu.VMEM(self.wide, BF16),
        ] + exchange_scratch(count, *self.local)
        self.mods = (3, MOD_ROWS, self.width)


def pairs(own, other, names):
    out = []
    for name in names:
        out += [own[name], other[name]]
    return out


def open_forward(sizes, u, cond, ada_w, ada_b, biases, segs, own, sections, cargos):
    count, width = sizes.count, sizes.width
    piece = ada_w.shape[1]
    inputs = [u, cond, ada_b, biases, *segs, ada_w] + [own[n] for n in ("qkv", "out", "one", "two")]
    plane = sections * count - 1
    results, carried = call(
        functools.partial(open_kernel, count, sections),
        0,
        inputs,
        5,
        [((sections, 6, MOD_ROWS, width), F32), ((sections,) + biases.shape, F32)]
        + [(own[n].shape, BF16) for n in ("qkv", "out", "one", "two")]
        + sizes.attend_outs,
        (2, 3, 4, 5),
        sizes.attend_scratch
        + [
            pltpu.VMEM(ada_w.shape, BF16),
            pltpu.VMEM((sections, MOD_ROWS, piece), F32),
            pltpu.VMEM((sections, count, MOD_ROWS, piece), F32),
            pltpu.VMEM((sections,) + biases.shape, F32),
        ]
        + semaphores(count)
        + [
            pltpu.SemaphoreType.DMA((plane + 1,)),
            pltpu.SemaphoreType.DMA((plane + 1,)),
            pltpu.SemaphoreType.DMA((4, 4)),
            pltpu.SemaphoreType.DMA((4, 4)),
            pltpu.SemaphoreType.DMA,
        ],
        2 * sizes.tokens * width * sizes.heads_width * 4,
        cargos,
    )
    other = dict(zip(("qkv", "out", "one", "two"), results[2:6]))
    return results[0], results[1], other, results[6:], carried


def attend_forward(sizes, block, u, mods, biases, segs, own, other, cargos):
    inputs = [u, mods, biases, *segs] + pairs(own, other, ("qkv", "out"))
    return call(
        functools.partial(attend_kernel, sizes.count, block),
        1,
        inputs,
        4,
        sizes.attend_outs,
        (),
        sizes.attend_scratch + semaphores(sizes.count),
        2 * sizes.tokens * sizes.width * sizes.heads_width * 4,
        cargos,
    )


def mlp_forward(sizes, block, middle, mods, biases, segs, own, other, cargos):
    inputs = [middle, mods, biases, segs[0]] + pairs(own, other, ("one", "two"))
    hidden = (sizes.rows, sizes.positions, sizes.hidden)
    return call(
        functools.partial(mlp_kernel, sizes.count, block),
        2 + block,
        inputs,
        4,
        [
            (sizes.local, BF16), (sizes.local, F32), (sizes.full, BF16),
            (hidden, F32), (hidden, BF16),
        ],
        (),
        [
            pltpu.VMEM(sizes.full, BF16),
            pltpu.VMEM(own["one"].shape, BF16),
            pltpu.VMEM(own["two"].shape, BF16),
        ]
        + exchange_scratch(sizes.count, *sizes.local)
        + semaphores(sizes.count),
        2 * sizes.tokens * sizes.width * sizes.hidden * 2,
        cargos,
    )


def mlp_backward(sizes, block, g, attend, mlp, mods, segs, own, other, cargos):
    out, branch, full, pre, act = mlp
    inputs = [g, attend[0], branch, mods, segs[0], full, pre, act]
    inputs += pairs(own, other, ("one", "two"))
    return call(
        functools.partial(mlp_back_kernel, sizes.count, block),
        4 + block,
        inputs,
        4,
        [
            (sizes.local, F32), (sizes.mods, F32),
            ((2,) + quarter((sizes.width, sizes.hidden)), BF16),
            ((2,) + quarter((sizes.width, sizes.hidden)), BF16),
            ((1, sizes.hidden), F32), ((1, sizes.width), F32),
        ],
        (),
        [
            pltpu.VMEM(sizes.full, BF16),
            pltpu.VMEM((sizes.rows, sizes.positions, sizes.hidden), BF16),
            pltpu.VMEM(own["one"].shape, BF16),
            pltpu.VMEM(own["two"].shape, BF16),
        ]
        + exchange_scratch(sizes.count, *sizes.local)
        + semaphores(sizes.count)
        + core_sum_scratch((sizes.width, sizes.hidden)) * 2,
        2 * sizes.tokens * sizes.width * sizes.hidden * 4,
        cargos,
    )


def attend_backward(sizes, block, d_middle, u, attend, mods, segs, own, other, cargos):
    middle, branch, full, q, k, v, probs, mixed = attend
    inputs = [d_middle, u, branch, mods, segs[0], full, q, k, v, probs, mixed]
    inputs += pairs(own, other, ("qkv", "out"))
    return call(
        functools.partial(attend_back_kernel, sizes.count, block),
        6 + block,
        inputs,
        4,
        [
            (sizes.local, F32), (sizes.mods, F32),
            ((2,) + quarter((3, sizes.width, sizes.heads_width)), BF16),
            ((2,) + quarter((sizes.width, sizes.heads_width)), BF16),
            ((2, sizes.heads_width), F32), ((1, sizes.width), F32),
        ],
        (),
        [
            pltpu.VMEM(sizes.full, BF16),
            pltpu.VMEM((4,) + sizes.wide, BF16),
            pltpu.VMEM((3, sizes.rows, sizes.positions, sizes.heads_width), BF16),
            pltpu.VMEM(own["qkv"].shape, BF16),
            pltpu.VMEM(own["out"].shape, BF16),
        ]
        + exchange_scratch(sizes.count, *sizes.local)
        + semaphores(sizes.count)
        + core_sum_scratch((3, sizes.width, sizes.heads_width))
        + core_sum_scratch((sizes.width, sizes.heads_width)),
        2 * sizes.tokens * sizes.width * sizes.heads_width * 8,
        cargos,
    )


def project(sizes, sent, weights, targets, biases, p2_b, token_count):
    tokens = sizes.rows * sizes.length
    p1, p2, p3 = weights
    lane, hidden = p1.shape[2], p2.shape[2]
    inputs = [sent, targets, biases, p2_b, p1, p2, p3]
    results, unused = call(
        functools.partial(project_kernel, token_count),
        9,
        inputs,
        3,
        [
            (sizes.local, F32), (p1.shape, BF16), (p2.shape, BF16), (p3.shape, BF16),
            ((sizes.count, MOD_ROWS, lane), F32),
        ],
        (),
        [
            pltpu.VMEM(p1.shape, BF16),
            pltpu.VMEM(p2.shape, BF16),
            pltpu.VMEM(p3.shape, BF16),
            pltpu.VMEM((2, tokens, sizes.width), BF16),
            pltpu.VMEM((2, 2 * tokens, lane), F32),
            pltpu.VMEM((2, 2 * tokens, lane), BF16),
            pltpu.VMEM((tokens, hidden), F32),
            pltpu.VMEM((2, tokens, hidden), BF16),
            pltpu.VMEM((2, tokens, hidden), BF16),
            pltpu.VMEM((2, 2 * tokens, HEAD_LANES), F32),
            pltpu.VMEM((2, tokens, hidden), BF16),
            pltpu.VMEM((2, tokens, hidden), BF16),
            pltpu.VMEM((2, tokens, sizes.width), BF16),
            pltpu.VMEM((2, 2 * tokens, lane), BF16),
            pltpu.SemaphoreType.DMA((3,)),
            pltpu.SemaphoreType.DMA((7,)),
            pltpu.SemaphoreType.DMA((7,)),
        ],
        12 * tokens * sum(math.prod(one.shape) for one in weights),
    )
    return results


def close_backward(sizes, grads, mod_grads, small, proj_small, cond, sections, replicas, cargos):
    count, width = sizes.count, sizes.width
    piece = 6 * width // count
    share = width // replicas
    inputs = [*grads, *mod_grads, *small, proj_small, cond]
    copies = 2 * count + 4 * (sections * replicas - 1)
    both = (sections * sizes.rows,) + sizes.local[1:]
    return call(
        functools.partial(close_kernel, count, sections, replicas),
        8,
        inputs,
        0,
        [
            (both, F32), ((share, piece), F32), ((1, piece), F32),
            ((MOD_ROWS, width), F32), (proj_small.shape[1:], F32),
        ],
        (),
        [
            pltpu.VMEM((count, sections, MOD_ROWS, piece), F32),
            pltpu.VMEM((count - 1, sections, MOD_ROWS, piece), F32),
            pltpu.VMEM((sections, MOD_ROWS, piece), F32),
            pltpu.VMEM((sections, replicas, MOD_ROWS, piece), F32),
            pltpu.VMEM((sections, MOD_ROWS, width), F32),
            pltpu.VMEM((sections, replicas, MOD_ROWS, width), F32),
            pltpu.VMEM((sections, replicas, MOD_ROWS, share), F32),
            pltpu.VMEM(sizes.local, BF16),
            pltpu.VMEM(sizes.local, BF16),
            pltpu.VMEM((count - 1,) + proj_small.shape[1:], F32),
            pltpu.VMEM(proj_small.shape[1:], F32),
            pltpu.VMEM((sections, replicas) + proj_small.shape[1:], F32),
            pltpu.SemaphoreType.DMA((copies,)),
            pltpu.SemaphoreType.DMA((copies,)),
        ],
        2 * sections * replicas * MOD_ROWS * share * piece,
        cargos,
    )


def halve(value, axis, bit, position):
    size = lax.axis_size(axis)
    mine = (lax.axis_index(axis) & bit) // bit
    keep = lax.dynamic_index_in_dim(value, mine, position, keepdims=False)
    give = lax.dynamic_index_in_dim(value, 1 - mine, position, keepdims=False)
    return keep + lax.ppermute(give, axis, [(i, i ^ bit) for i in range(size)])


def sum_beyond_quads(value):
    size = lax.axis_size("dp")
    if size == 4:
        return value
    quads = size // 4
    bits = quads.bit_length() - 1
    lead = value.ndim - 2
    shape = value.shape
    value = value.reshape(shape[:lead] + (2,) * bits + (shape[-2] // quads, shape[-1]))
    for bit in range(bits):
        value = halve(value, "dp", 4 << bit, lead + bits - 1 - bit)
    route = [(high * 4 + low, low * quads + high) for high in range(quads) for low in range(4)]
    return lax.ppermute(value, "dp", route)


def per_device(
    block_eight_input,
    cond,
    image_slot_index,
    targets,
    cot,
    ada_w,
    ada_b,
    query_key_value_weight,
    query_value_bias,
    attention_output_weight,
    attention_output_bias,
    hidden_weight,
    hidden_bias,
    output_weight_mlp,
    output_bias_mlp,
    p1_w,
    p1_b,
    p2_w,
    p2_b,
    p3_w,
    p3_b,
):
    section = lax.axis_index("section")
    tensor = lax.axis_index("tensor")
    is_first = section == 0
    count = lax.axis_size("tensor")
    sections = lax.axis_size("section")
    replicas = lax.axis_size("dp")
    length, replica_rows, width = block_eight_input.shape
    positions = length * count
    rows = replica_rows // sections
    total_token_count = positions * replica_rows * replicas
    heads_width = attention_output_weight.shape[1]
    hidden = hidden_weight.shape[2]

    def my_rows(value, axis):
        return lax.dynamic_slice_in_dim(value, section * rows, rows, axis)

    def to_rows(value):
        return jnp.transpose(my_rows(value, 1), (1, 0, 2))

    own = {
        "qkv": jnp.transpose(query_key_value_weight[0], (1, 0, 2)).reshape(3 * width, heads_width),
        "out": attention_output_weight[0],
        "one": hidden_weight[0],
        "two": output_weight_mlp[0],
    }

    def padded(value):
        return jnp.pad(value.astype(F32), ((0, 0), (0, width - value.shape[-1])))

    biases = jnp.concatenate(
        [
            padded(query_value_bias[0]), padded(attention_output_bias), padded(hidden_bias),
            padded(output_bias_mlp), jnp.zeros((MOD_ROWS - 5, width), F32),
        ],
        axis=0,
    )
    used = rows * IMAGES_PER_ROW
    cond_pad = jnp.pad(
        cond.reshape(sections, used, width), ((0, 0), (0, MOD_ROWS - used), (0, 0))
    )
    segs_full = my_rows(image_slot_index, 0)
    seg_own = lax.dynamic_slice_in_dim(segs_full, tensor * length, length, 1)
    segs = (seg_own[:, :, None], segs_full[:, :, None], segs_full[:, None, :])

    target_parts = my_rows(targets, 1).reshape(count, length, rows, targets.shape[2])
    target_parts = jnp.transpose(target_parts, (0, 2, 1, 3))
    lane = p1_b.shape[0]
    proj_biases = jnp.concatenate(
        [
            p1_b.astype(F32)[None],
            jnp.pad(p3_b.astype(F32), (0, lane - p3_b.shape[0]))[None],
            jnp.zeros((MOD_ROWS - 2, lane), F32),
        ],
        axis=0,
    )
    gather = ColumnGather((p1_w, p2_w, p3_w), target_parts, proj_biases, sections)

    u = to_rows(block_eight_input)
    sizes = Shapes(u, own, count)
    mods, bias_all, other, attend_one, carried = open_forward(
        sizes, u, cond_pad.reshape(-1, width), ada_w[0], ada_b, biases, segs, own, sections,
        (gather,),
    )
    *proj_weights, target_all, proj_bias_all = carried[0]
    mlp_one, carried = mlp_forward(
        sizes, 0, attend_one[0], mods, bias_all, segs, own, other,
        (LateShare(other["two"]), ShareAlong(proj_weights, 0)),
    )
    (other["two"],), proj_weights = carried
    first_out = mlp_one[0]
    attend_two, carried = attend_forward(
        sizes, 1, first_out, mods, bias_all, segs, own, other, (ShareAlong(proj_weights, 1),)
    )
    proj_weights = carried[0]
    mlp_two, carried = mlp_forward(
        sizes, 1, attend_two[0], mods, bias_all, segs, own, other, (ShareAlong(proj_weights, 2),)
    )
    proj_weights = carried[0]
    second_out = mlp_two[0]

    grad_sent, grad_p1, grad_p2, grad_p3, proj_small = project(
        sizes, first_out, proj_weights, target_all, proj_bias_all, p2_b[None], total_token_count
    )

    back = (mods, segs, own, other)
    (d_middle_two, mod_mlp_two, *mlp_grads_two), carried = mlp_backward(
        sizes, 1, to_rows(cot), attend_two, mlp_two, *back,
        [Swap(first_out, second_out), HalfSum(grad_p1, 0, "x")],
    )
    (other_out,), (grad_p1,) = carried
    (second_grad, mod_attend_two, *attend_grads_two), carried = attend_backward(
        sizes, 1, d_middle_two, first_out, attend_two, *back,
        [YSum(grad, BF16) for grad in mlp_grads_two[:2]]
        + [HalfSum(grad_p2, 1, "x", (0, 1)), HalfSum(grad_p3, 0, "x"), HalfSum(grad_p1, 0, "y")],
    )
    ((mlp_part_a,), (mlp_part_b,)), ((grad_p2_a,), (grad_p3,), (grad_p1,)) = (
        carried[:2], carried[2:]
    )
    (d_middle_one, mod_mlp_one, *mlp_grads_one), carried = mlp_backward(
        sizes, 0, second_grad + grad_sent, attend_one, mlp_one, *back,
        [YSum(grad, BF16) for grad in attend_grads_two[:2]]
        + [SectionSum(mlp_part_a, 1), HalfSum(grad_p2, 1, "x", (1, 1))]
        + [HalfSum(grad_p3, 0, "y"), HalfSum(grad_p2_a, 1, "y"), ColumnSum((grad_p1,), 0)],
    )
    attend_parts_two, sum_mlp_a = carried[:2], carried[2]
    (grad_p2_b,), (grad_p3,), (grad_p2_a,), (red_p1_w,) = carried[3:]
    (first_grad, mod_attend_one, *attend_grads_one), carried = attend_backward(
        sizes, 0, d_middle_one, u, attend_one, *back,
        [YSum(mlp_grads_one[0], BF16), SectionSum(mlp_grads_one[1], 0, BF16)]
        + [SectionSum(part, 1) for part, in attend_parts_two]
        + [SectionSum(mlp_part_b, 1), HalfSum(grad_p2_b, 1, "y"), ColumnSum((grad_p3,), 0)],
    )
    ((mlp_part_one,), (mlp_part_two,)), sums_attend_two = carried[:2], carried[2:4]
    sums_mlp_two, ((grad_p2_b,), (red_p3_w,)) = (sum_mlp_a, carried[4]), carried[5:]

    cond_act = silu(my_rows(cond, 0).astype(F32)).astype(BF16).astype(F32)
    share = width // replicas
    cond_cols = jnp.pad(cond_act.reshape(used, width), ((0, MOD_ROWS - used), (0, 0)))
    cond_cols = jnp.transpose(cond_cols.reshape(MOD_ROWS, replicas, share), (1, 0, 2))
    small = [
        attend_grads_one[2], attend_grads_one[3], mlp_grads_one[2], mlp_grads_one[3],
        attend_grads_two[2], attend_grads_two[3], mlp_grads_two[2], mlp_grads_two[3],
    ]
    (section_grad, grad_ada_w, grad_ada_b, small, proj_small), carried = close_backward(
        sizes, (first_grad, second_grad),
        (mod_attend_one, mod_mlp_one, mod_attend_two, mod_mlp_two),
        small, proj_small, cond_cols, sections, replicas,
        [LastSum(grad, 0) for grad in attend_grads_one[:2]]
        + [YSum(mlp_part_two, F32), SectionSum(mlp_part_one, 0)]
        + [ColumnSum((grad_p2_a, grad_p2_b), 1)],
    )
    sums_attend_one, sums_mlp_one = carried[:2], (carried[3], carried[2])
    (red_p2_w,) = carried[4]

    red_fc1, red_fc2, red_qkv, red_out = [
        sum_beyond_quads(jnp.where(is_first, one[0], two[0]))
        for one, two in zip(
            list(sums_mlp_one) + list(sums_attend_one), list(sums_mlp_two) + list(sums_attend_two)
        )
    ]
    red_p1_w, red_p3_w = sum_beyond_quads(red_p1_w), sum_beyond_quads(red_p3_w)
    if replicas > 4:
        red_p2_w = sum_beyond_quads(red_p2_w.T).T
    align_loss = -0.5 * proj_small[6, 0] / total_token_count
    own_out = jnp.where(is_first, first_out, second_out)
    section_out = jnp.where(
        is_first,
        jnp.concatenate([own_out, other_out], axis=0),
        jnp.concatenate([other_out, own_out], axis=0),
    )
    return (
        jnp.transpose(section_out, (1, 0, 2))[None],
        jnp.transpose(section_grad, (1, 0, 2))[None],
        align_loss,
        grad_ada_w[None],
        grad_ada_b,
        jnp.transpose(red_qkv, (1, 0, 2))[None],
        small[0:2, :heads_width][None],
        red_out.T[None],
        small[2:3],
        red_fc1[None],
        small[3:4, :hidden],
        red_fc2.T[None],
        small[4:5],
        red_p1_w,
        proj_small[0],
        red_p2_w,
        proj_small[2:6].reshape(-1)[: p2_b.shape[0]],
        red_p3_w,
        proj_small[1, : p3_b.shape[0]],
    )


def solution(mesh):
    in_specs = (
        P("tensor", "dp", None),
        P("dp", None, None),
        P("dp", None),
        P(None, "dp", "tensor"),
        P("tensor", "dp", None),
        P("section", None, "tensor"),
        P("section", "tensor"),
        P("section", None, None, "tensor"),
        P("section", None, "tensor"),
        P("section", "tensor", None),
        P("section", None),
        P("section", None, "tensor"),
        P("section", "tensor"),
        P("section", "tensor", None),
        P("section", None),
        P(None, "tensor"),
        P("tensor"),
        P("tensor", None),
        P(),
        P(None, "tensor"),
        P("tensor"),
    )
    out_specs = (
        P("section", "tensor", "dp", None),
        P("section", "tensor", "dp", None),
        P(),
        P("section", "dp", "tensor"),
        P("section", "tensor"),
        P("section", "dp", None, "tensor"),
        P("section", None, "tensor"),
        P("section", "tensor", "dp"),
        P("section", None),
        P("section", "dp", "tensor"),
        P("section", "tensor"),
        P("section", "tensor", "dp"),
        P("section", None),
        P(("section", "dp"), "tensor"),
        P("tensor"),
        P("tensor", ("section", "dp")),
        P(),
        P(("section", "dp"), "tensor"),
        P("tensor"),
    )
    return jax.shard_map(
        per_device, mesh=mesh, in_specs=in_specs, out_specs=out_specs, check_vma=False
    )
```

```python
import functools
import math

import jax
import jax.numpy as jnp
from jax import lax
from jax.experimental import pallas as pl
from jax.experimental.pallas import tpu as pltpu
from jax.sharding import PartitionSpec as P

HEAD_WIDTH = 72
HEAD_LANES = 128
IMAGES_PER_ROW = 3
NORM_EPS = 1e-06
COSINE_EPS = 1e-06
MASKED_SCORE = -1e30
HIGHEST = lax.Precision.HIGHEST
MESH = pl.DeviceIdType.MESH
F32 = jnp.float32
BF16 = jnp.bfloat16
NN = (((1,), (0,)), ((), ()))
NT = (((1,), (1,)), ((), ()))
TN = (((0,), (0,)), ((), ()))


def dot(left, right, form=NN):
    return lax.dot_general(left, right, form, preferred_element_type=F32)


def z_peers(count):
    me = lax.axis_index("tensor")
    return [{"tensor": lax.rem(me + step, count)} for step in range(1, count)]


def x_peer():
    return {"section": 1 - lax.axis_index("section")}


def core_bit():
    return lax.rem(lax.axis_index("dp"), 2)


def y_bit():
    return lax.rem(lax.axis_index("dp") // 2, 2)


def core_peer():
    return {"dp": lax.axis_index("dp") + 1 - 2 * core_bit()}


def y_peer():
    return {"dp": lax.axis_index("dp") + 2 - 4 * y_bit()}


def greet(peers):
    barrier = pltpu.get_barrier_semaphore()
    for peer in peers:
        pl.semaphore_signal(barrier, inc=1, device_id=peer, device_id_type=MESH)
    pl.semaphore_wait(barrier, len(peers))


def remote(source, target, send_sem, recv_sem, peer):
    copy = describe(source, target, send_sem, recv_sem, peer)
    copy.start()
    return copy


def local(source, target, sem):
    copy = pltpu.make_async_copy(source, target, sem)
    copy.start()
    return copy


def own_rows(me, length):
    return pl.ds(pl.multiple_of(me * length, 16), length)


def describe(source, target, send_sem, recv_sem, peer):
    return pltpu.make_async_remote_copy(
        src_ref=source,
        dst_ref=target,
        send_sem=send_sem,
        recv_sem=recv_sem,
        device_id=peer,
        device_id_type=MESH,
    )


def wait_all(copies):
    for copy in copies:
        copy.wait()


class Line:
    def __init__(self, length, sems):
        self.length, (self.ag_send, self.ag_recv, self.rs_send, self.rs_recv) = length, sems
        self.me = lax.axis_index("tensor")
        self.mirror = 3 - self.me
        self.near = self.me + 1 - 2 * lax.rem(self.me, 2)
        self.opposite = lax.rem(self.me + 2, 4)
        self.is_end = jnp.logical_or(self.me == 0, self.me == 3)
        self.is_middle = jnp.logical_not(self.is_end)

    def block(self, full, place, which, peer):
        part = full.at[:, own_rows(place, self.length)]
        return describe(
            part, part, self.ag_send.at[which], self.ag_recv.at[place], {"tensor": peer}
        )

    def start_gather(self, full):
        self.block(full, self.me, 0, self.opposite).start()
        self.block(full, self.me, 1, self.near).start()

        @pl.when(self.is_middle)
        def to_mirror():
            self.block(full, self.me, 2, self.mirror).start()

    def relay(self, full):
        self.block(full, self.opposite, 2, self.mirror).wait_recv()

        @pl.when(self.is_middle)
        def pass_on():
            self.block(full, self.opposite, 3, 3 - self.opposite).start()

    def finish_gather(self, full):
        self.block(full, self.near, 1, self.near).wait_recv()
        self.block(full, self.mirror, 1, self.near).wait_recv()
        self.block(full, self.me, 0, self.opposite).wait_send()
        self.block(full, self.me, 1, self.near).wait_send()

        @pl.when(self.is_middle)
        def sent():
            self.block(full, self.me, 2, self.mirror).wait_send()
            self.block(full, self.opposite, 3, 3 - self.opposite).wait_send()

    def scatter_sum(self, partial, buffers):
        send_buf, recv_buf, relay_buf = buffers
        me, relay_sem = self.me, 4

        def term(peer):
            return partial(own_rows(peer, self.length))

        def keep(which, value):
            send_buf[which] = value.astype(BF16).reshape(send_buf.shape[1:])

        self.to_mirror = describe(
            send_buf.at[0], recv_buf.at[me], self.rs_send.at[0], self.rs_recv.at[me],
            {"tensor": self.mirror},
        )
        self.to_relay = describe(
            send_buf.at[0], relay_buf, self.rs_send.at[0], self.rs_recv.at[relay_sem],
            {"tensor": self.near},
        )
        self.to_near = describe(
            send_buf.at[1], recv_buf.at[me], self.rs_send.at[1], self.rs_recv.at[me],
            {"tensor": self.near},
        )
        self.to_opposite = describe(
            send_buf.at[2], recv_buf.at[me], self.rs_send.at[2], self.rs_recv.at[me],
            {"tensor": self.opposite},
        )
        keep(0, term(self.mirror))

        @pl.when(self.is_end)
        def first_end():
            self.to_relay.start()
            relay_buf[...] = jnp.zeros_like(relay_buf)
            recv_buf[self.mirror] = jnp.zeros(recv_buf.shape[1:], BF16)

        @pl.when(self.is_middle)
        def first_middle():
            self.to_mirror.start()

        keep(1, term(self.near))
        self.to_near.start()
        last = term(self.opposite)

        @pl.when(self.is_middle)
        def relayed():
            self.to_relay.wait_recv()

        keep(2, last + relay_buf[...].reshape(last.shape).astype(F32))
        self.to_opposite.start()
        return term(me)

    def finish_sum(self, total, buffers):
        send_buf, recv_buf, relay_buf = buffers

        def got(source):
            describe(
                send_buf.at[1], recv_buf.at[source], self.rs_send.at[1], self.rs_recv.at[source],
                {"tensor": self.near},
            ).wait_recv()

        got(self.near)
        got(self.opposite)

        @pl.when(self.is_middle)
        def third():
            got(self.mirror)

        self.to_near.wait_send()
        self.to_opposite.wait_send()
        self.to_mirror.wait_send()
        for source in (self.near, self.opposite, self.mirror):
            total = total + recv_buf[source].reshape(total.shape).astype(F32)
        return total


def fetch(block, own_ref, other_ref, target, sem):
    mine = lax.axis_index("section") == block

    @pl.when(mine)
    def own_start():
        pltpu.make_async_copy(own_ref, target, sem).start()

    @pl.when(jnp.logical_not(mine))
    def other_start():
        pltpu.make_async_copy(other_ref, target, sem).start()

    return pltpu.make_async_copy(own_ref, target, sem)


def layer_norm(rows):
    centred = rows - jnp.mean(rows, axis=-1, keepdims=True)
    inverse = lax.rsqrt(jnp.mean(centred * centred, axis=-1, keepdims=True) + NORM_EPS)
    return centred * inverse, inverse


def norm_back(grad, normed, inverse):
    mean_grad = jnp.mean(grad, axis=-1, keepdims=True)
    mean_cross = jnp.mean(grad * normed, axis=-1, keepdims=True)
    return inverse * (grad - mean_grad - normed * mean_cross)


def token_mod(mod_ref, seg_ref, which):
    parts = []
    for row in range(seg_ref.shape[0]):
        seg = seg_ref[row]
        line = [
            mod_ref[which, pl.ds(row * IMAGES_PER_ROW + slot, 1), :]
            for slot in range(IMAGES_PER_ROW)
        ]
        value = line[-1]
        for slot in range(IMAGES_PER_ROW - 2, -1, -1):
            value = jnp.where(seg == slot, line[slot], value)
        parts.append(value)
    return jnp.concatenate(parts, axis=0)


def slot_sums(value, seg_ref, out_ref, which):
    length = seg_ref.shape[1]
    lines = []
    for row in range(seg_ref.shape[0]):
        seg = seg_ref[row]
        piece = value[row * length : (row + 1) * length]
        for slot in range(IMAGES_PER_ROW):
            lines.append(jnp.sum(jnp.where(seg == slot, piece, 0.0), axis=0, keepdims=True))
    spare = out_ref.shape[1] - len(lines)
    lines.append(jnp.zeros((spare, value.shape[1]), F32))
    out_ref[which] = jnp.concatenate(lines, axis=0)


def flat(ref):
    return ref[...].reshape(-1, ref.shape[-1])


def spread_matrix(width, which=0, total=None):
    lanes = width // HEAD_WIDTH * HEAD_LANES
    shape = (total or width, lanes)
    source = lax.broadcasted_iota(jnp.int32, shape, 0)
    target = lax.broadcasted_iota(jnp.int32, shape, 1)
    within = target & (HEAD_LANES - 1)
    head = target >> (HEAD_LANES.bit_length() - 1)
    hit = (within < HEAD_WIDTH) & (source == which * width + head * HEAD_WIDTH + within)
    return jnp.where(hit, 1.0, 0.0).astype(BF16)


def gelu_tanh(pre):
    inner = math.sqrt(2.0 / math.pi) * (pre + 0.044715 * (pre * pre * pre))
    return 0.5 * pre * (1.0 + jnp.tanh(inner))


def gelu_slope(pre):
    scale = math.sqrt(2.0 / math.pi)
    square = pre * pre
    tanh = jnp.tanh(scale * (pre + 0.044715 * (pre * square)))
    return 0.5 * (1.0 + tanh) + 0.5 * pre * (1.0 - tanh * tanh) * scale * (
        1.0 + 3 * 0.044715 * square
    )


def silu(value):
    return value / (1.0 + jnp.exp(-value))


class Share:
    def __init__(self, own, other, parts, sems):
        self.own, self.other, self.parts = own, other, parts
        self.send, self.recv = sems
        self.size = own.shape[0] // parts
        self.copies = []

    def rows(self, core, y):
        part = core if self.parts == 2 else core + 2 * y
        return pl.ds(pl.multiple_of(part * self.size, 16), self.size)

    def begin(self):
        rows = self.rows(core_bit(), y_bit())
        self.first = remote(
            self.own.at[rows], self.other.at[rows], self.send.at[0], self.recv.at[0], x_peer()
        )

    def forward(self, first):
        if first is not None:
            first.wait()
        mine = self.other.at[self.rows(core_bit(), y_bit())]
        self.copies.append(remote(mine, mine, self.send.at[1], self.recv.at[1], core_peer()))
        if self.parts == 4:
            self.second = remote(mine, mine, self.send.at[2], self.recv.at[2], y_peer())

    def forward_again(self):
        if self.parts == 4:
            self.second.wait()
            got = self.other.at[self.rows(core_bit(), 1 - y_bit())]
            self.copies.append(remote(got, got, self.send.at[3], self.recv.at[3], core_peer()))

    def finish(self):
        wait_all(self.copies)


class Cargo:
    inputs, outs, scratch, aliases, any_outs = (), (), (), {}, False

    def bind(self, inputs, outs, scratch):
        self.ins, self.out_refs, self.held = inputs, outs, scratch

    def peers(self):
        return []

    def begin(self):
        pass

    def middle(self):
        pass

    def late(self):
        pass

    def end(self):
        pass


def quarter(shape):
    return shape[:-2] + (shape[-2] // 4, shape[-1])


class CoreSum:
    def __init__(self, whole, got, out, sems):
        self.whole, self.got, self.out, self.sems = whole, got, out, sems
        self.size = whole.shape[-2] // 4

    def rows(self, core, y):
        part = pl.ds(pl.multiple_of((core + 2 * y) * self.size, 16), self.size)
        whole = self.whole
        return whole.at[:, part] if len(whole.shape) == 3 else whole.at[part]

    def begin(self):
        self.copies = [
            remote(
                self.rows(1 - core_bit(), y), self.got.at[y],
                self.sems.at[0, y], self.sems.at[1, y], core_peer(),
            )
            for y in range(2)
        ]

    def end(self):
        wait_all(self.copies)
        for y in range(2):
            mine = self.rows(core_bit(), y)[...]
            self.out[y] = (mine.astype(F32) + self.got[y].astype(F32)).astype(BF16)


def core_sum_scratch(shape):
    return [
        pltpu.VMEM(shape, BF16),
        pltpu.VMEM((2,) + quarter(shape), BF16),
        pltpu.SemaphoreType.DMA((2, 2)),
    ]


class YSum(Cargo):
    def __init__(self, parts, dtype):
        part = parts.shape[1:]
        self.inputs = (parts,)
        self.outs = ((part, dtype),)
        self.scratch = (
            pltpu.VMEM(part, BF16),
            pltpu.VMEM(part, BF16),
            pltpu.SemaphoreType.DMA((3,)),
        )

    def peers(self):
        return ["y"]

    def begin(self):
        mine, other, sems = self.held
        self.copies = [
            remote(self.ins[0].at[1 - y_bit()], other, sems.at[0], sems.at[1], y_peer()),
            local(self.ins[0].at[y_bit()], mine, sems.at[2]),
        ]

    def end(self):
        mine, other, sems = self.held
        out = self.out_refs[0]
        wait_all(self.copies)
        out[...] = (mine[...].astype(F32) + other[...].astype(F32)).astype(out.dtype)


class SectionSum(Cargo):
    def __init__(self, part, owner, dtype=F32):
        self.owner = owner
        self.inputs = (part,)
        self.outs = ((part.shape, dtype),)
        self.scratch = (
            pltpu.VMEM(part.shape, BF16),
            pltpu.VMEM(part.shape, BF16),
            pltpu.SemaphoreType.DMA((3,)),
        )

    def peers(self):
        return ["x"]

    def source(self):
        return self.ins[0]

    def begin(self):
        mine, other, sems = self.held
        self.copy = describe(self.source(), other, sems.at[0], sems.at[1], x_peer())
        self.load = pltpu.make_async_copy(self.source(), mine, sems.at[2])
        is_owner = lax.axis_index("section") == self.owner

        @pl.when(is_owner)
        def take():
            self.load.start()

        @pl.when(jnp.logical_not(is_owner))
        def give():
            self.copy.start()

    def end(self):
        mine, other, sems = self.held
        is_owner = lax.axis_index("section") == self.owner

        @pl.when(is_owner)
        def add():
            self.load.wait()
            self.copy.wait_recv()
            out = self.out_refs[0]
            out[...] = (mine[...].astype(F32) + other[...].astype(F32)).astype(out.dtype)

        @pl.when(jnp.logical_not(is_owner))
        def given():
            self.copy.wait_send()
            self.out_refs[0][...] = jnp.zeros_like(self.out_refs[0])


class LastSum(YSum):
    def __init__(self, parts, owner):
        super().__init__(parts, F32)
        part = parts.shape[1:]
        self.owner = owner
        self.scratch = self.scratch + (
            pltpu.VMEM(part, BF16),
            pltpu.VMEM(part, BF16),
            pltpu.SemaphoreType.DMA((2,)),
        )

    def peers(self):
        return ["y", "x"]

    def begin(self):
        self.held, self.last = self.held[:3], self.held[3:]
        super().begin()

    def middle(self):
        mine, other, sems = self.held
        total, got, last_sems = self.last
        wait_all(self.copies)
        total[...] = (mine[...].astype(F32) + other[...].astype(F32)).astype(BF16)
        self.copy = describe(total, got, last_sems.at[0], last_sems.at[1], x_peer())

        @pl.when(lax.axis_index("section") != self.owner)
        def give():
            self.copy.start()

    def end(self):
        total, got, last_sems = self.last
        is_owner = lax.axis_index("section") == self.owner

        @pl.when(is_owner)
        def add():
            self.copy.wait_recv()
            self.out_refs[0][...] = total[...].astype(F32) + got[...].astype(F32)

        @pl.when(jnp.logical_not(is_owner))
        def given():
            self.copy.wait_send()
            self.out_refs[0][...] = jnp.zeros_like(self.out_refs[0])


class Swap(Cargo):
    def __init__(self, one, two):
        self.inputs = (one, two)
        self.outs = ((one.shape, one.dtype),)
        self.scratch = (pltpu.VMEM(one.shape, one.dtype), pltpu.SemaphoreType.DMA((2,)))

    def peers(self):
        return ["x"]

    def begin(self):
        got, sems = self.held
        one, two = self.ins
        self.copy = describe(two, got, sems.at[0], sems.at[1], x_peer())
        is_first = lax.axis_index("section") == 0

        @pl.when(is_first)
        def give_two():
            self.copy.start()

        @pl.when(jnp.logical_not(is_first))
        def give_one():
            describe(one, got, sems.at[0], sems.at[1], x_peer()).start()

    def end(self):
        self.copy.wait()
        self.out_refs[0][...] = self.held[0][...]


def span(ref, axis, start, size):
    part = pl.ds(pl.multiple_of(start, 128 if axis == 1 else 16), size)
    lead = (slice(None),) * (len(ref.shape) - 2)
    return ref.at[lead + ((slice(None), part) if axis == 1 else (part, slice(None)))]


def cut(shape, axis, by):
    shape = list(shape)
    shape[axis - 2] //= by
    return tuple(shape)


class HalfSum(Cargo):
    def __init__(self, grad, axis, name, slots=None):
        self.slots = slots if slots is not None else (0, grad.shape[0])
        part = cut((self.slots[1],) + grad.shape[1:], axis, 2)
        self.axis, self.name, self.size = axis, name, part[axis - 2]
        self.inputs = (grad,)
        self.outs = ((part, BF16),)
        self.scratch = (
            pltpu.VMEM(part, BF16),
            pltpu.VMEM(part, BF16),
            pltpu.SemaphoreType.DMA((3,)),
        )

    def peers(self):
        return [self.name]

    def begin(self):
        mine, other, sems = self.held
        if self.name == "x":
            bit, peer = lax.axis_index("section"), x_peer()
        else:
            bit, peer = y_bit(), y_peer()
        grad = self.ins[0].at[pl.ds(*self.slots)]
        self.copies = [
            remote(
                span(grad, self.axis, (1 - bit) * self.size, self.size), other,
                sems.at[0], sems.at[1], peer,
            ),
            local(span(grad, self.axis, bit * self.size, self.size), mine, sems.at[2]),
        ]

    def end(self):
        mine, other, sems = self.held
        wait_all(self.copies)
        self.out_refs[0][...] = (mine[...].astype(F32) + other[...].astype(F32)).astype(BF16)


class ColumnGather(Cargo):
    any_outs = True

    def __init__(self, weights, axes, targets, biases):
        self.axes = axes
        self.inputs = (*weights, targets, biases)
        self.outs = tuple(((2,) + one.shape, BF16) for one in weights) + (
            ((2, 2) + targets.shape[1:], BF16),
            ((2, 2) + biases.shape, F32),
        )
        self.scratch = (
            pltpu.SemaphoreType.DMA((5, 6)),
            pltpu.SemaphoreType.DMA((5, 2, 2)),
            pltpu.SemaphoreType.DMA((5,)),
        )

    def peers(self):
        return ["core", "cross"]

    def pieces(self, target):
        tensor, core = lax.axis_index("tensor"), core_bit()
        eighth = lax.axis_index("section") * 4 + y_bit() * 2 + core
        slot, out = lax.rem(tensor, 2), []
        for source, place, axis in zip(self.ins[:3], self.out_refs[:3], self.axes):
            size = source.shape[axis] // 8
            out.append(
                (
                    span(source, axis, eighth * size, size),
                    span(place.at[slot], axis, eighth * size, size),
                )
            )
        out.append((self.ins[3].at[target], self.out_refs[3].at[slot, core]))
        out.append((self.ins[4], self.out_refs[4].at[slot, core]))
        return out

    def copies(self, step):
        tensor, core = lax.axis_index("tensor"), core_bit()
        send, recv, own = self.held
        target = lax.rem(tensor + step, 4)
        peer = {"tensor": target, "dp": lax.axis_index("dp") - core + tensor // 2}
        return [
            describe(source, place, send.at[i, step], recv.at[i, lax.rem(tensor, 2), core], peer)
            for i, (source, place) in enumerate(self.pieces(target))
        ]

    def stays(self):
        return core_bit() == lax.axis_index("tensor") // 2

    def own_copies(self):
        own = self.held[2]
        return [
            pltpu.make_async_copy(source, place, own.at[i])
            for i, (source, place) in enumerate(self.pieces(lax.axis_index("tensor")))
        ]

    def direct(self, step, i):
        if step == 2 or i > 2:
            return None
        return lax.axis_index("tensor") != (3 if step == 1 else 0)

    def each(self, which, act):
        for step in range(1, 4):
            for i, copy in enumerate(self.copies(step)):
                if i in which:
                    allowed = self.direct(step, i)
                    if allowed is None:
                        act(copy)
                    else:

                        @pl.when(allowed)
                        def go(copy=copy):
                            act(copy)

    def start(self, which):
        self.each(which, lambda copy: copy.start())

        @pl.when(self.stays())
        def keep():
            for i, copy in enumerate(self.own_copies()):
                if i in which:
                    copy.start()

        @pl.when(jnp.logical_not(self.stays()))
        def give():
            for i, copy in enumerate(self.copies(0)):
                if i in which:
                    copy.start()

    def passes_on(self):
        tensor, core = lax.axis_index("tensor"), core_bit()
        return jnp.logical_or(
            jnp.logical_and(tensor == 2, core == 0), jnp.logical_and(tensor == 1, core == 1)
        )

    def passed(self, i, other):
        send, recv, own = self.held
        tensor, slot = lax.axis_index("tensor"), core_bit()
        size = self.ins[i].shape[self.axes[i]] // 8
        eighth = lax.axis_index("section") * 4 + y_bit() * 2 + other
        part = span(self.out_refs[i].at[slot], self.axes[i], eighth * size, size)
        return describe(
            part, part, send.at[i, 4 + other], recv.at[i, slot, other], {"tensor": 3 * (tensor - 1)}
        )

    def relay(self, which):
        @pl.when(self.passes_on())
        def pass_on():
            for i in which:
                for other in range(2):
                    copy = self.passed(i, other)
                    copy.wait_recv()
                    copy.start()

    def begin(self):
        self.start((2, 3, 4))

    def middle(self):
        self.relay((2,))
        self.start((0,))

    def late(self):
        self.start((1,))

    def end(self):
        send, recv, own = self.held
        tensor, core = lax.axis_index("tensor"), core_bit()
        self.each(range(5), lambda copy: copy.wait_send())

        @pl.when(self.stays())
        def kept():
            for copy in self.own_copies():
                copy.wait()

        @pl.when(jnp.logical_not(self.stays()))
        def given():
            for copy in self.copies(0):
                copy.wait_send()

        @pl.when(self.passes_on())
        def passed_on():
            for i in range(3):
                for other in range(2):
                    self.passed(i, other).wait_send()

        for slot in range(2):
            for other in range(2):
                mine = jnp.logical_and(2 * core + slot == tensor, core == other)
                relayed = jnp.logical_and(self.passes_on(), core == slot)
                peer = {"tensor": lax.rem(tensor + 1, 4)}
                waits = [
                    describe(source, place, send.at[i, 1], recv.at[i, slot, other], peer)
                    for i, (source, place) in enumerate(self.pieces(tensor))
                ]

                @pl.when(jnp.logical_not(mine))
                def arrived(waits=waits):
                    for copy in waits[3:]:
                        copy.wait_recv()

                @pl.when(jnp.logical_not(jnp.logical_or(mine, relayed)))
                def weights_arrived(waits=waits):
                    for copy in waits[:3]:
                        copy.wait_recv()


class ShareAlong(Cargo):
    any_outs = True

    def __init__(self, weights, axes, stage):
        self.axes = axes
        self.inputs = tuple(weights)
        self.outs = tuple((one.shape, BF16) for one in weights)
        self.aliases = {0: 0, 1: 1, 2: 2}
        self.stage = stage
        self.scratch = (pltpu.SemaphoreType.DMA((4,)), pltpu.SemaphoreType.DMA((4,)))

    def peers(self):
        return ["x", "y"]

    def begin(self):
        send, recv = self.held
        section, y, self.copies = lax.axis_index("section"), y_bit(), []

        def give(which, start, parts, peer):
            ref, axis = self.out_refs[which], self.axes[which]
            size = ref.shape[axis + 1] // 4
            part = span(ref, axis, start * size, parts * size)
            i = len(self.copies)
            self.copies.append(remote(part, part, send.at[i], recv.at[i], peer))

        if self.stage == 0:
            give(1, 2 * section + y, 1, x_peer())
            give(0, 2 * section + y, 1, y_peer())
            give(2, 2 * section + y, 1, y_peer())
        elif self.stage == 1:
            give(0, 2 * section, 2, x_peer())
            give(1, y, 1, y_peer())
        else:
            give(2, 2 * section, 2, x_peer())
            give(1, 2 + y, 1, y_peer())

    def end(self):
        wait_all(self.copies)


class ColumnSum(Cargo):
    def __init__(self, grads, axis):
        self.axis = axis
        self.part = cut(grads[0].shape[1:], axis, 2)
        self.inputs = tuple(grads)
        self.outs = ((self.part, F32),)
        self.scratch = (
            pltpu.VMEM((4,) + self.part, BF16),
            pltpu.SemaphoreType.DMA((4,)),
            pltpu.SemaphoreType.DMA((4,)),
            pltpu.SemaphoreType.DMA,
        )

    def peers(self):
        return ["core", "cross"]

    def copy(self, slot, other):
        got, send, recv, own = self.held
        tensor, core = lax.axis_index("tensor"), core_bit()
        size = self.part[self.axis]
        ref = self.ins[0].at[slot] if len(self.ins) == 1 else self.ins[slot].at[0]
        source = span(ref, self.axis, other * size, size)
        peer = {"tensor": 2 * core + slot, "dp": lax.axis_index("dp") - core + other}
        mine = jnp.logical_and(2 * core + slot == tensor, core == other)
        away = describe(source, got.at[tensor], send.at[2 * slot + other], recv.at[tensor], peer)
        return mine, away, pltpu.make_async_copy(source, got.at[tensor], own)

    def each(self, act_away, act_own):
        for slot in range(2):
            for other in range(2):
                mine, away, own = self.copy(slot, other)

                @pl.when(mine)
                def stay(own=own):
                    act_own(own)

                @pl.when(jnp.logical_not(mine))
                def leave(away=away):
                    act_away(away)

    def begin(self):
        self.each(lambda copy: copy.start(), lambda copy: copy.start())

    def end(self):
        got, send, recv, own = self.held
        tensor, core = lax.axis_index("tensor"), core_bit()
        self.each(lambda copy: copy.wait_send(), lambda copy: copy.wait())
        for source in range(4):
            mine = jnp.logical_and(tensor == source, core == tensor // 2)

            @pl.when(jnp.logical_not(mine))
            def arrived(source=source):
                describe(
                    got.at[source], got.at[source], send.at[0], recv.at[source],
                    {"tensor": lax.rem(tensor + 1, 4)},
                ).wait_recv()

        total = got[0].astype(F32)
        for source in range(1, 4):
            total = total + got[source].astype(F32)
        self.out_refs[0][...] = total


def cross_peers():
    tensor, dp = lax.axis_index("tensor"), core_peer()["dp"]
    return [{"tensor": lax.rem(tensor + step, 4), "dp": dp} for step in range(1, 4)]


class Bundle:
    def __init__(self, cargos):
        self.cargos = cargos

    def peers(self, names=()):
        names = list(names) + [name for cargo in self.cargos for name in cargo.peers()]
        known = {"core": core_peer, "y": y_peer, "x": x_peer}
        cross = cross_peers() if "cross" in names else []
        return [make() for name, make in known.items() if name in names] + cross

    def begin(self):
        for cargo in self.cargos:
            cargo.begin()

    def middle(self):
        for cargo in self.cargos:
            cargo.middle()

    def late(self):
        for cargo in self.cargos:
            cargo.late()

    def end(self):
        for cargo in self.cargos:
            cargo.end()


def attend_body(
    count, peers, u_ref, mods, segs, biases, outs, scratch, sems, need_qkv, need_out, steps
):
    middle_ref, branch_ref, full_ref, q_ref, k_ref, v_ref, probs_ref, mixed_ref = outs
    full, wqkv, wo, mixed_wide = scratch[:4]
    buffers = scratch[4:7]
    seg_own, seg_col, seg_row = segs
    mod_ref = mods()
    me = lax.axis_index("tensor")
    rows, length, width = u_ref.shape
    heads_width = wo.shape[0]
    heads = heads_width // HEAD_WIDTH
    u = flat(u_ref).astype(F32)
    normed, unused = layer_norm(u)
    attn_in = normed * (1.0 + token_mod(mod_ref, seg_own, 1)) + token_mod(mod_ref, seg_own, 0)
    full[:, own_rows(me, length), :] = attn_in.astype(BF16).reshape(rows, length, width)
    if peers is not None:
        greet(peers)
    line = Line(length, sems)
    line.start_gather(full)
    spread = spread_matrix(heads_width)
    line.relay(full)
    steps[0]()
    need_qkv()
    line.finish_gather(full)
    full_ref[...] = full[...]
    tokens = flat(full)
    bias = biases()
    both = 3 * heads_width
    projected = (dot(tokens, wqkv[...]) + bias[0:1, :both]).astype(BF16)
    for which, target in enumerate((q_ref, k_ref, v_ref)):
        parts = dot(projected, spread_matrix(heads_width, which, both))
        target[...] = parts.astype(BF16).reshape(target.shape)

    def one_head(index, carry):
        row = index // heads
        head = lax.rem(index, heads)
        lanes = pl.ds(pl.multiple_of(head * HEAD_LANES, HEAD_LANES), HEAD_LANES)
        scores = dot(q_ref[row, :, lanes], k_ref[row, :, lanes], NT) * HEAD_WIDTH ** (-0.5)
        scores = jnp.where(seg_col[row] == seg_row[row], scores, MASKED_SCORE)
        raised = jnp.exp(scores - jnp.max(scores, axis=-1, keepdims=True))
        probs = raised / jnp.sum(raised, axis=-1, keepdims=True)
        probs_ref[index] = probs
        mixed_wide[row, :, lanes] = dot(probs.astype(BF16), v_ref[row, :, lanes]).astype(BF16)
        return carry

    steps[1]()
    lax.fori_loop(0, rows * heads, one_head, 0)
    mixed_ref[...] = dot(flat(mixed_wide), spread, NT).astype(BF16).reshape(mixed_ref.shape)
    need_out()

    def partial(which_rows):
        return dot(mixed_ref[:, which_rows, :].reshape(rows * length, heads_width), wo[...])

    total = line.scatter_sum(partial, buffers)
    steps[2]()
    branch = line.finish_sum(total, buffers) + bias[2:3, :]
    branch_ref[...] = branch.reshape(branch_ref.shape)
    middle = flat(u_ref).astype(F32) + token_mod(mod_ref, seg_own, 2) * branch
    middle_ref[...] = middle.reshape(middle_ref.shape)


def open_kernel(count, sections, *refs, cargo):
    u_ref, cond_ref, ada_b_ref, biases_ref, seg_own, seg_col, seg_row = refs[:7]
    ada_w, own_qkv, own_out, own_one, own_two = refs[7:12]
    mods_ref, bias_ref, other_qkv, other_out, other_one, other_two = refs[12:18]
    outs = refs[18:26]
    scratch = refs[26:33]
    ada, mod_src, mod_buf, bias_buf, w_sem, ag_send, ag_recv, rs_send, rs_recv = refs[33:42]
    mod_send, mod_recv, share_send, share_recv, ada_sem = refs[42:]
    wqkv, wo = scratch[1:3]
    section, tensor = lax.axis_index("section"), lax.axis_index("tensor")
    load_ada = local(ada_w, ada, ada_sem)
    shares = [
        Share(own, other, parts, (share_send.at[i], share_recv.at[i]))
        for i, (own, other, parts) in enumerate(
            (
                (own_qkv, other_qkv, 4), (own_out, other_out, 2),
                (own_one, other_one, 4), (own_two, other_two, 4),
            )
        )
    ]
    plane = [
        {"section": lax.rem(section + a, sections), "tensor": lax.rem(tensor + b, count)}
        for a in range(sections)
        for b in range(count)
        if a or b
    ]
    greet(plane + [core_peer(), y_peer()] + cross_peers())
    shares[0].begin()
    cargo.begin()
    cond_act = silu(cond_ref[...].astype(F32)).astype(BF16)
    load_ada.wait()
    mod = dot(cond_act, ada[...], NT) + ada_b_ref[...].astype(F32)
    mod_src[...] = mod.reshape(mod_src.shape)
    mod_buf[section, tensor] = mod_src[section]
    copies = [
        remote(
            mod_src.at[peer["section"]], mod_buf.at[section, tensor],
            mod_send.at[i], mod_recv.at[i], peer,
        )
        for i, peer in enumerate(plane)
    ]
    bias_buf[section] = biases_ref[...]
    bias_copy = remote(
        biases_ref, bias_buf.at[section],
        mod_send.at[len(plane)], mod_recv.at[len(plane)], x_peer(),
    )
    for share in shares[1:]:
        share.begin()

    def mods():
        wait_all(copies)
        width, piece = mods_ref.shape[-1], mod_buf.shape[-1]
        for block in range(sections):
            for which in range(6):
                parts, at = [], which * width
                while at < (which + 1) * width:
                    end = min((at // piece + 1) * piece, (which + 1) * width)
                    start = at - at // piece * piece
                    parts.append(mod_buf[block, at // piece][:, start : start + end - at])
                    at = end
                mods_ref[block, which] = (
                    jnp.concatenate(parts, axis=1) if len(parts) > 1 else parts[0]
                )
        return mods_ref.at[0]

    def biases():
        bias_copy.wait()
        bias_ref[...] = bias_buf[...]
        return bias_buf[0]

    def need_qkv():
        fetch(0, own_qkv, other_qkv, wqkv, w_sem.at[0]).wait()

    def need_out():
        shares[1].finish()
        fetch(0, own_out, other_out, wo, w_sem.at[1]).wait()

    def after_gather():
        shares[0].forward(shares[0].first)
        cargo.middle()
        shares[1].forward(shares[1].first)
        shares[0].forward_again()
        shares[0].finish()

    def before_heads():
        cargo.late()
        shares[2].forward(shares[2].first)

    def after_scatter():
        gather = cargo.cargos[0]
        gather.relay((0,))
        shares[2].forward_again()
        shares[3].forward(shares[3].first)
        gather.relay((1,))
        shares[2].finish()

    attend_body(
        count, None, u_ref, mods, (seg_own, seg_col, seg_row), biases, outs, scratch,
        (ag_send, ag_recv, rs_send, rs_recv), need_qkv, need_out,
        (after_gather, before_heads, after_scatter),
    )
    shares[3].forward_again()
    cargo.end()
    shares[3].finish()


def attend_kernel(count, block, *refs, cargo):
    u_ref, mods_ref, bias_ref, seg_own, seg_col, seg_row = refs[:6]
    own_qkv, other_qkv, own_out, other_out = refs[6:10]
    outs, scratch, w_sem = refs[10:18], refs[18:25], refs[25]
    load_qkv = fetch(block, own_qkv, other_qkv, scratch[1], w_sem.at[0])
    load_out = fetch(block, own_out, other_out, scratch[2], w_sem.at[1])
    attend_body(
        count, z_peers(count) + cargo.peers(), u_ref, lambda: mods_ref.at[block],
        (seg_own, seg_col, seg_row), lambda: bias_ref[block], outs, scratch, refs[26:30],
        load_qkv.wait, load_out.wait, (cargo.begin, cargo.middle, cargo.late),
    )
    cargo.end()


def mlp_kernel(
    count, block,
    middle_ref, mods_ref, bias_ref, seg_own, w1_own, w1_other, w2_own, w2_other,
    out_ref, branch_ref, full_ref, pre_ref, act_ref,
    full, w1, w2, send_buf, recv_buf, relay_buf, w_sem, *sems, cargo,
):
    me = lax.axis_index("tensor")
    rows, length, width = middle_ref.shape
    mod_ref = mods_ref.at[block]
    load_one = fetch(block, w1_own, w1_other, w1, w_sem.at[0])
    load_two = fetch(block, w2_own, w2_other, w2, w_sem.at[1])
    normed, unused = layer_norm(flat(middle_ref))
    mlp_in = normed * (1.0 + token_mod(mod_ref, seg_own, 4)) + token_mod(mod_ref, seg_own, 3)
    full[:, own_rows(me, length), :] = mlp_in.astype(BF16).reshape(rows, length, width)
    greet(z_peers(count) + cargo.peers())
    line = Line(length, sems)
    line.start_gather(full)
    cargo.begin()
    line.relay(full)
    load_one.wait()
    line.finish_gather(full)
    full_ref[...] = full[...]
    pre = dot(flat(full), w1[...]) + bias_ref[block, 3:4, : w1.shape[1]]
    pre_ref[...] = pre.reshape(pre_ref.shape)
    cargo.middle()
    act_ref[...] = gelu_tanh(pre).astype(BF16).reshape(act_ref.shape)
    load_two.wait()

    def partial(which_rows):
        return dot(act_ref[:, which_rows, :].reshape(rows * length, -1), w2[...])

    buffers = (send_buf, recv_buf, relay_buf)
    total = line.scatter_sum(partial, buffers)
    branch = line.finish_sum(total, buffers) + bias_ref[block, 4:5, :]
    cargo.end()
    branch_ref[...] = branch.reshape(branch_ref.shape)
    out = flat(middle_ref) + token_mod(mod_ref, seg_own, 5) * branch
    out_ref[...] = out.astype(BF16).reshape(out_ref.shape)


def mlp_back_kernel(count, block, *refs, cargo):
    g_ref, middle_ref, branch_ref, mods_ref, seg_own, full_ref, pre_ref, act_ref = refs[:8]
    w1_own, w1_other, w2_own, w2_other = refs[8:12]
    d_middle_ref, d_mod_ref, d_w1_ref, d_w2_ref, d_b1_ref, d_b2_ref = refs[12:18]
    full, d_pre, w1, w2, *buffers, w_sem = refs[18:26]
    sems = refs[26:30]
    w1_whole, w1_got, w1_sems, w2_whole, w2_got, w2_sems = refs[30:]
    w1_sum = CoreSum(w1_whole, w1_got, d_w1_ref, w1_sems)
    w2_sum = CoreSum(w2_whole, w2_got, d_w2_ref, w2_sems)
    me = lax.axis_index("tensor")
    rows, length, width = middle_ref.shape
    mod_ref = mods_ref.at[block]
    load_one = fetch(block, w1_own, w1_other, w1, w_sem.at[0])
    load_two = fetch(block, w2_own, w2_other, w2, w_sem.at[1])
    g = flat(g_ref).astype(F32)
    d_branch = (g * token_mod(mod_ref, seg_own, 5)).astype(BF16)
    full[:, own_rows(me, length), :] = d_branch.reshape(rows, length, width)
    greet(z_peers(count) + cargo.peers(["core"]))
    line = Line(length, sems)
    line.start_gather(full)
    cargo.begin()
    slot_sums(g * flat(branch_ref), seg_own, d_mod_ref, 2)
    line.relay(full)
    cargo.middle()
    load_two.wait()
    line.finish_gather(full)
    d_act = dot(flat(full), w2[...], NT)
    d_pre[...] = (d_act * gelu_slope(flat(pre_ref))).astype(BF16).reshape(d_pre.shape)
    load_one.wait()

    def partial(which_rows):
        return dot(d_pre[:, which_rows, :].reshape(rows * length, -1), w1[...], NT)

    total = line.scatter_sum(partial, buffers)
    w2_whole[...] = dot(flat(full), flat(act_ref), TN).astype(BF16)
    w2_sum.begin()
    w1_whole[...] = dot(flat(full_ref), flat(d_pre), TN).astype(BF16)
    w1_sum.begin()
    d_b2_ref[...] = jnp.sum(flat(full).astype(F32), axis=0, keepdims=True)
    d_b1_ref[...] = jnp.sum(flat(d_pre).astype(F32), axis=0, keepdims=True)
    d_in = line.finish_sum(total, buffers)
    normed, inverse = layer_norm(flat(middle_ref))
    d_middle = flat(g_ref).astype(F32) + norm_back(
        d_in * (1.0 + token_mod(mod_ref, seg_own, 4)), normed, inverse
    )
    d_middle_ref[...] = d_middle.reshape(d_middle_ref.shape)
    slot_sums(d_in, seg_own, d_mod_ref, 0)
    slot_sums(d_in * normed, seg_own, d_mod_ref, 1)
    w2_sum.end()
    w1_sum.end()
    cargo.end()


def attend_back_kernel(count, block, *refs, cargo):
    d_middle_ref, u_ref, branch_ref, mods_ref, seg_own, full_ref = refs[:6]
    q_ref, k_ref, v_ref, probs_ref, mixed_ref = refs[6:11]
    wqkv_own, wqkv_other, wo_own, wo_other = refs[11:15]
    d_in_ref, d_mod_ref, d_wqkv_ref, d_wo_ref, d_bqv_ref, d_bo_ref = refs[15:21]
    full, wide, narrow, wqkv, wo, *buffers, w_sem = refs[21:30]
    sems = refs[30:34]
    qkv_whole, qkv_got, qkv_sems, wo_whole, wo_got, wo_sems = refs[34:]
    qkv_sum = CoreSum(qkv_whole, qkv_got, d_wqkv_ref, qkv_sems)
    wo_sum = CoreSum(wo_whole, wo_got, d_wo_ref, wo_sems)
    me = lax.axis_index("tensor")
    rows, length, width = u_ref.shape
    heads_width = wo.shape[0]
    heads = heads_width // HEAD_WIDTH
    mod_ref = mods_ref.at[block]
    load_qkv = fetch(block, wqkv_own, wqkv_other, wqkv, w_sem.at[0])
    load_out = fetch(block, wo_own, wo_other, wo, w_sem.at[1])
    d_middle = flat(d_middle_ref)
    d_branch = (d_middle * token_mod(mod_ref, seg_own, 2)).astype(BF16)
    full[:, own_rows(me, length), :] = d_branch.reshape(rows, length, width)
    greet(z_peers(count) + cargo.peers(["core"]))
    line = Line(length, sems)
    line.start_gather(full)
    cargo.begin()
    slot_sums(d_middle * flat(branch_ref), seg_own, d_mod_ref, 2)
    spread = spread_matrix(heads_width)
    line.relay(full)
    cargo.middle()
    load_out.wait()
    line.finish_gather(full)
    d_mixed = dot(flat(full), wo[...], NT).astype(BF16)
    wide[3] = dot(d_mixed, spread).astype(BF16).reshape(wide.shape[1:])

    def one_head(index, carry):
        row = index // heads
        head = lax.rem(index, heads)
        lanes = pl.ds(pl.multiple_of(head * HEAD_LANES, HEAD_LANES), HEAD_LANES)
        grad = wide[3, row, :, lanes]
        probs = probs_ref[index]
        d_probs = dot(grad, v_ref[row, :, lanes], NT)
        d_scores = (
            probs * (d_probs - jnp.sum(d_probs * probs, axis=-1, keepdims=True))
        ).astype(BF16)
        scale = HEAD_WIDTH ** (-0.5)
        wide[0, row, :, lanes] = (dot(d_scores, k_ref[row, :, lanes]) * scale).astype(BF16)
        wide[1, row, :, lanes] = (dot(d_scores, q_ref[row, :, lanes], TN) * scale).astype(BF16)
        wide[2, row, :, lanes] = dot(probs.astype(BF16), grad, TN).astype(BF16)
        return carry

    lax.fori_loop(0, rows * heads, one_head, 0)
    both = 3 * heads_width
    gathered = 0.0
    for which in range(3):
        gathered = gathered + dot(
            flat(wide.at[which]), spread_matrix(heads_width, which, both), NT
        )
    narrow[...] = gathered.astype(BF16).reshape(narrow.shape)
    load_qkv.wait()

    def partial(which_rows):
        return dot(narrow[:, which_rows, :].reshape(rows * length, both), wqkv[...], NT)

    total = line.scatter_sum(partial, buffers)
    d_bo_ref[...] = jnp.sum(flat(full).astype(F32), axis=0, keepdims=True)
    d_bqv_ref[...] = jnp.sum(flat(narrow).astype(F32), axis=0, keepdims=True)
    wo_whole[...] = dot(flat(full), flat(mixed_ref), TN).astype(BF16)
    wo_sum.begin()
    qkv_whole[...] = dot(flat(full_ref), flat(narrow), TN).astype(BF16)
    qkv_sum.begin()
    d_attn_in = line.finish_sum(total, buffers)
    normed, inverse = layer_norm(flat(u_ref).astype(F32))
    d_in = flat(d_middle_ref) + norm_back(
        d_attn_in * (1.0 + token_mod(mod_ref, seg_own, 1)), normed, inverse
    )
    d_in_ref[...] = d_in.reshape(d_in_ref.shape)
    slot_sums(d_attn_in, seg_own, d_mod_ref, 0)
    slot_sums(d_attn_in * normed, seg_own, d_mod_ref, 1)
    wo_sum.end()
    qkv_sum.end()
    cargo.end()


def silu_slope(value):
    gate = 1.0 / (1.0 + jnp.exp(-value))
    return gate * (1.0 + value * (1.0 - gate))


def project_kernel(token_count, *refs, cargo):
    sent_ref, targets_ref, biases_ref, p2_b_ref, p1_any, p2_any, p3_any = refs[:7]
    d_sent_ref, d_p1_ref, d_p2_ref, d_p3_ref, small_ref = refs[7:12]
    p1, p2, p3, tokens, first_pre, first, second_pre, second, d_second, norms = refs[12:22]
    buf_a, buf_b, buf_c, d_first, load_sem, send, recv = refs[22:]
    core, peer = core_bit(), core_peer()
    loads = [
        local(source, place, load_sem.at[i])
        for i, (source, place) in enumerate(((p1_any, p1), (p2_any, p2), (p3_any, p3)))
    ]
    count = tokens.shape[1]
    tokens[core] = flat(sent_ref)
    greet([peer])

    def trade(ref, which):
        return remote(ref.at[core], ref.at[core], send.at[which], recv.at[which], peer)

    def give(buffer, value, which):
        buffer[0] = value.astype(BF16)
        return remote(buffer.at[0], buffer.at[1], send.at[which], recv.at[which], peer)

    def block(ref, side):
        return ref[side]

    copy = trade(tokens, 0)
    target = [
        targets_ref[slot].reshape(2 * count, targets_ref.shape[-1]).astype(F32) for slot in range(2)
    ]
    target_sq = sum(jnp.sum(one * one, axis=1, keepdims=True) for one in target)
    loads[0].wait()
    copy.wait()
    all_tokens = flat(tokens)
    for slot in range(2):
        pre = dot(all_tokens, p1[slot]) + biases_ref[slot, 0, 0:1, :]
        first_pre[slot] = pre
        first[slot] = silu(pre).astype(BF16)
    loads[1].wait()

    def second_term(side):
        rows = pl.ds(pl.multiple_of(side * count, 16), count)
        return dot(first[0, rows, :], p2[0]) + dot(first[1, rows, :], p2[1])

    copy = give(buf_a, second_term(1 - core), 1)
    pre = second_term(core)
    copy.wait()
    pre = pre + buf_a[1].astype(F32) + p2_b_ref[...].astype(F32)
    second_pre[...] = pre
    second[core] = silu(pre).astype(BF16)
    copy = trade(second, 2)
    loads[2].wait()
    copy.wait()
    all_second = flat(second)
    width = target[0].shape[1]
    predicted = [
        dot(all_second, p3[slot], NT) + biases_ref[slot, 0, 1:2, :width] for slot in range(2)
    ]
    pred_sq = sum(jnp.sum(one * one, axis=1, keepdims=True) for one in predicted)
    cross = sum(
        jnp.sum(one * two, axis=1, keepdims=True) for one, two in zip(predicted, target)
    )
    lanes = lax.broadcasted_iota(jnp.int32, norms.shape[1:], 1)
    norms[core] = jnp.where(lanes == 0, pred_sq, jnp.where(lanes == 1, cross, target_sq))
    copy = trade(norms, 3)
    copy.wait()
    total = norms[0] + norms[1]
    inv_pred = lax.rsqrt(total[:, 0:1] + COSINE_EPS)
    inv_target = lax.rsqrt(total[:, 2:3] + COSINE_EPS)
    cosine = total[:, 1:2] * inv_pred * inv_target
    side = lax.broadcasted_iota(jnp.int32, cosine.shape, 0)
    own = jnp.logical_and(side >= core * count, side < (core + 1) * count)
    loss = jnp.sum(jnp.where(own, cosine, 0.0), axis=0, keepdims=True)
    factor = -0.5 / token_count
    one_scale = factor * inv_pred * inv_target
    two_scale = factor * cosine * inv_pred * inv_pred
    d_pred = [
        (one_scale * two - two_scale * one).astype(BF16) for one, two in zip(predicted, target)
    ]
    small_ref[...] = jnp.zeros_like(small_ref)
    for slot in range(2):
        small_ref[2 * core + slot, 1:2, :width] = jnp.sum(
            d_pred[slot].astype(F32), axis=0, keepdims=True
        )

    def d_second_term(side):
        terms = 0.0
        for slot in range(2):
            mine = jnp.where(
                side == 0, d_pred[slot][:count].astype(F32), d_pred[slot][count:].astype(F32)
            )
            terms = terms + dot(mine.astype(BF16), p3[slot])
        return terms

    copy = give(buf_b, d_second_term(1 - core), 4)
    grad = d_second_term(core)
    for slot in range(2):
        d_p3_ref[slot] = dot(d_pred[slot], all_second, TN).astype(BF16)
    copy.wait()
    grad = ((grad + buf_b[1].astype(F32)) * silu_slope(second_pre[...])).astype(BF16)
    d_second[core] = grad
    copy = trade(d_second, 5)
    d_p2_b = jnp.sum(grad.astype(F32), axis=0, keepdims=True)
    lane = small_ref.shape[2]
    loss_row = jnp.where(lax.broadcasted_iota(jnp.int32, (1, lane), 1) == 0, loss, 0.0)
    for part in range(4):
        for row in range(d_p2_b.shape[1] // lane):
            small_ref[part, 2 + row : 3 + row, :] = d_p2_b[:, row * lane : (row + 1) * lane]
        small_ref[part, 6:7, :] = loss_row
    copy.wait()
    all_d_second = flat(d_second)
    for slot in range(2):
        back = dot(all_d_second, p2[slot], NT) * silu_slope(first_pre[slot])
        d_first[slot] = back.astype(BF16)
        small_ref[2 * core + slot, 0:1, :] = jnp.sum(
            d_first[slot].astype(F32), axis=0, keepdims=True
        )

    def d_sent_term(side):
        rows = pl.ds(pl.multiple_of(side * count, 16), count)
        return dot(d_first[0, rows, :], p1[0], NT) + dot(d_first[1, rows, :], p1[1], NT)

    copy = give(buf_c, d_sent_term(1 - core), 6)
    grad = d_sent_term(core)
    for slot in range(2):
        d_p2_ref[slot] = dot(first[slot], all_d_second, TN).astype(BF16)
        d_p1_ref[slot] = dot(all_tokens, d_first[slot], TN).astype(BF16)
    copy.wait()
    d_sent_ref[...] = (grad + buf_c[1].astype(F32)).reshape(d_sent_ref.shape)


def close_kernel(count, sections, replicas, *refs, cargo):
    grads_ref, mod_refs, small_refs, proj_ref, cond_ref = (
        refs[:2], refs[2:6], refs[6:14], refs[14], refs[15]
    )
    grad_ref, ada_w_ref, ada_b_ref, small_ref, proj_sum_ref = refs[16:21]
    z_src, z_buf, mod_src, mod_buf, small_src, small_buf, cond_buf = refs[21:28]
    place_src, place_buf, proj_got, proj_src, proj_buf = refs[28:33]
    sems = refs[33:35]
    section, tensor, replica = (lax.axis_index(name) for name in ("section", "tensor", "dp"))
    send, recv = sems
    others = [
        {"section": lax.rem(section + a, sections), "dp": lax.rem(replica + b, replicas)}
        for a in range(sections)
        for b in range(replicas)
        if a or b
    ]
    greet(z_peers(count) + others + cross_peers())
    for one in cargo.cargos:
        if isinstance(one, YSum):
            one.begin()
    piece = z_src.shape[-1]
    for block in range(sections):
        attend_mod, mlp_mod = mod_refs[2 * block : 2 * block + 2]
        width = attend_mod.shape[-1]
        for part in range(count):
            at, end, cuts = part * piece, (part + 1) * piece, []
            while at < end:
                which = at // width
                stop = min((which + 1) * width, end)
                ref = attend_mod if which < 3 else mlp_mod
                cuts.append(ref[which % 3][:, at - which * width : stop - which * width])
                at = stop
            z_src[part, block] = jnp.concatenate(cuts, axis=1) if len(cuts) > 1 else cuts[0]
    z_copies = [
        remote(z_src.at[peer["tensor"]], z_buf.at[i], send.at[i], recv.at[i], peer)
        for i, peer in enumerate(z_peers(count))
    ]
    at = count - 1
    z_copies += [
        remote(proj_ref.at[peer["tensor"]], proj_got.at[i], send.at[at + i], recv.at[at + i], peer)
        for i, peer in enumerate(z_peers(count))
    ]
    at = at + count - 1

    @pl.when(section == 0)
    def first_place():
        place_src[...] = grads_ref[1][...].astype(BF16)

    @pl.when(section != 0)
    def second_place():
        place_src[...] = grads_ref[0][...].astype(BF16)

    place_copy = remote(place_src, place_buf, send.at[at], recv.at[at], x_peer())
    at = at + 1
    both = small_refs[0].shape[-1]
    small_src[...] = jnp.zeros_like(small_src)
    for block in range(sections):
        d_bqv, d_bo, d_b1, d_b2 = small_refs[4 * block : 4 * block + 4]
        small_src[block, 0:1, :both] = d_bqv[...]
        small_src[block, 2:3, :] = d_bo[...]
        small_src[block, 3:4, : d_b1.shape[1]] = d_b1[...]
        small_src[block, 4:5, :] = d_b2[...]
    small_buf[section, replica] = small_src[section]
    cond_buf[section, replica] = cond_ref[replica]
    copies = []
    for peer in others:
        copies.append(
            remote(
                small_src.at[peer["section"]], small_buf.at[section, replica],
                send.at[at], recv.at[at], peer,
            )
        )
        copies.append(
            remote(
                cond_ref.at[peer["dp"]], cond_buf.at[section, replica],
                send.at[at + 1], recv.at[at + 1], peer,
            )
        )
        at = at + 2
    for one in cargo.cargos:
        if not isinstance(one, YSum):
            one.begin()
    wait_all(z_copies)
    mine, mine_proj = z_src[tensor], proj_ref[tensor]
    for step in range(count - 1):
        mine = mine + z_buf[step]
        mine_proj = mine_proj + proj_got[step]
    mod_src[...] = mine
    mod_buf[section, replica] = mod_src[section]
    proj_src[...] = mine_proj
    proj_buf[section, replica] = mine_proj
    for peer in others:
        copies.append(
            remote(
                mod_src.at[peer["section"]], mod_buf.at[section, replica],
                send.at[at], recv.at[at], peer,
            )
        )
        copies.append(
            remote(
                proj_src, proj_buf.at[section, replica], send.at[at + 1], recv.at[at + 1], peer
            )
        )
        at = at + 2
    for one in cargo.cargos:
        if isinstance(one, LastSum):
            one.middle()
    place_copy.wait()
    rows = place_buf.shape[0]

    @pl.when(section == 0)
    def first_out():
        grad_ref[:rows] = grads_ref[0][...]
        grad_ref[rows:] = place_buf[...].astype(F32)

    @pl.when(section != 0)
    def second_out():
        grad_ref[rows:] = grads_ref[1][...]
        grad_ref[:rows] = place_buf[...].astype(F32)

    wait_all(copies)
    small, proj_sum = small_buf[0, 0], proj_buf[0, 0]
    for a in range(sections):
        for b in range(replicas):
            if a or b:
                small = small + small_buf[a, b]
                proj_sum = proj_sum + proj_buf[a, b]
    small_ref[...] = small
    proj_sum_ref[...] = proj_sum
    mod_all = flat(mod_buf)
    ada_b_ref[...] = jnp.sum(mod_all, axis=0, keepdims=True)
    ada_w_ref[...] = lax.dot_general(
        flat(cond_buf), mod_all, TN, precision=HIGHEST, preferred_element_type=F32
    )
    cargo.end()


VMEM = pl.BlockSpec(memory_space=pltpu.VMEM)
ANY = pl.BlockSpec(memory_space=pl.ANY)
MOD_ROWS = 8
PROJECTOR_AXES = (0, 0, 1)


def call(kernel, number, inputs, in_any, outs, out_any, scratch, flops, cargos=()):
    own_in, own_out, own_scratch = len(inputs), len(outs), len(scratch)
    specs = [VMEM] * (own_in - in_any) + [ANY] * in_any
    out_specs = [ANY if i in out_any else VMEM for i in range(own_out)]
    inputs, outs, scratch, aliases = list(inputs), list(outs), list(scratch), {}
    for cargo in cargos:
        for source, target in cargo.aliases.items():
            aliases[len(inputs) + source] = len(outs) + target
        inputs += cargo.inputs
        outs += cargo.outs
        scratch += cargo.scratch
        specs += [ANY] * len(cargo.inputs)
        out_specs += [ANY if cargo.any_outs else VMEM] * len(cargo.outs)

    def body(*refs):
        parts = [list(refs[: len(inputs)])]
        parts.append(list(refs[len(inputs) : len(inputs) + len(outs)]))
        parts.append(list(refs[len(inputs) + len(outs) :]))
        base = parts[0][:own_in] + parts[1][:own_out] + parts[2][:own_scratch]
        at = [own_in, own_out, own_scratch]
        for cargo in cargos:
            held = []
            for i, items in enumerate((cargo.inputs, cargo.outs, cargo.scratch)):
                held.append(parts[i][at[i] : at[i] + len(items)])
                at[i] += len(items)
            cargo.bind(*held)
        kernel(*base, cargo=Bundle(cargos))

    moved = sum(math.prod(one.shape) * one.dtype.itemsize for one in inputs)
    results = pl.pallas_call(
        body,
        out_shape=[jax.ShapeDtypeStruct(shape, dtype) for shape, dtype in outs],
        in_specs=specs,
        out_specs=out_specs,
        scratch_shapes=scratch,
        input_output_aliases=aliases,
        compiler_params=pltpu.CompilerParams(
            collective_id=number, has_side_effects=True, vmem_limit_bytes=56 * 2**20
        ),
        cost_estimate=pl.CostEstimate(flops=flops, bytes_accessed=moved, transcendentals=0),
    )(*inputs)
    at, carried = own_out, []
    for cargo in cargos:
        carried.append(results[at : at + len(cargo.outs)])
        at += len(cargo.outs)
    return results[:own_out], carried


def exchange_scratch(count, rows, length, width):
    return [
        pltpu.VMEM((count - 1, rows, length, width), BF16),
        pltpu.VMEM((count, rows, length, width), BF16),
        pltpu.VMEM((rows, length, width), BF16),
    ]


def semaphores(count):
    return [pltpu.SemaphoreType.DMA((2,))] + [
        pltpu.SemaphoreType.DMA((size,)) for size in (count, count, count - 1, count + 1)
    ]


class Shapes:
    def __init__(self, u, own, count):
        self.rows, self.length, self.width = u.shape
        self.count = count
        self.positions = self.length * count
        self.tokens = self.rows * self.positions
        self.heads_width = own["out"].shape[0]
        self.hidden = own["one"].shape[1]
        self.heads = self.heads_width // HEAD_WIDTH
        self.local = (self.rows, self.length, self.width)
        self.full = (self.rows, self.positions, self.width)
        self.wide = (self.rows, self.positions, self.heads * HEAD_LANES)
        self.own = own
        self.attend_outs = [
            (self.local, F32), (self.local, F32), (self.full, BF16),
            (self.wide, BF16), (self.wide, BF16), (self.wide, BF16),
            ((self.rows * self.heads, self.positions, self.positions), F32),
            ((self.rows, self.positions, self.heads_width), BF16),
        ]
        self.attend_scratch = [
            pltpu.VMEM(self.full, BF16),
            pltpu.VMEM(own["qkv"].shape, BF16),
            pltpu.VMEM(own["out"].shape, BF16),
            pltpu.VMEM(self.wide, BF16),
        ] + exchange_scratch(count, *self.local)
        self.mods = (3, MOD_ROWS, self.width)


def pairs(own, other, names):
    out = []
    for name in names:
        out += [own[name], other[name]]
    return out


def open_forward(sizes, u, cond, ada_w, ada_b, biases, segs, own, sections, cargos):
    count, width = sizes.count, sizes.width
    piece = ada_w.shape[0]
    inputs = [u, cond, ada_b, biases, *segs, ada_w] + [own[n] for n in ("qkv", "out", "one", "two")]
    plane = sections * count - 1
    results, carried = call(
        functools.partial(open_kernel, count, sections),
        0,
        inputs,
        5,
        [((sections, 6, MOD_ROWS, width), F32), ((sections,) + biases.shape, F32)]
        + [(own[n].shape, BF16) for n in ("qkv", "out", "one", "two")]
        + sizes.attend_outs,
        (2, 3, 4, 5),
        sizes.attend_scratch
        + [
            pltpu.VMEM(ada_w.shape, BF16),
            pltpu.VMEM((sections, MOD_ROWS, piece), F32),
            pltpu.VMEM((sections, count, MOD_ROWS, piece), F32),
            pltpu.VMEM((sections,) + biases.shape, F32),
        ]
        + semaphores(count)
        + [
            pltpu.SemaphoreType.DMA((plane + 1,)),
            pltpu.SemaphoreType.DMA((plane + 1,)),
            pltpu.SemaphoreType.DMA((4, 4)),
            pltpu.SemaphoreType.DMA((4, 4)),
            pltpu.SemaphoreType.DMA,
        ],
        2 * sizes.tokens * width * sizes.heads_width * 4,
        cargos,
    )
    other = dict(zip(("qkv", "out", "one", "two"), results[2:6]))
    return results[0], results[1], other, results[6:], carried


def attend_forward(sizes, block, u, mods, biases, segs, own, other, cargos):
    inputs = [u, mods, biases, *segs] + pairs(own, other, ("qkv", "out"))
    return call(
        functools.partial(attend_kernel, sizes.count, block),
        1,
        inputs,
        4,
        sizes.attend_outs,
        (),
        sizes.attend_scratch + semaphores(sizes.count),
        2 * sizes.tokens * sizes.width * sizes.heads_width * 4,
        cargos,
    )


def mlp_forward(sizes, block, middle, mods, biases, segs, own, other, cargos):
    inputs = [middle, mods, biases, segs[0]] + pairs(own, other, ("one", "two"))
    hidden = (sizes.rows, sizes.positions, sizes.hidden)
    return call(
        functools.partial(mlp_kernel, sizes.count, block),
        2 + block,
        inputs,
        4,
        [
            (sizes.local, BF16), (sizes.local, F32), (sizes.full, BF16),
            (hidden, F32), (hidden, BF16),
        ],
        (),
        [
            pltpu.VMEM(sizes.full, BF16),
            pltpu.VMEM(own["one"].shape, BF16),
            pltpu.VMEM(own["two"].shape, BF16),
        ]
        + exchange_scratch(sizes.count, *sizes.local)
        + semaphores(sizes.count),
        2 * sizes.tokens * sizes.width * sizes.hidden * 2,
        cargos,
    )


def mlp_backward(sizes, block, g, attend, mlp, mods, segs, own, other, cargos):
    out, branch, full, pre, act = mlp
    inputs = [g, attend[0], branch, mods, segs[0], full, pre, act]
    inputs += pairs(own, other, ("one", "two"))
    return call(
        functools.partial(mlp_back_kernel, sizes.count, block),
        4 + block,
        inputs,
        4,
        [
            (sizes.local, F32), (sizes.mods, F32),
            ((2,) + quarter((sizes.width, sizes.hidden)), BF16),
            ((2,) + quarter((sizes.width, sizes.hidden)), BF16),
            ((1, sizes.hidden), F32), ((1, sizes.width), F32),
        ],
        (),
        [
            pltpu.VMEM(sizes.full, BF16),
            pltpu.VMEM((sizes.rows, sizes.positions, sizes.hidden), BF16),
            pltpu.VMEM(own["one"].shape, BF16),
            pltpu.VMEM(own["two"].shape, BF16),
        ]
        + exchange_scratch(sizes.count, *sizes.local)
        + semaphores(sizes.count)
        + core_sum_scratch((sizes.width, sizes.hidden)) * 2,
        2 * sizes.tokens * sizes.width * sizes.hidden * 4,
        cargos,
    )


def attend_backward(sizes, block, d_middle, u, attend, mods, segs, own, other, cargos):
    middle, branch, full, q, k, v, probs, mixed = attend
    inputs = [d_middle, u, branch, mods, segs[0], full, q, k, v, probs, mixed]
    inputs += pairs(own, other, ("qkv", "out"))
    return call(
        functools.partial(attend_back_kernel, sizes.count, block),
        6 + block,
        inputs,
        4,
        [
            (sizes.local, F32), (sizes.mods, F32),
            ((2,) + quarter((sizes.width, 3 * sizes.heads_width)), BF16),
            ((2,) + quarter((sizes.width, sizes.heads_width)), BF16),
            ((1, 3 * sizes.heads_width), F32), ((1, sizes.width), F32),
        ],
        (),
        [
            pltpu.VMEM(sizes.full, BF16),
            pltpu.VMEM((4,) + sizes.wide, BF16),
            pltpu.VMEM((sizes.rows, sizes.positions, 3 * sizes.heads_width), BF16),
            pltpu.VMEM(own["qkv"].shape, BF16),
            pltpu.VMEM(own["out"].shape, BF16),
        ]
        + exchange_scratch(sizes.count, *sizes.local)
        + semaphores(sizes.count)
        + core_sum_scratch((sizes.width, 3 * sizes.heads_width))
        + core_sum_scratch((sizes.width, sizes.heads_width)),
        2 * sizes.tokens * sizes.width * sizes.heads_width * 8,
        cargos,
    )


def project(sizes, sent, weights, targets, biases, p2_b, token_count):
    tokens = sizes.rows * sizes.length
    p1, p2, p3 = weights
    lane, hidden = p1.shape[2], p2.shape[2]
    inputs = [sent, targets, biases, p2_b, p1, p2, p3]
    results, unused = call(
        functools.partial(project_kernel, token_count),
        9,
        inputs,
        3,
        [
            (sizes.local, F32), (p1.shape, BF16), (p2.shape, BF16), (p3.shape, BF16),
            ((sizes.count, MOD_ROWS, lane), F32),
        ],
        (),
        [
            pltpu.VMEM(p1.shape, BF16),
            pltpu.VMEM(p2.shape, BF16),
            pltpu.VMEM(p3.shape, BF16),
            pltpu.VMEM((2, tokens, sizes.width), BF16),
            pltpu.VMEM((2, 2 * tokens, lane), F32),
            pltpu.VMEM((2, 2 * tokens, lane), BF16),
            pltpu.VMEM((tokens, hidden), F32),
            pltpu.VMEM((2, tokens, hidden), BF16),
            pltpu.VMEM((2, tokens, hidden), BF16),
            pltpu.VMEM((2, 2 * tokens, HEAD_LANES), F32),
            pltpu.VMEM((2, tokens, hidden), BF16),
            pltpu.VMEM((2, tokens, hidden), BF16),
            pltpu.VMEM((2, tokens, sizes.width), BF16),
            pltpu.VMEM((2, 2 * tokens, lane), BF16),
            pltpu.SemaphoreType.DMA((3,)),
            pltpu.SemaphoreType.DMA((7,)),
            pltpu.SemaphoreType.DMA((7,)),
        ],
        12 * tokens * sum(math.prod(one.shape) for one in weights),
    )
    return results


def close_backward(sizes, grads, mod_grads, small, proj_small, cond, sections, replicas, cargos):
    count, width = sizes.count, sizes.width
    piece = 6 * width // count
    share = width // replicas
    inputs = [*grads, *mod_grads, *small, proj_small, cond]
    copies = 2 * count + 4 * (sections * replicas - 1)
    both = (sections * sizes.rows,) + sizes.local[1:]
    return call(
        functools.partial(close_kernel, count, sections, replicas),
        8,
        inputs,
        0,
        [
            (both, F32), ((share, piece), F32), ((1, piece), F32),
            ((MOD_ROWS, width), F32), (proj_small.shape[1:], F32),
        ],
        (),
        [
            pltpu.VMEM((count, sections, MOD_ROWS, piece), F32),
            pltpu.VMEM((count - 1, sections, MOD_ROWS, piece), F32),
            pltpu.VMEM((sections, MOD_ROWS, piece), F32),
            pltpu.VMEM((sections, replicas, MOD_ROWS, piece), F32),
            pltpu.VMEM((sections, MOD_ROWS, width), F32),
            pltpu.VMEM((sections, replicas, MOD_ROWS, width), F32),
            pltpu.VMEM((sections, replicas, MOD_ROWS, share), F32),
            pltpu.VMEM(sizes.local, BF16),
            pltpu.VMEM(sizes.local, BF16),
            pltpu.VMEM((count - 1,) + proj_small.shape[1:], F32),
            pltpu.VMEM(proj_small.shape[1:], F32),
            pltpu.VMEM((sections, replicas) + proj_small.shape[1:], F32),
            pltpu.SemaphoreType.DMA((copies,)),
            pltpu.SemaphoreType.DMA((copies,)),
        ],
        2 * sections * replicas * MOD_ROWS * share * piece,
        cargos,
    )


def assemble_kernel(heads_width, *refs):
    fc1, fc2 = refs[0:2], refs[2:4]
    alone, (qkv, wo) = refs[4:9], (refs[9:11], refs[11:13])
    grad_ref, small, proj = refs[13:16]
    outs, sems = refs[16:-1], refs[-1]
    is_first = lax.axis_index("section") == 0
    waits = []
    for i, pair in enumerate((fc1, fc2)):
        waits.append(pltpu.make_async_copy(pair[0], outs[i], sems.at[i]))

        @pl.when(is_first)
        def take_one(pair=pair, i=i):
            pltpu.make_async_copy(pair[0], outs[i], sems.at[i]).start()

        @pl.when(jnp.logical_not(is_first))
        def take_two(pair=pair, i=i):
            pltpu.make_async_copy(pair[1], outs[i], sems.at[i]).start()

    for i, one in enumerate(alone):
        waits.append(local(one, outs[2 + i], sems.at[2 + i]))
    grad_out, qkv_out, wo_out, qv_b, out_b, fc1_b, fc2_b, p1_b, p2_b, p3_b, loss = outs[7:]
    for row in range(grad_ref.shape[0]):
        grad_out[:, row, :] = grad_ref[row]
    qkv_own = jnp.where(is_first, qkv[0][...], qkv[1][...])
    for which in range(3):
        qkv_out[which] = qkv_own[:, which * heads_width : (which + 1) * heads_width]
    wo_out[...] = jnp.where(is_first, wo[0][...], wo[1][...]).T
    qv_b[0:1, :] = small[0:1, :heads_width]
    qv_b[1:2, :] = small[0:1, 2 * heads_width : 3 * heads_width]
    out_b[...] = small[2:3, :]
    fc1_b[...] = small[3:4, :]
    fc2_b[...] = small[4:5, :]
    p1_b[...] = proj[0:1, :]
    p2_b[...] = jnp.concatenate([proj[2 + row : 3 + row, :] for row in range(4)], axis=1)
    p3_b[...] = proj[1:2, : p3_b.shape[1]]
    loss[...] = proj[6:7, :HEAD_LANES]
    wait_all(waits)


def assemble(choices, alone, section_grad, small, proj_small, heads_width):
    (fc1, fc2, qkv, wo) = choices
    inputs = [*fc1, *fc2, *alone, *qkv, *wo, section_grad, small, proj_small]
    both, length, width = section_grad.shape
    share, lane = fc1[0].shape[0], proj_small.shape[1]
    third = alone[4].shape[0]
    shapes = [fc1[0].shape, fc2[0].shape] + [one.shape for one in alone] + [
        (length, both, width), (3, share, heads_width), wo[0].shape[::-1], (2, heads_width),
        (1, width), (1, width), (1, width), (1, lane), (1, 4 * lane), (1, third), (1, HEAD_LANES),
    ]
    return pl.pallas_call(
        functools.partial(assemble_kernel, heads_width),
        out_shape=[jax.ShapeDtypeStruct(shape, F32) for shape in shapes],
        in_specs=[ANY] * 9 + [VMEM] * 7,
        out_specs=[ANY] * 7 + [VMEM] * 11,
        scratch_shapes=[pltpu.SemaphoreType.DMA((7,))],
        compiler_params=pltpu.CompilerParams(vmem_limit_bytes=40 * 2**20),
        cost_estimate=pl.CostEstimate(flops=1000, bytes_accessed=2**24, transcendentals=0),
    )(*inputs)


def halve(value, axis, bit, position):
    size = lax.axis_size(axis)
    mine = (lax.axis_index(axis) & bit) // bit
    keep = lax.dynamic_index_in_dim(value, mine, position, keepdims=False)
    give = lax.dynamic_index_in_dim(value, 1 - mine, position, keepdims=False)
    return keep + lax.ppermute(give, axis, [(i, i ^ bit) for i in range(size)])


def sum_beyond_quads(value):
    size = lax.axis_size("dp")
    if size == 4:
        return value
    quads = size // 4
    bits = quads.bit_length() - 1
    lead = value.ndim - 2
    shape = value.shape
    value = value.reshape(shape[:lead] + (2,) * bits + (shape[-2] // quads, shape[-1]))
    for bit in range(bits):
        value = halve(value, "dp", 4 << bit, lead + bits - 1 - bit)
    route = [(high * 4 + low, low * quads + high) for high in range(quads) for low in range(4)]
    return lax.ppermute(value, "dp", route)


def per_device(
    block_eight_input,
    cond,
    image_slot_index,
    targets,
    cot,
    ada_w,
    ada_b,
    query_key_value_weight,
    query_value_bias,
    attention_output_weight,
    attention_output_bias,
    hidden_weight,
    hidden_bias,
    output_weight_mlp,
    output_bias_mlp,
    p1_w,
    p1_b,
    p2_w,
    p2_b,
    p3_w,
    p3_b,
):
    section = lax.axis_index("section")
    tensor = lax.axis_index("tensor")
    is_first = section == 0
    count = lax.axis_size("tensor")
    sections = lax.axis_size("section")
    replicas = lax.axis_size("dp")
    length, replica_rows, width = block_eight_input.shape
    positions = length * count
    rows = replica_rows // sections
    total_token_count = positions * replica_rows * replicas
    heads_width = attention_output_weight.shape[1]
    hidden = hidden_weight.shape[2]

    def my_rows(value, axis):
        return lax.dynamic_slice_in_dim(value, section * rows, rows, axis)

    def to_rows(value):
        return jnp.transpose(my_rows(value, 1), (1, 0, 2))

    own = {
        "qkv": query_key_value_weight[0].reshape(width, 3 * heads_width),
        "out": attention_output_weight[0],
        "one": hidden_weight[0],
        "two": output_weight_mlp[0],
    }

    def padded(value):
        return jnp.pad(value.astype(F32), ((0, 0), (0, width - value.shape[-1])))

    biases = jnp.concatenate(
        [
            padded(
                jnp.concatenate(
                    [
                        query_value_bias[0, 0:1], jnp.zeros((1, heads_width), BF16),
                        query_value_bias[0, 1:2],
                    ],
                    axis=1,
                )
            ),
            jnp.zeros((1, width), F32), padded(attention_output_bias), padded(hidden_bias),
            padded(output_bias_mlp), jnp.zeros((MOD_ROWS - 5, width), F32),
        ],
        axis=0,
    )
    used = rows * IMAGES_PER_ROW
    cond_pad = jnp.pad(
        cond.reshape(sections, used, width), ((0, 0), (0, MOD_ROWS - used), (0, 0))
    )
    segs_full = my_rows(image_slot_index, 0)
    seg_own = lax.dynamic_slice_in_dim(segs_full, tensor * length, length, 1)
    segs = (seg_own[:, :, None], segs_full[:, :, None], segs_full[:, None, :])

    target_parts = my_rows(targets, 1).reshape(count, length, rows, targets.shape[2])
    target_parts = jnp.transpose(target_parts, (0, 2, 1, 3))
    lane = p1_b.shape[0]
    proj_biases = jnp.concatenate(
        [
            p1_b.astype(F32)[None],
            jnp.pad(p3_b.astype(F32), (0, lane - p3_b.shape[0]))[None],
            jnp.zeros((MOD_ROWS - 2, lane), F32),
        ],
        axis=0,
    )
    gather = ColumnGather((p1_w, p2_w, p3_w.T), PROJECTOR_AXES, target_parts, proj_biases)

    u = to_rows(block_eight_input)
    sizes = Shapes(u, own, count)
    mods, bias_all, other, attend_one, carried = open_forward(
        sizes, u, cond_pad.reshape(-1, width), ada_w[0].T, ada_b, biases, segs, own, sections,
        (gather,),
    )
    *proj_weights, target_all, proj_bias_all = carried[0]
    mlp_one, carried = mlp_forward(
        sizes, 0, attend_one[0], mods, bias_all, segs, own, other,
        (ShareAlong(proj_weights, PROJECTOR_AXES, 0),),
    )
    proj_weights = carried[0]
    first_out = mlp_one[0]
    attend_two, carried = attend_forward(
        sizes, 1, first_out, mods, bias_all, segs, own, other, (ShareAlong(proj_weights, PROJECTOR_AXES, 1),)
    )
    proj_weights = carried[0]
    mlp_two, carried = mlp_forward(
        sizes, 1, attend_two[0], mods, bias_all, segs, own, other, (ShareAlong(proj_weights, PROJECTOR_AXES, 2),)
    )
    proj_weights = carried[0]
    second_out = mlp_two[0]

    grad_sent, grad_p1, grad_p2, grad_p3, proj_small = project(
        sizes, first_out, proj_weights, target_all, proj_bias_all, p2_b[None], total_token_count
    )

    back = (mods, segs, own, other)
    (d_middle_two, mod_mlp_two, *mlp_grads_two), carried = mlp_backward(
        sizes, 1, to_rows(cot), attend_two, mlp_two, *back,
        [Swap(first_out, second_out), HalfSum(grad_p1, 0, "x")],
    )
    (other_out,), (grad_p1,) = carried
    (second_grad, mod_attend_two, *attend_grads_two), carried = attend_backward(
        sizes, 1, d_middle_two, first_out, attend_two, *back,
        [YSum(grad, BF16) for grad in mlp_grads_two[:2]]
        + [HalfSum(grad_p2, 1, "x", (0, 1)), HalfSum(grad_p3, 1, "x")],
    )
    ((mlp_part_a,), (mlp_part_b,)), ((grad_p2_a,), (grad_p3,)) = carried[:2], carried[2:]
    (d_middle_one, mod_mlp_one, *mlp_grads_one), carried = mlp_backward(
        sizes, 0, second_grad + grad_sent, attend_one, mlp_one, *back,
        [YSum(grad, BF16) for grad in attend_grads_two[:2]]
        + [SectionSum(mlp_part_a, 1), HalfSum(grad_p2, 1, "x", (1, 1))]
        + [HalfSum(grad_p1, 0, "y"), HalfSum(grad_p2_a, 1, "y")],
    )
    attend_parts_two, sum_mlp_a = carried[:2], carried[2]
    (grad_p2_b,), (grad_p1,), (grad_p2_a,) = carried[3:]
    (first_grad, mod_attend_one, *attend_grads_one), carried = attend_backward(
        sizes, 0, d_middle_one, u, attend_one, *back,
        [LastSum(mlp_grads_one[0], 0), SectionSum(mlp_grads_one[1], 0, BF16)]
        + [SectionSum(part, 1) for part, in attend_parts_two]
        + [SectionSum(mlp_part_b, 1), HalfSum(grad_p2_b, 1, "y"), HalfSum(grad_p3, 1, "y")]
        + [ColumnSum((grad_p1,), 0)],
    )
    sum_mlp_c, (mlp_part_two,), sums_attend_two = carried[0], carried[1], carried[2:4]
    sums_mlp_two, ((grad_p2_b,), (grad_p3,), (red_p1_w,)) = (sum_mlp_a, carried[4]), carried[5:]

    cond_act = silu(my_rows(cond, 0).astype(F32)).astype(BF16).astype(F32)
    share = width // replicas
    cond_cols = jnp.pad(cond_act.reshape(used, width), ((0, MOD_ROWS - used), (0, 0)))
    cond_cols = jnp.transpose(cond_cols.reshape(MOD_ROWS, replicas, share), (1, 0, 2))
    small = [
        attend_grads_one[2], attend_grads_one[3], mlp_grads_one[2], mlp_grads_one[3],
        attend_grads_two[2], attend_grads_two[3], mlp_grads_two[2], mlp_grads_two[3],
    ]
    (section_grad, grad_ada_w, grad_ada_b, small, proj_small), carried = close_backward(
        sizes, (first_grad, second_grad),
        (mod_attend_one, mod_mlp_one, mod_attend_two, mod_mlp_two),
        small, proj_small, cond_cols, sections, replicas,
        [LastSum(grad, 0) for grad in attend_grads_one[:2]]
        + [YSum(mlp_part_two, F32)]
        + [ColumnSum((grad_p2_a, grad_p2_b), 1), ColumnSum((grad_p3,), 1)],
    )
    sums_attend_one, sums_mlp_one = carried[:2], (sum_mlp_c, carried[2])
    (red_p2_w,), (red_p3_w,) = carried[3:]

    own_out = jnp.where(is_first, first_out, second_out)
    section_out = jnp.where(
        is_first,
        jnp.concatenate([own_out, other_out], axis=0),
        jnp.concatenate([other_out, own_out], axis=0),
    )
    section_out = jnp.transpose(section_out, (1, 0, 2))[None]
    choices = [
        (one[0], two[0])
        for one, two in zip(
            list(sums_mlp_one) + list(sums_attend_one), list(sums_mlp_two) + list(sums_attend_two)
        )
    ]
    if replicas == 4:
        alone = [grad_ada_w, grad_ada_b, red_p1_w, red_p2_w, red_p3_w]
        final = assemble(choices, alone, section_grad, small, proj_small, heads_width)
        red_fc1, red_fc2, grad_ada_w, grad_ada_b, red_p1_w, red_p2_w, red_p3_w = final[:7]
        section_grad, red_qkv, red_out, qv_b, out_b, fc1_b, fc2_b, p1_sum, p2_sum, p3_sum, loss = (
            final[7:]
        )
        red_p1_b, red_p2_b, red_p3_b = p1_sum[0], p2_sum[0], p3_sum[0]
        loss_total = loss[0, 0]
    else:
        red_fc1, red_fc2, red_qkv, red_out = [
            sum_beyond_quads(jnp.where(is_first, one, two)) for one, two in choices
        ]
        red_qkv = jnp.transpose(red_qkv.reshape(-1, 3, heads_width), (1, 0, 2))
        red_out = red_out.T
        red_p1_w = sum_beyond_quads(red_p1_w)
        red_p2_w, red_p3_w = sum_beyond_quads(red_p2_w.T).T, sum_beyond_quads(red_p3_w.T).T
        section_grad = jnp.transpose(section_grad, (1, 0, 2))
        qv_b = jnp.stack([small[0, :heads_width], small[0, 2 * heads_width : 3 * heads_width]])
        out_b, fc1_b, fc2_b = small[2:3], small[3:4], small[4:5]
        red_p1_b, red_p2_b = proj_small[0], proj_small[2:6].reshape(-1)
        red_p3_b, loss_total = proj_small[1, : p3_b.shape[0]], proj_small[6, 0]
    align_loss = -0.5 * loss_total / total_token_count
    return (
        section_out,
        section_grad[None],
        align_loss,
        grad_ada_w[None],
        grad_ada_b,
        jnp.transpose(red_qkv, (1, 0, 2))[None],
        qv_b[None],
        red_out[None],
        out_b,
        red_fc1[None],
        fc1_b[:, :hidden],
        red_fc2.T[None],
        fc2_b,
        red_p1_w,
        red_p1_b,
        red_p2_w,
        red_p2_b[: p2_b.shape[0]],
        red_p3_w.T,
        red_p3_b,
    )


def solution(mesh):
    in_specs = (
        P("tensor", "dp", None),
        P("dp", None, None),
        P("dp", None),
        P(None, "dp", "tensor"),
        P("tensor", "dp", None),
        P("section", None, "tensor"),
        P("section", "tensor"),
        P("section", None, None, "tensor"),
        P("section", None, "tensor"),
        P("section", "tensor", None),
        P("section", None),
        P("section", None, "tensor"),
        P("section", "tensor"),
        P("section", "tensor", None),
        P("section", None),
        P(None, "tensor"),
        P("tensor"),
        P("tensor", None),
        P(),
        P(None, "tensor"),
        P("tensor"),
    )
    out_specs = (
        P("section", "tensor", "dp", None),
        P("section", "tensor", "dp", None),
        P(),
        P("section", "dp", "tensor"),
        P("section", "tensor"),
        P("section", "dp", None, "tensor"),
        P("section", None, "tensor"),
        P("section", "tensor", "dp"),
        P("section", None),
        P("section", "dp", "tensor"),
        P("section", "tensor"),
        P("section", "tensor", "dp"),
        P("section", None),
        P(("section", "dp"), "tensor"),
        P("tensor"),
        P("tensor", ("section", "dp")),
        P(),
        P(("section", "dp"), "tensor"),
        P("tensor"),
    )
    return jax.shard_map(
        per_device, mesh=mesh, in_specs=in_specs, out_specs=out_specs, check_vma=False
    )
```

```python
import functools
import math

import jax
import jax.numpy as jnp
from jax import lax
from jax.experimental import pallas as pl
from jax.experimental.pallas import tpu as pltpu
from jax.sharding import PartitionSpec as P

HEAD_WIDTH = 72
HEAD_LANES = 128
IMAGES_PER_ROW = 3
NORM_EPS = 1e-06
COSINE_EPS = 1e-06
MASKED_SCORE = -1e30
HIGHEST = lax.Precision.HIGHEST
MESH = pl.DeviceIdType.MESH
F32 = jnp.float32
BF16 = jnp.bfloat16
NN = (((1,), (0,)), ((), ()))
NT = (((1,), (1,)), ((), ()))
TN = (((0,), (0,)), ((), ()))


def dot(left, right, form=NN):
    return lax.dot_general(left, right, form, preferred_element_type=F32)


def z_peers(count):
    me = lax.axis_index("tensor")
    return [{"tensor": lax.rem(me + step, count)} for step in range(1, count)]


def x_peer():
    return {"section": 1 - lax.axis_index("section")}


def core_bit():
    return lax.rem(lax.axis_index("dp"), 2)


def y_bit():
    return lax.rem(lax.axis_index("dp") // 2, 2)


def core_peer():
    return {"dp": lax.axis_index("dp") + 1 - 2 * core_bit()}


def y_peer():
    return {"dp": lax.axis_index("dp") + 2 - 4 * y_bit()}


def greet(peers):
    barrier = pltpu.get_barrier_semaphore()
    for peer in peers:
        pl.semaphore_signal(barrier, inc=1, device_id=peer, device_id_type=MESH)
    pl.semaphore_wait(barrier, len(peers))


def remote(source, target, send_sem, recv_sem, peer):
    copy = describe(source, target, send_sem, recv_sem, peer)
    copy.start()
    return copy


def local(source, target, sem):
    copy = pltpu.make_async_copy(source, target, sem)
    copy.start()
    return copy


def own_rows(me, length):
    return pl.ds(pl.multiple_of(me * length, 16), length)


def describe(source, target, send_sem, recv_sem, peer):
    return pltpu.make_async_remote_copy(
        src_ref=source,
        dst_ref=target,
        send_sem=send_sem,
        recv_sem=recv_sem,
        device_id=peer,
        device_id_type=MESH,
    )


def wait_all(copies):
    for copy in copies:
        copy.wait()


class Line:
    def __init__(self, length, sems):
        self.length, (self.ag_send, self.ag_recv, self.rs_send, self.rs_recv) = length, sems
        self.me = lax.axis_index("tensor")
        self.mirror = 3 - self.me
        self.near = self.me + 1 - 2 * lax.rem(self.me, 2)
        self.opposite = lax.rem(self.me + 2, 4)
        self.is_end = jnp.logical_or(self.me == 0, self.me == 3)
        self.is_middle = jnp.logical_not(self.is_end)

    def block(self, full, place, which, peer):
        part = full.at[:, own_rows(place, self.length)]
        return describe(
            part, part, self.ag_send.at[which], self.ag_recv.at[place], {"tensor": peer}
        )

    def start_gather(self, full):
        self.block(full, self.me, 0, self.opposite).start()
        self.block(full, self.me, 1, self.near).start()

        @pl.when(self.is_middle)
        def to_mirror():
            self.block(full, self.me, 2, self.mirror).start()

    def relay(self, full):
        self.block(full, self.opposite, 2, self.mirror).wait_recv()

        @pl.when(self.is_middle)
        def pass_on():
            self.block(full, self.opposite, 3, 3 - self.opposite).start()

    def arrived(self, full, place):
        self.block(full, place, 1, self.near).wait_recv()

    def finish_gather(self, full):
        self.arrived(full, self.near)
        self.arrived(full, self.mirror)
        self.sent(full)

    def sent(self, full):
        self.block(full, self.me, 0, self.opposite).wait_send()
        self.block(full, self.me, 1, self.near).wait_send()

        @pl.when(self.is_middle)
        def more_sent():
            self.block(full, self.me, 2, self.mirror).wait_send()
            self.block(full, self.opposite, 3, 3 - self.opposite).wait_send()

    def scatter_sum(self, partial, buffers, prepare=lambda place: None):
        send_buf, recv_buf, relay_buf = buffers
        me, relay_sem = self.me, 4

        def term(peer):
            return partial(own_rows(peer, self.length))

        def keep(which, value):
            send_buf[which] = value.astype(BF16).reshape(send_buf.shape[1:])

        self.to_mirror = describe(
            send_buf.at[0], recv_buf.at[me], self.rs_send.at[0], self.rs_recv.at[me],
            {"tensor": self.mirror},
        )
        self.to_relay = describe(
            send_buf.at[0], relay_buf, self.rs_send.at[0], self.rs_recv.at[relay_sem],
            {"tensor": self.near},
        )
        self.to_near = describe(
            send_buf.at[1], recv_buf.at[me], self.rs_send.at[1], self.rs_recv.at[me],
            {"tensor": self.near},
        )
        self.to_opposite = describe(
            send_buf.at[2], recv_buf.at[me], self.rs_send.at[2], self.rs_recv.at[me],
            {"tensor": self.opposite},
        )
        prepare(self.mirror)
        keep(0, term(self.mirror))

        @pl.when(self.is_end)
        def first_end():
            self.to_relay.start()
            relay_buf[...] = jnp.zeros_like(relay_buf)
            recv_buf[self.mirror] = jnp.zeros(recv_buf.shape[1:], BF16)

        @pl.when(self.is_middle)
        def first_middle():
            self.to_mirror.start()

        prepare(self.near)
        keep(1, term(self.near))
        self.to_near.start()
        last = term(self.opposite)

        @pl.when(self.is_middle)
        def relayed():
            self.to_relay.wait_recv()

        keep(2, last + relay_buf[...].reshape(last.shape).astype(F32))
        self.to_opposite.start()
        return term(me)

    def finish_sum(self, total, buffers):
        send_buf, recv_buf, relay_buf = buffers

        def got(source):
            describe(
                send_buf.at[1], recv_buf.at[source], self.rs_send.at[1], self.rs_recv.at[source],
                {"tensor": self.near},
            ).wait_recv()

        got(self.near)
        got(self.opposite)

        @pl.when(self.is_middle)
        def third():
            got(self.mirror)

        self.to_near.wait_send()
        self.to_opposite.wait_send()
        self.to_mirror.wait_send()
        for source in (self.near, self.opposite, self.mirror):
            total = total + recv_buf[source].reshape(total.shape).astype(F32)
        return total


def fetch(block, own_ref, other_ref, target, sem):
    mine = lax.axis_index("section") == block

    @pl.when(mine)
    def own_start():
        pltpu.make_async_copy(own_ref, target, sem).start()

    @pl.when(jnp.logical_not(mine))
    def other_start():
        pltpu.make_async_copy(other_ref, target, sem).start()

    return pltpu.make_async_copy(own_ref, target, sem)


def layer_norm(rows):
    centred = rows - jnp.mean(rows, axis=-1, keepdims=True)
    inverse = lax.rsqrt(jnp.mean(centred * centred, axis=-1, keepdims=True) + NORM_EPS)
    return centred * inverse, inverse


def norm_back(grad, normed, inverse):
    mean_grad = jnp.mean(grad, axis=-1, keepdims=True)
    mean_cross = jnp.mean(grad * normed, axis=-1, keepdims=True)
    return inverse * (grad - mean_grad - normed * mean_cross)


def token_mod(mod_ref, seg_ref, which):
    parts = []
    for row in range(seg_ref.shape[0]):
        seg = seg_ref[row]
        line = [
            mod_ref[which, pl.ds(row * IMAGES_PER_ROW + slot, 1), :]
            for slot in range(IMAGES_PER_ROW)
        ]
        value = line[-1]
        for slot in range(IMAGES_PER_ROW - 2, -1, -1):
            value = jnp.where(seg == slot, line[slot], value)
        parts.append(value)
    return jnp.concatenate(parts, axis=0)


def slot_sums(value, seg_ref, out_ref, which):
    length = seg_ref.shape[1]
    lines = []
    for row in range(seg_ref.shape[0]):
        seg = seg_ref[row]
        piece = value[row * length : (row + 1) * length]
        for slot in range(IMAGES_PER_ROW):
            lines.append(jnp.sum(jnp.where(seg == slot, piece, 0.0), axis=0, keepdims=True))
    spare = out_ref.shape[1] - len(lines)
    lines.append(jnp.zeros((spare, value.shape[1]), F32))
    out_ref[which] = jnp.concatenate(lines, axis=0)


def flat(ref):
    return ref[...].reshape(-1, ref.shape[-1])


def spread_matrix(width, which=0, total=None):
    lanes = width // HEAD_WIDTH * HEAD_LANES
    shape = (total or width, lanes)
    source = lax.broadcasted_iota(jnp.int32, shape, 0)
    target = lax.broadcasted_iota(jnp.int32, shape, 1)
    within = target & (HEAD_LANES - 1)
    head = target >> (HEAD_LANES.bit_length() - 1)
    hit = (within < HEAD_WIDTH) & (source == which * width + head * HEAD_WIDTH + within)
    return jnp.where(hit, 1.0, 0.0).astype(BF16)


def gelu_tanh(pre):
    inner = math.sqrt(2.0 / math.pi) * (pre + 0.044715 * (pre * pre * pre))
    return 0.5 * pre * (1.0 + jnp.tanh(inner))


def gelu_slope(pre):
    scale = math.sqrt(2.0 / math.pi)
    square = pre * pre
    tanh = jnp.tanh(scale * (pre + 0.044715 * (pre * square)))
    return 0.5 * (1.0 + tanh) + 0.5 * pre * (1.0 - tanh * tanh) * scale * (
        1.0 + 3 * 0.044715 * square
    )


def silu(value):
    return value / (1.0 + jnp.exp(-value))


class Share:
    def __init__(self, own, other, parts, sems):
        self.own, self.other, self.parts = own, other, parts
        self.send, self.recv = sems
        self.size = own.shape[0] // parts
        self.copies = []

    def rows(self, core, y):
        part = core if self.parts == 2 else core + 2 * y
        return pl.ds(pl.multiple_of(part * self.size, 16), self.size)

    def begin(self):
        rows = self.rows(core_bit(), y_bit())
        self.first = remote(
            self.own.at[rows], self.other.at[rows], self.send.at[0], self.recv.at[0], x_peer()
        )

    def forward(self, first):
        if first is not None:
            first.wait()
        mine = self.other.at[self.rows(core_bit(), y_bit())]
        self.copies.append(remote(mine, mine, self.send.at[1], self.recv.at[1], core_peer()))
        if self.parts == 4:
            self.second = remote(mine, mine, self.send.at[2], self.recv.at[2], y_peer())

    def forward_again(self):
        if self.parts == 4:
            self.second.wait()
            got = self.other.at[self.rows(core_bit(), 1 - y_bit())]
            self.copies.append(remote(got, got, self.send.at[3], self.recv.at[3], core_peer()))

    def finish(self):
        wait_all(self.copies)


class Cargo:
    inputs, outs, scratch, aliases, any_outs = (), (), (), {}, False

    def bind(self, inputs, outs, scratch):
        self.ins, self.out_refs, self.held = inputs, outs, scratch

    def peers(self):
        return []

    def begin(self):
        pass

    def middle(self):
        pass

    def late(self):
        pass

    def end(self):
        pass


def quarter(shape):
    return shape[:-2] + (shape[-2] // 4, shape[-1])


class CoreSum:
    def __init__(self, whole, got, out, sems):
        self.whole, self.got, self.out, self.sems = whole, got, out, sems
        self.size = whole.shape[-2] // 4

    def rows(self, core, y):
        part = pl.ds(pl.multiple_of((core + 2 * y) * self.size, 16), self.size)
        whole = self.whole
        return whole.at[:, part] if len(whole.shape) == 3 else whole.at[part]

    def begin(self):
        self.copies = [
            remote(
                self.rows(1 - core_bit(), y), self.got.at[y],
                self.sems.at[0, y], self.sems.at[1, y], core_peer(),
            )
            for y in range(2)
        ]

    def end(self):
        wait_all(self.copies)
        for y in range(2):
            mine = self.rows(core_bit(), y)[...]
            self.out[y] = (mine.astype(F32) + self.got[y].astype(F32)).astype(BF16)


def core_sum_scratch(shape):
    return [
        pltpu.VMEM(shape, BF16),
        pltpu.VMEM((2,) + quarter(shape), BF16),
        pltpu.SemaphoreType.DMA((2, 2)),
    ]


class YSum(Cargo):
    def __init__(self, parts, dtype):
        part = parts.shape[1:]
        self.inputs = (parts,)
        self.outs = ((part, dtype),)
        self.scratch = (
            pltpu.VMEM(part, BF16),
            pltpu.VMEM(part, BF16),
            pltpu.SemaphoreType.DMA((3,)),
        )

    def peers(self):
        return ["y"]

    def begin(self):
        mine, other, sems = self.held
        self.copies = [
            remote(self.ins[0].at[1 - y_bit()], other, sems.at[0], sems.at[1], y_peer()),
            local(self.ins[0].at[y_bit()], mine, sems.at[2]),
        ]

    def end(self):
        mine, other, sems = self.held
        out = self.out_refs[0]
        wait_all(self.copies)
        out[...] = (mine[...].astype(F32) + other[...].astype(F32)).astype(out.dtype)


class SectionSum(Cargo):
    def __init__(self, part, owner, dtype=F32):
        self.owner = owner
        self.inputs = (part,)
        self.outs = ((part.shape, dtype),)
        self.scratch = (
            pltpu.VMEM(part.shape, BF16),
            pltpu.VMEM(part.shape, BF16),
            pltpu.SemaphoreType.DMA((3,)),
        )

    def peers(self):
        return ["x"]

    def source(self):
        return self.ins[0]

    def begin(self):
        mine, other, sems = self.held
        self.copy = describe(self.source(), other, sems.at[0], sems.at[1], x_peer())
        self.load = pltpu.make_async_copy(self.source(), mine, sems.at[2])
        is_owner = lax.axis_index("section") == self.owner

        @pl.when(is_owner)
        def take():
            self.load.start()

        @pl.when(jnp.logical_not(is_owner))
        def give():
            self.copy.start()

    def end(self):
        mine, other, sems = self.held
        is_owner = lax.axis_index("section") == self.owner

        @pl.when(is_owner)
        def add():
            self.load.wait()
            self.copy.wait_recv()
            out = self.out_refs[0]
            out[...] = (mine[...].astype(F32) + other[...].astype(F32)).astype(out.dtype)

        @pl.when(jnp.logical_not(is_owner))
        def given():
            self.copy.wait_send()
            self.out_refs[0][...] = jnp.zeros_like(self.out_refs[0])


class LastSum(YSum):
    def __init__(self, parts, owner):
        super().__init__(parts, F32)
        part = parts.shape[1:]
        self.owner = owner
        self.scratch = self.scratch + (
            pltpu.VMEM(part, BF16),
            pltpu.VMEM(part, BF16),
            pltpu.SemaphoreType.DMA((2,)),
        )

    def peers(self):
        return ["y", "x"]

    def begin(self):
        self.held, self.last = self.held[:3], self.held[3:]
        super().begin()

    def middle(self):
        mine, other, sems = self.held
        total, got, last_sems = self.last
        wait_all(self.copies)
        total[...] = (mine[...].astype(F32) + other[...].astype(F32)).astype(BF16)
        self.copy = describe(total, got, last_sems.at[0], last_sems.at[1], x_peer())

        @pl.when(lax.axis_index("section") != self.owner)
        def give():
            self.copy.start()

    def end(self):
        total, got, last_sems = self.last
        is_owner = lax.axis_index("section") == self.owner

        @pl.when(is_owner)
        def add():
            self.copy.wait_recv()
            self.out_refs[0][...] = total[...].astype(F32) + got[...].astype(F32)

        @pl.when(jnp.logical_not(is_owner))
        def given():
            self.copy.wait_send()
            self.out_refs[0][...] = jnp.zeros_like(self.out_refs[0])


class Swap(Cargo):
    def __init__(self, one, two):
        self.inputs = (one, two)
        self.outs = ((one.shape, one.dtype),)
        self.scratch = (pltpu.VMEM(one.shape, one.dtype), pltpu.SemaphoreType.DMA((2,)))

    def peers(self):
        return ["x"]

    def begin(self):
        got, sems = self.held
        one, two = self.ins
        self.copy = describe(two, got, sems.at[0], sems.at[1], x_peer())
        is_first = lax.axis_index("section") == 0

        @pl.when(is_first)
        def give_two():
            self.copy.start()

        @pl.when(jnp.logical_not(is_first))
        def give_one():
            describe(one, got, sems.at[0], sems.at[1], x_peer()).start()

    def end(self):
        self.copy.wait()
        self.out_refs[0][...] = self.held[0][...]


def span(ref, axis, start, size):
    part = pl.ds(pl.multiple_of(start, 128 if axis == 1 else 16), size)
    lead = (slice(None),) * (len(ref.shape) - 2)
    return ref.at[lead + ((slice(None), part) if axis == 1 else (part, slice(None)))]


def cut(shape, axis, by):
    shape = list(shape)
    shape[axis - 2] //= by
    return tuple(shape)


class HalfSum(Cargo):
    def __init__(self, grad, axis, name, slots=None):
        self.slots = slots if slots is not None else (0, grad.shape[0])
        part = cut((self.slots[1],) + grad.shape[1:], axis, 2)
        self.axis, self.name, self.size = axis, name, part[axis - 2]
        self.inputs = (grad,)
        self.outs = ((part, BF16),)
        self.scratch = (
            pltpu.VMEM(part, BF16),
            pltpu.VMEM(part, BF16),
            pltpu.SemaphoreType.DMA((3,)),
        )

    def peers(self):
        return [self.name]

    def begin(self):
        mine, other, sems = self.held
        if self.name == "x":
            bit, peer = lax.axis_index("section"), x_peer()
        else:
            bit, peer = y_bit(), y_peer()
        grad = self.ins[0].at[pl.ds(*self.slots)]
        self.copies = [
            remote(
                span(grad, self.axis, (1 - bit) * self.size, self.size), other,
                sems.at[0], sems.at[1], peer,
            ),
            local(span(grad, self.axis, bit * self.size, self.size), mine, sems.at[2]),
        ]

    def end(self):
        mine, other, sems = self.held
        wait_all(self.copies)
        self.out_refs[0][...] = (mine[...].astype(F32) + other[...].astype(F32)).astype(BF16)


class ColumnGather(Cargo):
    any_outs = True

    def __init__(self, weights, axes, targets, biases):
        self.axes = axes
        self.inputs = (*weights, targets, biases)
        self.outs = tuple(((2,) + one.shape, BF16) for one in weights) + (
            ((2, 2) + targets.shape[1:], BF16),
            ((2, 2) + biases.shape, F32),
        )
        self.scratch = (
            pltpu.SemaphoreType.DMA((5, 6)),
            pltpu.SemaphoreType.DMA((5, 2, 2)),
            pltpu.SemaphoreType.DMA((5,)),
        )

    def peers(self):
        return ["core", "cross"]

    def pieces(self, target):
        tensor, core = lax.axis_index("tensor"), core_bit()
        eighth = lax.axis_index("section") * 4 + y_bit() * 2 + core
        slot, out = lax.rem(tensor, 2), []
        for source, place, axis in zip(self.ins[:3], self.out_refs[:3], self.axes):
            size = source.shape[axis] // 8
            out.append(
                (
                    span(source, axis, eighth * size, size),
                    span(place.at[slot], axis, eighth * size, size),
                )
            )
        out.append((self.ins[3].at[target], self.out_refs[3].at[slot, core]))
        out.append((self.ins[4], self.out_refs[4].at[slot, core]))
        return out

    def copies(self, step):
        tensor, core = lax.axis_index("tensor"), core_bit()
        send, recv, own = self.held
        target = lax.rem(tensor + step, 4)
        peer = {"tensor": target, "dp": lax.axis_index("dp") - core + tensor // 2}
        return [
            describe(source, place, send.at[i, step], recv.at[i, lax.rem(tensor, 2), core], peer)
            for i, (source, place) in enumerate(self.pieces(target))
        ]

    def stays(self):
        return core_bit() == lax.axis_index("tensor") // 2

    def own_copies(self):
        own = self.held[2]
        return [
            pltpu.make_async_copy(source, place, own.at[i])
            for i, (source, place) in enumerate(self.pieces(lax.axis_index("tensor")))
        ]

    def direct(self, step, i):
        if step == 2 or i > 2:
            return None
        return lax.axis_index("tensor") != (3 if step == 1 else 0)

    def each(self, which, act):
        for step in range(1, 4):
            for i, copy in enumerate(self.copies(step)):
                if i in which:
                    allowed = self.direct(step, i)
                    if allowed is None:
                        act(copy)
                    else:

                        @pl.when(allowed)
                        def go(copy=copy):
                            act(copy)

    def start(self, which):
        self.each(which, lambda copy: copy.start())

        @pl.when(self.stays())
        def keep():
            for i, copy in enumerate(self.own_copies()):
                if i in which:
                    copy.start()

        @pl.when(jnp.logical_not(self.stays()))
        def give():
            for i, copy in enumerate(self.copies(0)):
                if i in which:
                    copy.start()

    def passes_on(self):
        tensor, core = lax.axis_index("tensor"), core_bit()
        return jnp.logical_or(
            jnp.logical_and(tensor == 2, core == 0), jnp.logical_and(tensor == 1, core == 1)
        )

    def passed(self, i, other):
        send, recv, own = self.held
        tensor, slot = lax.axis_index("tensor"), core_bit()
        size = self.ins[i].shape[self.axes[i]] // 8
        eighth = lax.axis_index("section") * 4 + y_bit() * 2 + other
        part = span(self.out_refs[i].at[slot], self.axes[i], eighth * size, size)
        return describe(
            part, part, send.at[i, 4 + other], recv.at[i, slot, other], {"tensor": 3 * (tensor - 1)}
        )

    def relay(self, which):
        @pl.when(self.passes_on())
        def pass_on():
            for i in which:
                for other in range(2):
                    copy = self.passed(i, other)
                    copy.wait_recv()
                    copy.start()

    def begin(self):
        self.start((3, 4))

    def middle(self):
        self.start((0, 2))

    def end(self):
        send, recv, own = self.held
        tensor, core = lax.axis_index("tensor"), core_bit()
        self.each(range(5), lambda copy: copy.wait_send())

        @pl.when(self.stays())
        def kept():
            for copy in self.own_copies():
                copy.wait()

        @pl.when(jnp.logical_not(self.stays()))
        def given():
            for copy in self.copies(0):
                copy.wait_send()

        @pl.when(self.passes_on())
        def passed_on():
            for i in range(3):
                for other in range(2):
                    self.passed(i, other).wait_send()

        for slot in range(2):
            for other in range(2):
                mine = jnp.logical_and(2 * core + slot == tensor, core == other)
                relayed = jnp.logical_and(self.passes_on(), core == slot)
                peer = {"tensor": lax.rem(tensor + 1, 4)}
                waits = [
                    describe(source, place, send.at[i, 1], recv.at[i, slot, other], peer)
                    for i, (source, place) in enumerate(self.pieces(tensor))
                ]

                @pl.when(jnp.logical_not(mine))
                def arrived(waits=waits):
                    for copy in waits[3:]:
                        copy.wait_recv()

                @pl.when(jnp.logical_not(jnp.logical_or(mine, relayed)))
                def weights_arrived(waits=waits):
                    for copy in waits[:3]:
                        copy.wait_recv()


class ShareAlong(Cargo):
    any_outs = True

    def __init__(self, weights, axes, stage):
        self.axes = axes
        self.inputs = tuple(weights)
        self.outs = tuple((one.shape, BF16) for one in weights)
        self.aliases = {0: 0, 1: 1, 2: 2}
        self.stage = stage
        self.scratch = (pltpu.SemaphoreType.DMA((4,)), pltpu.SemaphoreType.DMA((4,)))

    def peers(self):
        return ["x", "y"]

    def begin(self):
        send, recv = self.held
        section, y, self.copies = lax.axis_index("section"), y_bit(), []

        def give(which, start, parts, peer):
            ref, axis = self.out_refs[which], self.axes[which]
            size = ref.shape[axis + 1] // 4
            part = span(ref, axis, start * size, parts * size)
            i = len(self.copies)
            self.copies.append(remote(part, part, send.at[i], recv.at[i], peer))

        if self.stage == 0:
            give(1, 2 * section + y, 1, x_peer())
            give(0, 2 * section + y, 1, y_peer())
            give(2, 2 * section + y, 1, y_peer())
        elif self.stage == 1:
            give(0, 2 * section, 2, x_peer())
            give(1, y, 1, y_peer())
        else:
            give(2, 2 * section, 2, x_peer())
            give(1, 2 + y, 1, y_peer())

    def end(self):
        wait_all(self.copies)


class ColumnSum(Cargo):
    def __init__(self, grads, axis):
        self.axis = axis
        self.part = cut(grads[0].shape[1:], axis, 2)
        self.inputs = tuple(grads)
        self.outs = ((self.part, F32),)
        self.scratch = (
            pltpu.VMEM((4,) + self.part, BF16),
            pltpu.SemaphoreType.DMA((4,)),
            pltpu.SemaphoreType.DMA((4,)),
            pltpu.SemaphoreType.DMA,
        )

    def peers(self):
        return ["core", "cross"]

    def copy(self, slot, other):
        got, send, recv, own = self.held
        tensor, core = lax.axis_index("tensor"), core_bit()
        size = self.part[self.axis]
        ref = self.ins[0].at[slot] if len(self.ins) == 1 else self.ins[slot].at[0]
        source = span(ref, self.axis, other * size, size)
        peer = {"tensor": 2 * core + slot, "dp": lax.axis_index("dp") - core + other}
        mine = jnp.logical_and(2 * core + slot == tensor, core == other)
        away = describe(source, got.at[tensor], send.at[2 * slot + other], recv.at[tensor], peer)
        return mine, away, pltpu.make_async_copy(source, got.at[tensor], own)

    def each(self, act_away, act_own):
        for slot in range(2):
            for other in range(2):
                mine, away, own = self.copy(slot, other)

                @pl.when(mine)
                def stay(own=own):
                    act_own(own)

                @pl.when(jnp.logical_not(mine))
                def leave(away=away):
                    act_away(away)

    def begin(self):
        self.each(lambda copy: copy.start(), lambda copy: copy.start())

    def end(self):
        got, send, recv, own = self.held
        tensor, core = lax.axis_index("tensor"), core_bit()
        self.each(lambda copy: copy.wait_send(), lambda copy: copy.wait())
        for source in range(4):
            mine = jnp.logical_and(tensor == source, core == tensor // 2)

            @pl.when(jnp.logical_not(mine))
            def arrived(source=source):
                describe(
                    got.at[source], got.at[source], send.at[0], recv.at[source],
                    {"tensor": lax.rem(tensor + 1, 4)},
                ).wait_recv()

        total = got[0].astype(F32)
        for source in range(1, 4):
            total = total + got[source].astype(F32)
        self.out_refs[0][...] = total


def cross_peers():
    tensor, dp = lax.axis_index("tensor"), core_peer()["dp"]
    return [{"tensor": lax.rem(tensor + step, 4), "dp": dp} for step in range(1, 4)]


class Bundle:
    def __init__(self, cargos):
        self.cargos = cargos
        self.loads, self.stores = {}, {}

    def load(self):
        for copy in self.loads.values():
            copy.start()

    def need(self, *which):
        for i in which:
            if i in self.loads:
                self.loads[i].wait()

    def flush(self, *which):
        for i in which:
            if i in self.stores:
                self.stores[i].start()

    def peers(self, names=()):
        names = list(names) + [name for cargo in self.cargos for name in cargo.peers()]
        known = {"core": core_peer, "y": y_peer, "x": x_peer}
        cross = cross_peers() if "cross" in names else []
        return [make() for name, make in known.items() if name in names] + cross

    def begin(self):
        for cargo in self.cargos:
            cargo.begin()

    def middle(self):
        for cargo in self.cargos:
            cargo.middle()

    def late(self):
        for cargo in self.cargos:
            cargo.late()

    def end(self):
        for copy in self.stores.values():
            copy.wait()
        for cargo in self.cargos:
            cargo.end()


def attend_body(
    count, peers, u_ref, mods, segs, biases, outs, scratch, sems, need_qkv, need_out, steps, flush
):
    middle_ref, branch_ref, full_ref, q_ref, k_ref, v_ref, probs_ref, mixed_ref = outs
    full, wqkv, wo, mixed_wide = (full_ref, *scratch[:3])
    buffers, spreads = scratch[3:6], scratch[6]
    seg_own, seg_col, seg_row = segs
    mod_ref = mods()
    me = lax.axis_index("tensor")
    rows, length, width = u_ref.shape
    heads_width = wo.shape[0]
    heads = heads_width // HEAD_WIDTH
    u = flat(u_ref).astype(F32)
    normed, unused = layer_norm(u)
    attn_in = normed * (1.0 + token_mod(mod_ref, seg_own, 1)) + token_mod(mod_ref, seg_own, 0)
    full[:, own_rows(me, length), :] = attn_in.astype(BF16).reshape(rows, length, width)
    if peers is not None:
        greet(peers)
    line = Line(length, sems)
    line.start_gather(full)
    spread = spread_matrix(heads_width)
    line.relay(full)
    steps[0]()
    both = 3 * heads_width
    for which in range(3):
        spreads[which] = spread_matrix(heads_width, which, both)
    need_qkv()
    line.finish_gather(full)
    flush(2)
    tokens = flat(full)
    bias = biases()
    projected = (dot(tokens, wqkv[...]) + bias[0:1, :both]).astype(BF16)
    for which, target in enumerate((q_ref, k_ref, v_ref)):
        parts = dot(projected, spreads[which])
        target[...] = parts.astype(BF16).reshape(target.shape)

    def one_head(index, carry):
        row = index // heads
        head = lax.rem(index, heads)
        lanes = pl.ds(pl.multiple_of(head * HEAD_LANES, HEAD_LANES), HEAD_LANES)
        scores = dot(q_ref[row, :, lanes], k_ref[row, :, lanes], NT) * HEAD_WIDTH ** (-0.5)
        scores = jnp.where(seg_col[row] == seg_row[row], scores, MASKED_SCORE)
        raised = jnp.exp(scores - jnp.max(scores, axis=-1, keepdims=True))
        probs = raised / jnp.sum(raised, axis=-1, keepdims=True)
        probs_ref[index] = probs
        mixed_wide[row, :, lanes] = dot(probs.astype(BF16), v_ref[row, :, lanes]).astype(BF16)
        return carry

    steps[1]()
    lax.fori_loop(0, rows * heads, one_head, 0)
    mixed_ref[...] = dot(flat(mixed_wide), spread, NT).astype(BF16).reshape(mixed_ref.shape)
    flush(3, 4, 5, 6, 7)
    need_out()

    def partial(which_rows):
        return dot(mixed_ref[:, which_rows, :].reshape(rows * length, heads_width), wo[...])

    total = line.scatter_sum(partial, buffers)
    steps[2]()
    branch = line.finish_sum(total, buffers) + bias[2:3, :]
    branch_ref[...] = branch.reshape(branch_ref.shape)
    middle = flat(u_ref).astype(F32) + token_mod(mod_ref, seg_own, 2) * branch
    middle_ref[...] = middle.reshape(middle_ref.shape)


def open_kernel(count, sections, *refs, cargo):
    u_ref, cond_ref, ada_b_ref, biases_ref, seg_own, seg_col, seg_row = refs[:7]
    ada_w, own_qkv, own_out, own_one, own_two = refs[7:12]
    mods_ref, bias_ref, other_qkv, other_out, other_one, other_two = refs[12:18]
    outs = refs[18:26]
    scratch = refs[26:33]
    ada, mod_src, mod_buf, bias_buf, w_sem, ag_send, ag_recv, rs_send, rs_recv = refs[33:42]
    mod_send, mod_recv, share_send, share_recv, ada_sem = refs[42:]
    wqkv, wo = scratch[:2]
    section, tensor = lax.axis_index("section"), lax.axis_index("tensor")
    load_ada = local(ada_w, ada, ada_sem)
    shares = [
        Share(own, other, parts, (share_send.at[i], share_recv.at[i]))
        for i, (own, other, parts) in enumerate(
            (
                (own_qkv, other_qkv, 4), (own_out, other_out, 2),
                (own_one, other_one, 4), (own_two, other_two, 4),
            )
        )
    ]
    plane = [
        {"section": lax.rem(section + a, sections), "tensor": lax.rem(tensor + b, count)}
        for a in range(sections)
        for b in range(count)
        if a or b
    ]
    greet(plane + [core_peer(), y_peer()] + cross_peers())
    cond_act = silu(cond_ref[...].astype(F32)).astype(BF16)
    load_ada.wait()
    mod = dot(cond_act, ada[...], NT) + ada_b_ref[...].astype(F32)
    mod_src[...] = mod.reshape(mod_src.shape)
    mod_buf[section, tensor] = mod_src[section]
    copies = [
        remote(
            mod_src.at[peer["section"]], mod_buf.at[section, tensor],
            mod_send.at[i], mod_recv.at[i], peer,
        )
        for i, peer in enumerate(plane)
    ]
    bias_buf[section] = biases_ref[...]
    bias_copy = remote(
        biases_ref, bias_buf.at[section],
        mod_send.at[len(plane)], mod_recv.at[len(plane)], x_peer(),
    )
    for share in shares:
        share.begin()
    cargo.begin()

    def mods():
        wait_all(copies)
        width, piece = mods_ref.shape[-1], mod_buf.shape[-1]
        for block in range(sections):
            for which in range(6):
                parts, at = [], which * width
                while at < (which + 1) * width:
                    end = min((at // piece + 1) * piece, (which + 1) * width)
                    start = at - at // piece * piece
                    parts.append(mod_buf[block, at // piece][:, start : start + end - at])
                    at = end
                mods_ref[block, which] = (
                    jnp.concatenate(parts, axis=1) if len(parts) > 1 else parts[0]
                )
        return mods_ref.at[0]

    def biases():
        bias_copy.wait()
        bias_ref[...] = bias_buf[...]
        return bias_buf[0]

    def need_qkv():
        fetch(0, own_qkv, other_qkv, wqkv, w_sem.at[0]).wait()

    def need_out():
        shares[1].finish()
        fetch(0, own_out, other_out, wo, w_sem.at[1]).wait()

    def after_gather():
        shares[0].forward(shares[0].first)
        cargo.middle()
        shares[1].forward(shares[1].first)
        shares[0].forward_again()
        shares[0].finish()

    def before_heads():
        cargo.late()
        shares[2].forward(shares[2].first)

    def after_scatter():
        cargo.cargos[0].start((1,))
        cargo.cargos[0].relay((0, 2))
        shares[2].forward_again()
        shares[3].forward(shares[3].first)
        shares[2].finish()

    attend_body(
        count, None, u_ref, mods, (seg_own, seg_col, seg_row), biases, outs, scratch,
        (ag_send, ag_recv, rs_send, rs_recv), need_qkv, need_out,
        (after_gather, before_heads, after_scatter),
        lambda *which: cargo.flush(*(6 + i for i in which)),
    )
    shares[3].forward_again()
    cargo.cargos[0].relay((1,))
    cargo.end()
    shares[3].finish()


def attend_kernel(count, block, *refs, cargo):
    u_ref, mods_ref, bias_ref, seg_own, seg_col, seg_row = refs[:6]
    own_qkv, other_qkv, own_out, other_out = refs[6:10]
    outs, scratch, w_sem = refs[10:18], refs[18:25], refs[25]
    load_qkv = fetch(block, own_qkv, other_qkv, scratch[0], w_sem.at[0])
    load_out = fetch(block, own_out, other_out, scratch[1], w_sem.at[1])
    attend_body(
        count, z_peers(count) + cargo.peers(), u_ref, lambda: mods_ref.at[block],
        (seg_own, seg_col, seg_row), lambda: bias_ref[block], outs, scratch, refs[26:30],
        load_qkv.wait, load_out.wait, (cargo.begin, cargo.middle, cargo.late), cargo.flush,
    )
    cargo.end()


def mlp_kernel(
    count, block,
    middle_ref, mods_ref, bias_ref, seg_own, w1_own, w1_other, w2_own, w2_other,
    out_ref, branch_ref, full_ref, pre_ref, act_ref,
    w1, w2, send_buf, recv_buf, relay_buf, w_sem, *sems, cargo,
):
    full = full_ref
    me = lax.axis_index("tensor")
    rows, length, width = middle_ref.shape
    mod_ref = mods_ref.at[block]
    load_one = fetch(block, w1_own, w1_other, w1, w_sem.at[0])
    load_two = fetch(block, w2_own, w2_other, w2, w_sem.at[1])
    normed, unused = layer_norm(flat(middle_ref))
    mlp_in = normed * (1.0 + token_mod(mod_ref, seg_own, 4)) + token_mod(mod_ref, seg_own, 3)
    full[:, own_rows(me, length), :] = mlp_in.astype(BF16).reshape(rows, length, width)
    greet(z_peers(count) + cargo.peers())
    line = Line(length, sems)
    line.start_gather(full)
    cargo.begin()
    line.relay(full)
    load_one.wait()
    load_two.wait()

    def hidden(place):
        which_rows = own_rows(place, length)
        pre = dot(full[:, which_rows, :].reshape(rows * length, width), w1[...])
        pre = pre + bias_ref[block, 3:4, : w1.shape[1]]
        pre_ref[:, which_rows, :] = pre.reshape(rows, length, -1)
        act_ref[:, which_rows, :] = gelu_tanh(pre).astype(BF16).reshape(rows, length, -1)

    def prepare(place):
        line.arrived(full, place)
        hidden(place)

    def partial(which_rows):
        return dot(act_ref[:, which_rows, :].reshape(rows * length, -1), w2[...])

    hidden(me)
    hidden(line.opposite)
    buffers = (send_buf, recv_buf, relay_buf)
    total = line.scatter_sum(partial, buffers, prepare)
    cargo.flush(2, 3, 4)
    line.sent(full)
    cargo.middle()
    branch = line.finish_sum(total, buffers) + bias_ref[block, 4:5, :]
    cargo.end()
    branch_ref[...] = branch.reshape(branch_ref.shape)
    out = flat(middle_ref) + token_mod(mod_ref, seg_own, 5) * branch
    out_ref[...] = out.astype(BF16).reshape(out_ref.shape)


def mlp_back_kernel(count, block, *refs, cargo):
    g_ref, middle_ref, branch_ref, mods_ref, seg_own, full_ref, pre_ref, act_ref = refs[:8]
    w1_own, w1_other, w2_own, w2_other = refs[8:12]
    d_middle_ref, d_mod_ref, d_w1_ref, d_w2_ref, d_b1_ref, d_b2_ref = refs[12:18]
    full, d_pre, w1, w2, *buffers, w_sem = refs[18:26]
    sems = refs[26:30]
    w1_whole, w1_got, w1_sems, w2_whole, w2_got, w2_sems, normed_buf = refs[30:]
    w1_sum = CoreSum(w1_whole, w1_got, d_w1_ref, w1_sems)
    w2_sum = CoreSum(w2_whole, w2_got, d_w2_ref, w2_sems)
    me = lax.axis_index("tensor")
    rows, length, width = middle_ref.shape
    mod_ref = mods_ref.at[block]
    load_one = fetch(block, w1_own, w1_other, w1, w_sem.at[0])
    load_two = fetch(block, w2_own, w2_other, w2, w_sem.at[1])
    cargo.load()
    g = flat(g_ref).astype(F32)
    d_branch = (g * token_mod(mod_ref, seg_own, 5)).astype(BF16)
    full[:, own_rows(me, length), :] = d_branch.reshape(rows, length, width)
    greet(z_peers(count) + cargo.peers(["core"]))
    line = Line(length, sems)
    line.start_gather(full)
    cargo.begin()
    slot_sums(g * flat(branch_ref), seg_own, d_mod_ref, 2)
    line.relay(full)
    cargo.middle()
    normed, inverse = layer_norm(flat(middle_ref))
    normed_buf[...] = normed
    load_two.wait()
    cargo.need(6)

    def d_hidden(place):
        which_rows = own_rows(place, length)
        d_act = dot(full[:, which_rows, :].reshape(rows * length, width), w2[...], NT)
        slope = gelu_slope(pre_ref[:, which_rows, :].reshape(rows * length, -1))
        d_pre[:, which_rows, :] = (d_act * slope).astype(BF16).reshape(rows, length, -1)

    def prepare(place):
        line.arrived(full, place)
        d_hidden(place)

    d_hidden(me)
    d_hidden(line.opposite)
    load_one.wait()

    def partial(which_rows):
        return dot(d_pre[:, which_rows, :].reshape(rows * length, -1), w1[...], NT)

    total = line.scatter_sum(partial, buffers, prepare)
    line.sent(full)
    cargo.need(5, 7)
    w2_whole[...] = dot(flat(full), flat(act_ref), TN).astype(BF16)
    w2_sum.begin()
    w1_whole[...] = dot(flat(full_ref), flat(d_pre), TN).astype(BF16)
    w1_sum.begin()
    d_b2_ref[...] = jnp.sum(flat(full).astype(F32), axis=0, keepdims=True)
    d_b1_ref[...] = jnp.sum(flat(d_pre).astype(F32), axis=0, keepdims=True)
    d_in = line.finish_sum(total, buffers)
    normed = normed_buf[...]
    d_middle = flat(g_ref).astype(F32) + norm_back(
        d_in * (1.0 + token_mod(mod_ref, seg_own, 4)), normed, inverse
    )
    d_middle_ref[...] = d_middle.reshape(d_middle_ref.shape)
    slot_sums(d_in, seg_own, d_mod_ref, 0)
    slot_sums(d_in * normed, seg_own, d_mod_ref, 1)
    w2_sum.end()
    w1_sum.end()
    cargo.end()


def attend_back_kernel(count, block, *refs, cargo):
    d_middle_ref, u_ref, branch_ref, mods_ref, seg_own, full_ref = refs[:6]
    q_ref, k_ref, v_ref, probs_ref, mixed_ref = refs[6:11]
    wqkv_own, wqkv_other, wo_own, wo_other = refs[11:15]
    d_in_ref, d_mod_ref, d_wqkv_ref, d_wo_ref, d_bqv_ref, d_bo_ref = refs[15:21]
    full, wide, narrow, wqkv, wo, *buffers, w_sem = refs[21:30]
    sems = refs[30:34]
    qkv_whole, qkv_got, qkv_sems, wo_whole, wo_got, wo_sems, spreads, normed_buf = refs[34:]
    qkv_sum = CoreSum(qkv_whole, qkv_got, d_wqkv_ref, qkv_sems)
    wo_sum = CoreSum(wo_whole, wo_got, d_wo_ref, wo_sems)
    me = lax.axis_index("tensor")
    rows, length, width = u_ref.shape
    heads_width = wo.shape[0]
    heads = heads_width // HEAD_WIDTH
    mod_ref = mods_ref.at[block]
    load_qkv = fetch(block, wqkv_own, wqkv_other, wqkv, w_sem.at[0])
    load_out = fetch(block, wo_own, wo_other, wo, w_sem.at[1])
    cargo.load()
    d_middle = flat(d_middle_ref)
    d_branch = (d_middle * token_mod(mod_ref, seg_own, 2)).astype(BF16)
    full[:, own_rows(me, length), :] = d_branch.reshape(rows, length, width)
    greet(z_peers(count) + cargo.peers(["core"]))
    line = Line(length, sems)
    line.start_gather(full)
    cargo.begin()
    slot_sums(d_middle * flat(branch_ref), seg_own, d_mod_ref, 2)
    line.relay(full)
    cargo.middle()
    spread = spread_matrix(heads_width)
    both = 3 * heads_width
    for which in range(3):
        spreads[which] = spread_matrix(heads_width, which, both)
    normed, inverse = layer_norm(flat(u_ref).astype(F32))
    normed_buf[...] = normed
    load_out.wait()
    line.finish_gather(full)
    d_mixed = dot(flat(full), wo[...], NT).astype(BF16)
    wide[3] = dot(d_mixed, spread).astype(BF16).reshape(wide.shape[1:])
    cargo.need(6, 7, 8, 9)

    def one_head(index, carry):
        row = index // heads
        head = lax.rem(index, heads)
        lanes = pl.ds(pl.multiple_of(head * HEAD_LANES, HEAD_LANES), HEAD_LANES)
        grad = wide[3, row, :, lanes]
        probs = probs_ref[index]
        d_probs = dot(grad, v_ref[row, :, lanes], NT)
        d_scores = (
            probs * (d_probs - jnp.sum(d_probs * probs, axis=-1, keepdims=True))
        ).astype(BF16)
        scale = HEAD_WIDTH ** (-0.5)
        wide[0, row, :, lanes] = (dot(d_scores, k_ref[row, :, lanes]) * scale).astype(BF16)
        wide[1, row, :, lanes] = (dot(d_scores, q_ref[row, :, lanes], TN) * scale).astype(BF16)
        wide[2, row, :, lanes] = dot(probs.astype(BF16), grad, TN).astype(BF16)
        return carry

    lax.fori_loop(0, rows * heads, one_head, 0)
    gathered = 0.0
    for which in range(3):
        gathered = gathered + dot(flat(wide.at[which]), spreads[which], NT)
    narrow[...] = gathered.astype(BF16).reshape(narrow.shape)
    load_qkv.wait()

    def partial(which_rows):
        return dot(narrow[:, which_rows, :].reshape(rows * length, both), wqkv[...], NT)

    total = line.scatter_sum(partial, buffers)
    d_bo_ref[...] = jnp.sum(flat(full).astype(F32), axis=0, keepdims=True)
    d_bqv_ref[...] = jnp.sum(flat(narrow).astype(F32), axis=0, keepdims=True)
    cargo.need(5, 10)
    wo_whole[...] = dot(flat(full), flat(mixed_ref), TN).astype(BF16)
    wo_sum.begin()
    qkv_whole[...] = dot(flat(full_ref), flat(narrow), TN).astype(BF16)
    qkv_sum.begin()
    d_attn_in = line.finish_sum(total, buffers)
    normed = normed_buf[...]
    d_in = flat(d_middle_ref) + norm_back(
        d_attn_in * (1.0 + token_mod(mod_ref, seg_own, 1)), normed, inverse
    )
    d_in_ref[...] = d_in.reshape(d_in_ref.shape)
    slot_sums(d_attn_in, seg_own, d_mod_ref, 0)
    slot_sums(d_attn_in * normed, seg_own, d_mod_ref, 1)
    wo_sum.end()
    qkv_sum.end()
    cargo.end()


def silu_slope(value):
    gate = 1.0 / (1.0 + jnp.exp(-value))
    return gate * (1.0 + value * (1.0 - gate))


def project_kernel(token_count, *refs, cargo):
    sent_ref, targets_ref, biases_ref, p2_b_ref, p1_any, p2_any, p3_any = refs[:7]
    d_sent_ref, d_p1_ref, d_p2_ref, d_p3_ref, small_ref = refs[7:12]
    p1, p2, p3, tokens, first_pre, first, second_pre, second, d_second, norms = refs[12:22]
    buf_a, buf_b, buf_c, d_first, load_sem, send, recv = refs[22:]
    core, peer = core_bit(), core_peer()
    loads = [
        local(source, place, load_sem.at[i])
        for i, (source, place) in enumerate(((p1_any, p1), (p2_any, p2), (p3_any, p3)))
    ]
    count = tokens.shape[1]
    tokens[core] = flat(sent_ref)
    greet([peer])

    def trade(ref, which):
        return remote(ref.at[core], ref.at[core], send.at[which], recv.at[which], peer)

    def give(buffer, value, which):
        buffer[0] = value.astype(BF16)
        return remote(buffer.at[0], buffer.at[1], send.at[which], recv.at[which], peer)

    def block(ref, side):
        return ref[side]

    copy = trade(tokens, 0)
    target = [
        targets_ref[slot].reshape(2 * count, targets_ref.shape[-1]).astype(F32) for slot in range(2)
    ]
    target_sq = sum(jnp.sum(one * one, axis=1, keepdims=True) for one in target)
    loads[0].wait()
    copy.wait()
    all_tokens = flat(tokens)
    for slot in range(2):
        pre = dot(all_tokens, p1[slot]) + biases_ref[slot, 0, 0:1, :]
        first_pre[slot] = pre
        first[slot] = silu(pre).astype(BF16)
    loads[1].wait()

    def second_term(side):
        rows = pl.ds(pl.multiple_of(side * count, 16), count)
        return dot(first[0, rows, :], p2[0]) + dot(first[1, rows, :], p2[1])

    copy = give(buf_a, second_term(1 - core), 1)
    pre = second_term(core)
    copy.wait()
    pre = pre + buf_a[1].astype(F32) + p2_b_ref[...].astype(F32)
    second_pre[...] = pre
    second[core] = silu(pre).astype(BF16)
    copy = trade(second, 2)
    loads[2].wait()
    copy.wait()
    all_second = flat(second)
    width = target[0].shape[1]
    predicted = [
        dot(all_second, p3[slot], NT) + biases_ref[slot, 0, 1:2, :width] for slot in range(2)
    ]
    pred_sq = sum(jnp.sum(one * one, axis=1, keepdims=True) for one in predicted)
    cross = sum(
        jnp.sum(one * two, axis=1, keepdims=True) for one, two in zip(predicted, target)
    )
    lanes = lax.broadcasted_iota(jnp.int32, norms.shape[1:], 1)
    norms[core] = jnp.where(lanes == 0, pred_sq, jnp.where(lanes == 1, cross, target_sq))
    copy = trade(norms, 3)
    copy.wait()
    total = norms[0] + norms[1]
    inv_pred = lax.rsqrt(total[:, 0:1] + COSINE_EPS)
    inv_target = lax.rsqrt(total[:, 2:3] + COSINE_EPS)
    cosine = total[:, 1:2] * inv_pred * inv_target
    side = lax.broadcasted_iota(jnp.int32, cosine.shape, 0)
    own = jnp.logical_and(side >= core * count, side < (core + 1) * count)
    loss = jnp.sum(jnp.where(own, cosine, 0.0), axis=0, keepdims=True)
    factor = -0.5 / token_count
    one_scale = factor * inv_pred * inv_target
    two_scale = factor * cosine * inv_pred * inv_pred
    d_pred = [
        (one_scale * two - two_scale * one).astype(BF16) for one, two in zip(predicted, target)
    ]
    small_ref[...] = jnp.zeros_like(small_ref)
    for slot in range(2):
        small_ref[2 * core + slot, 1:2, :width] = jnp.sum(
            d_pred[slot].astype(F32), axis=0, keepdims=True
        )

    def d_second_term(side):
        terms = 0.0
        for slot in range(2):
            mine = jnp.where(
                side == 0, d_pred[slot][:count].astype(F32), d_pred[slot][count:].astype(F32)
            )
            terms = terms + dot(mine.astype(BF16), p3[slot])
        return terms

    copy = give(buf_b, d_second_term(1 - core), 4)
    grad = d_second_term(core)
    for slot in range(2):
        d_p3_ref[slot] = dot(d_pred[slot], all_second, TN).astype(BF16)
    copy.wait()
    grad = ((grad + buf_b[1].astype(F32)) * silu_slope(second_pre[...])).astype(BF16)
    d_second[core] = grad
    copy = trade(d_second, 5)
    d_p2_b = jnp.sum(grad.astype(F32), axis=0, keepdims=True)
    lane = small_ref.shape[2]
    loss_row = jnp.where(lax.broadcasted_iota(jnp.int32, (1, lane), 1) == 0, loss, 0.0)
    for part in range(4):
        for row in range(d_p2_b.shape[1] // lane):
            small_ref[part, 2 + row : 3 + row, :] = d_p2_b[:, row * lane : (row + 1) * lane]
        small_ref[part, 6:7, :] = loss_row
    copy.wait()
    all_d_second = flat(d_second)
    for slot in range(2):
        back = dot(all_d_second, p2[slot], NT) * silu_slope(first_pre[slot])
        d_first[slot] = back.astype(BF16)
        small_ref[2 * core + slot, 0:1, :] = jnp.sum(
            d_first[slot].astype(F32), axis=0, keepdims=True
        )

    def d_sent_term(side):
        rows = pl.ds(pl.multiple_of(side * count, 16), count)
        return dot(d_first[0, rows, :], p1[0], NT) + dot(d_first[1, rows, :], p1[1], NT)

    copy = give(buf_c, d_sent_term(1 - core), 6)
    grad = d_sent_term(core)
    for slot in range(2):
        d_p2_ref[slot] = dot(first[slot], all_d_second, TN).astype(BF16)
        d_p1_ref[slot] = dot(all_tokens, d_first[slot], TN).astype(BF16)
    copy.wait()
    d_sent_ref[...] = (grad + buf_c[1].astype(F32)).reshape(d_sent_ref.shape)


def close_kernel(count, sections, replicas, *refs, cargo):
    grads_ref, mod_refs, small_refs, proj_ref, cond_ref = (
        refs[:2], refs[2:6], refs[6:14], refs[14], refs[15]
    )
    grad_ref, ada_w_ref, ada_b_ref, small_ref, proj_sum_ref = refs[16:21]
    z_src, z_buf, mod_src, mod_buf, small_src, small_buf, cond_buf = refs[21:28]
    place_src, place_buf, proj_got, proj_src, proj_buf = refs[28:33]
    sems = refs[33:35]
    section, tensor, replica = (lax.axis_index(name) for name in ("section", "tensor", "dp"))
    send, recv = sems
    others = [
        {"section": lax.rem(section + a, sections), "dp": lax.rem(replica + b, replicas)}
        for a in range(sections)
        for b in range(replicas)
        if a or b
    ]
    greet(z_peers(count) + others + cross_peers())
    last_sums = [one for one in cargo.cargos if isinstance(one, LastSum)]
    y_sums = [one for one in cargo.cargos if type(one) is YSum]
    for one in last_sums:
        one.begin()
    piece = z_src.shape[-1]
    for block in range(sections):
        attend_mod, mlp_mod = mod_refs[2 * block : 2 * block + 2]
        width = attend_mod.shape[-1]
        for part in range(count):
            at, end, cuts = part * piece, (part + 1) * piece, []
            while at < end:
                which = at // width
                stop = min((which + 1) * width, end)
                ref = attend_mod if which < 3 else mlp_mod
                cuts.append(ref[which % 3][:, at - which * width : stop - which * width])
                at = stop
            z_src[part, block] = jnp.concatenate(cuts, axis=1) if len(cuts) > 1 else cuts[0]
    z_copies = [
        remote(z_src.at[peer["tensor"]], z_buf.at[i], send.at[i], recv.at[i], peer)
        for i, peer in enumerate(z_peers(count))
    ]
    at = count - 1
    z_copies += [
        remote(proj_ref.at[peer["tensor"]], proj_got.at[i], send.at[at + i], recv.at[at + i], peer)
        for i, peer in enumerate(z_peers(count))
    ]
    at = at + count - 1

    @pl.when(section == 0)
    def first_place():
        place_src[...] = grads_ref[1][...].astype(BF16)

    @pl.when(section != 0)
    def second_place():
        place_src[...] = grads_ref[0][...].astype(BF16)

    place_copy = remote(place_src, place_buf, send.at[at], recv.at[at], x_peer())
    at = at + 1
    both = small_refs[0].shape[-1]
    small_src[...] = jnp.zeros_like(small_src)
    for block in range(sections):
        d_bqv, d_bo, d_b1, d_b2 = small_refs[4 * block : 4 * block + 4]
        small_src[block, 0:1, :both] = d_bqv[...]
        small_src[block, 2:3, :] = d_bo[...]
        small_src[block, 3:4, : d_b1.shape[1]] = d_b1[...]
        small_src[block, 4:5, :] = d_b2[...]
    small_buf[section, replica] = small_src[section]
    cond_buf[section, replica] = cond_ref[replica]
    copies = []
    for peer in others:
        copies.append(
            remote(
                small_src.at[peer["section"]], small_buf.at[section, replica],
                send.at[at], recv.at[at], peer,
            )
        )
        copies.append(
            remote(
                cond_ref.at[peer["dp"]], cond_buf.at[section, replica],
                send.at[at + 1], recv.at[at + 1], peer,
            )
        )
        at = at + 2
    for one in cargo.cargos:
        if not isinstance(one, YSum):
            one.begin()
    wait_all(z_copies)
    mine, mine_proj = z_src[tensor], proj_ref[tensor]
    for step in range(count - 1):
        mine = mine + z_buf[step]
        mine_proj = mine_proj + proj_got[step]
    mod_src[...] = mine
    mod_buf[section, replica] = mod_src[section]
    proj_src[...] = mine_proj
    proj_buf[section, replica] = mine_proj
    for peer in others:
        copies.append(
            remote(
                mod_src.at[peer["section"]], mod_buf.at[section, replica],
                send.at[at], recv.at[at], peer,
            )
        )
        copies.append(
            remote(
                proj_src, proj_buf.at[section, replica], send.at[at + 1], recv.at[at + 1], peer
            )
        )
        at = at + 2
    for one in last_sums:
        one.middle()
    for one in y_sums:
        one.begin()
    place_copy.wait()
    rows = place_buf.shape[0]

    @pl.when(section == 0)
    def first_out():
        grad_ref[:rows] = grads_ref[0][...]
        grad_ref[rows:] = place_buf[...].astype(F32)

    @pl.when(section != 0)
    def second_out():
        grad_ref[rows:] = grads_ref[1][...]
        grad_ref[:rows] = place_buf[...].astype(F32)

    wait_all(copies)
    small, proj_sum = small_buf[0, 0], proj_buf[0, 0]
    for a in range(sections):
        for b in range(replicas):
            if a or b:
                small = small + small_buf[a, b]
                proj_sum = proj_sum + proj_buf[a, b]
    small_ref[...] = small
    proj_sum_ref[...] = proj_sum
    mod_all = flat(mod_buf)
    ada_b_ref[...] = jnp.sum(mod_all, axis=0, keepdims=True)
    ada_w_ref[...] = lax.dot_general(
        flat(cond_buf), mod_all, TN, precision=HIGHEST, preferred_element_type=F32
    )
    cargo.end()


VMEM = pl.BlockSpec(memory_space=pltpu.VMEM)
ANY = pl.BlockSpec(memory_space=pl.ANY)
MOD_ROWS = 8
PROJECTOR_AXES = (0, 0, 1)


def call(
    kernel, number, inputs, in_any, outs, out_any, scratch, flops, cargos=(), lazy=(), streamed=()
):
    own_in, own_out, own_scratch = len(inputs), len(outs), len(scratch)
    specs = [VMEM] * (own_in - in_any) + [ANY] * in_any
    specs = [ANY if i in lazy else spec for i, spec in enumerate(specs)]
    out_specs = [ANY if i in out_any or i in streamed else VMEM for i in range(own_out)]
    inputs, outs, scratch, aliases = list(inputs), list(outs), list(scratch), {}
    moved_refs = len(lazy) + len(streamed)
    scratch += [pltpu.VMEM(inputs[i].shape, inputs[i].dtype) for i in lazy]
    scratch += [pltpu.VMEM(*outs[i]) for i in streamed]
    if moved_refs:
        scratch.append(pltpu.SemaphoreType.DMA((moved_refs,)))
        moved_refs += 1
    for cargo in cargos:
        for source, target in cargo.aliases.items():
            aliases[len(inputs) + source] = len(outs) + target
        inputs += cargo.inputs
        outs += cargo.outs
        scratch += cargo.scratch
        specs += [ANY] * len(cargo.inputs)
        out_specs += [ANY if cargo.any_outs else VMEM] * len(cargo.outs)

    def body(*refs):
        parts = [list(refs[: len(inputs)])]
        parts.append(list(refs[len(inputs) : len(inputs) + len(outs)]))
        parts.append(list(refs[len(inputs) + len(outs) :]))
        base = parts[0][:own_in] + parts[1][:own_out] + parts[2][:own_scratch]
        held = parts[2][own_scratch : own_scratch + moved_refs]
        bundle = Bundle(cargos)
        for k, i in enumerate(lazy):
            bundle.loads[i] = pltpu.make_async_copy(base[i], held[k], held[-1].at[k])
            base[i] = held[k]
        for k, i in enumerate(streamed, len(lazy)):
            bundle.stores[i] = pltpu.make_async_copy(held[k], base[own_in + i], held[-1].at[k])
            base[own_in + i] = held[k]
        at = [own_in, own_out, own_scratch + moved_refs]
        for cargo in cargos:
            held = []
            for i, items in enumerate((cargo.inputs, cargo.outs, cargo.scratch)):
                held.append(parts[i][at[i] : at[i] + len(items)])
                at[i] += len(items)
            cargo.bind(*held)
        kernel(*base, cargo=bundle)

    moved = sum(math.prod(one.shape) * one.dtype.itemsize for one in inputs)
    results = pl.pallas_call(
        body,
        out_shape=[jax.ShapeDtypeStruct(shape, dtype) for shape, dtype in outs],
        in_specs=specs,
        out_specs=out_specs,
        scratch_shapes=scratch,
        input_output_aliases=aliases,
        compiler_params=pltpu.CompilerParams(
            collective_id=number, has_side_effects=True, vmem_limit_bytes=56 * 2**20
        ),
        cost_estimate=pl.CostEstimate(flops=flops, bytes_accessed=moved, transcendentals=0),
    )(*inputs)
    at, carried = own_out, []
    for cargo in cargos:
        carried.append(results[at : at + len(cargo.outs)])
        at += len(cargo.outs)
    return results[:own_out], carried


def exchange_scratch(count, rows, length, width):
    return [
        pltpu.VMEM((count - 1, rows, length, width), BF16),
        pltpu.VMEM((count, rows, length, width), BF16),
        pltpu.VMEM((rows, length, width), BF16),
    ]


def semaphores(count):
    return [pltpu.SemaphoreType.DMA((2,))] + [
        pltpu.SemaphoreType.DMA((size,)) for size in (count, count, count - 1, count + 1)
    ]


class Shapes:
    def __init__(self, u, own, count):
        self.rows, self.length, self.width = u.shape
        self.count = count
        self.positions = self.length * count
        self.tokens = self.rows * self.positions
        self.heads_width = own["out"].shape[0]
        self.hidden = own["one"].shape[1]
        self.heads = self.heads_width // HEAD_WIDTH
        self.local = (self.rows, self.length, self.width)
        self.full = (self.rows, self.positions, self.width)
        self.wide = (self.rows, self.positions, self.heads * HEAD_LANES)
        self.own = own
        self.attend_outs = [
            (self.local, F32), (self.local, F32), (self.full, BF16),
            (self.wide, BF16), (self.wide, BF16), (self.wide, BF16),
            ((self.rows * self.heads, self.positions, self.positions), F32),
            ((self.rows, self.positions, self.heads_width), BF16),
        ]
        self.attend_scratch = [
            pltpu.VMEM(own["qkv"].shape, BF16),
            pltpu.VMEM(own["out"].shape, BF16),
            pltpu.VMEM(self.wide, BF16),
        ] + exchange_scratch(count, *self.local)
        self.spreads = pltpu.VMEM((3, 3 * self.heads_width, self.heads * HEAD_LANES), BF16)
        self.attend_scratch.append(self.spreads)
        self.mods = (3, MOD_ROWS, self.width)


def pairs(own, other, names):
    out = []
    for name in names:
        out += [own[name], other[name]]
    return out


def open_forward(sizes, u, cond, ada_w, ada_b, biases, segs, own, sections, cargos):
    count, width = sizes.count, sizes.width
    piece = ada_w.shape[0]
    inputs = [u, cond, ada_b, biases, *segs, ada_w] + [own[n] for n in ("qkv", "out", "one", "two")]
    plane = sections * count - 1
    results, carried = call(
        functools.partial(open_kernel, count, sections),
        0,
        inputs,
        5,
        [((sections, 6, MOD_ROWS, width), F32), ((sections,) + biases.shape, F32)]
        + [(own[n].shape, BF16) for n in ("qkv", "out", "one", "two")]
        + sizes.attend_outs,
        (2, 3, 4, 5),
        sizes.attend_scratch
        + [
            pltpu.VMEM(ada_w.shape, BF16),
            pltpu.VMEM((sections, MOD_ROWS, piece), F32),
            pltpu.VMEM((sections, count, MOD_ROWS, piece), F32),
            pltpu.VMEM((sections,) + biases.shape, F32),
        ]
        + semaphores(count)
        + [
            pltpu.SemaphoreType.DMA((plane + 1,)),
            pltpu.SemaphoreType.DMA((plane + 1,)),
            pltpu.SemaphoreType.DMA((4, 4)),
            pltpu.SemaphoreType.DMA((4, 4)),
            pltpu.SemaphoreType.DMA,
        ],
        2 * sizes.tokens * width * sizes.heads_width * 4,
        cargos,
        streamed=tuple(range(8, 14)),
    )
    other = dict(zip(("qkv", "out", "one", "two"), results[2:6]))
    return results[0], results[1], other, results[6:], carried


def attend_forward(sizes, block, u, mods, biases, segs, own, other, cargos):
    inputs = [u, mods, biases, *segs] + pairs(own, other, ("qkv", "out"))
    return call(
        functools.partial(attend_kernel, sizes.count, block),
        1,
        inputs,
        4,
        sizes.attend_outs,
        (),
        sizes.attend_scratch + semaphores(sizes.count),
        2 * sizes.tokens * sizes.width * sizes.heads_width * 4,
        cargos,
        streamed=tuple(range(2, 8)),
    )


def mlp_forward(sizes, block, middle, mods, biases, segs, own, other, cargos):
    inputs = [middle, mods, biases, segs[0]] + pairs(own, other, ("one", "two"))
    hidden = (sizes.rows, sizes.positions, sizes.hidden)
    return call(
        functools.partial(mlp_kernel, sizes.count, block),
        2 + block,
        inputs,
        4,
        [
            (sizes.local, BF16), (sizes.local, F32), (sizes.full, BF16),
            (hidden, F32), (hidden, BF16),
        ],
        (),
        [
            pltpu.VMEM(own["one"].shape, BF16),
            pltpu.VMEM(own["two"].shape, BF16),
        ]
        + exchange_scratch(sizes.count, *sizes.local)
        + semaphores(sizes.count),
        2 * sizes.tokens * sizes.width * sizes.hidden * 2,
        cargos,
        streamed=(2, 3, 4),
    )


def mlp_backward(sizes, block, g, attend, mlp, mods, segs, own, other, cargos):
    out, branch, full, pre, act = mlp
    inputs = [g, attend[0], branch, mods, segs[0], full, pre, act]
    inputs += pairs(own, other, ("one", "two"))
    return call(
        functools.partial(mlp_back_kernel, sizes.count, block),
        4 + block,
        inputs,
        4,
        [
            (sizes.local, F32), (sizes.mods, F32),
            ((2,) + quarter((sizes.width, sizes.hidden)), BF16),
            ((2,) + quarter((sizes.width, sizes.hidden)), BF16),
            ((1, sizes.hidden), F32), ((1, sizes.width), F32),
        ],
        (),
        [
            pltpu.VMEM(sizes.full, BF16),
            pltpu.VMEM((sizes.rows, sizes.positions, sizes.hidden), BF16),
            pltpu.VMEM(own["one"].shape, BF16),
            pltpu.VMEM(own["two"].shape, BF16),
        ]
        + exchange_scratch(sizes.count, *sizes.local)
        + semaphores(sizes.count)
        + core_sum_scratch((sizes.width, sizes.hidden)) * 2
        + [
            pltpu.VMEM((sizes.rows * sizes.length, sizes.width), F32),
        ],
        2 * sizes.tokens * sizes.width * sizes.hidden * 4,
        cargos,
        lazy=(5, 6, 7),
    )


def attend_backward(sizes, block, d_middle, u, attend, mods, segs, own, other, cargos):
    middle, branch, full, q, k, v, probs, mixed = attend
    inputs = [d_middle, u, branch, mods, segs[0], full, q, k, v, probs, mixed]
    inputs += pairs(own, other, ("qkv", "out"))
    return call(
        functools.partial(attend_back_kernel, sizes.count, block),
        6 + block,
        inputs,
        4,
        [
            (sizes.local, F32), (sizes.mods, F32),
            ((2,) + quarter((sizes.width, 3 * sizes.heads_width)), BF16),
            ((2,) + quarter((sizes.width, sizes.heads_width)), BF16),
            ((1, 3 * sizes.heads_width), F32), ((1, sizes.width), F32),
        ],
        (),
        [
            pltpu.VMEM(sizes.full, BF16),
            pltpu.VMEM((4,) + sizes.wide, BF16),
            pltpu.VMEM((sizes.rows, sizes.positions, 3 * sizes.heads_width), BF16),
            pltpu.VMEM(own["qkv"].shape, BF16),
            pltpu.VMEM(own["out"].shape, BF16),
        ]
        + exchange_scratch(sizes.count, *sizes.local)
        + semaphores(sizes.count)
        + core_sum_scratch((sizes.width, 3 * sizes.heads_width))
        + core_sum_scratch((sizes.width, sizes.heads_width))
        + [
            sizes.spreads,
            pltpu.VMEM((sizes.rows * sizes.length, sizes.width), F32),
        ],
        2 * sizes.tokens * sizes.width * sizes.heads_width * 8,
        cargos,
        lazy=(5, 6, 7, 8, 9, 10),
    )


def project(sizes, sent, weights, targets, biases, p2_b, token_count):
    tokens = sizes.rows * sizes.length
    p1, p2, p3 = weights
    lane, hidden = p1.shape[2], p2.shape[2]
    inputs = [sent, targets, biases, p2_b, p1, p2, p3]
    results, unused = call(
        functools.partial(project_kernel, token_count),
        9,
        inputs,
        3,
        [
            (sizes.local, F32), (p1.shape, BF16), (p2.shape, BF16), (p3.shape, BF16),
            ((sizes.count, MOD_ROWS, lane), F32),
        ],
        (),
        [
            pltpu.VMEM(p1.shape, BF16),
            pltpu.VMEM(p2.shape, BF16),
            pltpu.VMEM(p3.shape, BF16),
            pltpu.VMEM((2, tokens, sizes.width), BF16),
            pltpu.VMEM((2, 2 * tokens, lane), F32),
            pltpu.VMEM((2, 2 * tokens, lane), BF16),
            pltpu.VMEM((tokens, hidden), F32),
            pltpu.VMEM((2, tokens, hidden), BF16),
            pltpu.VMEM((2, tokens, hidden), BF16),
            pltpu.VMEM((2, 2 * tokens, HEAD_LANES), F32),
            pltpu.VMEM((2, tokens, hidden), BF16),
            pltpu.VMEM((2, tokens, hidden), BF16),
            pltpu.VMEM((2, tokens, sizes.width), BF16),
            pltpu.VMEM((2, 2 * tokens, lane), BF16),
            pltpu.SemaphoreType.DMA((3,)),
            pltpu.SemaphoreType.DMA((7,)),
            pltpu.SemaphoreType.DMA((7,)),
        ],
        12 * tokens * sum(math.prod(one.shape) for one in weights),
    )
    return results


def close_backward(sizes, grads, mod_grads, small, proj_small, cond, sections, replicas, cargos):
    count, width = sizes.count, sizes.width
    piece = 6 * width // count
    share = width // replicas
    inputs = [*grads, *mod_grads, *small, proj_small, cond]
    copies = 2 * count + 4 * (sections * replicas - 1)
    both = (sections * sizes.rows,) + sizes.local[1:]
    return call(
        functools.partial(close_kernel, count, sections, replicas),
        8,
        inputs,
        0,
        [
            (both, F32), ((share, piece), F32), ((1, piece), F32),
            ((MOD_ROWS, width), F32), (proj_small.shape[1:], F32),
        ],
        (),
        [
            pltpu.VMEM((count, sections, MOD_ROWS, piece), F32),
            pltpu.VMEM((count - 1, sections, MOD_ROWS, piece), F32),
            pltpu.VMEM((sections, MOD_ROWS, piece), F32),
            pltpu.VMEM((sections, replicas, MOD_ROWS, piece), F32),
            pltpu.VMEM((sections, MOD_ROWS, width), F32),
            pltpu.VMEM((sections, replicas, MOD_ROWS, width), F32),
            pltpu.VMEM((sections, replicas, MOD_ROWS, share), F32),
            pltpu.VMEM(sizes.local, BF16),
            pltpu.VMEM(sizes.local, BF16),
            pltpu.VMEM((count - 1,) + proj_small.shape[1:], F32),
            pltpu.VMEM(proj_small.shape[1:], F32),
            pltpu.VMEM((sections, replicas) + proj_small.shape[1:], F32),
            pltpu.SemaphoreType.DMA((copies,)),
            pltpu.SemaphoreType.DMA((copies,)),
        ],
        2 * sections * replicas * MOD_ROWS * share * piece,
        cargos,
    )


def assemble_kernel(heads_width, *refs):
    fc1, fc2 = refs[0:2], refs[2:4]
    alone, (qkv, wo) = refs[4:9], (refs[9:11], refs[11:13])
    grad_ref, small, proj = refs[13:16]
    outs, sems = refs[16:-1], refs[-1]
    is_first = lax.axis_index("section") == 0
    waits = []
    for i, pair in enumerate((fc1, fc2)):
        waits.append(pltpu.make_async_copy(pair[0], outs[i], sems.at[i]))

        @pl.when(is_first)
        def take_one(pair=pair, i=i):
            pltpu.make_async_copy(pair[0], outs[i], sems.at[i]).start()

        @pl.when(jnp.logical_not(is_first))
        def take_two(pair=pair, i=i):
            pltpu.make_async_copy(pair[1], outs[i], sems.at[i]).start()

    for i, one in enumerate(alone):
        waits.append(local(one, outs[2 + i], sems.at[2 + i]))
    grad_out, qkv_out, wo_out, qv_b, out_b, fc1_b, fc2_b, p1_b, p2_b, p3_b, loss = outs[7:]
    for row in range(grad_ref.shape[0]):
        grad_out[:, row, :] = grad_ref[row]
    qkv_own = jnp.where(is_first, qkv[0][...], qkv[1][...])
    for which in range(3):
        qkv_out[which] = qkv_own[:, which * heads_width : (which + 1) * heads_width]
    wo_out[...] = jnp.where(is_first, wo[0][...], wo[1][...]).T
    qv_b[0:1, :] = small[0:1, :heads_width]
    qv_b[1:2, :] = small[0:1, 2 * heads_width : 3 * heads_width]
    out_b[...] = small[2:3, :]
    fc1_b[...] = small[3:4, :]
    fc2_b[...] = small[4:5, :]
    p1_b[...] = proj[0:1, :]
    p2_b[...] = jnp.concatenate([proj[2 + row : 3 + row, :] for row in range(4)], axis=1)
    p3_b[...] = proj[1:2, : p3_b.shape[1]]
    loss[...] = proj[6:7, :HEAD_LANES]
    wait_all(waits)


def assemble(choices, alone, section_grad, small, proj_small, heads_width):
    (fc1, fc2, qkv, wo) = choices
    inputs = [*fc1, *fc2, *alone, *qkv, *wo, section_grad, small, proj_small]
    both, length, width = section_grad.shape
    share, lane = fc1[0].shape[0], proj_small.shape[1]
    third = alone[4].shape[0]
    shapes = [fc1[0].shape, fc2[0].shape] + [one.shape for one in alone] + [
        (length, both, width), (3, share, heads_width), wo[0].shape[::-1], (2, heads_width),
        (1, width), (1, width), (1, width), (1, lane), (1, 4 * lane), (1, third), (1, HEAD_LANES),
    ]
    return pl.pallas_call(
        functools.partial(assemble_kernel, heads_width),
        out_shape=[jax.ShapeDtypeStruct(shape, F32) for shape in shapes],
        in_specs=[ANY] * 9 + [VMEM] * 7,
        out_specs=[VMEM] * 18,
        scratch_shapes=[pltpu.SemaphoreType.DMA((7,))],
        compiler_params=pltpu.CompilerParams(vmem_limit_bytes=62 * 2**20),
        cost_estimate=pl.CostEstimate(flops=1000, bytes_accessed=2**24, transcendentals=0),
    )(*inputs)


def halve(value, axis, bit, position):
    size = lax.axis_size(axis)
    mine = (lax.axis_index(axis) & bit) // bit
    keep = lax.dynamic_index_in_dim(value, mine, position, keepdims=False)
    give = lax.dynamic_index_in_dim(value, 1 - mine, position, keepdims=False)
    return keep + lax.ppermute(give, axis, [(i, i ^ bit) for i in range(size)])


def sum_beyond_quads(value):
    size = lax.axis_size("dp")
    if size == 4:
        return value
    quads = size // 4
    bits = quads.bit_length() - 1
    lead = value.ndim - 2
    shape = value.shape
    value = value.reshape(shape[:lead] + (2,) * bits + (shape[-2] // quads, shape[-1]))
    for bit in range(bits):
        value = halve(value, "dp", 4 << bit, lead + bits - 1 - bit)
    route = [(high * 4 + low, low * quads + high) for high in range(quads) for low in range(4)]
    return lax.ppermute(value, "dp", route)


def per_device(
    block_eight_input,
    cond,
    image_slot_index,
    targets,
    cot,
    ada_w,
    ada_b,
    query_key_value_weight,
    query_value_bias,
    attention_output_weight,
    attention_output_bias,
    hidden_weight,
    hidden_bias,
    output_weight_mlp,
    output_bias_mlp,
    p1_w,
    p1_b,
    p2_w,
    p2_b,
    p3_w,
    p3_b,
):
    section = lax.axis_index("section")
    tensor = lax.axis_index("tensor")
    is_first = section == 0
    count = lax.axis_size("tensor")
    sections = lax.axis_size("section")
    replicas = lax.axis_size("dp")
    length, replica_rows, width = block_eight_input.shape
    positions = length * count
    rows = replica_rows // sections
    total_token_count = positions * replica_rows * replicas
    heads_width = attention_output_weight.shape[1]
    hidden = hidden_weight.shape[2]

    def my_rows(value, axis):
        return lax.dynamic_slice_in_dim(value, section * rows, rows, axis)

    def to_rows(value):
        return jnp.transpose(my_rows(value, 1), (1, 0, 2))

    own = {
        "qkv": query_key_value_weight[0].reshape(width, 3 * heads_width),
        "out": attention_output_weight[0],
        "one": hidden_weight[0],
        "two": output_weight_mlp[0],
    }

    def padded(value):
        return jnp.pad(value.astype(F32), ((0, 0), (0, width - value.shape[-1])))

    biases = jnp.concatenate(
        [
            padded(
                jnp.concatenate(
                    [
                        query_value_bias[0, 0:1], jnp.zeros((1, heads_width), BF16),
                        query_value_bias[0, 1:2],
                    ],
                    axis=1,
                )
            ),
            jnp.zeros((1, width), F32), padded(attention_output_bias), padded(hidden_bias),
            padded(output_bias_mlp), jnp.zeros((MOD_ROWS - 5, width), F32),
        ],
        axis=0,
    )
    used = rows * IMAGES_PER_ROW
    cond_pad = jnp.pad(
        cond.reshape(sections, used, width), ((0, 0), (0, MOD_ROWS - used), (0, 0))
    )
    segs_full = my_rows(image_slot_index, 0)
    seg_own = lax.dynamic_slice_in_dim(segs_full, tensor * length, length, 1)
    segs = (seg_own[:, :, None], segs_full[:, :, None], segs_full[:, None, :])

    target_parts = my_rows(targets, 1).reshape(count, length, rows, targets.shape[2])
    target_parts = jnp.transpose(target_parts, (0, 2, 1, 3))
    lane = p1_b.shape[0]
    proj_biases = jnp.concatenate(
        [
            p1_b.astype(F32)[None],
            jnp.pad(p3_b.astype(F32), (0, lane - p3_b.shape[0]))[None],
            jnp.zeros((MOD_ROWS - 2, lane), F32),
        ],
        axis=0,
    )
    gather = ColumnGather((p1_w, p2_w, p3_w.T), PROJECTOR_AXES, target_parts, proj_biases)

    u = to_rows(block_eight_input)
    sizes = Shapes(u, own, count)
    mods, bias_all, other, attend_one, carried = open_forward(
        sizes, u, cond_pad.reshape(-1, width), ada_w[0].T, ada_b, biases, segs, own, sections,
        (gather,),
    )
    *proj_weights, target_all, proj_bias_all = carried[0]
    mlp_one, carried = mlp_forward(
        sizes, 0, attend_one[0], mods, bias_all, segs, own, other,
        (ShareAlong(proj_weights, PROJECTOR_AXES, 0),),
    )
    proj_weights = carried[0]
    first_out = mlp_one[0]
    attend_two, carried = attend_forward(
        sizes, 1, first_out, mods, bias_all, segs, own, other, (ShareAlong(proj_weights, PROJECTOR_AXES, 1),)
    )
    proj_weights = carried[0]
    mlp_two, carried = mlp_forward(
        sizes, 1, attend_two[0], mods, bias_all, segs, own, other, (ShareAlong(proj_weights, PROJECTOR_AXES, 2),)
    )
    proj_weights = carried[0]
    second_out = mlp_two[0]

    grad_sent, grad_p1, grad_p2, grad_p3, proj_small = project(
        sizes, first_out, proj_weights, target_all, proj_bias_all, p2_b[None], total_token_count
    )

    back = (mods, segs, own, other)
    (d_middle_two, mod_mlp_two, *mlp_grads_two), carried = mlp_backward(
        sizes, 1, to_rows(cot), attend_two, mlp_two, *back,
        [Swap(first_out, second_out), HalfSum(grad_p1, 0, "x")],
    )
    (other_out,), (grad_p1,) = carried
    (second_grad, mod_attend_two, *attend_grads_two), carried = attend_backward(
        sizes, 1, d_middle_two, first_out, attend_two, *back,
        [YSum(grad, BF16) for grad in mlp_grads_two[:2]]
        + [HalfSum(grad_p2, 1, "x", (0, 1)), HalfSum(grad_p3, 1, "x")],
    )
    ((mlp_part_a,), (mlp_part_b,)), ((grad_p2_a,), (grad_p3,)) = carried[:2], carried[2:]
    (d_middle_one, mod_mlp_one, *mlp_grads_one), carried = mlp_backward(
        sizes, 0, second_grad + grad_sent, attend_one, mlp_one, *back,
        [YSum(grad, BF16) for grad in attend_grads_two[:2]]
        + [SectionSum(mlp_part_a, 1), HalfSum(grad_p2, 1, "x", (1, 1))]
        + [HalfSum(grad_p1, 0, "y"), HalfSum(grad_p2_a, 1, "y")],
    )
    attend_parts_two, sum_mlp_a = carried[:2], carried[2]
    (grad_p2_b,), (grad_p1,), (grad_p2_a,) = carried[3:]
    (first_grad, mod_attend_one, *attend_grads_one), carried = attend_backward(
        sizes, 0, d_middle_one, u, attend_one, *back,
        [LastSum(mlp_grads_one[0], 0), SectionSum(mlp_grads_one[1], 0, BF16)]
        + [SectionSum(part, 1) for part, in attend_parts_two]
        + [SectionSum(mlp_part_b, 1), HalfSum(grad_p2_b, 1, "y"), HalfSum(grad_p3, 1, "y")]
        + [ColumnSum((grad_p1,), 0)],
    )
    sum_mlp_c, (mlp_part_two,), sums_attend_two = carried[0], carried[1], carried[2:4]
    sums_mlp_two, ((grad_p2_b,), (grad_p3,), (red_p1_w,)) = (sum_mlp_a, carried[4]), carried[5:]

    cond_act = silu(my_rows(cond, 0).astype(F32)).astype(BF16).astype(F32)
    share = width // replicas
    cond_cols = jnp.pad(cond_act.reshape(used, width), ((0, MOD_ROWS - used), (0, 0)))
    cond_cols = jnp.transpose(cond_cols.reshape(MOD_ROWS, replicas, share), (1, 0, 2))
    small = [
        attend_grads_one[2], attend_grads_one[3], mlp_grads_one[2], mlp_grads_one[3],
        attend_grads_two[2], attend_grads_two[3], mlp_grads_two[2], mlp_grads_two[3],
    ]
    (section_grad, grad_ada_w, grad_ada_b, small, proj_small), carried = close_backward(
        sizes, (first_grad, second_grad),
        (mod_attend_one, mod_mlp_one, mod_attend_two, mod_mlp_two),
        small, proj_small, cond_cols, sections, replicas,
        [LastSum(grad, 0) for grad in attend_grads_one[:2]]
        + [YSum(mlp_part_two, F32)]
        + [ColumnSum((grad_p2_a, grad_p2_b), 1), ColumnSum((grad_p3,), 1)],
    )
    sums_attend_one, sums_mlp_one = carried[:2], (sum_mlp_c, carried[2])
    (red_p2_w,), (red_p3_w,) = carried[3:]

    own_out = jnp.where(is_first, first_out, second_out)
    section_out = jnp.where(
        is_first,
        jnp.concatenate([own_out, other_out], axis=0),
        jnp.concatenate([other_out, own_out], axis=0),
    )
    section_out = jnp.transpose(section_out, (1, 0, 2))[None]
    choices = [
        (one[0], two[0])
        for one, two in zip(
            list(sums_mlp_one) + list(sums_attend_one), list(sums_mlp_two) + list(sums_attend_two)
        )
    ]
    if replicas == 4:
        alone = [grad_ada_w, grad_ada_b, red_p1_w, red_p2_w, red_p3_w]
        final = assemble(choices, alone, section_grad, small, proj_small, heads_width)
        red_fc1, red_fc2, grad_ada_w, grad_ada_b, red_p1_w, red_p2_w, red_p3_w = final[:7]
        section_grad, red_qkv, red_out, qv_b, out_b, fc1_b, fc2_b, p1_sum, p2_sum, p3_sum, loss = (
            final[7:]
        )
        red_p1_b, red_p2_b, red_p3_b = p1_sum[0], p2_sum[0], p3_sum[0]
        loss_total = loss[0, 0]
    else:
        red_fc1, red_fc2, red_qkv, red_out = [
            sum_beyond_quads(jnp.where(is_first, one, two)) for one, two in choices
        ]
        red_qkv = jnp.transpose(red_qkv.reshape(-1, 3, heads_width), (1, 0, 2))
        red_out = red_out.T
        red_p1_w = sum_beyond_quads(red_p1_w)
        red_p2_w, red_p3_w = sum_beyond_quads(red_p2_w.T).T, sum_beyond_quads(red_p3_w.T).T
        section_grad = jnp.transpose(section_grad, (1, 0, 2))
        qv_b = jnp.stack([small[0, :heads_width], small[0, 2 * heads_width : 3 * heads_width]])
        out_b, fc1_b, fc2_b = small[2:3], small[3:4], small[4:5]
        red_p1_b, red_p2_b = proj_small[0], proj_small[2:6].reshape(-1)
        red_p3_b, loss_total = proj_small[1, : p3_b.shape[0]], proj_small[6, 0]
    align_loss = -0.5 * loss_total / total_token_count
    return (
        section_out,
        section_grad[None],
        align_loss,
        grad_ada_w[None],
        grad_ada_b,
        jnp.transpose(red_qkv, (1, 0, 2))[None],
        qv_b[None],
        red_out[None],
        out_b,
        red_fc1[None],
        fc1_b[:, :hidden],
        red_fc2.T[None],
        fc2_b,
        red_p1_w,
        red_p1_b,
        red_p2_w,
        red_p2_b[: p2_b.shape[0]],
        red_p3_w.T,
        red_p3_b,
    )


def solution(mesh):
    in_specs = (
        P("tensor", "dp", None),
        P("dp", None, None),
        P("dp", None),
        P(None, "dp", "tensor"),
        P("tensor", "dp", None),
        P("section", None, "tensor"),
        P("section", "tensor"),
        P("section", None, None, "tensor"),
        P("section", None, "tensor"),
        P("section", "tensor", None),
        P("section", None),
        P("section", None, "tensor"),
        P("section", "tensor"),
        P("section", "tensor", None),
        P("section", None),
        P(None, "tensor"),
        P("tensor"),
        P("tensor", None),
        P(),
        P(None, "tensor"),
        P("tensor"),
    )
    out_specs = (
        P("section", "tensor", "dp", None),
        P("section", "tensor", "dp", None),
        P(),
        P("section", "dp", "tensor"),
        P("section", "tensor"),
        P("section", "dp", None, "tensor"),
        P("section", None, "tensor"),
        P("section", "tensor", "dp"),
        P("section", None),
        P("section", "dp", "tensor"),
        P("section", "tensor"),
        P("section", "tensor", "dp"),
        P("section", None),
        P(("section", "dp"), "tensor"),
        P("tensor"),
        P("tensor", ("section", "dp")),
        P(),
        P(("section", "dp"), "tensor"),
        P("tensor"),
    )
    return jax.shard_map(
        per_device, mesh=mesh, in_specs=in_specs, out_specs=out_specs, check_vma=False
    )
```

```python
import functools
import math

import jax
import jax.numpy as jnp
from jax import lax
from jax.experimental import pallas as pl
from jax.experimental.pallas import tpu as pltpu
from jax.sharding import PartitionSpec as P

HEAD_WIDTH = 72
HEAD_LANES = 128
IMAGES_PER_ROW = 3
NORM_EPS = 1e-06
COSINE_EPS = 1e-06
MASKED_SCORE = -1e30
HIGHEST = lax.Precision.HIGHEST
MESH = pl.DeviceIdType.MESH
F32 = jnp.float32
BF16 = jnp.bfloat16
NN = (((1,), (0,)), ((), ()))
NT = (((1,), (1,)), ((), ()))
TN = (((0,), (0,)), ((), ()))


def dot(left, right, form=NN):
    return lax.dot_general(left, right, form, preferred_element_type=F32)


def z_peers(count):
    me = lax.axis_index("tensor")
    return [{"tensor": lax.rem(me + step, count)} for step in range(1, count)]


def x_peer():
    return {"section": 1 - lax.axis_index("section")}


def core_bit():
    return lax.rem(lax.axis_index("dp"), 2)


def y_bit():
    return lax.rem(lax.axis_index("dp") // 2, 2)


def core_peer():
    return {"dp": lax.axis_index("dp") + 1 - 2 * core_bit()}


def y_peer():
    return {"dp": lax.axis_index("dp") + 2 - 4 * y_bit()}


def greet(peers):
    barrier = pltpu.get_barrier_semaphore()
    for peer in peers:
        pl.semaphore_signal(barrier, inc=1, device_id=peer, device_id_type=MESH)
    pl.semaphore_wait(barrier, len(peers))


def remote(source, target, send_sem, recv_sem, peer):
    copy = describe(source, target, send_sem, recv_sem, peer)
    copy.start()
    return copy


def local(source, target, sem):
    copy = pltpu.make_async_copy(source, target, sem)
    copy.start()
    return copy


def own_rows(me, length):
    return pl.ds(pl.multiple_of(me * length, 16), length)


def describe(source, target, send_sem, recv_sem, peer):
    return pltpu.make_async_remote_copy(
        src_ref=source,
        dst_ref=target,
        send_sem=send_sem,
        recv_sem=recv_sem,
        device_id=peer,
        device_id_type=MESH,
    )


def wait_all(copies):
    for copy in copies:
        copy.wait()


class Line:
    def __init__(self, length, sems):
        self.length, (self.ag_send, self.ag_recv, self.rs_send, self.rs_recv) = length, sems
        self.me = lax.axis_index("tensor")
        self.mirror = 3 - self.me
        self.near = self.me + 1 - 2 * lax.rem(self.me, 2)
        self.opposite = lax.rem(self.me + 2, 4)
        self.is_end = jnp.logical_or(self.me == 0, self.me == 3)
        self.is_middle = jnp.logical_not(self.is_end)

    def block(self, full, place, which, peer):
        part = full.at[:, own_rows(place, self.length)]
        return describe(
            part, part, self.ag_send.at[which], self.ag_recv.at[place], {"tensor": peer}
        )

    def start_gather(self, full):
        self.block(full, self.me, 0, self.opposite).start()
        self.block(full, self.me, 1, self.near).start()

        @pl.when(self.is_middle)
        def to_mirror():
            self.block(full, self.me, 2, self.mirror).start()

    def relay(self, full):
        self.block(full, self.opposite, 2, self.mirror).wait_recv()

        @pl.when(self.is_middle)
        def pass_on():
            self.block(full, self.opposite, 3, 3 - self.opposite).start()

    def arrived(self, full, place):
        self.block(full, place, 1, self.near).wait_recv()

    def finish_gather(self, full):
        self.arrived(full, self.near)
        self.arrived(full, self.mirror)
        self.sent(full)

    def sent(self, full):
        self.block(full, self.me, 0, self.opposite).wait_send()
        self.block(full, self.me, 1, self.near).wait_send()

        @pl.when(self.is_middle)
        def more_sent():
            self.block(full, self.me, 2, self.mirror).wait_send()
            self.block(full, self.opposite, 3, 3 - self.opposite).wait_send()

    def scatter_sum(self, partial, buffers, prepare=lambda place: None):
        send_buf, recv_buf, relay_buf = buffers
        me, relay_sem = self.me, 4

        def term(peer):
            return partial(own_rows(peer, self.length))

        def keep(which, value):
            send_buf[which] = value.astype(BF16).reshape(send_buf.shape[1:])

        self.to_mirror = describe(
            send_buf.at[0], recv_buf.at[me], self.rs_send.at[0], self.rs_recv.at[me],
            {"tensor": self.mirror},
        )
        self.to_relay = describe(
            send_buf.at[0], relay_buf, self.rs_send.at[0], self.rs_recv.at[relay_sem],
            {"tensor": self.near},
        )
        self.to_near = describe(
            send_buf.at[1], recv_buf.at[me], self.rs_send.at[1], self.rs_recv.at[me],
            {"tensor": self.near},
        )
        self.to_opposite = describe(
            send_buf.at[2], recv_buf.at[me], self.rs_send.at[2], self.rs_recv.at[me],
            {"tensor": self.opposite},
        )
        prepare(self.mirror)
        keep(0, term(self.mirror))

        @pl.when(self.is_end)
        def first_end():
            self.to_relay.start()
            relay_buf[...] = jnp.zeros_like(relay_buf)
            recv_buf[self.mirror] = jnp.zeros(recv_buf.shape[1:], BF16)

        @pl.when(self.is_middle)
        def first_middle():
            self.to_mirror.start()

        prepare(self.near)
        keep(1, term(self.near))
        self.to_near.start()
        last = term(self.opposite)

        @pl.when(self.is_middle)
        def relayed():
            self.to_relay.wait_recv()

        keep(2, last + relay_buf[...].reshape(last.shape).astype(F32))
        self.to_opposite.start()
        return term(me)

    def finish_sum(self, total, buffers):
        send_buf, recv_buf, relay_buf = buffers

        def got(source):
            describe(
                send_buf.at[1], recv_buf.at[source], self.rs_send.at[1], self.rs_recv.at[source],
                {"tensor": self.near},
            ).wait_recv()

        got(self.near)
        got(self.opposite)

        @pl.when(self.is_middle)
        def third():
            got(self.mirror)

        self.to_near.wait_send()
        self.to_opposite.wait_send()
        self.to_mirror.wait_send()
        for source in (self.near, self.opposite, self.mirror):
            total = total + recv_buf[source].reshape(total.shape).astype(F32)
        return total


def fetch(block, own_ref, other_ref, target, sem):
    mine = lax.axis_index("section") == block

    @pl.when(mine)
    def own_start():
        pltpu.make_async_copy(own_ref, target, sem).start()

    @pl.when(jnp.logical_not(mine))
    def other_start():
        pltpu.make_async_copy(other_ref, target, sem).start()

    return pltpu.make_async_copy(own_ref, target, sem)


def layer_norm(rows):
    centred = rows - jnp.mean(rows, axis=-1, keepdims=True)
    inverse = lax.rsqrt(jnp.mean(centred * centred, axis=-1, keepdims=True) + NORM_EPS)
    return centred * inverse, inverse


def norm_back(grad, normed, inverse):
    mean_grad = jnp.mean(grad, axis=-1, keepdims=True)
    mean_cross = jnp.mean(grad * normed, axis=-1, keepdims=True)
    return inverse * (grad - mean_grad - normed * mean_cross)


def token_mod(mod_ref, seg_ref, which):
    parts = []
    for row in range(seg_ref.shape[0]):
        seg = seg_ref[row]
        line = [
            mod_ref[which, pl.ds(row * IMAGES_PER_ROW + slot, 1), :]
            for slot in range(IMAGES_PER_ROW)
        ]
        value = line[-1]
        for slot in range(IMAGES_PER_ROW - 2, -1, -1):
            value = jnp.where(seg == slot, line[slot], value)
        parts.append(value)
    return jnp.concatenate(parts, axis=0)


def slot_sums(value, seg_ref, out_ref, which):
    length = seg_ref.shape[1]
    lines = []
    for row in range(seg_ref.shape[0]):
        seg = seg_ref[row]
        piece = value[row * length : (row + 1) * length]
        for slot in range(IMAGES_PER_ROW):
            lines.append(jnp.sum(jnp.where(seg == slot, piece, 0.0), axis=0, keepdims=True))
    spare = out_ref.shape[1] - len(lines)
    lines.append(jnp.zeros((spare, value.shape[1]), F32))
    out_ref[which] = jnp.concatenate(lines, axis=0)


def flat(ref):
    return ref[...].reshape(-1, ref.shape[-1])


def spread_matrix(width, which=0, total=None):
    lanes = width // HEAD_WIDTH * HEAD_LANES
    shape = (total or width, lanes)
    source = lax.broadcasted_iota(jnp.int32, shape, 0)
    target = lax.broadcasted_iota(jnp.int32, shape, 1)
    within = target & (HEAD_LANES - 1)
    head = target >> (HEAD_LANES.bit_length() - 1)
    hit = (within < HEAD_WIDTH) & (source == which * width + head * HEAD_WIDTH + within)
    return jnp.where(hit, 1.0, 0.0).astype(BF16)


def gelu_tanh(pre):
    inner = math.sqrt(2.0 / math.pi) * (pre + 0.044715 * (pre * pre * pre))
    return 0.5 * pre * (1.0 + jnp.tanh(inner))


def gelu_slope(pre):
    scale = math.sqrt(2.0 / math.pi)
    square = pre * pre
    tanh = jnp.tanh(scale * (pre + 0.044715 * (pre * square)))
    return 0.5 * (1.0 + tanh) + 0.5 * pre * (1.0 - tanh * tanh) * scale * (
        1.0 + 3 * 0.044715 * square
    )


def silu(value):
    return value / (1.0 + jnp.exp(-value))


class Share:
    def __init__(self, own, other, parts, sems):
        self.own, self.other, self.parts = own, other, parts
        self.send, self.recv = sems
        self.size = own.shape[0] // parts
        self.copies = []

    def rows(self, core, y):
        part = core if self.parts == 2 else core + 2 * y
        return pl.ds(pl.multiple_of(part * self.size, 16), self.size)

    def begin(self):
        rows = self.rows(core_bit(), y_bit())
        self.first = remote(
            self.own.at[rows], self.other.at[rows], self.send.at[0], self.recv.at[0], x_peer()
        )

    def forward(self, first):
        if first is not None:
            first.wait()
        mine = self.other.at[self.rows(core_bit(), y_bit())]
        self.copies.append(remote(mine, mine, self.send.at[1], self.recv.at[1], core_peer()))
        if self.parts == 4:
            self.second = remote(mine, mine, self.send.at[2], self.recv.at[2], y_peer())

    def forward_again(self):
        if self.parts == 4:
            self.second.wait()
            got = self.other.at[self.rows(core_bit(), 1 - y_bit())]
            self.copies.append(remote(got, got, self.send.at[3], self.recv.at[3], core_peer()))

    def finish(self):
        wait_all(self.copies)


class Cargo:
    inputs, outs, scratch, aliases, any_outs = (), (), (), {}, False

    def bind(self, inputs, outs, scratch):
        self.ins, self.out_refs, self.held = inputs, outs, scratch

    def peers(self):
        return []

    def begin(self):
        pass

    def middle(self):
        pass

    def late(self):
        pass

    def end(self):
        pass


def quarter(shape):
    return shape[:-2] + (shape[-2] // 4, shape[-1])


class CoreSum:
    def __init__(self, whole, got, out, sems):
        self.whole, self.got, self.out, self.sems = whole, got, out, sems
        self.size = whole.shape[-2] // 4

    def rows(self, core, y):
        part = pl.ds(pl.multiple_of((core + 2 * y) * self.size, 16), self.size)
        whole = self.whole
        return whole.at[:, part] if len(whole.shape) == 3 else whole.at[part]

    def begin(self):
        self.copies = [
            remote(
                self.rows(1 - core_bit(), y), self.got.at[y],
                self.sems.at[0, y], self.sems.at[1, y], core_peer(),
            )
            for y in range(2)
        ]

    def end(self):
        wait_all(self.copies)
        for y in range(2):
            mine = self.rows(core_bit(), y)[...]
            self.out[y] = (mine.astype(F32) + self.got[y].astype(F32)).astype(BF16)


def core_sum_scratch(shape):
    return [
        pltpu.VMEM(shape, BF16),
        pltpu.VMEM((2,) + quarter(shape), BF16),
        pltpu.SemaphoreType.DMA((2, 2)),
    ]


class YSum(Cargo):
    def __init__(self, parts, dtype):
        part = parts.shape[1:]
        self.inputs = (parts,)
        self.outs = ((part, dtype),)
        self.scratch = (
            pltpu.VMEM(part, BF16),
            pltpu.VMEM(part, BF16),
            pltpu.SemaphoreType.DMA((3,)),
        )

    def peers(self):
        return ["y"]

    def begin(self):
        mine, other, sems = self.held
        self.copies = [
            remote(self.ins[0].at[1 - y_bit()], other, sems.at[0], sems.at[1], y_peer()),
            local(self.ins[0].at[y_bit()], mine, sems.at[2]),
        ]

    def end(self):
        mine, other, sems = self.held
        out = self.out_refs[0]
        wait_all(self.copies)
        out[...] = (mine[...].astype(F32) + other[...].astype(F32)).astype(out.dtype)


class SectionSum(Cargo):
    def __init__(self, part, owner, dtype=F32):
        self.owner = owner
        self.inputs = (part,)
        self.outs = ((part.shape, dtype),)
        self.scratch = (
            pltpu.VMEM(part.shape, BF16),
            pltpu.VMEM(part.shape, BF16),
            pltpu.SemaphoreType.DMA((3,)),
        )

    def peers(self):
        return ["x"]

    def source(self):
        return self.ins[0]

    def begin(self):
        mine, other, sems = self.held
        self.copy = describe(self.source(), other, sems.at[0], sems.at[1], x_peer())
        self.load = pltpu.make_async_copy(self.source(), mine, sems.at[2])
        is_owner = lax.axis_index("section") == self.owner

        @pl.when(is_owner)
        def take():
            self.load.start()

        @pl.when(jnp.logical_not(is_owner))
        def give():
            self.copy.start()

    def end(self):
        mine, other, sems = self.held
        is_owner = lax.axis_index("section") == self.owner

        @pl.when(is_owner)
        def add():
            self.load.wait()
            self.copy.wait_recv()
            out = self.out_refs[0]
            out[...] = (mine[...].astype(F32) + other[...].astype(F32)).astype(out.dtype)

        @pl.when(jnp.logical_not(is_owner))
        def given():
            self.copy.wait_send()
            self.out_refs[0][...] = jnp.zeros_like(self.out_refs[0])


class LastSum(YSum):
    def __init__(self, parts, owner):
        super().__init__(parts, F32)
        part = parts.shape[1:]
        self.owner = owner
        self.scratch = self.scratch + (
            pltpu.VMEM(part, BF16),
            pltpu.VMEM(part, BF16),
            pltpu.SemaphoreType.DMA((2,)),
        )

    def peers(self):
        return ["y", "x"]

    def begin(self):
        self.held, self.last = self.held[:3], self.held[3:]
        super().begin()

    def middle(self):
        mine, other, sems = self.held
        total, got, last_sems = self.last
        wait_all(self.copies)
        total[...] = (mine[...].astype(F32) + other[...].astype(F32)).astype(BF16)
        self.copy = describe(total, got, last_sems.at[0], last_sems.at[1], x_peer())

        @pl.when(lax.axis_index("section") != self.owner)
        def give():
            self.copy.start()

    def end(self):
        total, got, last_sems = self.last
        is_owner = lax.axis_index("section") == self.owner

        @pl.when(is_owner)
        def add():
            self.copy.wait_recv()
            self.out_refs[0][...] = total[...].astype(F32) + got[...].astype(F32)

        @pl.when(jnp.logical_not(is_owner))
        def given():
            self.copy.wait_send()
            self.out_refs[0][...] = jnp.zeros_like(self.out_refs[0])


class Swap(Cargo):
    def __init__(self, one, two):
        self.inputs = (one, two)
        self.outs = ((one.shape, one.dtype),)
        self.scratch = (pltpu.VMEM(one.shape, one.dtype), pltpu.SemaphoreType.DMA((2,)))

    def peers(self):
        return ["x"]

    def begin(self):
        got, sems = self.held
        one, two = self.ins
        self.copy = describe(two, got, sems.at[0], sems.at[1], x_peer())
        is_first = lax.axis_index("section") == 0

        @pl.when(is_first)
        def give_two():
            self.copy.start()

        @pl.when(jnp.logical_not(is_first))
        def give_one():
            describe(one, got, sems.at[0], sems.at[1], x_peer()).start()

    def end(self):
        self.copy.wait()
        self.out_refs[0][...] = self.held[0][...]


def span(ref, axis, start, size):
    part = pl.ds(pl.multiple_of(start, 128 if axis == 1 else 16), size)
    lead = (slice(None),) * (len(ref.shape) - 2)
    return ref.at[lead + ((slice(None), part) if axis == 1 else (part, slice(None)))]


def cut(shape, axis, by):
    shape = list(shape)
    shape[axis - 2] //= by
    return tuple(shape)


class HalfSum(Cargo):
    def __init__(self, grad, axis, name, slots=None):
        self.slots = slots if slots is not None else (0, grad.shape[0])
        part = cut((self.slots[1],) + grad.shape[1:], axis, 2)
        self.axis, self.name, self.size = axis, name, part[axis - 2]
        self.inputs = (grad,)
        self.outs = ((part, BF16),)
        self.scratch = (
            pltpu.VMEM(part, BF16),
            pltpu.VMEM(part, BF16),
            pltpu.SemaphoreType.DMA((3,)),
        )

    def peers(self):
        return [self.name]

    def begin(self):
        mine, other, sems = self.held
        if self.name == "x":
            bit, peer = lax.axis_index("section"), x_peer()
        else:
            bit, peer = y_bit(), y_peer()
        grad = self.ins[0].at[pl.ds(*self.slots)]
        self.copies = [
            remote(
                span(grad, self.axis, (1 - bit) * self.size, self.size), other,
                sems.at[0], sems.at[1], peer,
            ),
            local(span(grad, self.axis, bit * self.size, self.size), mine, sems.at[2]),
        ]

    def end(self):
        mine, other, sems = self.held
        wait_all(self.copies)
        self.out_refs[0][...] = (mine[...].astype(F32) + other[...].astype(F32)).astype(BF16)


class ColumnGather(Cargo):
    any_outs = True

    def __init__(self, weights, axes, targets, biases):
        self.axes = axes
        self.inputs = (*weights, targets, biases)
        self.outs = tuple(((2,) + one.shape, BF16) for one in weights) + (
            ((2, 2) + targets.shape[1:], BF16),
            ((2, 2) + biases.shape, F32),
        )
        self.scratch = (
            pltpu.SemaphoreType.DMA((5, 6)),
            pltpu.SemaphoreType.DMA((5, 2, 2)),
            pltpu.SemaphoreType.DMA((5,)),
        )

    def peers(self):
        return ["core", "cross"]

    def pieces(self, target):
        tensor, core = lax.axis_index("tensor"), core_bit()
        eighth = lax.axis_index("section") * 4 + y_bit() * 2 + core
        slot, out = lax.rem(tensor, 2), []
        for source, place, axis in zip(self.ins[:3], self.out_refs[:3], self.axes):
            size = source.shape[axis] // 8
            out.append(
                (
                    span(source, axis, eighth * size, size),
                    span(place.at[slot], axis, eighth * size, size),
                )
            )
        out.append((self.ins[3].at[target], self.out_refs[3].at[slot, core]))
        out.append((self.ins[4], self.out_refs[4].at[slot, core]))
        return out

    def copies(self, step):
        tensor, core = lax.axis_index("tensor"), core_bit()
        send, recv, own = self.held
        target = lax.rem(tensor + step, 4)
        peer = {"tensor": target, "dp": lax.axis_index("dp") - core + tensor // 2}
        return [
            describe(source, place, send.at[i, step], recv.at[i, lax.rem(tensor, 2), core], peer)
            for i, (source, place) in enumerate(self.pieces(target))
        ]

    def stays(self):
        return core_bit() == lax.axis_index("tensor") // 2

    def own_copies(self):
        own = self.held[2]
        return [
            pltpu.make_async_copy(source, place, own.at[i])
            for i, (source, place) in enumerate(self.pieces(lax.axis_index("tensor")))
        ]

    def direct(self, step, i):
        if step == 2 or i > 2:
            return None
        return lax.axis_index("tensor") != (3 if step == 1 else 0)

    def each(self, which, act):
        for step in range(1, 4):
            for i, copy in enumerate(self.copies(step)):
                if i in which:
                    allowed = self.direct(step, i)
                    if allowed is None:
                        act(copy)
                    else:

                        @pl.when(allowed)
                        def go(copy=copy):
                            act(copy)

    def start(self, which):
        self.each(which, lambda copy: copy.start())

        @pl.when(self.stays())
        def keep():
            for i, copy in enumerate(self.own_copies()):
                if i in which:
                    copy.start()

        @pl.when(jnp.logical_not(self.stays()))
        def give():
            for i, copy in enumerate(self.copies(0)):
                if i in which:
                    copy.start()

    def passes_on(self):
        tensor, core = lax.axis_index("tensor"), core_bit()
        return jnp.logical_or(
            jnp.logical_and(tensor == 2, core == 0), jnp.logical_and(tensor == 1, core == 1)
        )

    def passed(self, i, other):
        send, recv, own = self.held
        tensor, slot = lax.axis_index("tensor"), core_bit()
        size = self.ins[i].shape[self.axes[i]] // 8
        eighth = lax.axis_index("section") * 4 + y_bit() * 2 + other
        part = span(self.out_refs[i].at[slot], self.axes[i], eighth * size, size)
        return describe(
            part, part, send.at[i, 4 + other], recv.at[i, slot, other], {"tensor": 3 * (tensor - 1)}
        )

    def relay(self, which):
        @pl.when(self.passes_on())
        def pass_on():
            for i in which:
                for other in range(2):
                    copy = self.passed(i, other)
                    copy.wait_recv()
                    copy.start()

    def begin(self):
        self.start((3, 4))

    def middle(self):
        self.start((0, 2))

    def end(self):
        send, recv, own = self.held
        tensor, core = lax.axis_index("tensor"), core_bit()
        self.each(range(5), lambda copy: copy.wait_send())

        @pl.when(self.stays())
        def kept():
            for copy in self.own_copies():
                copy.wait()

        @pl.when(jnp.logical_not(self.stays()))
        def given():
            for copy in self.copies(0):
                copy.wait_send()

        @pl.when(self.passes_on())
        def passed_on():
            for i in range(3):
                for other in range(2):
                    self.passed(i, other).wait_send()

        for slot in range(2):
            for other in range(2):
                mine = jnp.logical_and(2 * core + slot == tensor, core == other)
                relayed = jnp.logical_and(self.passes_on(), core == slot)
                peer = {"tensor": lax.rem(tensor + 1, 4)}
                waits = [
                    describe(source, place, send.at[i, 1], recv.at[i, slot, other], peer)
                    for i, (source, place) in enumerate(self.pieces(tensor))
                ]

                @pl.when(jnp.logical_not(mine))
                def arrived(waits=waits):
                    for copy in waits[3:]:
                        copy.wait_recv()

                @pl.when(jnp.logical_not(jnp.logical_or(mine, relayed)))
                def weights_arrived(waits=waits):
                    for copy in waits[:3]:
                        copy.wait_recv()


class ShareAlong(Cargo):
    any_outs = True

    def __init__(self, weights, axes, stage):
        self.axes = axes
        self.inputs = tuple(weights)
        self.outs = tuple((one.shape, BF16) for one in weights)
        self.aliases = {0: 0, 1: 1, 2: 2}
        self.stage = stage
        self.scratch = (pltpu.SemaphoreType.DMA((4,)), pltpu.SemaphoreType.DMA((4,)))

    def peers(self):
        return ["x", "y"]

    def begin(self):
        send, recv = self.held
        section, y, self.copies = lax.axis_index("section"), y_bit(), []

        def give(which, start, parts, peer):
            ref, axis = self.out_refs[which], self.axes[which]
            size = ref.shape[axis + 1] // 4
            part = span(ref, axis, start * size, parts * size)
            i = len(self.copies)
            self.copies.append(remote(part, part, send.at[i], recv.at[i], peer))

        if self.stage == 0:
            give(1, 2 * section + y, 1, x_peer())
            give(0, 2 * section + y, 1, y_peer())
            give(2, 2 * section + y, 1, y_peer())
        elif self.stage == 1:
            give(0, 2 * section, 2, x_peer())
            give(1, y, 1, y_peer())
        else:
            give(2, 2 * section, 2, x_peer())
            give(1, 2 + y, 1, y_peer())

    def end(self):
        wait_all(self.copies)


class ColumnSum(Cargo):
    def __init__(self, grads, axis):
        self.axis = axis
        self.part = cut(grads[0].shape[1:], axis, 2)
        self.inputs = tuple(grads)
        self.outs = ((self.part, F32),)
        self.scratch = (
            pltpu.VMEM((4,) + self.part, BF16),
            pltpu.SemaphoreType.DMA((4,)),
            pltpu.SemaphoreType.DMA((4,)),
            pltpu.SemaphoreType.DMA,
        )

    def peers(self):
        return ["core", "cross"]

    def copy(self, slot, other):
        got, send, recv, own = self.held
        tensor, core = lax.axis_index("tensor"), core_bit()
        size = self.part[self.axis]
        ref = self.ins[0].at[slot] if len(self.ins) == 1 else self.ins[slot].at[0]
        source = span(ref, self.axis, other * size, size)
        peer = {"tensor": 2 * core + slot, "dp": lax.axis_index("dp") - core + other}
        mine = jnp.logical_and(2 * core + slot == tensor, core == other)
        away = describe(source, got.at[tensor], send.at[2 * slot + other], recv.at[tensor], peer)
        return mine, away, pltpu.make_async_copy(source, got.at[tensor], own)

    def each(self, act_away, act_own):
        for slot in range(2):
            for other in range(2):
                mine, away, own = self.copy(slot, other)

                @pl.when(mine)
                def stay(own=own):
                    act_own(own)

                @pl.when(jnp.logical_not(mine))
                def leave(away=away):
                    act_away(away)

    def begin(self):
        self.each(lambda copy: copy.start(), lambda copy: copy.start())

    def end(self):
        got, send, recv, own = self.held
        tensor, core = lax.axis_index("tensor"), core_bit()
        self.each(lambda copy: copy.wait_send(), lambda copy: copy.wait())
        for source in range(4):
            mine = jnp.logical_and(tensor == source, core == tensor // 2)

            @pl.when(jnp.logical_not(mine))
            def arrived(source=source):
                describe(
                    got.at[source], got.at[source], send.at[0], recv.at[source],
                    {"tensor": lax.rem(tensor + 1, 4)},
                ).wait_recv()

        total = got[0].astype(F32)
        for source in range(1, 4):
            total = total + got[source].astype(F32)
        self.out_refs[0][...] = total


def cross_peers():
    tensor, dp = lax.axis_index("tensor"), core_peer()["dp"]
    return [{"tensor": lax.rem(tensor + step, 4), "dp": dp} for step in range(1, 4)]


class Bundle:
    def __init__(self, cargos):
        self.cargos = cargos
        self.loads, self.stores = {}, {}

    def load(self):
        for copy in self.loads.values():
            copy.start()

    def need(self, *which):
        for i in which:
            if i in self.loads:
                self.loads[i].wait()

    def flush(self, *which):
        for i in which:
            if i in self.stores:
                self.stores[i].start()

    def peers(self, names=()):
        names = list(names) + [name for cargo in self.cargos for name in cargo.peers()]
        known = {"core": core_peer, "y": y_peer, "x": x_peer}
        cross = cross_peers() if "cross" in names else []
        return [make() for name, make in known.items() if name in names] + cross

    def begin(self):
        for cargo in self.cargos:
            cargo.begin()

    def middle(self):
        for cargo in self.cargos:
            cargo.middle()

    def late(self):
        for cargo in self.cargos:
            cargo.late()

    def end(self):
        for copy in self.stores.values():
            copy.wait()
        for cargo in self.cargos:
            cargo.end()


def attend_body(
    count, peers, u_ref, mods, segs, biases, outs, scratch, sems, need_qkv, need_out, steps, flush
):
    middle_ref, branch_ref, full_ref, q_ref, k_ref, v_ref, probs_ref, mixed_ref = outs
    full, wqkv, wo, mixed_wide = (full_ref, *scratch[:3])
    buffers, spreads = scratch[3:6], scratch[6]
    seg_own, seg_col, seg_row = segs
    mod_ref = mods()
    me = lax.axis_index("tensor")
    rows, length, width = u_ref.shape
    heads_width = wo.shape[0]
    heads = heads_width // HEAD_WIDTH
    u = flat(u_ref).astype(F32)
    normed, unused = layer_norm(u)
    attn_in = normed * (1.0 + token_mod(mod_ref, seg_own, 1)) + token_mod(mod_ref, seg_own, 0)
    full[:, own_rows(me, length), :] = attn_in.astype(BF16).reshape(rows, length, width)
    if peers is not None:
        greet(peers)
    line = Line(length, sems)
    line.start_gather(full)
    spread = spread_matrix(heads_width)
    line.relay(full)
    steps[0]()
    both = 3 * heads_width
    for which in range(3):
        spreads[which] = spread_matrix(heads_width, which, both)
    need_qkv()
    line.finish_gather(full)
    flush(2)
    tokens = flat(full)
    bias = biases()
    projected = (dot(tokens, wqkv[...]) + bias[0:1, :both]).astype(BF16)
    for which, target in enumerate((q_ref, k_ref, v_ref)):
        parts = dot(projected, spreads[which])
        target[...] = parts.astype(BF16).reshape(target.shape)

    def one_head(index, carry):
        row = index // heads
        head = lax.rem(index, heads)
        lanes = pl.ds(pl.multiple_of(head * HEAD_LANES, HEAD_LANES), HEAD_LANES)
        scores = dot(q_ref[row, :, lanes], k_ref[row, :, lanes], NT) * HEAD_WIDTH ** (-0.5)
        scores = jnp.where(seg_col[row] == seg_row[row], scores, MASKED_SCORE)
        raised = jnp.exp(scores - jnp.max(scores, axis=-1, keepdims=True))
        probs = raised / jnp.sum(raised, axis=-1, keepdims=True)
        probs_ref[index] = probs
        mixed_wide[row, :, lanes] = dot(probs.astype(BF16), v_ref[row, :, lanes]).astype(BF16)
        return carry

    steps[1]()
    lax.fori_loop(0, rows * heads, one_head, 0, unroll=4)
    mixed_ref[...] = dot(flat(mixed_wide), spread, NT).astype(BF16).reshape(mixed_ref.shape)
    flush(3, 4, 5, 6, 7)
    need_out()

    def partial(which_rows):
        return dot(mixed_ref[:, which_rows, :].reshape(rows * length, heads_width), wo[...])

    total = line.scatter_sum(partial, buffers)
    steps[2]()
    branch = line.finish_sum(total, buffers) + bias[2:3, :]
    branch_ref[...] = branch.reshape(branch_ref.shape)
    middle = flat(u_ref).astype(F32) + token_mod(mod_ref, seg_own, 2) * branch
    middle_ref[...] = middle.reshape(middle_ref.shape)


def open_kernel(count, sections, *refs, cargo):
    u_ref, cond_ref, ada_b_ref, biases_ref, seg_own, seg_col, seg_row = refs[:7]
    ada_w, own_qkv, own_out, own_one, own_two = refs[7:12]
    mods_ref, bias_ref, other_qkv, other_out, other_one, other_two = refs[12:18]
    outs = refs[18:26]
    scratch = refs[26:33]
    ada, mod_src, mod_buf, bias_buf, w_sem, ag_send, ag_recv, rs_send, rs_recv = refs[33:42]
    mod_send, mod_recv, share_send, share_recv, ada_sem = refs[42:]
    wqkv, wo = scratch[:2]
    section, tensor = lax.axis_index("section"), lax.axis_index("tensor")
    load_ada = local(ada_w, ada, ada_sem)
    shares = [
        Share(own, other, parts, (share_send.at[i], share_recv.at[i]))
        for i, (own, other, parts) in enumerate(
            (
                (own_qkv, other_qkv, 4), (own_out, other_out, 2),
                (own_one, other_one, 4), (own_two, other_two, 4),
            )
        )
    ]
    plane = [
        {"section": lax.rem(section + a, sections), "tensor": lax.rem(tensor + b, count)}
        for a in range(sections)
        for b in range(count)
        if a or b
    ]
    greet(plane + [core_peer(), y_peer()] + cross_peers())
    cond_act = silu(cond_ref[...].astype(F32)).astype(BF16)
    load_ada.wait()
    mod = dot(cond_act, ada[...], NT) + ada_b_ref[...].astype(F32)
    mod_src[...] = mod.reshape(mod_src.shape)
    mod_buf[section, tensor] = mod_src[section]
    copies = [
        remote(
            mod_src.at[peer["section"]], mod_buf.at[section, tensor],
            mod_send.at[i], mod_recv.at[i], peer,
        )
        for i, peer in enumerate(plane)
    ]
    bias_buf[section] = biases_ref[...]
    bias_copy = remote(
        biases_ref, bias_buf.at[section],
        mod_send.at[len(plane)], mod_recv.at[len(plane)], x_peer(),
    )
    for share in shares:
        share.begin()
    cargo.begin()

    def mods():
        wait_all(copies)
        width, piece = mods_ref.shape[-1], mod_buf.shape[-1]
        for block in range(sections):
            for which in range(6):
                parts, at = [], which * width
                while at < (which + 1) * width:
                    end = min((at // piece + 1) * piece, (which + 1) * width)
                    start = at - at // piece * piece
                    parts.append(mod_buf[block, at // piece][:, start : start + end - at])
                    at = end
                mods_ref[block, which] = (
                    jnp.concatenate(parts, axis=1) if len(parts) > 1 else parts[0]
                )
        return mods_ref.at[0]

    def biases():
        bias_copy.wait()
        bias_ref[...] = bias_buf[...]
        return bias_buf[0]

    def need_qkv():
        fetch(0, own_qkv, other_qkv, wqkv, w_sem.at[0]).wait()

    def need_out():
        shares[1].finish()
        fetch(0, own_out, other_out, wo, w_sem.at[1]).wait()

    def after_gather():
        shares[0].forward(shares[0].first)
        cargo.middle()
        shares[1].forward(shares[1].first)
        shares[0].forward_again()
        shares[0].finish()

    def before_heads():
        cargo.late()
        shares[2].forward(shares[2].first)

    def after_scatter():
        cargo.cargos[0].start((1,))
        cargo.cargos[0].relay((0, 2))
        shares[2].forward_again()
        shares[3].forward(shares[3].first)
        shares[2].finish()

    attend_body(
        count, None, u_ref, mods, (seg_own, seg_col, seg_row), biases, outs, scratch,
        (ag_send, ag_recv, rs_send, rs_recv), need_qkv, need_out,
        (after_gather, before_heads, after_scatter),
        lambda *which: cargo.flush(*(6 + i for i in which)),
    )
    shares[3].forward_again()
    cargo.cargos[0].relay((1,))
    cargo.end()
    shares[3].finish()


def attend_kernel(count, block, *refs, cargo):
    u_ref, mods_ref, bias_ref, seg_own, seg_col, seg_row = refs[:6]
    own_qkv, other_qkv, own_out, other_out = refs[6:10]
    outs, scratch, w_sem = refs[10:18], refs[18:25], refs[25]
    load_qkv = fetch(block, own_qkv, other_qkv, scratch[0], w_sem.at[0])
    load_out = fetch(block, own_out, other_out, scratch[1], w_sem.at[1])
    attend_body(
        count, z_peers(count) + cargo.peers(), u_ref, lambda: mods_ref.at[block],
        (seg_own, seg_col, seg_row), lambda: bias_ref[block], outs, scratch, refs[26:30],
        load_qkv.wait, load_out.wait, (cargo.begin, cargo.middle, cargo.late), cargo.flush,
    )
    cargo.end()


def mlp_kernel(
    count, block,
    middle_ref, mods_ref, bias_ref, seg_own, w1_own, w1_other, w2_own, w2_other,
    out_ref, branch_ref, full_ref, pre_ref, act_ref,
    w1, w2, send_buf, recv_buf, relay_buf, w_sem, *sems, cargo,
):
    full = full_ref
    me = lax.axis_index("tensor")
    rows, length, width = middle_ref.shape
    mod_ref = mods_ref.at[block]
    load_one = fetch(block, w1_own, w1_other, w1, w_sem.at[0])
    load_two = fetch(block, w2_own, w2_other, w2, w_sem.at[1])
    normed, unused = layer_norm(flat(middle_ref))
    mlp_in = normed * (1.0 + token_mod(mod_ref, seg_own, 4)) + token_mod(mod_ref, seg_own, 3)
    full[:, own_rows(me, length), :] = mlp_in.astype(BF16).reshape(rows, length, width)
    greet(z_peers(count) + cargo.peers())
    line = Line(length, sems)
    line.start_gather(full)
    cargo.begin()
    line.relay(full)
    load_one.wait()
    load_two.wait()

    def hidden(place):
        which_rows = own_rows(place, length)
        pre = dot(full[:, which_rows, :].reshape(rows * length, width), w1[...])
        pre = pre + bias_ref[block, 3:4, : w1.shape[1]]
        pre_ref[:, which_rows, :] = pre.reshape(rows, length, -1)
        act_ref[:, which_rows, :] = gelu_tanh(pre).astype(BF16).reshape(rows, length, -1)

    def prepare(place):
        line.arrived(full, place)
        hidden(place)

    def partial(which_rows):
        return dot(act_ref[:, which_rows, :].reshape(rows * length, -1), w2[...])

    hidden(me)
    hidden(line.opposite)
    buffers = (send_buf, recv_buf, relay_buf)
    total = line.scatter_sum(partial, buffers, prepare)
    cargo.flush(2, 3, 4)
    line.sent(full)
    cargo.middle()
    branch = line.finish_sum(total, buffers) + bias_ref[block, 4:5, :]
    cargo.end()
    branch_ref[...] = branch.reshape(branch_ref.shape)
    out = flat(middle_ref) + token_mod(mod_ref, seg_own, 5) * branch
    out_ref[...] = out.astype(BF16).reshape(out_ref.shape)


def mlp_back_kernel(count, block, given, *refs, cargo):
    g_refs, refs = refs[:given], refs[given:]
    g_ref = g_refs[0]
    middle_ref, branch_ref, mods_ref, seg_own, full_ref, pre_ref, act_ref = refs[:7]
    w1_own, w1_other, w2_own, w2_other = refs[7:11]
    d_middle_ref, d_mod_ref, d_w1_ref, d_w2_ref, d_b1_ref, d_b2_ref = refs[11:17]
    full, d_pre, w1, w2, *buffers, w_sem = refs[17:25]
    sems = refs[25:29]
    w1_whole, w1_got, w1_sems, w2_whole, w2_got, w2_sems, normed_buf, g_buf = refs[29:]
    w1_sum = CoreSum(w1_whole, w1_got, d_w1_ref, w1_sems)
    w2_sum = CoreSum(w2_whole, w2_got, d_w2_ref, w2_sems)
    me = lax.axis_index("tensor")
    rows, length, width = middle_ref.shape
    mod_ref = mods_ref.at[block]
    load_one = fetch(block, w1_own, w1_other, w1, w_sem.at[0])
    load_two = fetch(block, w2_own, w2_other, w2, w_sem.at[1])
    cargo.load()
    g = flat(g_ref).astype(F32)
    if len(g_refs) > 1:
        g = g + flat(g_refs[1])
    g_buf[...] = g
    d_branch = (g * token_mod(mod_ref, seg_own, 5)).astype(BF16)
    full[:, own_rows(me, length), :] = d_branch.reshape(rows, length, width)
    greet(z_peers(count) + cargo.peers(["core"]))
    line = Line(length, sems)
    line.start_gather(full)
    cargo.begin()
    slot_sums(g * flat(branch_ref), seg_own, d_mod_ref, 2)
    line.relay(full)
    cargo.middle()
    normed, inverse = layer_norm(flat(middle_ref))
    normed_buf[...] = normed
    load_two.wait()
    cargo.need(given + 5)

    def d_hidden(place):
        which_rows = own_rows(place, length)
        d_act = dot(full[:, which_rows, :].reshape(rows * length, width), w2[...], NT)
        slope = gelu_slope(pre_ref[:, which_rows, :].reshape(rows * length, -1))
        d_pre[:, which_rows, :] = (d_act * slope).astype(BF16).reshape(rows, length, -1)

    def prepare(place):
        line.arrived(full, place)
        d_hidden(place)

    d_hidden(me)
    d_hidden(line.opposite)
    load_one.wait()

    def partial(which_rows):
        return dot(d_pre[:, which_rows, :].reshape(rows * length, -1), w1[...], NT)

    total = line.scatter_sum(partial, buffers, prepare)
    line.sent(full)
    cargo.need(given + 4, given + 6)
    w2_whole[...] = dot(flat(full), flat(act_ref), TN).astype(BF16)
    w2_sum.begin()
    w1_whole[...] = dot(flat(full_ref), flat(d_pre), TN).astype(BF16)
    w1_sum.begin()
    d_b2_ref[...] = jnp.sum(flat(full).astype(F32), axis=0, keepdims=True)
    d_b1_ref[...] = jnp.sum(flat(d_pre).astype(F32), axis=0, keepdims=True)
    d_in = line.finish_sum(total, buffers)
    normed = normed_buf[...]
    d_middle = g_buf[...] + norm_back(
        d_in * (1.0 + token_mod(mod_ref, seg_own, 4)), normed, inverse
    )
    d_middle_ref[...] = d_middle.reshape(d_middle_ref.shape)
    slot_sums(d_in, seg_own, d_mod_ref, 0)
    slot_sums(d_in * normed, seg_own, d_mod_ref, 1)
    w2_sum.end()
    w1_sum.end()
    cargo.end()


def attend_back_kernel(count, block, *refs, cargo):
    d_middle_ref, u_ref, branch_ref, mods_ref, seg_own, full_ref = refs[:6]
    q_ref, k_ref, v_ref, probs_ref, mixed_ref = refs[6:11]
    wqkv_own, wqkv_other, wo_own, wo_other = refs[11:15]
    d_in_ref, d_mod_ref, d_wqkv_ref, d_wo_ref, d_bqv_ref, d_bo_ref = refs[15:21]
    full, wide, narrow, wqkv, wo, *buffers, w_sem = refs[21:30]
    sems = refs[30:34]
    qkv_whole, qkv_got, qkv_sems, wo_whole, wo_got, wo_sems, spreads, normed_buf = refs[34:]
    qkv_sum = CoreSum(qkv_whole, qkv_got, d_wqkv_ref, qkv_sems)
    wo_sum = CoreSum(wo_whole, wo_got, d_wo_ref, wo_sems)
    me = lax.axis_index("tensor")
    rows, length, width = u_ref.shape
    heads_width = wo.shape[0]
    heads = heads_width // HEAD_WIDTH
    mod_ref = mods_ref.at[block]
    load_qkv = fetch(block, wqkv_own, wqkv_other, wqkv, w_sem.at[0])
    load_out = fetch(block, wo_own, wo_other, wo, w_sem.at[1])
    cargo.load()
    d_middle = flat(d_middle_ref)
    d_branch = (d_middle * token_mod(mod_ref, seg_own, 2)).astype(BF16)
    full[:, own_rows(me, length), :] = d_branch.reshape(rows, length, width)
    greet(z_peers(count) + cargo.peers(["core"]))
    line = Line(length, sems)
    line.start_gather(full)
    cargo.begin()
    slot_sums(d_middle * flat(branch_ref), seg_own, d_mod_ref, 2)
    line.relay(full)
    cargo.middle()
    spread = spread_matrix(heads_width)
    both = 3 * heads_width
    for which in range(3):
        spreads[which] = spread_matrix(heads_width, which, both)
    normed, inverse = layer_norm(flat(u_ref).astype(F32))
    normed_buf[...] = normed
    load_out.wait()
    line.finish_gather(full)
    d_mixed = dot(flat(full), wo[...], NT).astype(BF16)
    wide[3] = dot(d_mixed, spread).astype(BF16).reshape(wide.shape[1:])
    cargo.need(6, 7, 8, 9)

    def one_head(index, carry):
        row = index // heads
        head = lax.rem(index, heads)
        lanes = pl.ds(pl.multiple_of(head * HEAD_LANES, HEAD_LANES), HEAD_LANES)
        grad = wide[3, row, :, lanes]
        probs = probs_ref[index]
        d_probs = dot(grad, v_ref[row, :, lanes], NT)
        d_scores = (
            probs * (d_probs - jnp.sum(d_probs * probs, axis=-1, keepdims=True))
        ).astype(BF16)
        scale = HEAD_WIDTH ** (-0.5)
        wide[0, row, :, lanes] = (dot(d_scores, k_ref[row, :, lanes]) * scale).astype(BF16)
        wide[1, row, :, lanes] = (dot(d_scores, q_ref[row, :, lanes], TN) * scale).astype(BF16)
        wide[2, row, :, lanes] = dot(probs.astype(BF16), grad, TN).astype(BF16)
        return carry

    lax.fori_loop(0, rows * heads, one_head, 0, unroll=8)
    gathered = 0.0
    for which in range(3):
        gathered = gathered + dot(flat(wide.at[which]), spreads[which], NT)
    narrow[...] = gathered.astype(BF16).reshape(narrow.shape)
    load_qkv.wait()

    def partial(which_rows):
        return dot(narrow[:, which_rows, :].reshape(rows * length, both), wqkv[...], NT)

    total = line.scatter_sum(partial, buffers)
    d_bo_ref[...] = jnp.sum(flat(full).astype(F32), axis=0, keepdims=True)
    d_bqv_ref[...] = jnp.sum(flat(narrow).astype(F32), axis=0, keepdims=True)
    cargo.need(5, 10)
    wo_whole[...] = dot(flat(full), flat(mixed_ref), TN).astype(BF16)
    wo_sum.begin()
    qkv_whole[...] = dot(flat(full_ref), flat(narrow), TN).astype(BF16)
    qkv_sum.begin()
    d_attn_in = line.finish_sum(total, buffers)
    normed = normed_buf[...]
    d_in = flat(d_middle_ref) + norm_back(
        d_attn_in * (1.0 + token_mod(mod_ref, seg_own, 1)), normed, inverse
    )
    d_in_ref[...] = d_in.reshape(d_in_ref.shape)
    slot_sums(d_attn_in, seg_own, d_mod_ref, 0)
    slot_sums(d_attn_in * normed, seg_own, d_mod_ref, 1)
    wo_sum.end()
    qkv_sum.end()
    cargo.end()


def silu_slope(value):
    gate = 1.0 / (1.0 + jnp.exp(-value))
    return gate * (1.0 + value * (1.0 - gate))


def project_kernel(token_count, *refs, cargo):
    sent_ref, targets_ref, biases_ref, p2_b_ref, p1_any, p2_any, p3_any = refs[:7]
    d_sent_ref, d_p1_ref, d_p2_ref, d_p3_ref, small_ref = refs[7:12]
    p1, p2, p3, tokens, first_pre, first, second_pre, second, d_second, norms = refs[12:22]
    buf_a, buf_b, buf_c, d_first, load_sem, send, recv = refs[22:]
    core, peer = core_bit(), core_peer()
    loads = [
        local(source, place, load_sem.at[i])
        for i, (source, place) in enumerate(((p1_any, p1), (p2_any, p2), (p3_any, p3)))
    ]
    count = tokens.shape[1]
    tokens[core] = flat(sent_ref)
    greet([peer])

    def trade(ref, which):
        return remote(ref.at[core], ref.at[core], send.at[which], recv.at[which], peer)

    def give(buffer, value, which):
        buffer[0] = value.astype(BF16)
        return remote(buffer.at[0], buffer.at[1], send.at[which], recv.at[which], peer)

    def block(ref, side):
        return ref[side]

    copy = trade(tokens, 0)
    target = [
        targets_ref[slot].reshape(2 * count, targets_ref.shape[-1]).astype(F32) for slot in range(2)
    ]
    target_sq = sum(jnp.sum(one * one, axis=1, keepdims=True) for one in target)
    loads[0].wait()
    copy.wait()
    all_tokens = flat(tokens)
    for slot in range(2):
        pre = dot(all_tokens, p1[slot]) + biases_ref[slot, 0, 0:1, :]
        first_pre[slot] = pre
        first[slot] = silu(pre).astype(BF16)
    loads[1].wait()

    def second_term(side):
        rows = pl.ds(pl.multiple_of(side * count, 16), count)
        return dot(first[0, rows, :], p2[0]) + dot(first[1, rows, :], p2[1])

    copy = give(buf_a, second_term(1 - core), 1)
    pre = second_term(core)
    copy.wait()
    pre = pre + buf_a[1].astype(F32) + p2_b_ref[...].astype(F32)
    second_pre[...] = pre
    second[core] = silu(pre).astype(BF16)
    copy = trade(second, 2)
    loads[2].wait()
    copy.wait()
    all_second = flat(second)
    width = target[0].shape[1]
    predicted = [
        dot(all_second, p3[slot], NT) + biases_ref[slot, 0, 1:2, :width] for slot in range(2)
    ]
    pred_sq = sum(jnp.sum(one * one, axis=1, keepdims=True) for one in predicted)
    cross = sum(
        jnp.sum(one * two, axis=1, keepdims=True) for one, two in zip(predicted, target)
    )
    lanes = lax.broadcasted_iota(jnp.int32, norms.shape[1:], 1)
    norms[core] = jnp.where(lanes == 0, pred_sq, jnp.where(lanes == 1, cross, target_sq))
    copy = trade(norms, 3)
    copy.wait()
    total = norms[0] + norms[1]
    inv_pred = lax.rsqrt(total[:, 0:1] + COSINE_EPS)
    inv_target = lax.rsqrt(total[:, 2:3] + COSINE_EPS)
    cosine = total[:, 1:2] * inv_pred * inv_target
    side = lax.broadcasted_iota(jnp.int32, cosine.shape, 0)
    own = jnp.logical_and(side >= core * count, side < (core + 1) * count)
    loss = jnp.sum(jnp.where(own, cosine, 0.0), axis=0, keepdims=True)
    factor = -0.5 / token_count
    one_scale = factor * inv_pred * inv_target
    two_scale = factor * cosine * inv_pred * inv_pred
    d_pred = [
        (one_scale * two - two_scale * one).astype(BF16) for one, two in zip(predicted, target)
    ]
    small_ref[...] = jnp.zeros_like(small_ref)
    for slot in range(2):
        small_ref[2 * core + slot, 1:2, :width] = jnp.sum(
            d_pred[slot].astype(F32), axis=0, keepdims=True
        )

    def d_second_term(side):
        terms = 0.0
        for slot in range(2):
            mine = jnp.where(
                side == 0, d_pred[slot][:count].astype(F32), d_pred[slot][count:].astype(F32)
            )
            terms = terms + dot(mine.astype(BF16), p3[slot])
        return terms

    copy = give(buf_b, d_second_term(1 - core), 4)
    grad = d_second_term(core)
    for slot in range(2):
        d_p3_ref[slot] = dot(d_pred[slot], all_second, TN).astype(BF16)
    copy.wait()
    grad = ((grad + buf_b[1].astype(F32)) * silu_slope(second_pre[...])).astype(BF16)
    d_second[core] = grad
    copy = trade(d_second, 5)
    d_p2_b = jnp.sum(grad.astype(F32), axis=0, keepdims=True)
    lane = small_ref.shape[2]
    loss_row = jnp.where(lax.broadcasted_iota(jnp.int32, (1, lane), 1) == 0, loss, 0.0)
    for part in range(4):
        for row in range(d_p2_b.shape[1] // lane):
            small_ref[part, 2 + row : 3 + row, :] = d_p2_b[:, row * lane : (row + 1) * lane]
        small_ref[part, 6:7, :] = loss_row
    copy.wait()
    all_d_second = flat(d_second)
    for slot in range(2):
        back = dot(all_d_second, p2[slot], NT) * silu_slope(first_pre[slot])
        d_first[slot] = back.astype(BF16)
        small_ref[2 * core + slot, 0:1, :] = jnp.sum(
            d_first[slot].astype(F32), axis=0, keepdims=True
        )

    def d_sent_term(side):
        rows = pl.ds(pl.multiple_of(side * count, 16), count)
        return dot(d_first[0, rows, :], p1[0], NT) + dot(d_first[1, rows, :], p1[1], NT)

    copy = give(buf_c, d_sent_term(1 - core), 6)
    grad = d_sent_term(core)
    for slot in range(2):
        d_p2_ref[slot] = dot(first[slot], all_d_second, TN).astype(BF16)
        d_p1_ref[slot] = dot(all_tokens, d_first[slot], TN).astype(BF16)
    copy.wait()
    d_sent_ref[...] = (grad + buf_c[1].astype(F32)).reshape(d_sent_ref.shape)


def close_kernel(count, sections, replicas, *refs, cargo):
    grads_ref, mod_refs, small_refs, proj_ref, cond_ref = (
        refs[:2], refs[2:6], refs[6:14], refs[14], refs[15]
    )
    grad_ref, ada_w_ref, ada_b_ref, small_ref, proj_sum_ref = refs[16:21]
    z_src, z_buf, mod_src, mod_buf, small_src, small_buf, cond_buf = refs[21:28]
    place_src, place_buf, proj_got, proj_src, proj_buf = refs[28:33]
    sems = refs[33:35]
    section, tensor, replica = (lax.axis_index(name) for name in ("section", "tensor", "dp"))
    send, recv = sems
    others = [
        {"section": lax.rem(section + a, sections), "dp": lax.rem(replica + b, replicas)}
        for a in range(sections)
        for b in range(replicas)
        if a or b
    ]
    greet(z_peers(count) + others + cross_peers())
    last_sums = [one for one in cargo.cargos if isinstance(one, LastSum)]
    y_sums = [one for one in cargo.cargos if type(one) is YSum]
    for one in last_sums:
        one.begin()
    piece = z_src.shape[-1]
    for block in range(sections):
        attend_mod, mlp_mod = mod_refs[2 * block : 2 * block + 2]
        width = attend_mod.shape[-1]
        for part in range(count):
            at, end, cuts = part * piece, (part + 1) * piece, []
            while at < end:
                which = at // width
                stop = min((which + 1) * width, end)
                ref = attend_mod if which < 3 else mlp_mod
                cuts.append(ref[which % 3][:, at - which * width : stop - which * width])
                at = stop
            z_src[part, block] = jnp.concatenate(cuts, axis=1) if len(cuts) > 1 else cuts[0]
    z_copies = [
        remote(z_src.at[peer["tensor"]], z_buf.at[i], send.at[i], recv.at[i], peer)
        for i, peer in enumerate(z_peers(count))
    ]
    at = count - 1
    z_copies += [
        remote(proj_ref.at[peer["tensor"]], proj_got.at[i], send.at[at + i], recv.at[at + i], peer)
        for i, peer in enumerate(z_peers(count))
    ]
    at = at + count - 1

    @pl.when(section == 0)
    def first_place():
        place_src[...] = grads_ref[1][...].astype(BF16)

    @pl.when(section != 0)
    def second_place():
        place_src[...] = grads_ref[0][...].astype(BF16)

    place_copy = remote(place_src, place_buf, send.at[at], recv.at[at], x_peer())
    at = at + 1
    both = small_refs[0].shape[-1]
    small_src[...] = jnp.zeros_like(small_src)
    for block in range(sections):
        d_bqv, d_bo, d_b1, d_b2 = small_refs[4 * block : 4 * block + 4]
        small_src[block, 0:1, :both] = d_bqv[...]
        small_src[block, 2:3, :] = d_bo[...]
        small_src[block, 3:4, : d_b1.shape[1]] = d_b1[...]
        small_src[block, 4:5, :] = d_b2[...]
    small_buf[section, replica] = small_src[section]
    cond_buf[section, replica] = cond_ref[replica]
    copies = []
    for peer in others:
        copies.append(
            remote(
                small_src.at[peer["section"]], small_buf.at[section, replica],
                send.at[at], recv.at[at], peer,
            )
        )
        copies.append(
            remote(
                cond_ref.at[peer["dp"]], cond_buf.at[section, replica],
                send.at[at + 1], recv.at[at + 1], peer,
            )
        )
        at = at + 2
    for one in cargo.cargos:
        if not isinstance(one, YSum):
            one.begin()
    wait_all(z_copies)
    mine, mine_proj = z_src[tensor], proj_ref[tensor]
    for step in range(count - 1):
        mine = mine + z_buf[step]
        mine_proj = mine_proj + proj_got[step]
    mod_src[...] = mine
    mod_buf[section, replica] = mod_src[section]
    proj_src[...] = mine_proj
    proj_buf[section, replica] = mine_proj
    for peer in others:
        copies.append(
            remote(
                mod_src.at[peer["section"]], mod_buf.at[section, replica],
                send.at[at], recv.at[at], peer,
            )
        )
        copies.append(
            remote(
                proj_src, proj_buf.at[section, replica], send.at[at + 1], recv.at[at + 1], peer
            )
        )
        at = at + 2
    for one in last_sums:
        one.middle()
    for one in y_sums:
        one.begin()
    place_copy.wait()
    rows = place_buf.shape[0]

    @pl.when(section == 0)
    def first_out():
        grad_ref[:rows] = grads_ref[0][...]
        grad_ref[rows:] = place_buf[...].astype(F32)

    @pl.when(section != 0)
    def second_out():
        grad_ref[rows:] = grads_ref[1][...]
        grad_ref[:rows] = place_buf[...].astype(F32)

    wait_all(copies)
    small, proj_sum = small_buf[0, 0], proj_buf[0, 0]
    for a in range(sections):
        for b in range(replicas):
            if a or b:
                small = small + small_buf[a, b]
                proj_sum = proj_sum + proj_buf[a, b]
    small_ref[...] = small
    proj_sum_ref[...] = proj_sum
    mod_all = flat(mod_buf)
    ada_b_ref[...] = jnp.sum(mod_all, axis=0, keepdims=True)
    ada_w_ref[...] = lax.dot_general(
        flat(cond_buf), mod_all, TN, precision=HIGHEST, preferred_element_type=F32
    )
    cargo.end()


VMEM = pl.BlockSpec(memory_space=pltpu.VMEM)
ANY = pl.BlockSpec(memory_space=pl.ANY)
MOD_ROWS = 8
PROJECTOR_AXES = (0, 0, 1)


def call(
    kernel, number, inputs, in_any, outs, out_any, scratch, flops, cargos=(), lazy=(), streamed=()
):
    own_in, own_out, own_scratch = len(inputs), len(outs), len(scratch)
    specs = [VMEM] * (own_in - in_any) + [ANY] * in_any
    specs = [ANY if i in lazy else spec for i, spec in enumerate(specs)]
    out_specs = [ANY if i in out_any or i in streamed else VMEM for i in range(own_out)]
    inputs, outs, scratch, aliases = list(inputs), list(outs), list(scratch), {}
    moved_refs = len(lazy) + len(streamed)
    scratch += [pltpu.VMEM(inputs[i].shape, inputs[i].dtype) for i in lazy]
    scratch += [pltpu.VMEM(*outs[i]) for i in streamed]
    if moved_refs:
        scratch.append(pltpu.SemaphoreType.DMA((moved_refs,)))
        moved_refs += 1
    for cargo in cargos:
        for source, target in cargo.aliases.items():
            aliases[len(inputs) + source] = len(outs) + target
        inputs += cargo.inputs
        outs += cargo.outs
        scratch += cargo.scratch
        specs += [ANY] * len(cargo.inputs)
        out_specs += [ANY if cargo.any_outs else VMEM] * len(cargo.outs)

    def body(*refs):
        parts = [list(refs[: len(inputs)])]
        parts.append(list(refs[len(inputs) : len(inputs) + len(outs)]))
        parts.append(list(refs[len(inputs) + len(outs) :]))
        base = parts[0][:own_in] + parts[1][:own_out] + parts[2][:own_scratch]
        held = parts[2][own_scratch : own_scratch + moved_refs]
        bundle = Bundle(cargos)
        for k, i in enumerate(lazy):
            bundle.loads[i] = pltpu.make_async_copy(base[i], held[k], held[-1].at[k])
            base[i] = held[k]
        for k, i in enumerate(streamed, len(lazy)):
            bundle.stores[i] = pltpu.make_async_copy(held[k], base[own_in + i], held[-1].at[k])
            base[own_in + i] = held[k]
        at = [own_in, own_out, own_scratch + moved_refs]
        for cargo in cargos:
            held = []
            for i, items in enumerate((cargo.inputs, cargo.outs, cargo.scratch)):
                held.append(parts[i][at[i] : at[i] + len(items)])
                at[i] += len(items)
            cargo.bind(*held)
        kernel(*base, cargo=bundle)

    moved = sum(math.prod(one.shape) * one.dtype.itemsize for one in inputs)
    results = pl.pallas_call(
        body,
        out_shape=[jax.ShapeDtypeStruct(shape, dtype) for shape, dtype in outs],
        in_specs=specs,
        out_specs=out_specs,
        scratch_shapes=scratch,
        input_output_aliases=aliases,
        compiler_params=pltpu.CompilerParams(
            collective_id=number, has_side_effects=True, vmem_limit_bytes=56 * 2**20
        ),
        cost_estimate=pl.CostEstimate(flops=flops, bytes_accessed=moved, transcendentals=0),
    )(*inputs)
    at, carried = own_out, []
    for cargo in cargos:
        carried.append(results[at : at + len(cargo.outs)])
        at += len(cargo.outs)
    return results[:own_out], carried


def exchange_scratch(count, rows, length, width):
    return [
        pltpu.VMEM((count - 1, rows, length, width), BF16),
        pltpu.VMEM((count, rows, length, width), BF16),
        pltpu.VMEM((rows, length, width), BF16),
    ]


def semaphores(count):
    return [pltpu.SemaphoreType.DMA((2,))] + [
        pltpu.SemaphoreType.DMA((size,)) for size in (count, count, count - 1, count + 1)
    ]


class Shapes:
    def __init__(self, u, own, count):
        self.rows, self.length, self.width = u.shape
        self.count = count
        self.positions = self.length * count
        self.tokens = self.rows * self.positions
        self.heads_width = own["out"].shape[0]
        self.hidden = own["one"].shape[1]
        self.heads = self.heads_width // HEAD_WIDTH
        self.local = (self.rows, self.length, self.width)
        self.full = (self.rows, self.positions, self.width)
        self.wide = (self.rows, self.positions, self.heads * HEAD_LANES)
        self.own = own
        self.attend_outs = [
            (self.local, F32), (self.local, F32), (self.full, BF16),
            (self.wide, BF16), (self.wide, BF16), (self.wide, BF16),
            ((self.rows * self.heads, self.positions, self.positions), F32),
            ((self.rows, self.positions, self.heads_width), BF16),
        ]
        self.attend_scratch = [
            pltpu.VMEM(own["qkv"].shape, BF16),
            pltpu.VMEM(own["out"].shape, BF16),
            pltpu.VMEM(self.wide, BF16),
        ] + exchange_scratch(count, *self.local)
        self.spreads = pltpu.VMEM((3, 3 * self.heads_width, self.heads * HEAD_LANES), BF16)
        self.attend_scratch.append(self.spreads)
        self.mods = (3, MOD_ROWS, self.width)


def pairs(own, other, names):
    out = []
    for name in names:
        out += [own[name], other[name]]
    return out


def open_forward(sizes, u, cond, ada_w, ada_b, biases, segs, own, sections, cargos):
    count, width = sizes.count, sizes.width
    piece = ada_w.shape[0]
    inputs = [u, cond, ada_b, biases, *segs, ada_w] + [own[n] for n in ("qkv", "out", "one", "two")]
    plane = sections * count - 1
    results, carried = call(
        functools.partial(open_kernel, count, sections),
        0,
        inputs,
        5,
        [((sections, 6, MOD_ROWS, width), F32), ((sections,) + biases.shape, F32)]
        + [(own[n].shape, BF16) for n in ("qkv", "out", "one", "two")]
        + sizes.attend_outs,
        (2, 3, 4, 5),
        sizes.attend_scratch
        + [
            pltpu.VMEM(ada_w.shape, BF16),
            pltpu.VMEM((sections, MOD_ROWS, piece), F32),
            pltpu.VMEM((sections, count, MOD_ROWS, piece), F32),
            pltpu.VMEM((sections,) + biases.shape, F32),
        ]
        + semaphores(count)
        + [
            pltpu.SemaphoreType.DMA((plane + 1,)),
            pltpu.SemaphoreType.DMA((plane + 1,)),
            pltpu.SemaphoreType.DMA((4, 4)),
            pltpu.SemaphoreType.DMA((4, 4)),
            pltpu.SemaphoreType.DMA,
        ],
        2 * sizes.tokens * width * sizes.heads_width * 4,
        cargos,
        streamed=tuple(range(8, 14)),
    )
    other = dict(zip(("qkv", "out", "one", "two"), results[2:6]))
    return results[0], results[1], other, results[6:], carried


def attend_forward(sizes, block, u, mods, biases, segs, own, other, cargos):
    inputs = [u, mods, biases, *segs] + pairs(own, other, ("qkv", "out"))
    return call(
        functools.partial(attend_kernel, sizes.count, block),
        1,
        inputs,
        4,
        sizes.attend_outs,
        (),
        sizes.attend_scratch + semaphores(sizes.count),
        2 * sizes.tokens * sizes.width * sizes.heads_width * 4,
        cargos,
        streamed=tuple(range(2, 8)),
    )


def mlp_forward(sizes, block, middle, mods, biases, segs, own, other, cargos):
    inputs = [middle, mods, biases, segs[0]] + pairs(own, other, ("one", "two"))
    hidden = (sizes.rows, sizes.positions, sizes.hidden)
    return call(
        functools.partial(mlp_kernel, sizes.count, block),
        2 + block,
        inputs,
        4,
        [
            (sizes.local, BF16), (sizes.local, F32), (sizes.full, BF16),
            (hidden, F32), (hidden, BF16),
        ],
        (),
        [
            pltpu.VMEM(own["one"].shape, BF16),
            pltpu.VMEM(own["two"].shape, BF16),
        ]
        + exchange_scratch(sizes.count, *sizes.local)
        + semaphores(sizes.count),
        2 * sizes.tokens * sizes.width * sizes.hidden * 2,
        cargos,
        streamed=(2, 3, 4),
    )


def mlp_backward(sizes, block, grads, attend, mlp, mods, segs, own, other, cargos):
    out, branch, full, pre, act = mlp
    inputs = [*grads, attend[0], branch, mods, segs[0], full, pre, act]
    given = len(grads)
    inputs += pairs(own, other, ("one", "two"))
    return call(
        functools.partial(mlp_back_kernel, sizes.count, block, given),
        4 + block,
        inputs,
        4,
        [
            (sizes.local, F32), (sizes.mods, F32),
            ((2,) + quarter((sizes.width, sizes.hidden)), BF16),
            ((2,) + quarter((sizes.width, sizes.hidden)), BF16),
            ((1, sizes.hidden), F32), ((1, sizes.width), F32),
        ],
        (),
        [
            pltpu.VMEM(sizes.full, BF16),
            pltpu.VMEM((sizes.rows, sizes.positions, sizes.hidden), BF16),
            pltpu.VMEM(own["one"].shape, BF16),
            pltpu.VMEM(own["two"].shape, BF16),
        ]
        + exchange_scratch(sizes.count, *sizes.local)
        + semaphores(sizes.count)
        + core_sum_scratch((sizes.width, sizes.hidden)) * 2
        + [
            pltpu.VMEM((sizes.rows * sizes.length, sizes.width), F32),
            pltpu.VMEM((sizes.rows * sizes.length, sizes.width), F32),
        ],
        2 * sizes.tokens * sizes.width * sizes.hidden * 4,
        cargos,
        lazy=(given + 4, given + 5, given + 6),
    )


def attend_backward(sizes, block, d_middle, u, attend, mods, segs, own, other, cargos):
    middle, branch, full, q, k, v, probs, mixed = attend
    inputs = [d_middle, u, branch, mods, segs[0], full, q, k, v, probs, mixed]
    inputs += pairs(own, other, ("qkv", "out"))
    return call(
        functools.partial(attend_back_kernel, sizes.count, block),
        6 + block,
        inputs,
        4,
        [
            (sizes.local, F32), (sizes.mods, F32),
            ((2,) + quarter((sizes.width, 3 * sizes.heads_width)), BF16),
            ((2,) + quarter((sizes.width, sizes.heads_width)), BF16),
            ((1, 3 * sizes.heads_width), F32), ((1, sizes.width), F32),
        ],
        (),
        [
            pltpu.VMEM(sizes.full, BF16),
            pltpu.VMEM((4,) + sizes.wide, BF16),
            pltpu.VMEM((sizes.rows, sizes.positions, 3 * sizes.heads_width), BF16),
            pltpu.VMEM(own["qkv"].shape, BF16),
            pltpu.VMEM(own["out"].shape, BF16),
        ]
        + exchange_scratch(sizes.count, *sizes.local)
        + semaphores(sizes.count)
        + core_sum_scratch((sizes.width, 3 * sizes.heads_width))
        + core_sum_scratch((sizes.width, sizes.heads_width))
        + [
            sizes.spreads,
            pltpu.VMEM((sizes.rows * sizes.length, sizes.width), F32),
        ],
        2 * sizes.tokens * sizes.width * sizes.heads_width * 8,
        cargos,
        lazy=(5, 6, 7, 8, 9, 10),
    )


def project(sizes, sent, weights, targets, biases, p2_b, token_count):
    tokens = sizes.rows * sizes.length
    p1, p2, p3 = weights
    lane, hidden = p1.shape[2], p2.shape[2]
    inputs = [sent, targets, biases, p2_b, p1, p2, p3]
    results, unused = call(
        functools.partial(project_kernel, token_count),
        9,
        inputs,
        3,
        [
            (sizes.local, F32), (p1.shape, BF16), (p2.shape, BF16), (p3.shape, BF16),
            ((sizes.count, MOD_ROWS, lane), F32),
        ],
        (),
        [
            pltpu.VMEM(p1.shape, BF16),
            pltpu.VMEM(p2.shape, BF16),
            pltpu.VMEM(p3.shape, BF16),
            pltpu.VMEM((2, tokens, sizes.width), BF16),
            pltpu.VMEM((2, 2 * tokens, lane), F32),
            pltpu.VMEM((2, 2 * tokens, lane), BF16),
            pltpu.VMEM((tokens, hidden), F32),
            pltpu.VMEM((2, tokens, hidden), BF16),
            pltpu.VMEM((2, tokens, hidden), BF16),
            pltpu.VMEM((2, 2 * tokens, HEAD_LANES), F32),
            pltpu.VMEM((2, tokens, hidden), BF16),
            pltpu.VMEM((2, tokens, hidden), BF16),
            pltpu.VMEM((2, tokens, sizes.width), BF16),
            pltpu.VMEM((2, 2 * tokens, lane), BF16),
            pltpu.SemaphoreType.DMA((3,)),
            pltpu.SemaphoreType.DMA((7,)),
            pltpu.SemaphoreType.DMA((7,)),
        ],
        12 * tokens * sum(math.prod(one.shape) for one in weights),
    )
    return results


def close_backward(sizes, grads, mod_grads, small, proj_small, cond, sections, replicas, cargos):
    count, width = sizes.count, sizes.width
    piece = 6 * width // count
    share = width // replicas
    inputs = [*grads, *mod_grads, *small, proj_small, cond]
    copies = 2 * count + 4 * (sections * replicas - 1)
    both = (sections * sizes.rows,) + sizes.local[1:]
    return call(
        functools.partial(close_kernel, count, sections, replicas),
        8,
        inputs,
        0,
        [
            (both, F32), ((share, piece), F32), ((1, piece), F32),
            ((MOD_ROWS, width), F32), (proj_small.shape[1:], F32),
        ],
        (),
        [
            pltpu.VMEM((count, sections, MOD_ROWS, piece), F32),
            pltpu.VMEM((count - 1, sections, MOD_ROWS, piece), F32),
            pltpu.VMEM((sections, MOD_ROWS, piece), F32),
            pltpu.VMEM((sections, replicas, MOD_ROWS, piece), F32),
            pltpu.VMEM((sections, MOD_ROWS, width), F32),
            pltpu.VMEM((sections, replicas, MOD_ROWS, width), F32),
            pltpu.VMEM((sections, replicas, MOD_ROWS, share), F32),
            pltpu.VMEM(sizes.local, BF16),
            pltpu.VMEM(sizes.local, BF16),
            pltpu.VMEM((count - 1,) + proj_small.shape[1:], F32),
            pltpu.VMEM(proj_small.shape[1:], F32),
            pltpu.VMEM((sections, replicas) + proj_small.shape[1:], F32),
            pltpu.SemaphoreType.DMA((copies,)),
            pltpu.SemaphoreType.DMA((copies,)),
        ],
        2 * sections * replicas * MOD_ROWS * share * piece,
        cargos,
    )


def assemble_kernel(heads_width, *refs):
    fc1, fc2 = refs[0:2], refs[2:4]
    alone, (qkv, wo) = refs[4:9], (refs[9:11], refs[11:13])
    grad_ref, small, proj = refs[13:16]
    outs, sems = refs[16:-1], refs[-1]
    is_first = lax.axis_index("section") == 0
    waits = []
    for i, pair in enumerate((fc1, fc2)):
        waits.append(pltpu.make_async_copy(pair[0], outs[i], sems.at[i]))

        @pl.when(is_first)
        def take_one(pair=pair, i=i):
            pltpu.make_async_copy(pair[0], outs[i], sems.at[i]).start()

        @pl.when(jnp.logical_not(is_first))
        def take_two(pair=pair, i=i):
            pltpu.make_async_copy(pair[1], outs[i], sems.at[i]).start()

    for i, one in enumerate(alone):
        waits.append(local(one, outs[2 + i], sems.at[2 + i]))
    grad_out, qkv_out, wo_out, qv_b, out_b, fc1_b, fc2_b, p1_b, p2_b, p3_b, loss = outs[7:]
    for row in range(grad_ref.shape[0]):
        grad_out[:, row, :] = grad_ref[row]
    qkv_own = jnp.where(is_first, qkv[0][...], qkv[1][...])
    for which in range(3):
        qkv_out[which] = qkv_own[:, which * heads_width : (which + 1) * heads_width]
    wo_out[...] = jnp.where(is_first, wo[0][...], wo[1][...]).T
    qv_b[0:1, :] = small[0:1, :heads_width]
    qv_b[1:2, :] = small[0:1, 2 * heads_width : 3 * heads_width]
    out_b[...] = small[2:3, :]
    fc1_b[...] = small[3:4, :]
    fc2_b[...] = small[4:5, :]
    p1_b[...] = proj[0:1, :]
    p2_b[...] = jnp.concatenate([proj[2 + row : 3 + row, :] for row in range(4)], axis=1)
    p3_b[...] = proj[1:2, : p3_b.shape[1]]
    loss[...] = proj[6:7, :HEAD_LANES]
    wait_all(waits)


def assemble(choices, alone, section_grad, small, proj_small, heads_width):
    (fc1, fc2, qkv, wo) = choices
    inputs = [*fc1, *fc2, *alone, *qkv, *wo, section_grad, small, proj_small]
    both, length, width = section_grad.shape
    share, lane = fc1[0].shape[0], proj_small.shape[1]
    third = alone[4].shape[0]
    shapes = [fc1[0].shape, fc2[0].shape] + [one.shape for one in alone] + [
        (length, both, width), (3, share, heads_width), wo[0].shape[::-1], (2, heads_width),
        (1, width), (1, width), (1, width), (1, lane), (1, 4 * lane), (1, third), (1, HEAD_LANES),
    ]
    return pl.pallas_call(
        functools.partial(assemble_kernel, heads_width),
        out_shape=[jax.ShapeDtypeStruct(shape, F32) for shape in shapes],
        in_specs=[ANY] * 9 + [VMEM] * 7,
        out_specs=[VMEM] * 18,
        scratch_shapes=[pltpu.SemaphoreType.DMA((7,))],
        compiler_params=pltpu.CompilerParams(vmem_limit_bytes=62 * 2**20),
        cost_estimate=pl.CostEstimate(flops=1000, bytes_accessed=2**24, transcendentals=0),
    )(*inputs)


def halve(value, axis, bit, position):
    size = lax.axis_size(axis)
    mine = (lax.axis_index(axis) & bit) // bit
    keep = lax.dynamic_index_in_dim(value, mine, position, keepdims=False)
    give = lax.dynamic_index_in_dim(value, 1 - mine, position, keepdims=False)
    return keep + lax.ppermute(give, axis, [(i, i ^ bit) for i in range(size)])


def sum_beyond_quads(value):
    size = lax.axis_size("dp")
    if size == 4:
        return value
    quads = size // 4
    bits = quads.bit_length() - 1
    lead = value.ndim - 2
    shape = value.shape
    value = value.reshape(shape[:lead] + (2,) * bits + (shape[-2] // quads, shape[-1]))
    for bit in range(bits):
        value = halve(value, "dp", 4 << bit, lead + bits - 1 - bit)
    route = [(high * 4 + low, low * quads + high) for high in range(quads) for low in range(4)]
    return lax.ppermute(value, "dp", route)


def per_device(
    block_eight_input,
    cond,
    image_slot_index,
    targets,
    cot,
    ada_w,
    ada_b,
    query_key_value_weight,
    query_value_bias,
    attention_output_weight,
    attention_output_bias,
    hidden_weight,
    hidden_bias,
    output_weight_mlp,
    output_bias_mlp,
    p1_w,
    p1_b,
    p2_w,
    p2_b,
    p3_w,
    p3_b,
):
    section = lax.axis_index("section")
    tensor = lax.axis_index("tensor")
    is_first = section == 0
    count = lax.axis_size("tensor")
    sections = lax.axis_size("section")
    replicas = lax.axis_size("dp")
    length, replica_rows, width = block_eight_input.shape
    positions = length * count
    rows = replica_rows // sections
    total_token_count = positions * replica_rows * replicas
    heads_width = attention_output_weight.shape[1]
    hidden = hidden_weight.shape[2]

    def my_rows(value, axis):
        return lax.dynamic_slice_in_dim(value, section * rows, rows, axis)

    def to_rows(value):
        return jnp.transpose(my_rows(value, 1), (1, 0, 2))

    own = {
        "qkv": query_key_value_weight[0].reshape(width, 3 * heads_width),
        "out": attention_output_weight[0],
        "one": hidden_weight[0],
        "two": output_weight_mlp[0],
    }

    def padded(value):
        return jnp.pad(value.astype(F32), ((0, 0), (0, width - value.shape[-1])))

    biases = jnp.concatenate(
        [
            padded(
                jnp.concatenate(
                    [
                        query_value_bias[0, 0:1], jnp.zeros((1, heads_width), BF16),
                        query_value_bias[0, 1:2],
                    ],
                    axis=1,
                )
            ),
            jnp.zeros((1, width), F32), padded(attention_output_bias), padded(hidden_bias),
            padded(output_bias_mlp), jnp.zeros((MOD_ROWS - 5, width), F32),
        ],
        axis=0,
    )
    used = rows * IMAGES_PER_ROW
    cond_pad = jnp.pad(
        cond.reshape(sections, used, width), ((0, 0), (0, MOD_ROWS - used), (0, 0))
    )
    segs_full = my_rows(image_slot_index, 0)
    seg_own = lax.dynamic_slice_in_dim(segs_full, tensor * length, length, 1)
    segs = (seg_own[:, :, None], segs_full[:, :, None], segs_full[:, None, :])

    target_parts = my_rows(targets, 1).reshape(count, length, rows, targets.shape[2])
    target_parts = jnp.transpose(target_parts, (0, 2, 1, 3))
    lane = p1_b.shape[0]
    proj_biases = jnp.concatenate(
        [
            p1_b.astype(F32)[None],
            jnp.pad(p3_b.astype(F32), (0, lane - p3_b.shape[0]))[None],
            jnp.zeros((MOD_ROWS - 2, lane), F32),
        ],
        axis=0,
    )
    gather = ColumnGather((p1_w, p2_w, p3_w.T), PROJECTOR_AXES, target_parts, proj_biases)

    u = to_rows(block_eight_input)
    sizes = Shapes(u, own, count)
    mods, bias_all, other, attend_one, carried = open_forward(
        sizes, u, cond_pad.reshape(-1, width), ada_w[0].T, ada_b, biases, segs, own, sections,
        (gather,),
    )
    *proj_weights, target_all, proj_bias_all = carried[0]
    mlp_one, carried = mlp_forward(
        sizes, 0, attend_one[0], mods, bias_all, segs, own, other,
        (ShareAlong(proj_weights, PROJECTOR_AXES, 0),),
    )
    proj_weights = carried[0]
    first_out = mlp_one[0]
    attend_two, carried = attend_forward(
        sizes, 1, first_out, mods, bias_all, segs, own, other, (ShareAlong(proj_weights, PROJECTOR_AXES, 1),)
    )
    proj_weights = carried[0]
    mlp_two, carried = mlp_forward(
        sizes, 1, attend_two[0], mods, bias_all, segs, own, other, (ShareAlong(proj_weights, PROJECTOR_AXES, 2),)
    )
    proj_weights = carried[0]
    second_out = mlp_two[0]

    grad_sent, grad_p1, grad_p2, grad_p3, proj_small = project(
        sizes, first_out, proj_weights, target_all, proj_bias_all, p2_b[None], total_token_count
    )

    back = (mods, segs, own, other)
    (d_middle_two, mod_mlp_two, *mlp_grads_two), carried = mlp_backward(
        sizes, 1, [to_rows(cot)], attend_two, mlp_two, *back,
        [
            Swap(first_out, second_out), HalfSum(grad_p1, 0, "x"),
            HalfSum(grad_p3, 1, "x", (0, 1)),
        ],
    )
    (other_out,), (grad_p1,), (grad_p3_a,) = carried
    (second_grad, mod_attend_two, *attend_grads_two), carried = attend_backward(
        sizes, 1, d_middle_two, first_out, attend_two, *back,
        [YSum(grad, BF16) for grad in mlp_grads_two[:2]]
        + [HalfSum(grad_p2, 1, "x", (0, 1)), HalfSum(grad_p3, 1, "x", (1, 1))]
        + [HalfSum(grad_p1, 0, "y", (0, 1))],
    )
    (mlp_part_a,), (mlp_part_b,), (grad_p2_a,), (grad_p3_b,), (grad_p1_a,) = carried
    (d_middle_one, mod_mlp_one, *mlp_grads_one), carried = mlp_backward(
        sizes, 0, [second_grad, grad_sent], attend_one, mlp_one, *back,
        [YSum(grad, BF16) for grad in attend_grads_two[:2]]
        + [SectionSum(mlp_part_a, 1), HalfSum(grad_p2, 1, "x", (1, 1))]
        + [HalfSum(grad_p1, 0, "y", (1, 1)), HalfSum(grad_p2_a, 1, "y")],
    )
    attend_parts_two, sum_mlp_a = carried[:2], carried[2]
    (grad_p2_b,), (grad_p1_b,), (grad_p2_a,) = carried[3:]
    (first_grad, mod_attend_one, *attend_grads_one), carried = attend_backward(
        sizes, 0, d_middle_one, u, attend_one, *back,
        [LastSum(mlp_grads_one[0], 0), SectionSum(mlp_grads_one[1], 0, BF16)]
        + [SectionSum(part, 1) for part, in attend_parts_two]
        + [SectionSum(mlp_part_b, 1), HalfSum(grad_p2_b, 1, "y")]
        + [HalfSum(grad_p3_a, 1, "y"), HalfSum(grad_p3_b, 1, "y")]
        + [ColumnSum((grad_p1_a, grad_p1_b), 0)],
    )
    sum_mlp_c, (mlp_part_two,), sums_attend_two = carried[0], carried[1], carried[2:4]
    sums_mlp_two = (sum_mlp_a, carried[4])
    (grad_p2_b,), (grad_p3_a,), (grad_p3_b,), (red_p1_w,) = carried[5:]

    cond_act = silu(my_rows(cond, 0).astype(F32)).astype(BF16).astype(F32)
    share = width // replicas
    cond_cols = jnp.pad(cond_act.reshape(used, width), ((0, MOD_ROWS - used), (0, 0)))
    cond_cols = jnp.transpose(cond_cols.reshape(MOD_ROWS, replicas, share), (1, 0, 2))
    small = [
        attend_grads_one[2], attend_grads_one[3], mlp_grads_one[2], mlp_grads_one[3],
        attend_grads_two[2], attend_grads_two[3], mlp_grads_two[2], mlp_grads_two[3],
    ]
    (section_grad, grad_ada_w, grad_ada_b, small, proj_small), carried = close_backward(
        sizes, (first_grad, second_grad),
        (mod_attend_one, mod_mlp_one, mod_attend_two, mod_mlp_two),
        small, proj_small, cond_cols, sections, replicas,
        [LastSum(grad, 0) for grad in attend_grads_one[:2]]
        + [YSum(mlp_part_two, F32)]
        + [ColumnSum((grad_p2_a, grad_p2_b), 1), ColumnSum((grad_p3_a, grad_p3_b), 1)],
    )
    sums_attend_one, sums_mlp_one = carried[:2], (sum_mlp_c, carried[2])
    (red_p2_w,), (red_p3_w,) = carried[3:]

    own_out = jnp.where(is_first, first_out, second_out)
    section_out = jnp.where(
        is_first,
        jnp.concatenate([own_out, other_out], axis=0),
        jnp.concatenate([other_out, own_out], axis=0),
    )
    section_out = jnp.transpose(section_out, (1, 0, 2))[None]
    choices = [
        (one[0], two[0])
        for one, two in zip(
            list(sums_mlp_one) + list(sums_attend_one), list(sums_mlp_two) + list(sums_attend_two)
        )
    ]
    if replicas == 4:
        alone = [grad_ada_w, grad_ada_b, red_p1_w, red_p2_w, red_p3_w]
        final = assemble(choices, alone, section_grad, small, proj_small, heads_width)
        red_fc1, red_fc2, grad_ada_w, grad_ada_b, red_p1_w, red_p2_w, red_p3_w = final[:7]
        section_grad, red_qkv, red_out, qv_b, out_b, fc1_b, fc2_b, p1_sum, p2_sum, p3_sum, loss = (
            final[7:]
        )
        red_p1_b, red_p2_b, red_p3_b = p1_sum[0], p2_sum[0], p3_sum[0]
        loss_total = loss[0, 0]
    else:
        red_fc1, red_fc2, red_qkv, red_out = [
            sum_beyond_quads(jnp.where(is_first, one, two)) for one, two in choices
        ]
        red_qkv = jnp.transpose(red_qkv.reshape(-1, 3, heads_width), (1, 0, 2))
        red_out = red_out.T
        red_p1_w = sum_beyond_quads(red_p1_w)
        red_p2_w, red_p3_w = sum_beyond_quads(red_p2_w.T).T, sum_beyond_quads(red_p3_w.T).T
        section_grad = jnp.transpose(section_grad, (1, 0, 2))
        qv_b = jnp.stack([small[0, :heads_width], small[0, 2 * heads_width : 3 * heads_width]])
        out_b, fc1_b, fc2_b = small[2:3], small[3:4], small[4:5]
        red_p1_b, red_p2_b = proj_small[0], proj_small[2:6].reshape(-1)
        red_p3_b, loss_total = proj_small[1, : p3_b.shape[0]], proj_small[6, 0]
    align_loss = -0.5 * loss_total / total_token_count
    return (
        section_out,
        section_grad[None],
        align_loss,
        grad_ada_w[None],
        grad_ada_b,
        jnp.transpose(red_qkv, (1, 0, 2))[None],
        qv_b[None],
        red_out[None],
        out_b,
        red_fc1[None],
        fc1_b[:, :hidden],
        red_fc2.T[None],
        fc2_b,
        red_p1_w,
        red_p1_b,
        red_p2_w,
        red_p2_b[: p2_b.shape[0]],
        red_p3_w.T,
        red_p3_b,
    )


def solution(mesh):
    in_specs = (
        P("tensor", "dp", None),
        P("dp", None, None),
        P("dp", None),
        P(None, "dp", "tensor"),
        P("tensor", "dp", None),
        P("section", None, "tensor"),
        P("section", "tensor"),
        P("section", None, None, "tensor"),
        P("section", None, "tensor"),
        P("section", "tensor", None),
        P("section", None),
        P("section", None, "tensor"),
        P("section", "tensor"),
        P("section", "tensor", None),
        P("section", None),
        P(None, "tensor"),
        P("tensor"),
        P("tensor", None),
        P(),
        P(None, "tensor"),
        P("tensor"),
    )
    out_specs = (
        P("section", "tensor", "dp", None),
        P("section", "tensor", "dp", None),
        P(),
        P("section", "dp", "tensor"),
        P("section", "tensor"),
        P("section", "dp", None, "tensor"),
        P("section", None, "tensor"),
        P("section", "tensor", "dp"),
        P("section", None),
        P("section", "dp", "tensor"),
        P("section", "tensor"),
        P("section", "tensor", "dp"),
        P("section", None),
        P(("section", "dp"), "tensor"),
        P("tensor"),
        P("tensor", ("section", "dp")),
        P(),
        P(("section", "dp"), "tensor"),
        P("tensor"),
    )
    return jax.shard_map(
        per_device, mesh=mesh, in_specs=in_specs, out_specs=out_specs, check_vma=False
    )
```

```python
import functools
import math

import jax
import jax.numpy as jnp
from jax import lax
from jax.experimental import pallas as pl
from jax.experimental.pallas import tpu as pltpu
from jax.sharding import PartitionSpec as P

HEAD_WIDTH = 72
HEAD_LANES = 128
IMAGES_PER_ROW = 3
NORM_EPS = 1e-06
COSINE_EPS = 1e-06
MASKED_SCORE = -1e30
HIGHEST = lax.Precision.HIGHEST
MESH = pl.DeviceIdType.MESH
F32 = jnp.float32
BF16 = jnp.bfloat16
NN = (((1,), (0,)), ((), ()))
NT = (((1,), (1,)), ((), ()))
TN = (((0,), (0,)), ((), ()))


def dot(left, right, form=NN):
    return lax.dot_general(left, right, form, preferred_element_type=F32)


def z_peers(count):
    me = lax.axis_index("tensor")
    return [{"tensor": lax.rem(me + step, count)} for step in range(1, count)]


def x_peer():
    return {"section": 1 - lax.axis_index("section")}


def core_bit():
    return lax.rem(lax.axis_index("dp"), 2)


def y_bit():
    return lax.rem(lax.axis_index("dp") // 2, 2)


def core_peer():
    return {"dp": lax.axis_index("dp") + 1 - 2 * core_bit()}


def y_peer():
    return {"dp": lax.axis_index("dp") + 2 - 4 * y_bit()}


def call_peers(peers):
    barrier = pltpu.get_barrier_semaphore()
    for peer in peers:
        pl.semaphore_signal(barrier, inc=1, device_id=peer, device_id_type=MESH)
    return lambda: pl.semaphore_wait(barrier, len(peers))


def greet(peers):
    call_peers(peers)()


def remote(source, target, send_sem, recv_sem, peer):
    copy = describe(source, target, send_sem, recv_sem, peer)
    copy.start()
    return copy


def local(source, target, sem):
    copy = pltpu.make_async_copy(source, target, sem)
    copy.start()
    return copy


def own_rows(me, length):
    return pl.ds(pl.multiple_of(me * length, 16), length)


def describe(source, target, send_sem, recv_sem, peer):
    return pltpu.make_async_remote_copy(
        src_ref=source,
        dst_ref=target,
        send_sem=send_sem,
        recv_sem=recv_sem,
        device_id=peer,
        device_id_type=MESH,
    )


def wait_all(copies):
    for copy in copies:
        copy.wait()


class Line:
    def __init__(self, length, sems):
        self.length, (self.ag_send, self.ag_recv, self.rs_send, self.rs_recv) = length, sems
        self.me = lax.axis_index("tensor")
        self.mirror = 3 - self.me
        self.near = self.me + 1 - 2 * lax.rem(self.me, 2)
        self.opposite = lax.rem(self.me + 2, 4)
        self.is_end = jnp.logical_or(self.me == 0, self.me == 3)
        self.is_middle = jnp.logical_not(self.is_end)

    def block(self, full, place, which, peer):
        part = full.at[:, own_rows(place, self.length)]
        return describe(
            part, part, self.ag_send.at[which], self.ag_recv.at[place], {"tensor": peer}
        )

    def start_gather(self, full):
        self.block(full, self.me, 0, self.opposite).start()
        self.block(full, self.me, 1, self.near).start()

        @pl.when(self.is_middle)
        def to_mirror():
            self.block(full, self.me, 2, self.mirror).start()

    def relay(self, full):
        self.block(full, self.opposite, 2, self.mirror).wait_recv()

        @pl.when(self.is_middle)
        def pass_on():
            self.block(full, self.opposite, 3, 3 - self.opposite).start()

    def arrived(self, full, place):
        self.block(full, place, 1, self.near).wait_recv()

    def finish_gather(self, full):
        self.arrived(full, self.near)
        self.arrived(full, self.mirror)
        self.sent(full)

    def sent(self, full):
        self.block(full, self.me, 0, self.opposite).wait_send()
        self.block(full, self.me, 1, self.near).wait_send()

        @pl.when(self.is_middle)
        def more_sent():
            self.block(full, self.me, 2, self.mirror).wait_send()
            self.block(full, self.opposite, 3, 3 - self.opposite).wait_send()

    def scatter_sum(self, partial, buffers, prepare=lambda place: None):
        send_buf, recv_buf, relay_buf = buffers
        me, relay_sem = self.me, 4

        def term(peer):
            return partial(own_rows(peer, self.length))

        def keep(which, value):
            send_buf[which] = value.astype(BF16).reshape(send_buf.shape[1:])

        self.to_mirror = describe(
            send_buf.at[0], recv_buf.at[me], self.rs_send.at[0], self.rs_recv.at[me],
            {"tensor": self.mirror},
        )
        self.to_relay = describe(
            send_buf.at[0], relay_buf, self.rs_send.at[0], self.rs_recv.at[relay_sem],
            {"tensor": self.near},
        )
        self.to_near = describe(
            send_buf.at[1], recv_buf.at[me], self.rs_send.at[1], self.rs_recv.at[me],
            {"tensor": self.near},
        )
        self.to_opposite = describe(
            send_buf.at[2], recv_buf.at[me], self.rs_send.at[2], self.rs_recv.at[me],
            {"tensor": self.opposite},
        )
        prepare(self.mirror)
        keep(0, term(self.mirror))

        @pl.when(self.is_end)
        def first_end():
            self.to_relay.start()
            relay_buf[...] = jnp.zeros_like(relay_buf)
            recv_buf[self.mirror] = jnp.zeros(recv_buf.shape[1:], BF16)

        @pl.when(self.is_middle)
        def first_middle():
            self.to_mirror.start()

        prepare(self.near)
        keep(1, term(self.near))
        self.to_near.start()
        last = term(self.opposite)

        @pl.when(self.is_middle)
        def relayed():
            self.to_relay.wait_recv()

        keep(2, last + relay_buf[...].reshape(last.shape).astype(F32))
        self.to_opposite.start()
        return term(me)

    def finish_sum(self, total, buffers):
        send_buf, recv_buf, relay_buf = buffers

        def got(source):
            describe(
                send_buf.at[1], recv_buf.at[source], self.rs_send.at[1], self.rs_recv.at[source],
                {"tensor": self.near},
            ).wait_recv()

        got(self.near)
        got(self.opposite)

        @pl.when(self.is_middle)
        def third():
            got(self.mirror)

        self.to_near.wait_send()
        self.to_opposite.wait_send()
        self.to_mirror.wait_send()
        for source in (self.near, self.opposite, self.mirror):
            total = total + recv_buf[source].reshape(total.shape).astype(F32)
        return total


def fetch(block, own_ref, other_ref, target, sem):
    mine = lax.axis_index("section") == block

    @pl.when(mine)
    def own_start():
        pltpu.make_async_copy(own_ref, target, sem).start()

    @pl.when(jnp.logical_not(mine))
    def other_start():
        pltpu.make_async_copy(other_ref, target, sem).start()

    return pltpu.make_async_copy(own_ref, target, sem)


def layer_norm(rows):
    centred = rows - jnp.mean(rows, axis=-1, keepdims=True)
    inverse = lax.rsqrt(jnp.mean(centred * centred, axis=-1, keepdims=True) + NORM_EPS)
    return centred * inverse, inverse


def norm_back(grad, normed, inverse):
    mean_grad = jnp.mean(grad, axis=-1, keepdims=True)
    mean_cross = jnp.mean(grad * normed, axis=-1, keepdims=True)
    return inverse * (grad - mean_grad - normed * mean_cross)


def token_mod(mod_ref, seg_ref, which):
    parts = []
    for row in range(seg_ref.shape[0]):
        seg = seg_ref[row]
        line = [
            mod_ref[which, pl.ds(row * IMAGES_PER_ROW + slot, 1), :]
            for slot in range(IMAGES_PER_ROW)
        ]
        value = line[-1]
        for slot in range(IMAGES_PER_ROW - 2, -1, -1):
            value = jnp.where(seg == slot, line[slot], value)
        parts.append(value)
    return jnp.concatenate(parts, axis=0)


def slot_sums(value, seg_ref, out_ref, which):
    length = seg_ref.shape[1]
    lines = []
    for row in range(seg_ref.shape[0]):
        seg = seg_ref[row]
        piece = value[row * length : (row + 1) * length]
        for slot in range(IMAGES_PER_ROW):
            lines.append(jnp.sum(jnp.where(seg == slot, piece, 0.0), axis=0, keepdims=True))
    spare = out_ref.shape[1] - len(lines)
    lines.append(jnp.zeros((spare, value.shape[1]), F32))
    out_ref[which] = jnp.concatenate(lines, axis=0)


def flat(ref):
    return ref[...].reshape(-1, ref.shape[-1])


def spread_matrix(width, which=0, total=None):
    lanes = width // HEAD_WIDTH * HEAD_LANES
    shape = (total or width, lanes)
    source = lax.broadcasted_iota(jnp.int32, shape, 0)
    target = lax.broadcasted_iota(jnp.int32, shape, 1)
    within = target & (HEAD_LANES - 1)
    head = target >> (HEAD_LANES.bit_length() - 1)
    hit = (within < HEAD_WIDTH) & (source == which * width + head * HEAD_WIDTH + within)
    return jnp.where(hit, 1.0, 0.0).astype(BF16)


def gelu_tanh(pre):
    inner = math.sqrt(2.0 / math.pi) * (pre + 0.044715 * (pre * pre * pre))
    return 0.5 * pre * (1.0 + jnp.tanh(inner))


def gelu_slope(pre):
    scale = math.sqrt(2.0 / math.pi)
    square = pre * pre
    tanh = jnp.tanh(scale * (pre + 0.044715 * (pre * square)))
    return 0.5 * (1.0 + tanh) + 0.5 * pre * (1.0 - tanh * tanh) * scale * (
        1.0 + 3 * 0.044715 * square
    )


def silu(value):
    return value / (1.0 + jnp.exp(-value))


class Share:
    def __init__(self, own, other, parts, sems):
        self.own, self.other, self.parts = own, other, parts
        self.send, self.recv = sems
        self.size = own.shape[0] // parts
        self.copies = []

    def rows(self, core, y):
        part = core if self.parts == 2 else core + 2 * y
        return pl.ds(pl.multiple_of(part * self.size, 16), self.size)

    def begin(self):
        rows = self.rows(core_bit(), y_bit())
        self.first = remote(
            self.own.at[rows], self.other.at[rows], self.send.at[0], self.recv.at[0], x_peer()
        )

    def forward(self, first):
        if first is not None:
            first.wait()
        mine = self.other.at[self.rows(core_bit(), y_bit())]
        self.copies.append(remote(mine, mine, self.send.at[1], self.recv.at[1], core_peer()))
        if self.parts == 4:
            self.second = remote(mine, mine, self.send.at[2], self.recv.at[2], y_peer())

    def forward_again(self):
        if self.parts == 4:
            self.second.wait()
            got = self.other.at[self.rows(core_bit(), 1 - y_bit())]
            self.copies.append(remote(got, got, self.send.at[3], self.recv.at[3], core_peer()))

    def finish(self):
        wait_all(self.copies)


class Cargo:
    inputs, outs, scratch, aliases, any_outs = (), (), (), {}, False

    def bind(self, inputs, outs, scratch):
        self.ins, self.out_refs, self.held = inputs, outs, scratch

    def peers(self):
        return []

    def begin(self):
        pass

    def middle(self):
        pass

    def late(self):
        pass

    def end(self):
        pass


def quarter(shape):
    return shape[:-2] + (shape[-2] // 4, shape[-1])


class CoreSum:
    def __init__(self, whole, got, out, sems):
        self.whole, self.got, self.out, self.sems = whole, got, out, sems
        self.size = whole.shape[-2] // 4

    def rows(self, core, y):
        part = pl.ds(pl.multiple_of((core + 2 * y) * self.size, 16), self.size)
        whole = self.whole
        return whole.at[:, part] if len(whole.shape) == 3 else whole.at[part]

    def begin(self):
        self.copies = [
            remote(
                self.rows(1 - core_bit(), y), self.got.at[y],
                self.sems.at[0, y], self.sems.at[1, y], core_peer(),
            )
            for y in range(2)
        ]

    def end(self):
        wait_all(self.copies)
        for y in range(2):
            mine = self.rows(core_bit(), y)[...]
            self.out[y] = (mine.astype(F32) + self.got[y].astype(F32)).astype(BF16)


def core_sum_scratch(shape):
    return [
        pltpu.VMEM(shape, BF16),
        pltpu.VMEM((2,) + quarter(shape), BF16),
        pltpu.SemaphoreType.DMA((2, 2)),
    ]


class YSum(Cargo):
    def __init__(self, parts, dtype):
        part = parts.shape[1:]
        self.inputs = (parts,)
        self.outs = ((part, dtype),)
        self.scratch = (
            pltpu.VMEM(part, BF16),
            pltpu.VMEM(part, BF16),
            pltpu.SemaphoreType.DMA((3,)),
        )

    def peers(self):
        return ["y"]

    def begin(self):
        mine, other, sems = self.held
        self.copies = [
            remote(self.ins[0].at[1 - y_bit()], other, sems.at[0], sems.at[1], y_peer()),
            local(self.ins[0].at[y_bit()], mine, sems.at[2]),
        ]

    def end(self):
        mine, other, sems = self.held
        out = self.out_refs[0]
        wait_all(self.copies)
        out[...] = (mine[...].astype(F32) + other[...].astype(F32)).astype(out.dtype)


class SectionSum(Cargo):
    def __init__(self, part, owner, dtype=F32):
        self.owner = owner
        self.inputs = (part,)
        self.outs = ((part.shape, dtype),)
        self.scratch = (
            pltpu.VMEM(part.shape, BF16),
            pltpu.VMEM(part.shape, BF16),
            pltpu.SemaphoreType.DMA((3,)),
        )

    def peers(self):
        return ["x"]

    def source(self):
        return self.ins[0]

    def begin(self):
        mine, other, sems = self.held
        self.copy = describe(self.source(), other, sems.at[0], sems.at[1], x_peer())
        self.load = pltpu.make_async_copy(self.source(), mine, sems.at[2])
        is_owner = lax.axis_index("section") == self.owner

        @pl.when(is_owner)
        def take():
            self.load.start()

        @pl.when(jnp.logical_not(is_owner))
        def give():
            self.copy.start()

    def end(self):
        mine, other, sems = self.held
        is_owner = lax.axis_index("section") == self.owner

        @pl.when(is_owner)
        def add():
            self.load.wait()
            self.copy.wait_recv()
            out = self.out_refs[0]
            out[...] = (mine[...].astype(F32) + other[...].astype(F32)).astype(out.dtype)

        @pl.when(jnp.logical_not(is_owner))
        def given():
            self.copy.wait_send()
            self.out_refs[0][...] = jnp.zeros_like(self.out_refs[0])


class LastSum(YSum):
    def __init__(self, parts, owner):
        super().__init__(parts, F32)
        part = parts.shape[1:]
        self.owner = owner
        self.scratch = self.scratch + (
            pltpu.VMEM(part, BF16),
            pltpu.VMEM(part, BF16),
            pltpu.SemaphoreType.DMA((2,)),
        )

    def peers(self):
        return ["y", "x"]

    def begin(self):
        self.held, self.last = self.held[:3], self.held[3:]
        super().begin()

    def middle(self):
        mine, other, sems = self.held
        total, got, last_sems = self.last
        wait_all(self.copies)
        total[...] = (mine[...].astype(F32) + other[...].astype(F32)).astype(BF16)
        self.copy = describe(total, got, last_sems.at[0], last_sems.at[1], x_peer())

        @pl.when(lax.axis_index("section") != self.owner)
        def give():
            self.copy.start()

    def end(self):
        total, got, last_sems = self.last
        is_owner = lax.axis_index("section") == self.owner

        @pl.when(is_owner)
        def add():
            self.copy.wait_recv()
            self.out_refs[0][...] = total[...].astype(F32) + got[...].astype(F32)

        @pl.when(jnp.logical_not(is_owner))
        def given():
            self.copy.wait_send()
            self.out_refs[0][...] = jnp.zeros_like(self.out_refs[0])


class Swap(Cargo):
    def __init__(self, one, two):
        self.inputs = (one, two)
        self.outs = ((one.shape, one.dtype),)
        self.scratch = (pltpu.VMEM(one.shape, one.dtype), pltpu.SemaphoreType.DMA((2,)))

    def peers(self):
        return ["x"]

    def begin(self):
        got, sems = self.held
        one, two = self.ins
        self.copy = describe(two, got, sems.at[0], sems.at[1], x_peer())
        is_first = lax.axis_index("section") == 0

        @pl.when(is_first)
        def give_two():
            self.copy.start()

        @pl.when(jnp.logical_not(is_first))
        def give_one():
            describe(one, got, sems.at[0], sems.at[1], x_peer()).start()

    def end(self):
        self.copy.wait()
        self.out_refs[0][...] = self.held[0][...]


def span(ref, axis, start, size):
    part = pl.ds(pl.multiple_of(start, 128 if axis == 1 else 16), size)
    lead = (slice(None),) * (len(ref.shape) - 2)
    return ref.at[lead + ((slice(None), part) if axis == 1 else (part, slice(None)))]


def cut(shape, axis, by):
    shape = list(shape)
    shape[axis - 2] //= by
    return tuple(shape)


class HalfSum(Cargo):
    def __init__(self, grad, axis, name, slots=None):
        self.slots = slots if slots is not None else (0, grad.shape[0])
        part = cut((self.slots[1],) + grad.shape[1:], axis, 2)
        self.axis, self.name, self.size = axis, name, part[axis - 2]
        self.inputs = (grad,)
        self.outs = ((part, BF16),)
        self.scratch = (
            pltpu.VMEM(part, BF16),
            pltpu.VMEM(part, BF16),
            pltpu.SemaphoreType.DMA((3,)),
        )

    def peers(self):
        return [self.name]

    def begin(self):
        mine, other, sems = self.held
        if self.name == "x":
            bit, peer = lax.axis_index("section"), x_peer()
        else:
            bit, peer = y_bit(), y_peer()
        grad = self.ins[0].at[pl.ds(*self.slots)]
        self.copies = [
            remote(
                span(grad, self.axis, (1 - bit) * self.size, self.size), other,
                sems.at[0], sems.at[1], peer,
            ),
            local(span(grad, self.axis, bit * self.size, self.size), mine, sems.at[2]),
        ]

    def end(self):
        mine, other, sems = self.held
        wait_all(self.copies)
        self.out_refs[0][...] = (mine[...].astype(F32) + other[...].astype(F32)).astype(BF16)


class ColumnGather(Cargo):
    any_outs = True

    def __init__(self, weights, axes, targets, biases):
        self.axes = axes
        self.inputs = (*weights, targets, biases)
        self.outs = tuple(((2,) + one.shape, BF16) for one in weights) + (
            ((2, 2) + targets.shape[1:], BF16),
            ((2, 2) + biases.shape, F32),
        )
        self.scratch = (
            pltpu.SemaphoreType.DMA((5, 6)),
            pltpu.SemaphoreType.DMA((5, 2, 2)),
            pltpu.SemaphoreType.DMA((5,)),
        )

    def peers(self):
        return ["core", "cross"]

    def pieces(self, target):
        tensor, core = lax.axis_index("tensor"), core_bit()
        eighth = lax.axis_index("section") * 4 + y_bit() * 2 + core
        slot, out = lax.rem(tensor, 2), []
        for source, place, axis in zip(self.ins[:3], self.out_refs[:3], self.axes):
            size = source.shape[axis] // 8
            out.append(
                (
                    span(source, axis, eighth * size, size),
                    span(place.at[slot], axis, eighth * size, size),
                )
            )
        out.append((self.ins[3].at[target], self.out_refs[3].at[slot, core]))
        out.append((self.ins[4], self.out_refs[4].at[slot, core]))
        return out

    def copies(self, step):
        tensor, core = lax.axis_index("tensor"), core_bit()
        send, recv, own = self.held
        target = lax.rem(tensor + step, 4)
        peer = {"tensor": target, "dp": lax.axis_index("dp") - core + tensor // 2}
        return [
            describe(source, place, send.at[i, step], recv.at[i, lax.rem(tensor, 2), core], peer)
            for i, (source, place) in enumerate(self.pieces(target))
        ]

    def stays(self):
        return core_bit() == lax.axis_index("tensor") // 2

    def own_copies(self):
        own = self.held[2]
        return [
            pltpu.make_async_copy(source, place, own.at[i])
            for i, (source, place) in enumerate(self.pieces(lax.axis_index("tensor")))
        ]

    def direct(self, step, i):
        if step == 2 or i > 2:
            return None
        return lax.axis_index("tensor") != (3 if step == 1 else 0)

    def each(self, which, act):
        for step in range(1, 4):
            for i, copy in enumerate(self.copies(step)):
                if i in which:
                    allowed = self.direct(step, i)
                    if allowed is None:
                        act(copy)
                    else:

                        @pl.when(allowed)
                        def go(copy=copy):
                            act(copy)

    def start(self, which):
        self.each(which, lambda copy: copy.start())

        @pl.when(self.stays())
        def keep():
            for i, copy in enumerate(self.own_copies()):
                if i in which:
                    copy.start()

        @pl.when(jnp.logical_not(self.stays()))
        def give():
            for i, copy in enumerate(self.copies(0)):
                if i in which:
                    copy.start()

    def passes_on(self):
        tensor, core = lax.axis_index("tensor"), core_bit()
        return jnp.logical_or(
            jnp.logical_and(tensor == 2, core == 0), jnp.logical_and(tensor == 1, core == 1)
        )

    def passed(self, i, other):
        send, recv, own = self.held
        tensor, slot = lax.axis_index("tensor"), core_bit()
        size = self.ins[i].shape[self.axes[i]] // 8
        eighth = lax.axis_index("section") * 4 + y_bit() * 2 + other
        part = span(self.out_refs[i].at[slot], self.axes[i], eighth * size, size)
        return describe(
            part, part, send.at[i, 4 + other], recv.at[i, slot, other], {"tensor": 3 * (tensor - 1)}
        )

    def relay(self, which):
        @pl.when(self.passes_on())
        def pass_on():
            for i in which:
                for other in range(2):
                    copy = self.passed(i, other)
                    copy.wait_recv()
                    copy.start()

    def begin(self):
        self.start((3, 4))

    def middle(self):
        self.start((0, 2))

    def end(self):
        send, recv, own = self.held
        tensor, core = lax.axis_index("tensor"), core_bit()
        self.each(range(5), lambda copy: copy.wait_send())

        @pl.when(self.stays())
        def kept():
            for copy in self.own_copies():
                copy.wait()

        @pl.when(jnp.logical_not(self.stays()))
        def given():
            for copy in self.copies(0):
                copy.wait_send()

        @pl.when(self.passes_on())
        def passed_on():
            for i in range(3):
                for other in range(2):
                    self.passed(i, other).wait_send()

        for slot in range(2):
            for other in range(2):
                mine = jnp.logical_and(2 * core + slot == tensor, core == other)
                relayed = jnp.logical_and(self.passes_on(), core == slot)
                peer = {"tensor": lax.rem(tensor + 1, 4)}
                waits = [
                    describe(source, place, send.at[i, 1], recv.at[i, slot, other], peer)
                    for i, (source, place) in enumerate(self.pieces(tensor))
                ]

                @pl.when(jnp.logical_not(mine))
                def arrived(waits=waits):
                    for copy in waits[3:]:
                        copy.wait_recv()

                @pl.when(jnp.logical_not(jnp.logical_or(mine, relayed)))
                def weights_arrived(waits=waits):
                    for copy in waits[:3]:
                        copy.wait_recv()


class ShareAlong(Cargo):
    any_outs = True

    def __init__(self, weights, axes, stage):
        self.axes = axes
        self.inputs = tuple(weights)
        self.outs = tuple((one.shape, BF16) for one in weights)
        self.aliases = {0: 0, 1: 1, 2: 2}
        self.stage = stage
        self.scratch = (pltpu.SemaphoreType.DMA((4,)), pltpu.SemaphoreType.DMA((4,)))

    def peers(self):
        return ["x", "y"]

    def begin(self):
        send, recv = self.held
        section, y, self.copies = lax.axis_index("section"), y_bit(), []

        def give(which, start, parts, peer):
            ref, axis = self.out_refs[which], self.axes[which]
            size = ref.shape[axis + 1] // 4
            part = span(ref, axis, start * size, parts * size)
            i = len(self.copies)
            self.copies.append(remote(part, part, send.at[i], recv.at[i], peer))

        if self.stage == 0:
            give(1, 2 * section + y, 1, x_peer())
            give(0, 2 * section + y, 1, y_peer())
            give(2, 2 * section + y, 1, y_peer())
        elif self.stage == 1:
            give(0, 2 * section, 2, x_peer())
            give(1, y, 1, y_peer())
        else:
            give(2, 2 * section, 2, x_peer())
            give(1, 2 + y, 1, y_peer())

    def end(self):
        wait_all(self.copies)


class ColumnSum(Cargo):
    def __init__(self, grads, axis):
        self.axis = axis
        self.part = cut(grads[0].shape[1:], axis, 2)
        self.inputs = tuple(grads)
        self.outs = ((self.part, F32),)
        self.scratch = (
            pltpu.VMEM((4,) + self.part, BF16),
            pltpu.SemaphoreType.DMA((4,)),
            pltpu.SemaphoreType.DMA((4,)),
            pltpu.SemaphoreType.DMA,
        )

    def peers(self):
        return ["core", "cross"]

    def copy(self, slot, other):
        got, send, recv, own = self.held
        tensor, core = lax.axis_index("tensor"), core_bit()
        size = self.part[self.axis]
        ref = self.ins[0].at[slot] if len(self.ins) == 1 else self.ins[slot].at[0]
        source = span(ref, self.axis, other * size, size)
        peer = {"tensor": 2 * core + slot, "dp": lax.axis_index("dp") - core + other}
        mine = jnp.logical_and(2 * core + slot == tensor, core == other)
        away = describe(source, got.at[tensor], send.at[2 * slot + other], recv.at[tensor], peer)
        return mine, away, pltpu.make_async_copy(source, got.at[tensor], own)

    def each(self, act_away, act_own):
        for slot in range(2):
            for other in range(2):
                mine, away, own = self.copy(slot, other)

                @pl.when(mine)
                def stay(own=own):
                    act_own(own)

                @pl.when(jnp.logical_not(mine))
                def leave(away=away):
                    act_away(away)

    def begin(self):
        self.each(lambda copy: copy.start(), lambda copy: copy.start())

    def end(self):
        got, send, recv, own = self.held
        tensor, core = lax.axis_index("tensor"), core_bit()
        self.each(lambda copy: copy.wait_send(), lambda copy: copy.wait())
        for source in range(4):
            mine = jnp.logical_and(tensor == source, core == tensor // 2)

            @pl.when(jnp.logical_not(mine))
            def arrived(source=source):
                describe(
                    got.at[source], got.at[source], send.at[0], recv.at[source],
                    {"tensor": lax.rem(tensor + 1, 4)},
                ).wait_recv()

        total = got[0].astype(F32)
        for source in range(1, 4):
            total = total + got[source].astype(F32)
        self.out_refs[0][...] = total


def cross_peers():
    tensor, dp = lax.axis_index("tensor"), core_peer()["dp"]
    return [{"tensor": lax.rem(tensor + step, 4), "dp": dp} for step in range(1, 4)]


class Bundle:
    def __init__(self, cargos):
        self.cargos = cargos
        self.loads, self.stores = {}, {}

    def load(self):
        for copy in self.loads.values():
            copy.start()

    def need(self, *which):
        for i in which:
            if i in self.loads:
                self.loads[i].wait()

    def flush(self, *which):
        for i in which:
            if i in self.stores:
                self.stores[i].start()

    def peers(self, names=()):
        names = list(names) + [name for cargo in self.cargos for name in cargo.peers()]
        known = {"core": core_peer, "y": y_peer, "x": x_peer}
        cross = cross_peers() if "cross" in names else []
        return [make() for name, make in known.items() if name in names] + cross

    def begin(self):
        for cargo in self.cargos:
            cargo.begin()

    def middle(self):
        for cargo in self.cargos:
            cargo.middle()

    def late(self):
        for cargo in self.cargos:
            cargo.late()

    def end(self):
        for copy in self.stores.values():
            copy.wait()
        for cargo in self.cargos:
            cargo.end()


def attend_body(
    count, peers, u_ref, mods, segs, biases, outs, scratch, sems, need_qkv, need_out, steps, flush
):
    middle_ref, branch_ref, full_ref, q_ref, k_ref, v_ref, probs_ref, mixed_ref = outs
    full, wqkv, wo, mixed_wide = (full_ref, *scratch[:3])
    buffers, spreads = scratch[3:6], scratch[6]
    seg_own, seg_col, seg_row = segs
    await_peers = call_peers(peers) if peers is not None else None
    mod_ref = mods()
    me = lax.axis_index("tensor")
    rows, length, width = u_ref.shape
    heads_width = wo.shape[0]
    heads = heads_width // HEAD_WIDTH
    u = flat(u_ref).astype(F32)
    normed, unused = layer_norm(u)
    attn_in = normed * (1.0 + token_mod(mod_ref, seg_own, 1)) + token_mod(mod_ref, seg_own, 0)
    full[:, own_rows(me, length), :] = attn_in.astype(BF16).reshape(rows, length, width)
    if peers is not None:
        await_peers()
    line = Line(length, sems)
    line.start_gather(full)
    spread = spread_matrix(heads_width)
    line.relay(full)
    steps[0]()
    both = 3 * heads_width
    for which in range(3):
        spreads[which] = spread_matrix(heads_width, which, both)
    need_qkv()
    line.finish_gather(full)
    flush(2)
    tokens = flat(full)
    bias = biases()
    projected = (dot(tokens, wqkv[...]) + bias[0:1, :both]).astype(BF16)
    for which, target in enumerate((q_ref, k_ref, v_ref)):
        parts = dot(projected, spreads[which])
        target[...] = parts.astype(BF16).reshape(target.shape)

    def one_head(index, carry):
        row = index // heads
        head = lax.rem(index, heads)
        lanes = pl.ds(pl.multiple_of(head * HEAD_LANES, HEAD_LANES), HEAD_LANES)
        scores = dot(q_ref[row, :, lanes], k_ref[row, :, lanes], NT) * HEAD_WIDTH ** (-0.5)
        scores = jnp.where(seg_col[row] == seg_row[row], scores, MASKED_SCORE)
        raised = jnp.exp(scores - jnp.max(scores, axis=-1, keepdims=True))
        probs = raised / jnp.sum(raised, axis=-1, keepdims=True)
        probs_ref[index] = probs
        mixed_wide[row, :, lanes] = dot(probs.astype(BF16), v_ref[row, :, lanes]).astype(BF16)
        return carry

    steps[1]()
    lax.fori_loop(0, rows * heads, one_head, 0, unroll=4)
    mixed_ref[...] = dot(flat(mixed_wide), spread, NT).astype(BF16).reshape(mixed_ref.shape)
    flush(3, 4, 5, 6, 7)
    need_out()

    def partial(which_rows):
        return dot(mixed_ref[:, which_rows, :].reshape(rows * length, heads_width), wo[...])

    total = line.scatter_sum(partial, buffers)
    steps[2]()
    branch = line.finish_sum(total, buffers) + bias[2:3, :]
    branch_ref[...] = branch.reshape(branch_ref.shape)
    middle = flat(u_ref).astype(F32) + token_mod(mod_ref, seg_own, 2) * branch
    middle_ref[...] = middle.reshape(middle_ref.shape)


def open_kernel(count, sections, *refs, cargo):
    u_ref, cond_ref, ada_b_ref, biases_ref, seg_own, seg_col, seg_row = refs[:7]
    ada_w, own_qkv, own_out, own_one, own_two = refs[7:12]
    mods_ref, bias_ref, other_qkv, other_out, other_one, other_two = refs[12:18]
    outs = refs[18:26]
    scratch = refs[26:33]
    ada, mod_src, mod_buf, bias_buf, w_sem, ag_send, ag_recv, rs_send, rs_recv = refs[33:42]
    mod_send, mod_recv, share_send, share_recv, ada_sem = refs[42:]
    wqkv, wo = scratch[:2]
    section, tensor = lax.axis_index("section"), lax.axis_index("tensor")
    load_ada = local(ada_w, ada, ada_sem)
    shares = [
        Share(own, other, parts, (share_send.at[i], share_recv.at[i]))
        for i, (own, other, parts) in enumerate(
            (
                (own_qkv, other_qkv, 4), (own_out, other_out, 2),
                (own_one, other_one, 4), (own_two, other_two, 4),
            )
        )
    ]
    plane = [
        {"section": lax.rem(section + a, sections), "tensor": lax.rem(tensor + b, count)}
        for a in range(sections)
        for b in range(count)
        if a or b
    ]
    greet(plane + [core_peer(), y_peer()] + cross_peers())
    cond_act = silu(cond_ref[...].astype(F32)).astype(BF16)
    load_ada.wait()
    mod = dot(cond_act, ada[...], NT) + ada_b_ref[...].astype(F32)
    mod_src[...] = mod.reshape(mod_src.shape)
    mod_buf[section, tensor] = mod_src[section]
    copies = [
        remote(
            mod_src.at[peer["section"]], mod_buf.at[section, tensor],
            mod_send.at[i], mod_recv.at[i], peer,
        )
        for i, peer in enumerate(plane)
    ]
    bias_buf[section] = biases_ref[...]
    bias_copy = remote(
        biases_ref, bias_buf.at[section],
        mod_send.at[len(plane)], mod_recv.at[len(plane)], x_peer(),
    )
    for share in shares:
        share.begin()
    cargo.begin()

    def mods():
        wait_all(copies)
        width, piece = mods_ref.shape[-1], mod_buf.shape[-1]
        for block in range(sections):
            for which in range(6):
                parts, at = [], which * width
                while at < (which + 1) * width:
                    end = min((at // piece + 1) * piece, (which + 1) * width)
                    start = at - at // piece * piece
                    parts.append(mod_buf[block, at // piece][:, start : start + end - at])
                    at = end
                mods_ref[block, which] = (
                    jnp.concatenate(parts, axis=1) if len(parts) > 1 else parts[0]
                )
        return mods_ref.at[0]

    def biases():
        bias_copy.wait()
        bias_ref[...] = bias_buf[...]
        return bias_buf[0]

    def need_qkv():
        fetch(0, own_qkv, other_qkv, wqkv, w_sem.at[0]).wait()

    def need_out():
        shares[1].finish()
        fetch(0, own_out, other_out, wo, w_sem.at[1]).wait()

    def after_gather():
        shares[0].forward(shares[0].first)
        cargo.middle()
        shares[1].forward(shares[1].first)
        shares[0].forward_again()
        shares[0].finish()

    def before_heads():
        cargo.late()
        shares[2].forward(shares[2].first)

    def after_scatter():
        cargo.cargos[0].start((1,))
        cargo.cargos[0].relay((0, 2))
        shares[2].forward_again()
        shares[3].forward(shares[3].first)
        shares[2].finish()

    attend_body(
        count, None, u_ref, mods, (seg_own, seg_col, seg_row), biases, outs, scratch,
        (ag_send, ag_recv, rs_send, rs_recv), need_qkv, need_out,
        (after_gather, before_heads, after_scatter),
        lambda *which: cargo.flush(*(6 + i for i in which)),
    )
    shares[3].forward_again()
    cargo.cargos[0].relay((1,))
    cargo.end()
    shares[3].finish()


def attend_kernel(count, block, *refs, cargo):
    u_ref, mods_ref, bias_ref, seg_own, seg_col, seg_row = refs[:6]
    own_qkv, other_qkv, own_out, other_out = refs[6:10]
    outs, scratch, w_sem = refs[10:18], refs[18:25], refs[25]
    load_qkv = fetch(block, own_qkv, other_qkv, scratch[0], w_sem.at[0])
    load_out = fetch(block, own_out, other_out, scratch[1], w_sem.at[1])
    attend_body(
        count, z_peers(count) + cargo.peers(), u_ref, lambda: mods_ref.at[block],
        (seg_own, seg_col, seg_row), lambda: bias_ref[block], outs, scratch, refs[26:30],
        load_qkv.wait, load_out.wait, (cargo.begin, cargo.middle, cargo.late), cargo.flush,
    )
    cargo.end()


def mlp_kernel(
    count, block,
    middle_ref, mods_ref, bias_ref, seg_own, w1_own, w1_other, w2_own, w2_other,
    out_ref, branch_ref, full_ref, pre_ref, act_ref,
    w1, w2, send_buf, recv_buf, relay_buf, w_sem, *sems, cargo,
):
    full = full_ref
    await_peers = call_peers(z_peers(count) + cargo.peers())
    me = lax.axis_index("tensor")
    rows, length, width = middle_ref.shape
    mod_ref = mods_ref.at[block]
    load_one = fetch(block, w1_own, w1_other, w1, w_sem.at[0])
    load_two = fetch(block, w2_own, w2_other, w2, w_sem.at[1])
    normed, unused = layer_norm(flat(middle_ref))
    mlp_in = normed * (1.0 + token_mod(mod_ref, seg_own, 4)) + token_mod(mod_ref, seg_own, 3)
    full[:, own_rows(me, length), :] = mlp_in.astype(BF16).reshape(rows, length, width)
    await_peers()
    line = Line(length, sems)
    line.start_gather(full)
    cargo.begin()
    line.relay(full)
    load_one.wait()
    load_two.wait()

    def hidden(place):
        which_rows = own_rows(place, length)
        pre = dot(full[:, which_rows, :].reshape(rows * length, width), w1[...])
        pre = pre + bias_ref[block, 3:4, : w1.shape[1]]
        pre_ref[:, which_rows, :] = pre.reshape(rows, length, -1)
        act_ref[:, which_rows, :] = gelu_tanh(pre).astype(BF16).reshape(rows, length, -1)

    def prepare(place):
        line.arrived(full, place)
        hidden(place)

    def partial(which_rows):
        return dot(act_ref[:, which_rows, :].reshape(rows * length, -1), w2[...])

    hidden(me)
    hidden(line.opposite)
    buffers = (send_buf, recv_buf, relay_buf)
    total = line.scatter_sum(partial, buffers, prepare)
    cargo.flush(2, 3, 4)
    line.sent(full)
    cargo.middle()
    branch = line.finish_sum(total, buffers) + bias_ref[block, 4:5, :]
    cargo.end()
    branch_ref[...] = branch.reshape(branch_ref.shape)
    out = flat(middle_ref) + token_mod(mod_ref, seg_own, 5) * branch
    out_ref[...] = out.astype(BF16).reshape(out_ref.shape)


def mlp_back_kernel(count, block, given, *refs, cargo):
    g_refs, refs = refs[:given], refs[given:]
    g_ref = g_refs[0]
    middle_ref, branch_ref, mods_ref, seg_own, full_ref, pre_ref, act_ref = refs[:7]
    w1_own, w1_other, w2_own, w2_other = refs[7:11]
    d_middle_ref, d_mod_ref, d_w1_ref, d_w2_ref, d_b1_ref, d_b2_ref = refs[11:17]
    full, d_pre, w1, w2, *buffers, w_sem = refs[17:25]
    sems = refs[25:29]
    w1_whole, w1_got, w1_sems, w2_whole, w2_got, w2_sems, normed_buf, g_buf = refs[29:]
    w1_sum = CoreSum(w1_whole, w1_got, d_w1_ref, w1_sems)
    w2_sum = CoreSum(w2_whole, w2_got, d_w2_ref, w2_sems)
    me = lax.axis_index("tensor")
    rows, length, width = middle_ref.shape
    mod_ref = mods_ref.at[block]
    load_one = fetch(block, w1_own, w1_other, w1, w_sem.at[0])
    load_two = fetch(block, w2_own, w2_other, w2, w_sem.at[1])
    await_peers = call_peers(z_peers(count) + cargo.peers(["core"]))
    cargo.load()
    g = flat(g_ref).astype(F32)
    if len(g_refs) > 1:
        g = g + flat(g_refs[1])
    g_buf[...] = g
    d_branch = (g * token_mod(mod_ref, seg_own, 5)).astype(BF16)
    full[:, own_rows(me, length), :] = d_branch.reshape(rows, length, width)
    await_peers()
    line = Line(length, sems)
    line.start_gather(full)
    cargo.begin()
    slot_sums(g * flat(branch_ref), seg_own, d_mod_ref, 2)
    line.relay(full)
    cargo.middle()
    normed, inverse = layer_norm(flat(middle_ref))
    normed_buf[...] = normed
    load_two.wait()
    cargo.need(given + 5)

    def d_hidden(place):
        which_rows = own_rows(place, length)
        d_act = dot(full[:, which_rows, :].reshape(rows * length, width), w2[...], NT)
        slope = gelu_slope(pre_ref[:, which_rows, :].reshape(rows * length, -1))
        d_pre[:, which_rows, :] = (d_act * slope).astype(BF16).reshape(rows, length, -1)

    def prepare(place):
        line.arrived(full, place)
        d_hidden(place)

    d_hidden(me)
    d_hidden(line.opposite)
    load_one.wait()

    def partial(which_rows):
        return dot(d_pre[:, which_rows, :].reshape(rows * length, -1), w1[...], NT)

    total = line.scatter_sum(partial, buffers, prepare)
    line.sent(full)
    cargo.need(given + 4, given + 6)
    w2_whole[...] = dot(flat(full), flat(act_ref), TN).astype(BF16)
    w2_sum.begin()
    w1_whole[...] = dot(flat(full_ref), flat(d_pre), TN).astype(BF16)
    w1_sum.begin()
    d_b2_ref[...] = jnp.sum(flat(full).astype(F32), axis=0, keepdims=True)
    d_b1_ref[...] = jnp.sum(flat(d_pre).astype(F32), axis=0, keepdims=True)
    d_in = line.finish_sum(total, buffers)
    normed = normed_buf[...]
    d_middle = g_buf[...] + norm_back(
        d_in * (1.0 + token_mod(mod_ref, seg_own, 4)), normed, inverse
    )
    d_middle_ref[...] = d_middle.reshape(d_middle_ref.shape)
    slot_sums(d_in, seg_own, d_mod_ref, 0)
    slot_sums(d_in * normed, seg_own, d_mod_ref, 1)
    w2_sum.end()
    w1_sum.end()
    cargo.end()


def attend_back_kernel(count, block, *refs, cargo):
    d_middle_ref, u_ref, branch_ref, mods_ref, seg_own, full_ref = refs[:6]
    q_ref, k_ref, v_ref, probs_ref, mixed_ref = refs[6:11]
    wqkv_own, wqkv_other, wo_own, wo_other = refs[11:15]
    d_in_ref, d_mod_ref, d_wqkv_ref, d_wo_ref, d_bqv_ref, d_bo_ref = refs[15:21]
    full, wide, narrow, wqkv, wo, *buffers, w_sem = refs[21:30]
    sems = refs[30:34]
    qkv_whole, qkv_got, qkv_sems, wo_whole, wo_got, wo_sems, spreads, normed_buf = refs[34:]
    qkv_sum = CoreSum(qkv_whole, qkv_got, d_wqkv_ref, qkv_sems)
    wo_sum = CoreSum(wo_whole, wo_got, d_wo_ref, wo_sems)
    me = lax.axis_index("tensor")
    rows, length, width = u_ref.shape
    heads_width = wo.shape[0]
    heads = heads_width // HEAD_WIDTH
    mod_ref = mods_ref.at[block]
    load_qkv = fetch(block, wqkv_own, wqkv_other, wqkv, w_sem.at[0])
    load_out = fetch(block, wo_own, wo_other, wo, w_sem.at[1])
    await_peers = call_peers(z_peers(count) + cargo.peers(["core"]))
    cargo.load()
    d_middle = flat(d_middle_ref)
    d_branch = (d_middle * token_mod(mod_ref, seg_own, 2)).astype(BF16)
    full[:, own_rows(me, length), :] = d_branch.reshape(rows, length, width)
    await_peers()
    line = Line(length, sems)
    line.start_gather(full)
    cargo.begin()
    slot_sums(d_middle * flat(branch_ref), seg_own, d_mod_ref, 2)
    line.relay(full)
    cargo.middle()
    spread = spread_matrix(heads_width)
    both = 3 * heads_width
    for which in range(3):
        spreads[which] = spread_matrix(heads_width, which, both)
    normed, inverse = layer_norm(flat(u_ref).astype(F32))
    normed_buf[...] = normed
    load_out.wait()
    line.finish_gather(full)
    d_mixed = dot(flat(full), wo[...], NT).astype(BF16)
    wide[3] = dot(d_mixed, spread).astype(BF16).reshape(wide.shape[1:])
    cargo.need(6, 7, 8, 9)

    def one_head(index, carry):
        row = index // heads
        head = lax.rem(index, heads)
        lanes = pl.ds(pl.multiple_of(head * HEAD_LANES, HEAD_LANES), HEAD_LANES)
        grad = wide[3, row, :, lanes]
        probs = probs_ref[index]
        d_probs = dot(grad, v_ref[row, :, lanes], NT)
        d_scores = (
            probs * (d_probs - jnp.sum(d_probs * probs, axis=-1, keepdims=True))
        ).astype(BF16)
        scale = HEAD_WIDTH ** (-0.5)
        wide[0, row, :, lanes] = (dot(d_scores, k_ref[row, :, lanes]) * scale).astype(BF16)
        wide[1, row, :, lanes] = (dot(d_scores, q_ref[row, :, lanes], TN) * scale).astype(BF16)
        wide[2, row, :, lanes] = dot(probs.astype(BF16), grad, TN).astype(BF16)
        return carry

    lax.fori_loop(0, rows * heads, one_head, 0, unroll=8)
    gathered = 0.0
    for which in range(3):
        gathered = gathered + dot(flat(wide.at[which]), spreads[which], NT)
    narrow[...] = gathered.astype(BF16).reshape(narrow.shape)
    load_qkv.wait()

    def partial(which_rows):
        return dot(narrow[:, which_rows, :].reshape(rows * length, both), wqkv[...], NT)

    total = line.scatter_sum(partial, buffers)
    d_bo_ref[...] = jnp.sum(flat(full).astype(F32), axis=0, keepdims=True)
    d_bqv_ref[...] = jnp.sum(flat(narrow).astype(F32), axis=0, keepdims=True)
    cargo.need(5, 10)
    wo_whole[...] = dot(flat(full), flat(mixed_ref), TN).astype(BF16)
    wo_sum.begin()
    qkv_whole[...] = dot(flat(full_ref), flat(narrow), TN).astype(BF16)
    qkv_sum.begin()
    d_attn_in = line.finish_sum(total, buffers)
    normed = normed_buf[...]
    d_in = flat(d_middle_ref) + norm_back(
        d_attn_in * (1.0 + token_mod(mod_ref, seg_own, 1)), normed, inverse
    )
    d_in_ref[...] = d_in.reshape(d_in_ref.shape)
    slot_sums(d_attn_in, seg_own, d_mod_ref, 0)
    slot_sums(d_attn_in * normed, seg_own, d_mod_ref, 1)
    wo_sum.end()
    qkv_sum.end()
    cargo.end()


def silu_slope(value):
    gate = 1.0 / (1.0 + jnp.exp(-value))
    return gate * (1.0 + value * (1.0 - gate))


def project_kernel(token_count, *refs, cargo):
    sent_ref, targets_ref, biases_ref, p2_b_ref, p1_any, p2_any, p3_any = refs[:7]
    d_sent_ref, d_p1_ref, d_p2_ref, d_p3_ref, small_ref = refs[7:12]
    p1, p2, p3, tokens, first_pre, first, second_pre, second, d_second, norms = refs[12:22]
    buf_a, buf_b, buf_c, d_first, load_sem, send, recv = refs[22:]
    core, peer = core_bit(), core_peer()
    loads = [
        local(source, place, load_sem.at[i])
        for i, (source, place) in enumerate(((p1_any, p1), (p2_any, p2), (p3_any, p3)))
    ]
    count = tokens.shape[1]
    tokens[core] = flat(sent_ref)
    greet([peer])

    def trade(ref, which):
        return remote(ref.at[core], ref.at[core], send.at[which], recv.at[which], peer)

    def give(buffer, value, which):
        buffer[0] = value.astype(BF16)
        return remote(buffer.at[0], buffer.at[1], send.at[which], recv.at[which], peer)

    def block(ref, side):
        return ref[side]

    copy = trade(tokens, 0)
    target = [
        targets_ref[slot].reshape(2 * count, targets_ref.shape[-1]).astype(F32) for slot in range(2)
    ]
    target_sq = sum(jnp.sum(one * one, axis=1, keepdims=True) for one in target)
    loads[0].wait()
    copy.wait()
    all_tokens = flat(tokens)
    for slot in range(2):
        pre = dot(all_tokens, p1[slot]) + biases_ref[slot, 0, 0:1, :]
        first_pre[slot] = pre
        first[slot] = silu(pre).astype(BF16)
    loads[1].wait()

    def second_term(side):
        rows = pl.ds(pl.multiple_of(side * count, 16), count)
        return dot(first[0, rows, :], p2[0]) + dot(first[1, rows, :], p2[1])

    copy = give(buf_a, second_term(1 - core), 1)
    pre = second_term(core)
    copy.wait()
    pre = pre + buf_a[1].astype(F32) + p2_b_ref[...].astype(F32)
    second_pre[...] = pre
    second[core] = silu(pre).astype(BF16)
    copy = trade(second, 2)
    loads[2].wait()
    copy.wait()
    all_second = flat(second)
    width = target[0].shape[1]
    predicted = [
        dot(all_second, p3[slot], NT) + biases_ref[slot, 0, 1:2, :width] for slot in range(2)
    ]
    pred_sq = sum(jnp.sum(one * one, axis=1, keepdims=True) for one in predicted)
    cross = sum(
        jnp.sum(one * two, axis=1, keepdims=True) for one, two in zip(predicted, target)
    )
    lanes = lax.broadcasted_iota(jnp.int32, norms.shape[1:], 1)
    norms[core] = jnp.where(lanes == 0, pred_sq, jnp.where(lanes == 1, cross, target_sq))
    copy = trade(norms, 3)
    copy.wait()
    total = norms[0] + norms[1]
    inv_pred = lax.rsqrt(total[:, 0:1] + COSINE_EPS)
    inv_target = lax.rsqrt(total[:, 2:3] + COSINE_EPS)
    cosine = total[:, 1:2] * inv_pred * inv_target
    side = lax.broadcasted_iota(jnp.int32, cosine.shape, 0)
    own = jnp.logical_and(side >= core * count, side < (core + 1) * count)
    loss = jnp.sum(jnp.where(own, cosine, 0.0), axis=0, keepdims=True)
    factor = -0.5 / token_count
    one_scale = factor * inv_pred * inv_target
    two_scale = factor * cosine * inv_pred * inv_pred
    d_pred = [
        (one_scale * two - two_scale * one).astype(BF16) for one, two in zip(predicted, target)
    ]
    small_ref[...] = jnp.zeros_like(small_ref)
    for slot in range(2):
        small_ref[2 * core + slot, 1:2, :width] = jnp.sum(
            d_pred[slot].astype(F32), axis=0, keepdims=True
        )

    def d_second_term(side):
        terms = 0.0
        for slot in range(2):
            mine = jnp.where(
                side == 0, d_pred[slot][:count].astype(F32), d_pred[slot][count:].astype(F32)
            )
            terms = terms + dot(mine.astype(BF16), p3[slot])
        return terms

    copy = give(buf_b, d_second_term(1 - core), 4)
    grad = d_second_term(core)
    for slot in range(2):
        d_p3_ref[slot] = dot(d_pred[slot], all_second, TN).astype(BF16)
    copy.wait()
    grad = ((grad + buf_b[1].astype(F32)) * silu_slope(second_pre[...])).astype(BF16)
    d_second[core] = grad
    copy = trade(d_second, 5)
    d_p2_b = jnp.sum(grad.astype(F32), axis=0, keepdims=True)
    lane = small_ref.shape[2]
    loss_row = jnp.where(lax.broadcasted_iota(jnp.int32, (1, lane), 1) == 0, loss, 0.0)
    for part in range(4):
        for row in range(d_p2_b.shape[1] // lane):
            small_ref[part, 2 + row : 3 + row, :] = d_p2_b[:, row * lane : (row + 1) * lane]
        small_ref[part, 6:7, :] = loss_row
    copy.wait()
    all_d_second = flat(d_second)
    for slot in range(2):
        back = dot(all_d_second, p2[slot], NT) * silu_slope(first_pre[slot])
        d_first[slot] = back.astype(BF16)
        small_ref[2 * core + slot, 0:1, :] = jnp.sum(
            d_first[slot].astype(F32), axis=0, keepdims=True
        )

    def d_sent_term(side):
        rows = pl.ds(pl.multiple_of(side * count, 16), count)
        return dot(d_first[0, rows, :], p1[0], NT) + dot(d_first[1, rows, :], p1[1], NT)

    copy = give(buf_c, d_sent_term(1 - core), 6)
    grad = d_sent_term(core)
    for slot in range(2):
        d_p2_ref[slot] = dot(first[slot], all_d_second, TN).astype(BF16)
        d_p1_ref[slot] = dot(all_tokens, d_first[slot], TN).astype(BF16)
    copy.wait()
    d_sent_ref[...] = (grad + buf_c[1].astype(F32)).reshape(d_sent_ref.shape)


def close_kernel(count, sections, replicas, *refs, cargo):
    grads_ref, mod_refs, small_refs, proj_ref, cond_ref = (
        refs[:2], refs[2:6], refs[6:14], refs[14], refs[15]
    )
    grad_ref, ada_w_ref, ada_b_ref, small_ref, proj_sum_ref = refs[16:21]
    z_src, z_buf, mod_src, mod_buf, small_src, small_buf, cond_buf = refs[21:28]
    place_src, place_buf, proj_got, proj_src, proj_buf = refs[28:33]
    sems = refs[33:35]
    section, tensor, replica = (lax.axis_index(name) for name in ("section", "tensor", "dp"))
    send, recv = sems
    others = [
        {"section": lax.rem(section + a, sections), "dp": lax.rem(replica + b, replicas)}
        for a in range(sections)
        for b in range(replicas)
        if a or b
    ]
    greet(z_peers(count) + others + cross_peers())
    last_sums = [one for one in cargo.cargos if isinstance(one, LastSum)]
    y_sums = [one for one in cargo.cargos if type(one) is YSum]
    for one in last_sums:
        one.begin()
    piece = z_src.shape[-1]
    for block in range(sections):
        attend_mod, mlp_mod = mod_refs[2 * block : 2 * block + 2]
        width = attend_mod.shape[-1]
        for part in range(count):
            at, end, cuts = part * piece, (part + 1) * piece, []
            while at < end:
                which = at // width
                stop = min((which + 1) * width, end)
                ref = attend_mod if which < 3 else mlp_mod
                cuts.append(ref[which % 3][:, at - which * width : stop - which * width])
                at = stop
            z_src[part, block] = jnp.concatenate(cuts, axis=1) if len(cuts) > 1 else cuts[0]
    z_copies = [
        remote(z_src.at[peer["tensor"]], z_buf.at[i], send.at[i], recv.at[i], peer)
        for i, peer in enumerate(z_peers(count))
    ]
    at = count - 1
    z_copies += [
        remote(proj_ref.at[peer["tensor"]], proj_got.at[i], send.at[at + i], recv.at[at + i], peer)
        for i, peer in enumerate(z_peers(count))
    ]
    at = at + count - 1

    @pl.when(section == 0)
    def first_place():
        place_src[...] = grads_ref[1][...].astype(BF16)

    @pl.when(section != 0)
    def second_place():
        place_src[...] = grads_ref[0][...].astype(BF16)

    place_copy = remote(place_src, place_buf, send.at[at], recv.at[at], x_peer())
    at = at + 1
    both = small_refs[0].shape[-1]
    small_src[...] = jnp.zeros_like(small_src)
    for block in range(sections):
        d_bqv, d_bo, d_b1, d_b2 = small_refs[4 * block : 4 * block + 4]
        small_src[block, 0:1, :both] = d_bqv[...]
        small_src[block, 2:3, :] = d_bo[...]
        small_src[block, 3:4, : d_b1.shape[1]] = d_b1[...]
        small_src[block, 4:5, :] = d_b2[...]
    small_buf[section, replica] = small_src[section]
    cond_buf[section, replica] = cond_ref[replica]
    copies = []
    for peer in others:
        copies.append(
            remote(
                small_src.at[peer["section"]], small_buf.at[section, replica],
                send.at[at], recv.at[at], peer,
            )
        )
        copies.append(
            remote(
                cond_ref.at[peer["dp"]], cond_buf.at[section, replica],
                send.at[at + 1], recv.at[at + 1], peer,
            )
        )
        at = at + 2
    for one in cargo.cargos:
        if not isinstance(one, YSum):
            one.begin()
    wait_all(z_copies)
    mine, mine_proj = z_src[tensor], proj_ref[tensor]
    for step in range(count - 1):
        mine = mine + z_buf[step]
        mine_proj = mine_proj + proj_got[step]
    mod_src[...] = mine
    mod_buf[section, replica] = mod_src[section]
    proj_src[...] = mine_proj
    proj_buf[section, replica] = mine_proj
    for peer in others:
        copies.append(
            remote(
                mod_src.at[peer["section"]], mod_buf.at[section, replica],
                send.at[at], recv.at[at], peer,
            )
        )
        copies.append(
            remote(
                proj_src, proj_buf.at[section, replica], send.at[at + 1], recv.at[at + 1], peer
            )
        )
        at = at + 2
    for one in last_sums:
        one.middle()
    for one in y_sums:
        one.begin()
    place_copy.wait()
    rows = place_buf.shape[0]

    @pl.when(section == 0)
    def first_out():
        grad_ref[:rows] = grads_ref[0][...]
        grad_ref[rows:] = place_buf[...].astype(F32)

    @pl.when(section != 0)
    def second_out():
        grad_ref[rows:] = grads_ref[1][...]
        grad_ref[:rows] = place_buf[...].astype(F32)

    wait_all(copies)
    small, proj_sum = small_buf[0, 0], proj_buf[0, 0]
    for a in range(sections):
        for b in range(replicas):
            if a or b:
                small = small + small_buf[a, b]
                proj_sum = proj_sum + proj_buf[a, b]
    small_ref[...] = small
    proj_sum_ref[...] = proj_sum
    mod_all = flat(mod_buf)
    ada_b_ref[...] = jnp.sum(mod_all, axis=0, keepdims=True)
    ada_w_ref[...] = lax.dot_general(
        flat(cond_buf), mod_all, TN, precision=HIGHEST, preferred_element_type=F32
    )
    cargo.end()


VMEM = pl.BlockSpec(memory_space=pltpu.VMEM)
ANY = pl.BlockSpec(memory_space=pl.ANY)
MOD_ROWS = 8
PROJECTOR_AXES = (0, 0, 1)


def call(
    kernel, number, inputs, in_any, outs, out_any, scratch, flops, cargos=(), lazy=(), streamed=()
):
    own_in, own_out, own_scratch = len(inputs), len(outs), len(scratch)
    specs = [VMEM] * (own_in - in_any) + [ANY] * in_any
    specs = [ANY if i in lazy else spec for i, spec in enumerate(specs)]
    out_specs = [ANY if i in out_any or i in streamed else VMEM for i in range(own_out)]
    inputs, outs, scratch, aliases = list(inputs), list(outs), list(scratch), {}
    moved_refs = len(lazy) + len(streamed)
    scratch += [pltpu.VMEM(inputs[i].shape, inputs[i].dtype) for i in lazy]
    scratch += [pltpu.VMEM(*outs[i]) for i in streamed]
    if moved_refs:
        scratch.append(pltpu.SemaphoreType.DMA((moved_refs,)))
        moved_refs += 1
    for cargo in cargos:
        for source, target in cargo.aliases.items():
            aliases[len(inputs) + source] = len(outs) + target
        inputs += cargo.inputs
        outs += cargo.outs
        scratch += cargo.scratch
        specs += [ANY] * len(cargo.inputs)
        out_specs += [ANY if cargo.any_outs else VMEM] * len(cargo.outs)

    def body(*refs):
        parts = [list(refs[: len(inputs)])]
        parts.append(list(refs[len(inputs) : len(inputs) + len(outs)]))
        parts.append(list(refs[len(inputs) + len(outs) :]))
        base = parts[0][:own_in] + parts[1][:own_out] + parts[2][:own_scratch]
        held = parts[2][own_scratch : own_scratch + moved_refs]
        bundle = Bundle(cargos)
        for k, i in enumerate(lazy):
            bundle.loads[i] = pltpu.make_async_copy(base[i], held[k], held[-1].at[k])
            base[i] = held[k]
        for k, i in enumerate(streamed, len(lazy)):
            bundle.stores[i] = pltpu.make_async_copy(held[k], base[own_in + i], held[-1].at[k])
            base[own_in + i] = held[k]
        at = [own_in, own_out, own_scratch + moved_refs]
        for cargo in cargos:
            held = []
            for i, items in enumerate((cargo.inputs, cargo.outs, cargo.scratch)):
                held.append(parts[i][at[i] : at[i] + len(items)])
                at[i] += len(items)
            cargo.bind(*held)
        kernel(*base, cargo=bundle)

    moved = sum(math.prod(one.shape) * one.dtype.itemsize for one in inputs)
    results = pl.pallas_call(
        body,
        out_shape=[jax.ShapeDtypeStruct(shape, dtype) for shape, dtype in outs],
        in_specs=specs,
        out_specs=out_specs,
        scratch_shapes=scratch,
        input_output_aliases=aliases,
        compiler_params=pltpu.CompilerParams(
            collective_id=number, has_side_effects=True, vmem_limit_bytes=56 * 2**20
        ),
        cost_estimate=pl.CostEstimate(flops=flops, bytes_accessed=moved, transcendentals=0),
    )(*inputs)
    at, carried = own_out, []
    for cargo in cargos:
        carried.append(results[at : at + len(cargo.outs)])
        at += len(cargo.outs)
    return results[:own_out], carried


def exchange_scratch(count, rows, length, width):
    return [
        pltpu.VMEM((count - 1, rows, length, width), BF16),
        pltpu.VMEM((count, rows, length, width), BF16),
        pltpu.VMEM((rows, length, width), BF16),
    ]


def semaphores(count):
    return [pltpu.SemaphoreType.DMA((2,))] + [
        pltpu.SemaphoreType.DMA((size,)) for size in (count, count, count - 1, count + 1)
    ]


class Shapes:
    def __init__(self, u, own, count):
        self.rows, self.length, self.width = u.shape
        self.count = count
        self.positions = self.length * count
        self.tokens = self.rows * self.positions
        self.heads_width = own["out"].shape[0]
        self.hidden = own["one"].shape[1]
        self.heads = self.heads_width // HEAD_WIDTH
        self.local = (self.rows, self.length, self.width)
        self.full = (self.rows, self.positions, self.width)
        self.wide = (self.rows, self.positions, self.heads * HEAD_LANES)
        self.own = own
        self.attend_outs = [
            (self.local, F32), (self.local, F32), (self.full, BF16),
            (self.wide, BF16), (self.wide, BF16), (self.wide, BF16),
            ((self.rows * self.heads, self.positions, self.positions), F32),
            ((self.rows, self.positions, self.heads_width), BF16),
        ]
        self.attend_scratch = [
            pltpu.VMEM(own["qkv"].shape, BF16),
            pltpu.VMEM(own["out"].shape, BF16),
            pltpu.VMEM(self.wide, BF16),
        ] + exchange_scratch(count, *self.local)
        self.spreads = pltpu.VMEM((3, 3 * self.heads_width, self.heads * HEAD_LANES), BF16)
        self.attend_scratch.append(self.spreads)
        self.mods = (3, MOD_ROWS, self.width)


def pairs(own, other, names):
    out = []
    for name in names:
        out += [own[name], other[name]]
    return out


def open_forward(sizes, u, cond, ada_w, ada_b, biases, segs, own, sections, cargos):
    count, width = sizes.count, sizes.width
    piece = ada_w.shape[0]
    inputs = [u, cond, ada_b, biases, *segs, ada_w] + [own[n] for n in ("qkv", "out", "one", "two")]
    plane = sections * count - 1
    results, carried = call(
        functools.partial(open_kernel, count, sections),
        0,
        inputs,
        5,
        [((sections, 6, MOD_ROWS, width), F32), ((sections,) + biases.shape, F32)]
        + [(own[n].shape, BF16) for n in ("qkv", "out", "one", "two")]
        + sizes.attend_outs,
        (2, 3, 4, 5),
        sizes.attend_scratch
        + [
            pltpu.VMEM(ada_w.shape, BF16),
            pltpu.VMEM((sections, MOD_ROWS, piece), F32),
            pltpu.VMEM((sections, count, MOD_ROWS, piece), F32),
            pltpu.VMEM((sections,) + biases.shape, F32),
        ]
        + semaphores(count)
        + [
            pltpu.SemaphoreType.DMA((plane + 1,)),
            pltpu.SemaphoreType.DMA((plane + 1,)),
            pltpu.SemaphoreType.DMA((4, 4)),
            pltpu.SemaphoreType.DMA((4, 4)),
            pltpu.SemaphoreType.DMA,
        ],
        2 * sizes.tokens * width * sizes.heads_width * 4,
        cargos,
        streamed=tuple(range(8, 14)),
    )
    other = dict(zip(("qkv", "out", "one", "two"), results[2:6]))
    return results[0], results[1], other, results[6:], carried


def attend_forward(sizes, block, u, mods, biases, segs, own, other, cargos):
    inputs = [u, mods, biases, *segs] + pairs(own, other, ("qkv", "out"))
    return call(
        functools.partial(attend_kernel, sizes.count, block),
        1,
        inputs,
        4,
        sizes.attend_outs,
        (),
        sizes.attend_scratch + semaphores(sizes.count),
        2 * sizes.tokens * sizes.width * sizes.heads_width * 4,
        cargos,
        streamed=tuple(range(2, 8)),
    )


def mlp_forward(sizes, block, middle, mods, biases, segs, own, other, cargos):
    inputs = [middle, mods, biases, segs[0]] + pairs(own, other, ("one", "two"))
    hidden = (sizes.rows, sizes.positions, sizes.hidden)
    return call(
        functools.partial(mlp_kernel, sizes.count, block),
        2 + block,
        inputs,
        4,
        [
            (sizes.local, BF16), (sizes.local, F32), (sizes.full, BF16),
            (hidden, F32), (hidden, BF16),
        ],
        (),
        [
            pltpu.VMEM(own["one"].shape, BF16),
            pltpu.VMEM(own["two"].shape, BF16),
        ]
        + exchange_scratch(sizes.count, *sizes.local)
        + semaphores(sizes.count),
        2 * sizes.tokens * sizes.width * sizes.hidden * 2,
        cargos,
        streamed=(2, 3, 4),
    )


def mlp_backward(sizes, block, grads, attend, mlp, mods, segs, own, other, cargos):
    out, branch, full, pre, act = mlp
    inputs = [*grads, attend[0], branch, mods, segs[0], full, pre, act]
    given = len(grads)
    inputs += pairs(own, other, ("one", "two"))
    return call(
        functools.partial(mlp_back_kernel, sizes.count, block, given),
        4 + block,
        inputs,
        4,
        [
            (sizes.local, F32), (sizes.mods, F32),
            ((2,) + quarter((sizes.width, sizes.hidden)), BF16),
            ((2,) + quarter((sizes.width, sizes.hidden)), BF16),
            ((1, sizes.hidden), F32), ((1, sizes.width), F32),
        ],
        (),
        [
            pltpu.VMEM(sizes.full, BF16),
            pltpu.VMEM((sizes.rows, sizes.positions, sizes.hidden), BF16),
            pltpu.VMEM(own["one"].shape, BF16),
            pltpu.VMEM(own["two"].shape, BF16),
        ]
        + exchange_scratch(sizes.count, *sizes.local)
        + semaphores(sizes.count)
        + core_sum_scratch((sizes.width, sizes.hidden)) * 2
        + [
            pltpu.VMEM((sizes.rows * sizes.length, sizes.width), F32),
            pltpu.VMEM((sizes.rows * sizes.length, sizes.width), F32),
        ],
        2 * sizes.tokens * sizes.width * sizes.hidden * 4,
        cargos,
        lazy=(given + 4, given + 5, given + 6),
    )


def attend_backward(sizes, block, d_middle, u, attend, mods, segs, own, other, cargos):
    middle, branch, full, q, k, v, probs, mixed = attend
    inputs = [d_middle, u, branch, mods, segs[0], full, q, k, v, probs, mixed]
    inputs += pairs(own, other, ("qkv", "out"))
    return call(
        functools.partial(attend_back_kernel, sizes.count, block),
        6 + block,
        inputs,
        4,
        [
            (sizes.local, F32), (sizes.mods, F32),
            ((2,) + quarter((sizes.width, 3 * sizes.heads_width)), BF16),
            ((2,) + quarter((sizes.width, sizes.heads_width)), BF16),
            ((1, 3 * sizes.heads_width), F32), ((1, sizes.width), F32),
        ],
        (),
        [
            pltpu.VMEM(sizes.full, BF16),
            pltpu.VMEM((4,) + sizes.wide, BF16),
            pltpu.VMEM((sizes.rows, sizes.positions, 3 * sizes.heads_width), BF16),
            pltpu.VMEM(own["qkv"].shape, BF16),
            pltpu.VMEM(own["out"].shape, BF16),
        ]
        + exchange_scratch(sizes.count, *sizes.local)
        + semaphores(sizes.count)
        + core_sum_scratch((sizes.width, 3 * sizes.heads_width))
        + core_sum_scratch((sizes.width, sizes.heads_width))
        + [
            sizes.spreads,
            pltpu.VMEM((sizes.rows * sizes.length, sizes.width), F32),
        ],
        2 * sizes.tokens * sizes.width * sizes.heads_width * 8,
        cargos,
        lazy=(5, 6, 7, 8, 9, 10),
    )


def project(sizes, sent, weights, targets, biases, p2_b, token_count):
    tokens = sizes.rows * sizes.length
    p1, p2, p3 = weights
    lane, hidden = p1.shape[2], p2.shape[2]
    inputs = [sent, targets, biases, p2_b, p1, p2, p3]
    results, unused = call(
        functools.partial(project_kernel, token_count),
        9,
        inputs,
        3,
        [
            (sizes.local, F32), (p1.shape, BF16), (p2.shape, BF16), (p3.shape, BF16),
            ((sizes.count, MOD_ROWS, lane), F32),
        ],
        (),
        [
            pltpu.VMEM(p1.shape, BF16),
            pltpu.VMEM(p2.shape, BF16),
            pltpu.VMEM(p3.shape, BF16),
            pltpu.VMEM((2, tokens, sizes.width), BF16),
            pltpu.VMEM((2, 2 * tokens, lane), F32),
            pltpu.VMEM((2, 2 * tokens, lane), BF16),
            pltpu.VMEM((tokens, hidden), F32),
            pltpu.VMEM((2, tokens, hidden), BF16),
            pltpu.VMEM((2, tokens, hidden), BF16),
            pltpu.VMEM((2, 2 * tokens, HEAD_LANES), F32),
            pltpu.VMEM((2, tokens, hidden), BF16),
            pltpu.VMEM((2, tokens, hidden), BF16),
            pltpu.VMEM((2, tokens, sizes.width), BF16),
            pltpu.VMEM((2, 2 * tokens, lane), BF16),
            pltpu.SemaphoreType.DMA((3,)),
            pltpu.SemaphoreType.DMA((7,)),
            pltpu.SemaphoreType.DMA((7,)),
        ],
        12 * tokens * sum(math.prod(one.shape) for one in weights),
    )
    return results


def close_backward(sizes, grads, mod_grads, small, proj_small, cond, sections, replicas, cargos):
    count, width = sizes.count, sizes.width
    piece = 6 * width // count
    share = width // replicas
    inputs = [*grads, *mod_grads, *small, proj_small, cond]
    copies = 2 * count + 4 * (sections * replicas - 1)
    both = (sections * sizes.rows,) + sizes.local[1:]
    return call(
        functools.partial(close_kernel, count, sections, replicas),
        8,
        inputs,
        0,
        [
            (both, F32), ((share, piece), F32), ((1, piece), F32),
            ((MOD_ROWS, width), F32), (proj_small.shape[1:], F32),
        ],
        (),
        [
            pltpu.VMEM((count, sections, MOD_ROWS, piece), F32),
            pltpu.VMEM((count - 1, sections, MOD_ROWS, piece), F32),
            pltpu.VMEM((sections, MOD_ROWS, piece), F32),
            pltpu.VMEM((sections, replicas, MOD_ROWS, piece), F32),
            pltpu.VMEM((sections, MOD_ROWS, width), F32),
            pltpu.VMEM((sections, replicas, MOD_ROWS, width), F32),
            pltpu.VMEM((sections, replicas, MOD_ROWS, share), F32),
            pltpu.VMEM(sizes.local, BF16),
            pltpu.VMEM(sizes.local, BF16),
            pltpu.VMEM((count - 1,) + proj_small.shape[1:], F32),
            pltpu.VMEM(proj_small.shape[1:], F32),
            pltpu.VMEM((sections, replicas) + proj_small.shape[1:], F32),
            pltpu.SemaphoreType.DMA((copies,)),
            pltpu.SemaphoreType.DMA((copies,)),
        ],
        2 * sections * replicas * MOD_ROWS * share * piece,
        cargos,
    )


def assemble_kernel(heads_width, *refs):
    fc1, fc2 = refs[0:2], refs[2:4]
    alone, (qkv, wo) = refs[4:9], (refs[9:11], refs[11:13])
    grad_ref, small, proj = refs[13:16]
    outs, sems = refs[16:-1], refs[-1]
    is_first = lax.axis_index("section") == 0
    waits = []
    for i, pair in enumerate((fc1, fc2)):
        waits.append(pltpu.make_async_copy(pair[0], outs[i], sems.at[i]))

        @pl.when(is_first)
        def take_one(pair=pair, i=i):
            pltpu.make_async_copy(pair[0], outs[i], sems.at[i]).start()

        @pl.when(jnp.logical_not(is_first))
        def take_two(pair=pair, i=i):
            pltpu.make_async_copy(pair[1], outs[i], sems.at[i]).start()

    for i, one in enumerate(alone):
        waits.append(local(one, outs[2 + i], sems.at[2 + i]))
    grad_out, qkv_out, wo_out, qv_b, out_b, fc1_b, fc2_b, p1_b, p2_b, p3_b, loss = outs[7:]
    for row in range(grad_ref.shape[0]):
        grad_out[:, row, :] = grad_ref[row]
    qkv_own = jnp.where(is_first, qkv[0][...], qkv[1][...])
    for which in range(3):
        qkv_out[which] = qkv_own[:, which * heads_width : (which + 1) * heads_width]
    wo_out[...] = jnp.where(is_first, wo[0][...], wo[1][...]).T
    qv_b[0:1, :] = small[0:1, :heads_width]
    qv_b[1:2, :] = small[0:1, 2 * heads_width : 3 * heads_width]
    out_b[...] = small[2:3, :]
    fc1_b[...] = small[3:4, :]
    fc2_b[...] = small[4:5, :]
    p1_b[...] = proj[0:1, :]
    p2_b[...] = jnp.concatenate([proj[2 + row : 3 + row, :] for row in range(4)], axis=1)
    p3_b[...] = proj[1:2, : p3_b.shape[1]]
    loss[...] = proj[6:7, :HEAD_LANES]
    wait_all(waits)


def assemble(choices, alone, section_grad, small, proj_small, heads_width):
    (fc1, fc2, qkv, wo) = choices
    inputs = [*fc1, *fc2, *alone, *qkv, *wo, section_grad, small, proj_small]
    both, length, width = section_grad.shape
    share, lane = fc1[0].shape[0], proj_small.shape[1]
    third = alone[4].shape[0]
    shapes = [fc1[0].shape, fc2[0].shape] + [one.shape for one in alone] + [
        (length, both, width), (3, share, heads_width), wo[0].shape[::-1], (2, heads_width),
        (1, width), (1, width), (1, width), (1, lane), (1, 4 * lane), (1, third), (1, HEAD_LANES),
    ]
    return pl.pallas_call(
        functools.partial(assemble_kernel, heads_width),
        out_shape=[jax.ShapeDtypeStruct(shape, F32) for shape in shapes],
        in_specs=[ANY] * 9 + [VMEM] * 7,
        out_specs=[VMEM] * 18,
        scratch_shapes=[pltpu.SemaphoreType.DMA((7,))],
        compiler_params=pltpu.CompilerParams(vmem_limit_bytes=62 * 2**20),
        cost_estimate=pl.CostEstimate(flops=1000, bytes_accessed=2**24, transcendentals=0),
    )(*inputs)


def halve(value, axis, bit, position):
    size = lax.axis_size(axis)
    mine = (lax.axis_index(axis) & bit) // bit
    keep = lax.dynamic_index_in_dim(value, mine, position, keepdims=False)
    give = lax.dynamic_index_in_dim(value, 1 - mine, position, keepdims=False)
    return keep + lax.ppermute(give, axis, [(i, i ^ bit) for i in range(size)])


def sum_beyond_quads(value):
    size = lax.axis_size("dp")
    if size == 4:
        return value
    quads = size // 4
    bits = quads.bit_length() - 1
    lead = value.ndim - 2
    shape = value.shape
    value = value.reshape(shape[:lead] + (2,) * bits + (shape[-2] // quads, shape[-1]))
    for bit in range(bits):
        value = halve(value, "dp", 4 << bit, lead + bits - 1 - bit)
    route = [(high * 4 + low, low * quads + high) for high in range(quads) for low in range(4)]
    return lax.ppermute(value, "dp", route)


def per_device(
    block_eight_input,
    cond,
    image_slot_index,
    targets,
    cot,
    ada_w,
    ada_b,
    query_key_value_weight,
    query_value_bias,
    attention_output_weight,
    attention_output_bias,
    hidden_weight,
    hidden_bias,
    output_weight_mlp,
    output_bias_mlp,
    p1_w,
    p1_b,
    p2_w,
    p2_b,
    p3_w,
    p3_b,
):
    section = lax.axis_index("section")
    tensor = lax.axis_index("tensor")
    is_first = section == 0
    count = lax.axis_size("tensor")
    sections = lax.axis_size("section")
    replicas = lax.axis_size("dp")
    length, replica_rows, width = block_eight_input.shape
    positions = length * count
    rows = replica_rows // sections
    total_token_count = positions * replica_rows * replicas
    heads_width = attention_output_weight.shape[1]
    hidden = hidden_weight.shape[2]

    def my_rows(value, axis):
        return lax.dynamic_slice_in_dim(value, section * rows, rows, axis)

    def to_rows(value):
        return jnp.transpose(my_rows(value, 1), (1, 0, 2))

    own = {
        "qkv": query_key_value_weight[0].reshape(width, 3 * heads_width),
        "out": attention_output_weight[0],
        "one": hidden_weight[0],
        "two": output_weight_mlp[0],
    }

    def padded(value):
        return jnp.pad(value.astype(F32), ((0, 0), (0, width - value.shape[-1])))

    biases = jnp.concatenate(
        [
            padded(
                jnp.concatenate(
                    [
                        query_value_bias[0, 0:1], jnp.zeros((1, heads_width), BF16),
                        query_value_bias[0, 1:2],
                    ],
                    axis=1,
                )
            ),
            jnp.zeros((1, width), F32), padded(attention_output_bias), padded(hidden_bias),
            padded(output_bias_mlp), jnp.zeros((MOD_ROWS - 5, width), F32),
        ],
        axis=0,
    )
    used = rows * IMAGES_PER_ROW
    cond_pad = jnp.pad(
        cond.reshape(sections, used, width), ((0, 0), (0, MOD_ROWS - used), (0, 0))
    )
    segs_full = my_rows(image_slot_index, 0)
    seg_own = lax.dynamic_slice_in_dim(segs_full, tensor * length, length, 1)
    segs = (seg_own[:, :, None], segs_full[:, :, None], segs_full[:, None, :])

    target_parts = my_rows(targets, 1).reshape(count, length, rows, targets.shape[2])
    target_parts = jnp.transpose(target_parts, (0, 2, 1, 3))
    lane = p1_b.shape[0]
    proj_biases = jnp.concatenate(
        [
            p1_b.astype(F32)[None],
            jnp.pad(p3_b.astype(F32), (0, lane - p3_b.shape[0]))[None],
            jnp.zeros((MOD_ROWS - 2, lane), F32),
        ],
        axis=0,
    )
    gather = ColumnGather((p1_w, p2_w, p3_w.T), PROJECTOR_AXES, target_parts, proj_biases)

    u = to_rows(block_eight_input)
    sizes = Shapes(u, own, count)
    mods, bias_all, other, attend_one, carried = open_forward(
        sizes, u, cond_pad.reshape(-1, width), ada_w[0].T, ada_b, biases, segs, own, sections,
        (gather,),
    )
    *proj_weights, target_all, proj_bias_all = carried[0]
    mlp_one, carried = mlp_forward(
        sizes, 0, attend_one[0], mods, bias_all, segs, own, other,
        (ShareAlong(proj_weights, PROJECTOR_AXES, 0),),
    )
    proj_weights = carried[0]
    first_out = mlp_one[0]
    attend_two, carried = attend_forward(
        sizes, 1, first_out, mods, bias_all, segs, own, other, (ShareAlong(proj_weights, PROJECTOR_AXES, 1),)
    )
    proj_weights = carried[0]
    mlp_two, carried = mlp_forward(
        sizes, 1, attend_two[0], mods, bias_all, segs, own, other, (ShareAlong(proj_weights, PROJECTOR_AXES, 2),)
    )
    proj_weights = carried[0]
    second_out = mlp_two[0]

    grad_sent, grad_p1, grad_p2, grad_p3, proj_small = project(
        sizes, first_out, proj_weights, target_all, proj_bias_all, p2_b[None], total_token_count
    )

    back = (mods, segs, own, other)
    (d_middle_two, mod_mlp_two, *mlp_grads_two), carried = mlp_backward(
        sizes, 1, [to_rows(cot)], attend_two, mlp_two, *back,
        [
            Swap(first_out, second_out), HalfSum(grad_p1, 0, "x"),
            HalfSum(grad_p3, 1, "x", (0, 1)),
        ],
    )
    (other_out,), (grad_p1,), (grad_p3_a,) = carried
    (second_grad, mod_attend_two, *attend_grads_two), carried = attend_backward(
        sizes, 1, d_middle_two, first_out, attend_two, *back,
        [YSum(grad, BF16) for grad in mlp_grads_two[:2]]
        + [HalfSum(grad_p2, 1, "x", (0, 1)), HalfSum(grad_p3, 1, "x", (1, 1))]
        + [HalfSum(grad_p1, 0, "y", (0, 1))],
    )
    (mlp_part_a,), (mlp_part_b,), (grad_p2_a,), (grad_p3_b,), (grad_p1_a,) = carried
    (d_middle_one, mod_mlp_one, *mlp_grads_one), carried = mlp_backward(
        sizes, 0, [second_grad, grad_sent], attend_one, mlp_one, *back,
        [YSum(grad, BF16) for grad in attend_grads_two[:2]]
        + [SectionSum(mlp_part_a, 1), HalfSum(grad_p2, 1, "x", (1, 1))]
        + [HalfSum(grad_p1, 0, "y", (1, 1)), HalfSum(grad_p2_a, 1, "y")],
    )
    attend_parts_two, sum_mlp_a = carried[:2], carried[2]
    (grad_p2_b,), (grad_p1_b,), (grad_p2_a,) = carried[3:]
    (first_grad, mod_attend_one, *attend_grads_one), carried = attend_backward(
        sizes, 0, d_middle_one, u, attend_one, *back,
        [LastSum(mlp_grads_one[0], 0), SectionSum(mlp_grads_one[1], 0, BF16)]
        + [SectionSum(part, 1) for part, in attend_parts_two]
        + [SectionSum(mlp_part_b, 1), HalfSum(grad_p2_b, 1, "y")]
        + [HalfSum(grad_p3_a, 1, "y"), HalfSum(grad_p3_b, 1, "y")]
        + [ColumnSum((grad_p1_a, grad_p1_b), 0)],
    )
    sum_mlp_c, (mlp_part_two,), sums_attend_two = carried[0], carried[1], carried[2:4]
    sums_mlp_two = (sum_mlp_a, carried[4])
    (grad_p2_b,), (grad_p3_a,), (grad_p3_b,), (red_p1_w,) = carried[5:]

    cond_act = silu(my_rows(cond, 0).astype(F32)).astype(BF16).astype(F32)
    share = width // replicas
    cond_cols = jnp.pad(cond_act.reshape(used, width), ((0, MOD_ROWS - used), (0, 0)))
    cond_cols = jnp.transpose(cond_cols.reshape(MOD_ROWS, replicas, share), (1, 0, 2))
    small = [
        attend_grads_one[2], attend_grads_one[3], mlp_grads_one[2], mlp_grads_one[3],
        attend_grads_two[2], attend_grads_two[3], mlp_grads_two[2], mlp_grads_two[3],
    ]
    (section_grad, grad_ada_w, grad_ada_b, small, proj_small), carried = close_backward(
        sizes, (first_grad, second_grad),
        (mod_attend_one, mod_mlp_one, mod_attend_two, mod_mlp_two),
        small, proj_small, cond_cols, sections, replicas,
        [LastSum(grad, 0) for grad in attend_grads_one[:2]]
        + [YSum(mlp_part_two, F32)]
        + [ColumnSum((grad_p2_a, grad_p2_b), 1), ColumnSum((grad_p3_a, grad_p3_b), 1)],
    )
    sums_attend_one, sums_mlp_one = carried[:2], (sum_mlp_c, carried[2])
    (red_p2_w,), (red_p3_w,) = carried[3:]

    own_out = jnp.where(is_first, first_out, second_out)
    section_out = jnp.where(
        is_first,
        jnp.concatenate([own_out, other_out], axis=0),
        jnp.concatenate([other_out, own_out], axis=0),
    )
    section_out = jnp.transpose(section_out, (1, 0, 2))[None]
    choices = [
        (one[0], two[0])
        for one, two in zip(
            list(sums_mlp_one) + list(sums_attend_one), list(sums_mlp_two) + list(sums_attend_two)
        )
    ]
    if replicas == 4:
        alone = [grad_ada_w, grad_ada_b, red_p1_w, red_p2_w, red_p3_w]
        final = assemble(choices, alone, section_grad, small, proj_small, heads_width)
        red_fc1, red_fc2, grad_ada_w, grad_ada_b, red_p1_w, red_p2_w, red_p3_w = final[:7]
        section_grad, red_qkv, red_out, qv_b, out_b, fc1_b, fc2_b, p1_sum, p2_sum, p3_sum, loss = (
            final[7:]
        )
        red_p1_b, red_p2_b, red_p3_b = p1_sum[0], p2_sum[0], p3_sum[0]
        loss_total = loss[0, 0]
    else:
        red_fc1, red_fc2, red_qkv, red_out = [
            sum_beyond_quads(jnp.where(is_first, one, two)) for one, two in choices
        ]
        red_qkv = jnp.transpose(red_qkv.reshape(-1, 3, heads_width), (1, 0, 2))
        red_out = red_out.T
        red_p1_w = sum_beyond_quads(red_p1_w)
        red_p2_w, red_p3_w = sum_beyond_quads(red_p2_w.T).T, sum_beyond_quads(red_p3_w.T).T
        section_grad = jnp.transpose(section_grad, (1, 0, 2))
        qv_b = jnp.stack([small[0, :heads_width], small[0, 2 * heads_width : 3 * heads_width]])
        out_b, fc1_b, fc2_b = small[2:3], small[3:4], small[4:5]
        red_p1_b, red_p2_b = proj_small[0], proj_small[2:6].reshape(-1)
        red_p3_b, loss_total = proj_small[1, : p3_b.shape[0]], proj_small[6, 0]
    align_loss = -0.5 * loss_total / total_token_count
    return (
        section_out,
        section_grad[None],
        align_loss,
        grad_ada_w[None],
        grad_ada_b,
        jnp.transpose(red_qkv, (1, 0, 2))[None],
        qv_b[None],
        red_out[None],
        out_b,
        red_fc1[None],
        fc1_b[:, :hidden],
        red_fc2.T[None],
        fc2_b,
        red_p1_w,
        red_p1_b,
        red_p2_w,
        red_p2_b[: p2_b.shape[0]],
        red_p3_w.T,
        red_p3_b,
    )


def solution(mesh):
    in_specs = (
        P("tensor", "dp", None),
        P("dp", None, None),
        P("dp", None),
        P(None, "dp", "tensor"),
        P("tensor", "dp", None),
        P("section", None, "tensor"),
        P("section", "tensor"),
        P("section", None, None, "tensor"),
        P("section", None, "tensor"),
        P("section", "tensor", None),
        P("section", None),
        P("section", None, "tensor"),
        P("section", "tensor"),
        P("section", "tensor", None),
        P("section", None),
        P(None, "tensor"),
        P("tensor"),
        P("tensor", None),
        P(),
        P(None, "tensor"),
        P("tensor"),
    )
    out_specs = (
        P("section", "tensor", "dp", None),
        P("section", "tensor", "dp", None),
        P(),
        P("section", "dp", "tensor"),
        P("section", "tensor"),
        P("section", "dp", None, "tensor"),
        P("section", None, "tensor"),
        P("section", "tensor", "dp"),
        P("section", None),
        P("section", "dp", "tensor"),
        P("section", "tensor"),
        P("section", "tensor", "dp"),
        P("section", None),
        P(("section", "dp"), "tensor"),
        P("tensor"),
        P("tensor", ("section", "dp")),
        P(),
        P(("section", "dp"), "tensor"),
        P("tensor"),
    )
    return jax.shard_map(
        per_device, mesh=mesh, in_specs=in_specs, out_specs=out_specs, check_vma=False
    )
```

```python
import functools
import math

import jax
import jax.numpy as jnp
from jax import lax
from jax.experimental import pallas as pl
from jax.experimental.pallas import tpu as pltpu
from jax.sharding import PartitionSpec as P

HEAD_WIDTH = 72
HEAD_LANES = 128
IMAGES_PER_ROW = 3
NORM_EPS = 1e-06
COSINE_EPS = 1e-06
MASKED_SCORE = -1e30
HIGHEST = lax.Precision.HIGHEST
MESH = pl.DeviceIdType.MESH
F32 = jnp.float32
BF16 = jnp.bfloat16
NN = (((1,), (0,)), ((), ()))
NT = (((1,), (1,)), ((), ()))
TN = (((0,), (0,)), ((), ()))


def dot(left, right, form=NN):
    return lax.dot_general(left, right, form, preferred_element_type=F32)


def z_peers(count):
    me = lax.axis_index("tensor")
    return [{"tensor": lax.rem(me + step, count)} for step in range(1, count)]


def x_peer():
    return {"section": 1 - lax.axis_index("section")}


def core_bit():
    return lax.rem(lax.axis_index("dp"), 2)


def y_bit():
    return lax.rem(lax.axis_index("dp") // 2, 2)


def core_peer():
    return {"dp": lax.axis_index("dp") + 1 - 2 * core_bit()}


def y_peer():
    return {"dp": lax.axis_index("dp") + 2 - 4 * y_bit()}


def call_peers(peers):
    barrier = pltpu.get_barrier_semaphore()
    for peer in peers:
        pl.semaphore_signal(barrier, inc=1, device_id=peer, device_id_type=MESH)
    return lambda: pl.semaphore_wait(barrier, len(peers))


def greet(peers):
    call_peers(peers)()


def remote(source, target, send_sem, recv_sem, peer):
    copy = describe(source, target, send_sem, recv_sem, peer)
    copy.start()
    return copy


def local(source, target, sem):
    copy = pltpu.make_async_copy(source, target, sem)
    copy.start()
    return copy


def own_rows(me, length):
    return pl.ds(pl.multiple_of(me * length, 16), length)


def describe(source, target, send_sem, recv_sem, peer):
    return pltpu.make_async_remote_copy(
        src_ref=source,
        dst_ref=target,
        send_sem=send_sem,
        recv_sem=recv_sem,
        device_id=peer,
        device_id_type=MESH,
    )


def wait_all(copies):
    for copy in copies:
        copy.wait()


class Line:
    def __init__(self, length, sems):
        self.length, (self.ag_send, self.ag_recv, self.rs_send, self.rs_recv) = length, sems
        self.me = lax.axis_index("tensor")
        self.mirror = 3 - self.me
        self.near = self.me + 1 - 2 * lax.rem(self.me, 2)
        self.opposite = lax.rem(self.me + 2, 4)
        self.is_end = jnp.logical_or(self.me == 0, self.me == 3)
        self.is_middle = jnp.logical_not(self.is_end)

    def block(self, full, place, which, peer):
        part = full.at[:, own_rows(place, self.length)]
        return describe(
            part, part, self.ag_send.at[which], self.ag_recv.at[place], {"tensor": peer}
        )

    def start_gather(self, full):
        self.block(full, self.me, 0, self.opposite).start()
        self.block(full, self.me, 1, self.near).start()

        @pl.when(self.is_middle)
        def to_mirror():
            self.block(full, self.me, 2, self.mirror).start()

    def relay(self, full):
        self.block(full, self.opposite, 2, self.mirror).wait_recv()

        @pl.when(self.is_middle)
        def pass_on():
            self.block(full, self.opposite, 3, 3 - self.opposite).start()

    def arrived(self, full, place):
        self.block(full, place, 1, self.near).wait_recv()

    def finish_gather(self, full):
        self.arrived(full, self.near)
        self.arrived(full, self.mirror)
        self.sent(full)

    def sent(self, full):
        self.block(full, self.me, 0, self.opposite).wait_send()
        self.block(full, self.me, 1, self.near).wait_send()

        @pl.when(self.is_middle)
        def more_sent():
            self.block(full, self.me, 2, self.mirror).wait_send()
            self.block(full, self.opposite, 3, 3 - self.opposite).wait_send()

    def scatter_sum(self, partial, buffers, prepare=lambda place: None):
        send_buf, recv_buf, relay_buf = buffers
        me, relay_sem = self.me, 4

        def term(peer):
            return partial(own_rows(peer, self.length))

        def keep(which, value):
            send_buf[which] = value.astype(BF16).reshape(send_buf.shape[1:])

        self.to_mirror = describe(
            send_buf.at[0], recv_buf.at[me], self.rs_send.at[0], self.rs_recv.at[me],
            {"tensor": self.mirror},
        )
        self.to_relay = describe(
            send_buf.at[0], relay_buf, self.rs_send.at[0], self.rs_recv.at[relay_sem],
            {"tensor": self.near},
        )
        self.to_near = describe(
            send_buf.at[1], recv_buf.at[me], self.rs_send.at[1], self.rs_recv.at[me],
            {"tensor": self.near},
        )
        self.to_opposite = describe(
            send_buf.at[2], recv_buf.at[me], self.rs_send.at[2], self.rs_recv.at[me],
            {"tensor": self.opposite},
        )
        prepare(self.mirror)
        keep(0, term(self.mirror))

        @pl.when(self.is_end)
        def first_end():
            self.to_relay.start()
            relay_buf[...] = jnp.zeros_like(relay_buf)
            recv_buf[self.mirror] = jnp.zeros(recv_buf.shape[1:], BF16)

        @pl.when(self.is_middle)
        def first_middle():
            self.to_mirror.start()

        prepare(self.near)
        keep(1, term(self.near))
        self.to_near.start()
        last = term(self.opposite)

        @pl.when(self.is_middle)
        def relayed():
            self.to_relay.wait_recv()

        keep(2, last + relay_buf[...].reshape(last.shape).astype(F32))
        self.to_opposite.start()
        return term(me)

    def finish_sum(self, total, buffers):
        send_buf, recv_buf, relay_buf = buffers

        def got(source):
            describe(
                send_buf.at[1], recv_buf.at[source], self.rs_send.at[1], self.rs_recv.at[source],
                {"tensor": self.near},
            ).wait_recv()

        got(self.near)
        got(self.opposite)

        @pl.when(self.is_middle)
        def third():
            got(self.mirror)

        self.to_near.wait_send()
        self.to_opposite.wait_send()
        self.to_mirror.wait_send()
        for source in (self.near, self.opposite, self.mirror):
            total = total + recv_buf[source].reshape(total.shape).astype(F32)
        return total


def fetch(block, own_ref, other_ref, target, sem):
    mine = lax.axis_index("section") == block

    @pl.when(mine)
    def own_start():
        pltpu.make_async_copy(own_ref, target, sem).start()

    @pl.when(jnp.logical_not(mine))
    def other_start():
        pltpu.make_async_copy(other_ref, target, sem).start()

    return pltpu.make_async_copy(own_ref, target, sem)


def layer_norm(rows):
    centred = rows - jnp.mean(rows, axis=-1, keepdims=True)
    inverse = lax.rsqrt(jnp.mean(centred * centred, axis=-1, keepdims=True) + NORM_EPS)
    return centred * inverse, inverse


def norm_back(grad, normed, inverse):
    mean_grad = jnp.mean(grad, axis=-1, keepdims=True)
    mean_cross = jnp.mean(grad * normed, axis=-1, keepdims=True)
    return inverse * (grad - mean_grad - normed * mean_cross)


def token_mod(mod_ref, seg_ref, which):
    parts = []
    for row in range(seg_ref.shape[0]):
        seg = seg_ref[row]
        line = [
            mod_ref[which, pl.ds(row * IMAGES_PER_ROW + slot, 1), :]
            for slot in range(IMAGES_PER_ROW)
        ]
        value = line[-1]
        for slot in range(IMAGES_PER_ROW - 2, -1, -1):
            value = jnp.where(seg == slot, line[slot], value)
        parts.append(value)
    return jnp.concatenate(parts, axis=0)


def slot_sums(value, seg_ref, out_ref, which):
    length = seg_ref.shape[1]
    lines = []
    for row in range(seg_ref.shape[0]):
        seg = seg_ref[row]
        piece = value[row * length : (row + 1) * length]
        for slot in range(IMAGES_PER_ROW):
            lines.append(jnp.sum(jnp.where(seg == slot, piece, 0.0), axis=0, keepdims=True))
    spare = out_ref.shape[1] - len(lines)
    lines.append(jnp.zeros((spare, value.shape[1]), F32))
    out_ref[which] = jnp.concatenate(lines, axis=0)


def flat(ref):
    return ref[...].reshape(-1, ref.shape[-1])


def spread_matrix(width, which=0, total=None):
    lanes = width // HEAD_WIDTH * HEAD_LANES
    shape = (total or width, lanes)
    source = lax.broadcasted_iota(jnp.int32, shape, 0)
    target = lax.broadcasted_iota(jnp.int32, shape, 1)
    within = target & (HEAD_LANES - 1)
    head = target >> (HEAD_LANES.bit_length() - 1)
    hit = (within < HEAD_WIDTH) & (source == which * width + head * HEAD_WIDTH + within)
    return jnp.where(hit, 1.0, 0.0).astype(BF16)


def gelu_tanh(pre):
    inner = math.sqrt(2.0 / math.pi) * (pre + 0.044715 * (pre * pre * pre))
    return 0.5 * pre * (1.0 + jnp.tanh(inner))


def gelu_slope(pre):
    scale = math.sqrt(2.0 / math.pi)
    square = pre * pre
    tanh = jnp.tanh(scale * (pre + 0.044715 * (pre * square)))
    return 0.5 * (1.0 + tanh) + 0.5 * pre * (1.0 - tanh * tanh) * scale * (
        1.0 + 3 * 0.044715 * square
    )


def silu(value):
    return value / (1.0 + jnp.exp(-value))


class Share:
    def __init__(self, own, other, parts, sems):
        self.own, self.other, self.parts = own, other, parts
        self.send, self.recv = sems
        self.size = own.shape[0] // parts
        self.copies = []

    def rows(self, core, y):
        part = core if self.parts == 2 else core + 2 * y
        return pl.ds(pl.multiple_of(part * self.size, 16), self.size)

    def begin(self):
        rows = self.rows(core_bit(), y_bit())
        self.first = remote(
            self.own.at[rows], self.other.at[rows], self.send.at[0], self.recv.at[0], x_peer()
        )

    def forward(self, first):
        if first is not None:
            first.wait()
        mine = self.other.at[self.rows(core_bit(), y_bit())]
        self.copies.append(remote(mine, mine, self.send.at[1], self.recv.at[1], core_peer()))
        if self.parts == 4:
            self.second = remote(mine, mine, self.send.at[2], self.recv.at[2], y_peer())

    def forward_again(self):
        if self.parts == 4:
            self.second.wait()
            got = self.other.at[self.rows(core_bit(), 1 - y_bit())]
            self.copies.append(remote(got, got, self.send.at[3], self.recv.at[3], core_peer()))

    def finish(self):
        wait_all(self.copies)


class Cargo:
    inputs, outs, scratch, aliases, any_outs = (), (), (), {}, False

    def bind(self, inputs, outs, scratch):
        self.ins, self.out_refs, self.held = inputs, outs, scratch

    def peers(self):
        return []

    def begin(self):
        pass

    def middle(self):
        pass

    def late(self):
        pass

    def end(self):
        pass


def quarter(shape):
    return shape[:-2] + (shape[-2] // 4, shape[-1])


class CoreSum:
    def __init__(self, whole, got, out, sems):
        self.whole, self.got, self.out, self.sems = whole, got, out, sems
        self.size = whole.shape[-2] // 4

    def rows(self, core, y):
        part = pl.ds(pl.multiple_of((core + 2 * y) * self.size, 16), self.size)
        whole = self.whole
        return whole.at[:, part] if len(whole.shape) == 3 else whole.at[part]

    def begin(self):
        self.copies = [
            remote(
                self.rows(1 - core_bit(), y), self.got.at[y],
                self.sems.at[0, y], self.sems.at[1, y], core_peer(),
            )
            for y in range(2)
        ]

    def end(self):
        wait_all(self.copies)
        for y in range(2):
            mine = self.rows(core_bit(), y)[...]
            self.out[y] = (mine.astype(F32) + self.got[y].astype(F32)).astype(BF16)


def core_sum_scratch(shape):
    return [
        pltpu.VMEM(shape, BF16),
        pltpu.VMEM((2,) + quarter(shape), BF16),
        pltpu.SemaphoreType.DMA((2, 2)),
    ]


class YSum(Cargo):
    def __init__(self, parts, dtype):
        part = parts.shape[1:]
        self.inputs = (parts,)
        self.outs = ((part, dtype),)
        self.scratch = (
            pltpu.VMEM(part, BF16),
            pltpu.VMEM(part, BF16),
            pltpu.SemaphoreType.DMA((3,)),
        )

    def peers(self):
        return ["y"]

    def begin(self):
        mine, other, sems = self.held
        self.copies = [
            remote(self.ins[0].at[1 - y_bit()], other, sems.at[0], sems.at[1], y_peer()),
            local(self.ins[0].at[y_bit()], mine, sems.at[2]),
        ]

    def end(self):
        mine, other, sems = self.held
        out = self.out_refs[0]
        wait_all(self.copies)
        out[...] = (mine[...].astype(F32) + other[...].astype(F32)).astype(out.dtype)


class SectionSum(Cargo):
    def __init__(self, part, owner, dtype=F32):
        self.owner = owner
        self.inputs = (part,)
        self.outs = ((part.shape, dtype),)
        self.scratch = (
            pltpu.VMEM(part.shape, BF16),
            pltpu.VMEM(part.shape, BF16),
            pltpu.SemaphoreType.DMA((3,)),
        )

    def peers(self):
        return ["x"]

    def source(self):
        return self.ins[0]

    def begin(self):
        mine, other, sems = self.held
        self.copy = describe(self.source(), other, sems.at[0], sems.at[1], x_peer())
        self.load = pltpu.make_async_copy(self.source(), mine, sems.at[2])
        is_owner = lax.axis_index("section") == self.owner

        @pl.when(is_owner)
        def take():
            self.load.start()

        @pl.when(jnp.logical_not(is_owner))
        def give():
            self.copy.start()

    def end(self):
        mine, other, sems = self.held
        is_owner = lax.axis_index("section") == self.owner

        @pl.when(is_owner)
        def add():
            self.load.wait()
            self.copy.wait_recv()
            out = self.out_refs[0]
            out[...] = (mine[...].astype(F32) + other[...].astype(F32)).astype(out.dtype)

        @pl.when(jnp.logical_not(is_owner))
        def given():
            self.copy.wait_send()
            self.out_refs[0][...] = jnp.zeros_like(self.out_refs[0])


class LastSum(YSum):
    def __init__(self, parts, owner):
        super().__init__(parts, F32)
        part = parts.shape[1:]
        self.owner = owner
        self.scratch = self.scratch + (
            pltpu.VMEM(part, BF16),
            pltpu.VMEM(part, BF16),
            pltpu.SemaphoreType.DMA((2,)),
        )

    def peers(self):
        return ["y", "x"]

    def begin(self):
        self.held, self.last = self.held[:3], self.held[3:]
        super().begin()

    def middle(self):
        mine, other, sems = self.held
        total, got, last_sems = self.last
        wait_all(self.copies)
        total[...] = (mine[...].astype(F32) + other[...].astype(F32)).astype(BF16)
        self.copy = describe(total, got, last_sems.at[0], last_sems.at[1], x_peer())

        @pl.when(lax.axis_index("section") != self.owner)
        def give():
            self.copy.start()

    def end(self):
        total, got, last_sems = self.last
        is_owner = lax.axis_index("section") == self.owner

        @pl.when(is_owner)
        def add():
            self.copy.wait_recv()
            self.out_refs[0][...] = total[...].astype(F32) + got[...].astype(F32)

        @pl.when(jnp.logical_not(is_owner))
        def given():
            self.copy.wait_send()
            self.out_refs[0][...] = jnp.zeros_like(self.out_refs[0])


class Swap(Cargo):
    def __init__(self, one, two):
        self.inputs = (one, two)
        self.outs = ((one.shape, one.dtype),)
        self.scratch = (pltpu.VMEM(one.shape, one.dtype), pltpu.SemaphoreType.DMA((2,)))

    def peers(self):
        return ["x"]

    def begin(self):
        got, sems = self.held
        one, two = self.ins
        self.copy = describe(two, got, sems.at[0], sems.at[1], x_peer())
        is_first = lax.axis_index("section") == 0

        @pl.when(is_first)
        def give_two():
            self.copy.start()

        @pl.when(jnp.logical_not(is_first))
        def give_one():
            describe(one, got, sems.at[0], sems.at[1], x_peer()).start()

    def end(self):
        self.copy.wait()
        self.out_refs[0][...] = self.held[0][...]


def span(ref, axis, start, size):
    part = pl.ds(pl.multiple_of(start, 128 if axis == 1 else 16), size)
    lead = (slice(None),) * (len(ref.shape) - 2)
    return ref.at[lead + ((slice(None), part) if axis == 1 else (part, slice(None)))]


def cut(shape, axis, by):
    shape = list(shape)
    shape[axis - 2] //= by
    return tuple(shape)


class HalfSum(Cargo):
    def __init__(self, grad, axis, name, slots=None):
        self.slots = slots if slots is not None else (0, grad.shape[0])
        part = cut((self.slots[1],) + grad.shape[1:], axis, 2)
        self.axis, self.name, self.size = axis, name, part[axis - 2]
        self.inputs = (grad,)
        self.outs = ((part, BF16),)
        self.scratch = (
            pltpu.VMEM(part, BF16),
            pltpu.VMEM(part, BF16),
            pltpu.SemaphoreType.DMA((3,)),
        )

    def peers(self):
        return [self.name]

    def begin(self):
        mine, other, sems = self.held
        if self.name == "x":
            bit, peer = lax.axis_index("section"), x_peer()
        else:
            bit, peer = y_bit(), y_peer()
        grad = self.ins[0].at[pl.ds(*self.slots)]
        self.copies = [
            remote(
                span(grad, self.axis, (1 - bit) * self.size, self.size), other,
                sems.at[0], sems.at[1], peer,
            ),
            local(span(grad, self.axis, bit * self.size, self.size), mine, sems.at[2]),
        ]

    def end(self):
        mine, other, sems = self.held
        wait_all(self.copies)
        self.out_refs[0][...] = (mine[...].astype(F32) + other[...].astype(F32)).astype(BF16)


class ColumnGather(Cargo):
    any_outs = True

    def __init__(self, weights, axes, targets, biases):
        self.axes = axes
        self.inputs = (*weights, targets, biases)
        self.outs = tuple(((2,) + one.shape, BF16) for one in weights) + (
            ((2, 2) + targets.shape[1:], BF16),
            ((2, 2) + biases.shape, F32),
        )
        self.scratch = (
            pltpu.SemaphoreType.DMA((5, 6)),
            pltpu.SemaphoreType.DMA((5, 2, 2)),
            pltpu.SemaphoreType.DMA((5,)),
        )

    def peers(self):
        return ["core", "cross"]

    def pieces(self, target):
        tensor, core = lax.axis_index("tensor"), core_bit()
        eighth = lax.axis_index("section") * 4 + y_bit() * 2 + core
        slot, out = lax.rem(tensor, 2), []
        for source, place, axis in zip(self.ins[:3], self.out_refs[:3], self.axes):
            size = source.shape[axis] // 8
            out.append(
                (
                    span(source, axis, eighth * size, size),
                    span(place.at[slot], axis, eighth * size, size),
                )
            )
        out.append((self.ins[3].at[target], self.out_refs[3].at[slot, core]))
        out.append((self.ins[4], self.out_refs[4].at[slot, core]))
        return out

    def copies(self, step):
        tensor, core = lax.axis_index("tensor"), core_bit()
        send, recv, own = self.held
        target = lax.rem(tensor + step, 4)
        peer = {"tensor": target, "dp": lax.axis_index("dp") - core + tensor // 2}
        return [
            describe(source, place, send.at[i, step], recv.at[i, lax.rem(tensor, 2), core], peer)
            for i, (source, place) in enumerate(self.pieces(target))
        ]

    def stays(self):
        return core_bit() == lax.axis_index("tensor") // 2

    def own_copies(self):
        own = self.held[2]
        return [
            pltpu.make_async_copy(source, place, own.at[i])
            for i, (source, place) in enumerate(self.pieces(lax.axis_index("tensor")))
        ]

    def direct(self, step, i):
        if step == 2 or i > 2:
            return None
        return lax.axis_index("tensor") != (3 if step == 1 else 0)

    def each(self, which, act):
        for step in range(1, 4):
            for i, copy in enumerate(self.copies(step)):
                if i in which:
                    allowed = self.direct(step, i)
                    if allowed is None:
                        act(copy)
                    else:

                        @pl.when(allowed)
                        def go(copy=copy):
                            act(copy)

    def start(self, which):
        self.each(which, lambda copy: copy.start())

        @pl.when(self.stays())
        def keep():
            for i, copy in enumerate(self.own_copies()):
                if i in which:
                    copy.start()

        @pl.when(jnp.logical_not(self.stays()))
        def give():
            for i, copy in enumerate(self.copies(0)):
                if i in which:
                    copy.start()

    def passes_on(self):
        tensor, core = lax.axis_index("tensor"), core_bit()
        return jnp.logical_or(
            jnp.logical_and(tensor == 2, core == 0), jnp.logical_and(tensor == 1, core == 1)
        )

    def passed(self, i, other):
        send, recv, own = self.held
        tensor, slot = lax.axis_index("tensor"), core_bit()
        size = self.ins[i].shape[self.axes[i]] // 8
        eighth = lax.axis_index("section") * 4 + y_bit() * 2 + other
        part = span(self.out_refs[i].at[slot], self.axes[i], eighth * size, size)
        return describe(
            part, part, send.at[i, 4 + other], recv.at[i, slot, other], {"tensor": 3 * (tensor - 1)}
        )

    def relay(self, which):
        @pl.when(self.passes_on())
        def pass_on():
            for i in which:
                for other in range(2):
                    copy = self.passed(i, other)
                    copy.wait_recv()
                    copy.start()

    def begin(self):
        self.start((3, 4))

    def middle(self):
        self.start((0, 2))

    def end(self):
        send, recv, own = self.held
        tensor, core = lax.axis_index("tensor"), core_bit()
        self.each(range(5), lambda copy: copy.wait_send())

        @pl.when(self.stays())
        def kept():
            for copy in self.own_copies():
                copy.wait()

        @pl.when(jnp.logical_not(self.stays()))
        def given():
            for copy in self.copies(0):
                copy.wait_send()

        @pl.when(self.passes_on())
        def passed_on():
            for i in range(3):
                for other in range(2):
                    self.passed(i, other).wait_send()

        for slot in range(2):
            for other in range(2):
                mine = jnp.logical_and(2 * core + slot == tensor, core == other)
                relayed = jnp.logical_and(self.passes_on(), core == slot)
                peer = {"tensor": lax.rem(tensor + 1, 4)}
                waits = [
                    describe(source, place, send.at[i, 1], recv.at[i, slot, other], peer)
                    for i, (source, place) in enumerate(self.pieces(tensor))
                ]

                @pl.when(jnp.logical_not(mine))
                def arrived(waits=waits):
                    for copy in waits[3:]:
                        copy.wait_recv()

                @pl.when(jnp.logical_not(jnp.logical_or(mine, relayed)))
                def weights_arrived(waits=waits):
                    for copy in waits[:3]:
                        copy.wait_recv()


class ShareAlong(Cargo):
    any_outs = True

    def __init__(self, weights, axes, stage):
        self.axes = axes
        self.inputs = tuple(weights)
        self.outs = tuple((one.shape, BF16) for one in weights)
        self.aliases = {0: 0, 1: 1, 2: 2}
        self.stage = stage
        self.scratch = (pltpu.SemaphoreType.DMA((4,)), pltpu.SemaphoreType.DMA((4,)))

    def peers(self):
        return ["x", "y"]

    def begin(self):
        send, recv = self.held
        section, y, self.copies = lax.axis_index("section"), y_bit(), []

        def give(which, start, parts, peer):
            ref, axis = self.out_refs[which], self.axes[which]
            size = ref.shape[axis + 1] // 4
            part = span(ref, axis, start * size, parts * size)
            i = len(self.copies)
            self.copies.append(remote(part, part, send.at[i], recv.at[i], peer))

        if self.stage == 0:
            give(1, 2 * section + y, 1, x_peer())
            give(0, 2 * section + y, 1, y_peer())
            give(2, 2 * section + y, 1, y_peer())
        elif self.stage == 1:
            give(0, 2 * section, 2, x_peer())
            give(1, y, 1, y_peer())
        else:
            give(2, 2 * section, 2, x_peer())
            give(1, 2 + y, 1, y_peer())

    def end(self):
        wait_all(self.copies)


class ColumnSum(Cargo):
    def __init__(self, grads, axis):
        self.axis = axis
        self.part = cut(grads[0].shape[1:], axis, 2)
        self.inputs = tuple(grads)
        self.outs = ((self.part, F32),)
        self.scratch = (
            pltpu.VMEM((4,) + self.part, BF16),
            pltpu.SemaphoreType.DMA((4,)),
            pltpu.SemaphoreType.DMA((4,)),
            pltpu.SemaphoreType.DMA,
        )

    def peers(self):
        return ["core", "cross"]

    def copy(self, slot, other):
        got, send, recv, own = self.held
        tensor, core = lax.axis_index("tensor"), core_bit()
        size = self.part[self.axis]
        ref = self.ins[0].at[slot] if len(self.ins) == 1 else self.ins[slot].at[0]
        source = span(ref, self.axis, other * size, size)
        peer = {"tensor": 2 * core + slot, "dp": lax.axis_index("dp") - core + other}
        mine = jnp.logical_and(2 * core + slot == tensor, core == other)
        away = describe(source, got.at[tensor], send.at[2 * slot + other], recv.at[tensor], peer)
        return mine, away, pltpu.make_async_copy(source, got.at[tensor], own)

    def each(self, act_away, act_own):
        for slot in range(2):
            for other in range(2):
                mine, away, own = self.copy(slot, other)

                @pl.when(mine)
                def stay(own=own):
                    act_own(own)

                @pl.when(jnp.logical_not(mine))
                def leave(away=away):
                    act_away(away)

    def begin(self):
        self.each(lambda copy: copy.start(), lambda copy: copy.start())

    def end(self):
        got, send, recv, own = self.held
        tensor, core = lax.axis_index("tensor"), core_bit()
        self.each(lambda copy: copy.wait_send(), lambda copy: copy.wait())
        for source in range(4):
            mine = jnp.logical_and(tensor == source, core == tensor // 2)

            @pl.when(jnp.logical_not(mine))
            def arrived(source=source):
                describe(
                    got.at[source], got.at[source], send.at[0], recv.at[source],
                    {"tensor": lax.rem(tensor + 1, 4)},
                ).wait_recv()

        total = got[0].astype(F32)
        for source in range(1, 4):
            total = total + got[source].astype(F32)
        self.out_refs[0][...] = total


def cross_peers():
    tensor, dp = lax.axis_index("tensor"), core_peer()["dp"]
    return [{"tensor": lax.rem(tensor + step, 4), "dp": dp} for step in range(1, 4)]


class Bundle:
    def __init__(self, cargos):
        self.cargos = cargos
        self.loads, self.stores = {}, {}

    def load(self):
        for copy in self.loads.values():
            copy.start()

    def need(self, *which):
        for i in which:
            if i in self.loads:
                self.loads[i].wait()

    def flush(self, *which):
        for i in which:
            if i in self.stores:
                self.stores[i].start()

    def peers(self, names=()):
        names = list(names) + [name for cargo in self.cargos for name in cargo.peers()]
        known = {"core": core_peer, "y": y_peer, "x": x_peer}
        cross = cross_peers() if "cross" in names else []
        return [make() for name, make in known.items() if name in names] + cross

    def begin(self):
        for cargo in self.cargos:
            cargo.begin()

    def middle(self):
        for cargo in self.cargos:
            cargo.middle()

    def late(self):
        for cargo in self.cargos:
            cargo.late()

    def end(self):
        for copy in self.stores.values():
            copy.wait()
        for cargo in self.cargos:
            cargo.end()


def attend_body(
    count, peers, u_ref, mods, segs, biases, outs, scratch, sems, need_qkv, need_out, steps, flush
):
    middle_ref, branch_ref, full_ref, q_ref, k_ref, v_ref, probs_ref, mixed_ref = outs
    full, wqkv, wo, mixed_wide = (full_ref, *scratch[:3])
    buffers, spreads = scratch[3:6], scratch[6]
    seg_own, seg_col, seg_row = segs
    await_peers = call_peers(peers) if peers is not None else None
    mod_ref = mods()
    me = lax.axis_index("tensor")
    rows, length, width = u_ref.shape
    heads_width = wo.shape[0]
    heads = heads_width // HEAD_WIDTH
    u = flat(u_ref).astype(F32)
    normed, unused = layer_norm(u)
    attn_in = normed * (1.0 + token_mod(mod_ref, seg_own, 1)) + token_mod(mod_ref, seg_own, 0)
    full[:, own_rows(me, length), :] = attn_in.astype(BF16).reshape(rows, length, width)
    if peers is not None:
        await_peers()
    line = Line(length, sems)
    line.start_gather(full)
    spread = spread_matrix(heads_width)
    line.relay(full)
    steps[0]()
    both = 3 * heads_width
    for which in range(3):
        spreads[which] = spread_matrix(heads_width, which, both)
    need_qkv()
    line.finish_gather(full)
    flush(2)
    tokens = flat(full)
    bias = biases()
    projected = (dot(tokens, wqkv[...]) + bias[0:1, :both]).astype(BF16)
    for which, target in enumerate((q_ref, k_ref, v_ref)):
        parts = dot(projected, spreads[which])
        target[...] = parts.astype(BF16).reshape(target.shape)

    def one_head(index, carry):
        row = index // heads
        head = lax.rem(index, heads)
        lanes = pl.ds(pl.multiple_of(head * HEAD_LANES, HEAD_LANES), HEAD_LANES)
        scores = dot(q_ref[row, :, lanes], k_ref[row, :, lanes], NT) * HEAD_WIDTH ** (-0.5)
        scores = jnp.where(seg_col[row] == seg_row[row], scores, MASKED_SCORE)
        raised = jnp.exp(scores - jnp.max(scores, axis=-1, keepdims=True))
        probs = raised / jnp.sum(raised, axis=-1, keepdims=True)
        probs_ref[index] = probs
        mixed_wide[row, :, lanes] = dot(probs.astype(BF16), v_ref[row, :, lanes]).astype(BF16)
        return carry

    steps[1]()
    lax.fori_loop(0, rows * heads, one_head, 0, unroll=8)
    mixed_ref[...] = dot(flat(mixed_wide), spread, NT).astype(BF16).reshape(mixed_ref.shape)
    flush(3, 4, 5, 6, 7)
    need_out()

    def partial(which_rows):
        return dot(mixed_ref[:, which_rows, :].reshape(rows * length, heads_width), wo[...])

    total = line.scatter_sum(partial, buffers)
    steps[2]()
    branch = line.finish_sum(total, buffers) + bias[2:3, :]
    branch_ref[...] = branch.reshape(branch_ref.shape)
    middle = flat(u_ref).astype(F32) + token_mod(mod_ref, seg_own, 2) * branch
    middle_ref[...] = middle.reshape(middle_ref.shape)


def open_kernel(count, sections, *refs, cargo):
    u_ref, cond_ref, ada_b_ref, biases_ref, seg_own, seg_col, seg_row = refs[:7]
    ada_w, own_qkv, own_out, own_one, own_two = refs[7:12]
    mods_ref, bias_ref, other_qkv, other_out, other_one, other_two = refs[12:18]
    outs = refs[18:26]
    scratch = refs[26:33]
    ada, mod_src, mod_buf, bias_buf, w_sem, ag_send, ag_recv, rs_send, rs_recv = refs[33:42]
    mod_send, mod_recv, share_send, share_recv, ada_sem = refs[42:]
    wqkv, wo = scratch[:2]
    section, tensor = lax.axis_index("section"), lax.axis_index("tensor")
    load_ada = local(ada_w, ada, ada_sem)
    shares = [
        Share(own, other, parts, (share_send.at[i], share_recv.at[i]))
        for i, (own, other, parts) in enumerate(
            (
                (own_qkv, other_qkv, 4), (own_out, other_out, 2),
                (own_one, other_one, 4), (own_two, other_two, 4),
            )
        )
    ]
    plane = [
        {"section": lax.rem(section + a, sections), "tensor": lax.rem(tensor + b, count)}
        for a in range(sections)
        for b in range(count)
        if a or b
    ]
    greet(plane + [core_peer(), y_peer()] + cross_peers())
    cond_act = silu(cond_ref[...].astype(F32)).astype(BF16)
    load_ada.wait()
    mod = dot(cond_act, ada[...], NT) + ada_b_ref[...].astype(F32)
    mod_src[...] = mod.reshape(mod_src.shape)
    mod_buf[section, tensor] = mod_src[section]
    copies = [
        remote(
            mod_src.at[peer["section"]], mod_buf.at[section, tensor],
            mod_send.at[i], mod_recv.at[i], peer,
        )
        for i, peer in enumerate(plane)
    ]
    bias_buf[section] = biases_ref[...]
    bias_copy = remote(
        biases_ref, bias_buf.at[section],
        mod_send.at[len(plane)], mod_recv.at[len(plane)], x_peer(),
    )
    for share in shares:
        share.begin()
    cargo.begin()

    def mods():
        wait_all(copies)
        width, piece = mods_ref.shape[-1], mod_buf.shape[-1]
        for block in range(sections):
            for which in range(6):
                parts, at = [], which * width
                while at < (which + 1) * width:
                    end = min((at // piece + 1) * piece, (which + 1) * width)
                    start = at - at // piece * piece
                    parts.append(mod_buf[block, at // piece][:, start : start + end - at])
                    at = end
                mods_ref[block, which] = (
                    jnp.concatenate(parts, axis=1) if len(parts) > 1 else parts[0]
                )
        return mods_ref.at[0]

    def biases():
        bias_copy.wait()
        bias_ref[...] = bias_buf[...]
        return bias_buf[0]

    def need_qkv():
        fetch(0, own_qkv, other_qkv, wqkv, w_sem.at[0]).wait()

    def need_out():
        shares[1].finish()
        fetch(0, own_out, other_out, wo, w_sem.at[1]).wait()

    def after_gather():
        shares[0].forward(shares[0].first)
        cargo.middle()
        shares[1].forward(shares[1].first)
        shares[0].forward_again()
        shares[0].finish()

    def before_heads():
        cargo.late()
        shares[2].forward(shares[2].first)

    def after_scatter():
        cargo.cargos[0].start((1,))
        cargo.cargos[0].relay((0, 2))
        shares[2].forward_again()
        shares[3].forward(shares[3].first)
        shares[2].finish()

    attend_body(
        count, None, u_ref, mods, (seg_own, seg_col, seg_row), biases, outs, scratch,
        (ag_send, ag_recv, rs_send, rs_recv), need_qkv, need_out,
        (after_gather, before_heads, after_scatter),
        lambda *which: cargo.flush(*(6 + i for i in which)),
    )
    shares[3].forward_again()
    cargo.cargos[0].relay((1,))
    cargo.end()
    shares[3].finish()


def attend_kernel(count, block, *refs, cargo):
    u_ref, mods_ref, bias_ref, seg_own, seg_col, seg_row = refs[:6]
    own_qkv, other_qkv, own_out, other_out = refs[6:10]
    outs, scratch, w_sem = refs[10:18], refs[18:25], refs[25]
    load_qkv = fetch(block, own_qkv, other_qkv, scratch[0], w_sem.at[0])
    load_out = fetch(block, own_out, other_out, scratch[1], w_sem.at[1])
    attend_body(
        count, z_peers(count) + cargo.peers(), u_ref, lambda: mods_ref.at[block],
        (seg_own, seg_col, seg_row), lambda: bias_ref[block], outs, scratch, refs[26:30],
        load_qkv.wait, load_out.wait, (cargo.begin, cargo.middle, cargo.late), cargo.flush,
    )
    cargo.end()


def mlp_kernel(
    count, block,
    middle_ref, mods_ref, bias_ref, seg_own, w1_own, w1_other, w2_own, w2_other,
    out_ref, branch_ref, full_ref, pre_ref, act_ref,
    w1, w2, send_buf, recv_buf, relay_buf, w_sem, *sems, cargo,
):
    full = full_ref
    await_peers = call_peers(z_peers(count) + cargo.peers())
    me = lax.axis_index("tensor")
    rows, length, width = middle_ref.shape
    mod_ref = mods_ref.at[block]
    load_one = fetch(block, w1_own, w1_other, w1, w_sem.at[0])
    load_two = fetch(block, w2_own, w2_other, w2, w_sem.at[1])
    normed, unused = layer_norm(flat(middle_ref))
    mlp_in = normed * (1.0 + token_mod(mod_ref, seg_own, 4)) + token_mod(mod_ref, seg_own, 3)
    full[:, own_rows(me, length), :] = mlp_in.astype(BF16).reshape(rows, length, width)
    await_peers()
    line = Line(length, sems)
    line.start_gather(full)
    cargo.begin()
    line.relay(full)
    load_one.wait()
    load_two.wait()

    def hidden(place):
        which_rows = own_rows(place, length)
        pre = dot(full[:, which_rows, :].reshape(rows * length, width), w1[...])
        pre = pre + bias_ref[block, 3:4, : w1.shape[1]]
        pre_ref[:, which_rows, :] = pre.reshape(rows, length, -1)
        act_ref[:, which_rows, :] = gelu_tanh(pre).astype(BF16).reshape(rows, length, -1)

    def prepare(place):
        line.arrived(full, place)
        hidden(place)

    def partial(which_rows):
        return dot(act_ref[:, which_rows, :].reshape(rows * length, -1), w2[...])

    hidden(me)
    hidden(line.opposite)
    buffers = (send_buf, recv_buf, relay_buf)
    total = line.scatter_sum(partial, buffers, prepare)
    cargo.flush(2, 3, 4)
    line.sent(full)
    cargo.middle()
    branch = line.finish_sum(total, buffers) + bias_ref[block, 4:5, :]
    cargo.end()
    branch_ref[...] = branch.reshape(branch_ref.shape)
    out = flat(middle_ref) + token_mod(mod_ref, seg_own, 5) * branch
    out_ref[...] = out.astype(BF16).reshape(out_ref.shape)


def mlp_back_kernel(count, block, given, *refs, cargo):
    g_refs, refs = refs[:given], refs[given:]
    g_ref = g_refs[0]
    middle_ref, branch_ref, mods_ref, seg_own, full_ref, pre_ref, act_ref = refs[:7]
    w1_own, w1_other, w2_own, w2_other = refs[7:11]
    d_middle_ref, d_mod_ref, d_w1_ref, d_w2_ref, d_b1_ref, d_b2_ref = refs[11:17]
    full, d_pre, w1, w2, *buffers, w_sem = refs[17:25]
    sems = refs[25:29]
    w1_whole, w1_got, w1_sems, w2_whole, w2_got, w2_sems, normed_buf, g_buf = refs[29:]
    w1_sum = CoreSum(w1_whole, w1_got, d_w1_ref, w1_sems)
    w2_sum = CoreSum(w2_whole, w2_got, d_w2_ref, w2_sems)
    me = lax.axis_index("tensor")
    rows, length, width = middle_ref.shape
    mod_ref = mods_ref.at[block]
    load_one = fetch(block, w1_own, w1_other, w1, w_sem.at[0])
    load_two = fetch(block, w2_own, w2_other, w2, w_sem.at[1])
    await_peers = call_peers(z_peers(count) + cargo.peers(["core"]))
    cargo.load()
    g = flat(g_ref).astype(F32)
    if len(g_refs) > 1:
        g = g + flat(g_refs[1])
    g_buf[...] = g
    d_branch = (g * token_mod(mod_ref, seg_own, 5)).astype(BF16)
    full[:, own_rows(me, length), :] = d_branch.reshape(rows, length, width)
    await_peers()
    line = Line(length, sems)
    line.start_gather(full)
    cargo.begin()
    slot_sums(g * flat(branch_ref), seg_own, d_mod_ref, 2)
    line.relay(full)
    cargo.middle()
    normed, inverse = layer_norm(flat(middle_ref))
    normed_buf[...] = normed
    load_two.wait()
    cargo.need(given + 5)

    def d_hidden(place):
        which_rows = own_rows(place, length)
        d_act = dot(full[:, which_rows, :].reshape(rows * length, width), w2[...], NT)
        slope = gelu_slope(pre_ref[:, which_rows, :].reshape(rows * length, -1))
        d_pre[:, which_rows, :] = (d_act * slope).astype(BF16).reshape(rows, length, -1)

    def prepare(place):
        line.arrived(full, place)
        d_hidden(place)

    d_hidden(me)
    d_hidden(line.opposite)
    load_one.wait()

    def partial(which_rows):
        return dot(d_pre[:, which_rows, :].reshape(rows * length, -1), w1[...], NT)

    total = line.scatter_sum(partial, buffers, prepare)
    line.sent(full)
    cargo.need(given + 4, given + 6)
    w2_whole[...] = dot(flat(full), flat(act_ref), TN).astype(BF16)
    w2_sum.begin()
    w1_whole[...] = dot(flat(full_ref), flat(d_pre), TN).astype(BF16)
    w1_sum.begin()
    d_b2_ref[...] = jnp.sum(flat(full).astype(F32), axis=0, keepdims=True)
    d_b1_ref[...] = jnp.sum(flat(d_pre).astype(F32), axis=0, keepdims=True)
    d_in = line.finish_sum(total, buffers)
    normed = normed_buf[...]
    d_middle = g_buf[...] + norm_back(
        d_in * (1.0 + token_mod(mod_ref, seg_own, 4)), normed, inverse
    )
    d_middle_ref[...] = d_middle.reshape(d_middle_ref.shape)
    slot_sums(d_in, seg_own, d_mod_ref, 0)
    slot_sums(d_in * normed, seg_own, d_mod_ref, 1)
    w2_sum.end()
    w1_sum.end()
    cargo.end()


def attend_back_kernel(count, block, *refs, cargo):
    d_middle_ref, u_ref, branch_ref, mods_ref, seg_own, full_ref = refs[:6]
    q_ref, k_ref, v_ref, probs_ref, mixed_ref = refs[6:11]
    wqkv_own, wqkv_other, wo_own, wo_other = refs[11:15]
    d_in_ref, d_mod_ref, d_wqkv_ref, d_wo_ref, d_bqv_ref, d_bo_ref = refs[15:21]
    full, wide, narrow, wqkv, wo, *buffers, w_sem = refs[21:30]
    sems = refs[30:34]
    qkv_whole, qkv_got, qkv_sems, wo_whole, wo_got, wo_sems, spreads, normed_buf = refs[34:]
    qkv_sum = CoreSum(qkv_whole, qkv_got, d_wqkv_ref, qkv_sems)
    wo_sum = CoreSum(wo_whole, wo_got, d_wo_ref, wo_sems)
    me = lax.axis_index("tensor")
    rows, length, width = u_ref.shape
    heads_width = wo.shape[0]
    heads = heads_width // HEAD_WIDTH
    mod_ref = mods_ref.at[block]
    load_qkv = fetch(block, wqkv_own, wqkv_other, wqkv, w_sem.at[0])
    load_out = fetch(block, wo_own, wo_other, wo, w_sem.at[1])
    await_peers = call_peers(z_peers(count) + cargo.peers(["core"]))
    cargo.load()
    d_middle = flat(d_middle_ref)
    d_branch = (d_middle * token_mod(mod_ref, seg_own, 2)).astype(BF16)
    full[:, own_rows(me, length), :] = d_branch.reshape(rows, length, width)
    await_peers()
    line = Line(length, sems)
    line.start_gather(full)
    cargo.begin()
    slot_sums(d_middle * flat(branch_ref), seg_own, d_mod_ref, 2)
    line.relay(full)
    cargo.middle()
    spread = spread_matrix(heads_width)
    both = 3 * heads_width
    for which in range(3):
        spreads[which] = spread_matrix(heads_width, which, both)
    normed, inverse = layer_norm(flat(u_ref).astype(F32))
    normed_buf[...] = normed
    load_out.wait()
    line.finish_gather(full)
    d_mixed = dot(flat(full), wo[...], NT).astype(BF16)
    wide[3] = dot(d_mixed, spread).astype(BF16).reshape(wide.shape[1:])
    cargo.need(6, 7, 8, 9)

    def one_head(index, carry):
        row = index // heads
        head = lax.rem(index, heads)
        lanes = pl.ds(pl.multiple_of(head * HEAD_LANES, HEAD_LANES), HEAD_LANES)
        grad = wide[3, row, :, lanes]
        probs = probs_ref[index]
        d_probs = dot(grad, v_ref[row, :, lanes], NT)
        d_scores = (
            probs * (d_probs - jnp.sum(d_probs * probs, axis=-1, keepdims=True))
        ).astype(BF16)
        scale = HEAD_WIDTH ** (-0.5)
        wide[0, row, :, lanes] = (dot(d_scores, k_ref[row, :, lanes]) * scale).astype(BF16)
        wide[1, row, :, lanes] = (dot(d_scores, q_ref[row, :, lanes], TN) * scale).astype(BF16)
        wide[2, row, :, lanes] = dot(probs.astype(BF16), grad, TN).astype(BF16)
        return carry

    lax.fori_loop(0, rows * heads, one_head, 0, unroll=8)
    gathered = 0.0
    for which in range(3):
        gathered = gathered + dot(flat(wide.at[which]), spreads[which], NT)
    narrow[...] = gathered.astype(BF16).reshape(narrow.shape)
    load_qkv.wait()

    def partial(which_rows):
        return dot(narrow[:, which_rows, :].reshape(rows * length, both), wqkv[...], NT)

    total = line.scatter_sum(partial, buffers)
    d_bo_ref[...] = jnp.sum(flat(full).astype(F32), axis=0, keepdims=True)
    d_bqv_ref[...] = jnp.sum(flat(narrow).astype(F32), axis=0, keepdims=True)
    cargo.need(5, 10)
    wo_whole[...] = dot(flat(full), flat(mixed_ref), TN).astype(BF16)
    wo_sum.begin()
    qkv_whole[...] = dot(flat(full_ref), flat(narrow), TN).astype(BF16)
    qkv_sum.begin()
    d_attn_in = line.finish_sum(total, buffers)
    normed = normed_buf[...]
    d_in = flat(d_middle_ref) + norm_back(
        d_attn_in * (1.0 + token_mod(mod_ref, seg_own, 1)), normed, inverse
    )
    d_in_ref[...] = d_in.reshape(d_in_ref.shape)
    slot_sums(d_attn_in, seg_own, d_mod_ref, 0)
    slot_sums(d_attn_in * normed, seg_own, d_mod_ref, 1)
    wo_sum.end()
    qkv_sum.end()
    cargo.end()


def silu_slope(value):
    gate = 1.0 / (1.0 + jnp.exp(-value))
    return gate * (1.0 + value * (1.0 - gate))


def project_kernel(token_count, *refs, cargo):
    sent_ref, targets_ref, biases_ref, p2_b_ref, p1_any, p2_any, p3_any = refs[:7]
    d_sent_ref, d_p1_ref, d_p2_ref, d_p3_ref, small_ref = refs[7:12]
    p1, p2, p3, tokens, first_pre, first, second_pre, second, d_second, norms = refs[12:22]
    buf_a, buf_b, buf_c, d_first, load_sem, send, recv = refs[22:]
    core, peer = core_bit(), core_peer()
    loads = [
        local(source, place, load_sem.at[i])
        for i, (source, place) in enumerate(((p1_any, p1), (p2_any, p2), (p3_any, p3)))
    ]
    count = tokens.shape[1]
    tokens[core] = flat(sent_ref)
    greet([peer])

    def trade(ref, which):
        return remote(ref.at[core], ref.at[core], send.at[which], recv.at[which], peer)

    def give(buffer, value, which):
        buffer[0] = value.astype(BF16)
        return remote(buffer.at[0], buffer.at[1], send.at[which], recv.at[which], peer)

    def block(ref, side):
        return ref[side]

    copy = trade(tokens, 0)
    target = [
        targets_ref[slot].reshape(2 * count, targets_ref.shape[-1]).astype(F32) for slot in range(2)
    ]
    target_sq = sum(jnp.sum(one * one, axis=1, keepdims=True) for one in target)
    loads[0].wait()
    copy.wait()
    all_tokens = flat(tokens)
    for slot in range(2):
        pre = dot(all_tokens, p1[slot]) + biases_ref[slot, 0, 0:1, :]
        first_pre[slot] = pre
        first[slot] = silu(pre).astype(BF16)
    loads[1].wait()

    def second_term(side):
        rows = pl.ds(pl.multiple_of(side * count, 16), count)
        return dot(first[0, rows, :], p2[0]) + dot(first[1, rows, :], p2[1])

    copy = give(buf_a, second_term(1 - core), 1)
    pre = second_term(core)
    copy.wait()
    pre = pre + buf_a[1].astype(F32) + p2_b_ref[...].astype(F32)
    second_pre[...] = pre
    second[core] = silu(pre).astype(BF16)
    copy = trade(second, 2)
    loads[2].wait()
    copy.wait()
    all_second = flat(second)
    width = target[0].shape[1]
    predicted = [
        dot(all_second, p3[slot], NT) + biases_ref[slot, 0, 1:2, :width] for slot in range(2)
    ]
    pred_sq = sum(jnp.sum(one * one, axis=1, keepdims=True) for one in predicted)
    cross = sum(
        jnp.sum(one * two, axis=1, keepdims=True) for one, two in zip(predicted, target)
    )
    lanes = lax.broadcasted_iota(jnp.int32, norms.shape[1:], 1)
    norms[core] = jnp.where(lanes == 0, pred_sq, jnp.where(lanes == 1, cross, target_sq))
    copy = trade(norms, 3)
    copy.wait()
    total = norms[0] + norms[1]
    inv_pred = lax.rsqrt(total[:, 0:1] + COSINE_EPS)
    inv_target = lax.rsqrt(total[:, 2:3] + COSINE_EPS)
    cosine = total[:, 1:2] * inv_pred * inv_target
    side = lax.broadcasted_iota(jnp.int32, cosine.shape, 0)
    own = jnp.logical_and(side >= core * count, side < (core + 1) * count)
    loss = jnp.sum(jnp.where(own, cosine, 0.0), axis=0, keepdims=True)
    factor = -0.5 / token_count
    one_scale = factor * inv_pred * inv_target
    two_scale = factor * cosine * inv_pred * inv_pred
    d_pred = [
        (one_scale * two - two_scale * one).astype(BF16) for one, two in zip(predicted, target)
    ]
    small_ref[...] = jnp.zeros_like(small_ref)
    for slot in range(2):
        small_ref[2 * core + slot, 1:2, :width] = jnp.sum(
            d_pred[slot].astype(F32), axis=0, keepdims=True
        )

    def d_second_term(side):
        terms = 0.0
        for slot in range(2):
            mine = jnp.where(
                side == 0, d_pred[slot][:count].astype(F32), d_pred[slot][count:].astype(F32)
            )
            terms = terms + dot(mine.astype(BF16), p3[slot])
        return terms

    copy = give(buf_b, d_second_term(1 - core), 4)
    grad = d_second_term(core)
    for slot in range(2):
        d_p3_ref[slot] = dot(d_pred[slot], all_second, TN).astype(BF16)
    copy.wait()
    grad = ((grad + buf_b[1].astype(F32)) * silu_slope(second_pre[...])).astype(BF16)
    d_second[core] = grad
    copy = trade(d_second, 5)
    d_p2_b = jnp.sum(grad.astype(F32), axis=0, keepdims=True)
    lane = small_ref.shape[2]
    loss_row = jnp.where(lax.broadcasted_iota(jnp.int32, (1, lane), 1) == 0, loss, 0.0)
    for part in range(4):
        for row in range(d_p2_b.shape[1] // lane):
            small_ref[part, 2 + row : 3 + row, :] = d_p2_b[:, row * lane : (row + 1) * lane]
        small_ref[part, 6:7, :] = loss_row
    copy.wait()
    all_d_second = flat(d_second)
    for slot in range(2):
        back = dot(all_d_second, p2[slot], NT) * silu_slope(first_pre[slot])
        d_first[slot] = back.astype(BF16)
        small_ref[2 * core + slot, 0:1, :] = jnp.sum(
            d_first[slot].astype(F32), axis=0, keepdims=True
        )

    def d_sent_term(side):
        rows = pl.ds(pl.multiple_of(side * count, 16), count)
        return dot(d_first[0, rows, :], p1[0], NT) + dot(d_first[1, rows, :], p1[1], NT)

    copy = give(buf_c, d_sent_term(1 - core), 6)
    grad = d_sent_term(core)
    for slot in range(2):
        d_p2_ref[slot] = dot(first[slot], all_d_second, TN).astype(BF16)
        d_p1_ref[slot] = dot(all_tokens, d_first[slot], TN).astype(BF16)
    copy.wait()
    d_sent_ref[...] = (grad + buf_c[1].astype(F32)).reshape(d_sent_ref.shape)


def close_kernel(count, sections, replicas, *refs, cargo):
    grads_ref, mod_refs, small_refs, proj_ref, cond_ref = (
        refs[:2], refs[2:6], refs[6:14], refs[14], refs[15]
    )
    grad_ref, ada_w_ref, ada_b_ref, small_ref, proj_sum_ref = refs[16:21]
    z_src, z_buf, mod_src, mod_buf, small_src, small_buf, cond_buf = refs[21:28]
    place_src, place_buf, proj_got, proj_src, proj_buf = refs[28:33]
    sems = refs[33:35]
    section, tensor, replica = (lax.axis_index(name) for name in ("section", "tensor", "dp"))
    send, recv = sems
    others = [
        {"section": lax.rem(section + a, sections), "dp": lax.rem(replica + b, replicas)}
        for a in range(sections)
        for b in range(replicas)
        if a or b
    ]
    greet(z_peers(count) + others + cross_peers())
    last_sums = [one for one in cargo.cargos if isinstance(one, LastSum)]
    y_sums = [one for one in cargo.cargos if type(one) is YSum]
    for one in last_sums:
        one.begin()
    piece = z_src.shape[-1]
    for block in range(sections):
        attend_mod, mlp_mod = mod_refs[2 * block : 2 * block + 2]
        width = attend_mod.shape[-1]
        for part in range(count):
            at, end, cuts = part * piece, (part + 1) * piece, []
            while at < end:
                which = at // width
                stop = min((which + 1) * width, end)
                ref = attend_mod if which < 3 else mlp_mod
                cuts.append(ref[which % 3][:, at - which * width : stop - which * width])
                at = stop
            z_src[part, block] = jnp.concatenate(cuts, axis=1) if len(cuts) > 1 else cuts[0]
    z_copies = [
        remote(z_src.at[peer["tensor"]], z_buf.at[i], send.at[i], recv.at[i], peer)
        for i, peer in enumerate(z_peers(count))
    ]
    at = count - 1
    z_copies += [
        remote(proj_ref.at[peer["tensor"]], proj_got.at[i], send.at[at + i], recv.at[at + i], peer)
        for i, peer in enumerate(z_peers(count))
    ]
    at = at + count - 1

    @pl.when(section == 0)
    def first_place():
        place_src[...] = grads_ref[1][...].astype(BF16)

    @pl.when(section != 0)
    def second_place():
        place_src[...] = grads_ref[0][...].astype(BF16)

    place_copy = remote(place_src, place_buf, send.at[at], recv.at[at], x_peer())
    at = at + 1
    both = small_refs[0].shape[-1]
    small_src[...] = jnp.zeros_like(small_src)
    for block in range(sections):
        d_bqv, d_bo, d_b1, d_b2 = small_refs[4 * block : 4 * block + 4]
        small_src[block, 0:1, :both] = d_bqv[...]
        small_src[block, 2:3, :] = d_bo[...]
        small_src[block, 3:4, : d_b1.shape[1]] = d_b1[...]
        small_src[block, 4:5, :] = d_b2[...]
    small_buf[section, replica] = small_src[section]
    cond_buf[section, replica] = cond_ref[replica]
    copies = []
    for peer in others:
        copies.append(
            remote(
                small_src.at[peer["section"]], small_buf.at[section, replica],
                send.at[at], recv.at[at], peer,
            )
        )
        copies.append(
            remote(
                cond_ref.at[peer["dp"]], cond_buf.at[section, replica],
                send.at[at + 1], recv.at[at + 1], peer,
            )
        )
        at = at + 2
    for one in cargo.cargos:
        if not isinstance(one, YSum):
            one.begin()
    wait_all(z_copies)
    mine, mine_proj = z_src[tensor], proj_ref[tensor]
    for step in range(count - 1):
        mine = mine + z_buf[step]
        mine_proj = mine_proj + proj_got[step]
    mod_src[...] = mine
    mod_buf[section, replica] = mod_src[section]
    proj_src[...] = mine_proj
    proj_buf[section, replica] = mine_proj
    for peer in others:
        copies.append(
            remote(
                mod_src.at[peer["section"]], mod_buf.at[section, replica],
                send.at[at], recv.at[at], peer,
            )
        )
        copies.append(
            remote(
                proj_src, proj_buf.at[section, replica], send.at[at + 1], recv.at[at + 1], peer
            )
        )
        at = at + 2
    for one in last_sums:
        one.middle()
    for one in y_sums:
        one.begin()
    place_copy.wait()
    rows = place_buf.shape[0]

    @pl.when(section == 0)
    def first_out():
        grad_ref[:rows] = grads_ref[0][...]
        grad_ref[rows:] = place_buf[...].astype(F32)

    @pl.when(section != 0)
    def second_out():
        grad_ref[rows:] = grads_ref[1][...]
        grad_ref[:rows] = place_buf[...].astype(F32)

    wait_all(copies)
    small, proj_sum = small_buf[0, 0], proj_buf[0, 0]
    for a in range(sections):
        for b in range(replicas):
            if a or b:
                small = small + small_buf[a, b]
                proj_sum = proj_sum + proj_buf[a, b]
    small_ref[...] = small
    proj_sum_ref[...] = proj_sum
    mod_all = flat(mod_buf)
    ada_b_ref[...] = jnp.sum(mod_all, axis=0, keepdims=True)
    ada_w_ref[...] = lax.dot_general(
        flat(cond_buf), mod_all, TN, precision=HIGHEST, preferred_element_type=F32
    )
    cargo.end()


VMEM = pl.BlockSpec(memory_space=pltpu.VMEM)
ANY = pl.BlockSpec(memory_space=pl.ANY)
MOD_ROWS = 8
PROJECTOR_AXES = (0, 0, 1)


def call(
    kernel, number, inputs, in_any, outs, out_any, scratch, flops, cargos=(), lazy=(), streamed=()
):
    own_in, own_out, own_scratch = len(inputs), len(outs), len(scratch)
    specs = [VMEM] * (own_in - in_any) + [ANY] * in_any
    specs = [ANY if i in lazy else spec for i, spec in enumerate(specs)]
    out_specs = [ANY if i in out_any or i in streamed else VMEM for i in range(own_out)]
    inputs, outs, scratch, aliases = list(inputs), list(outs), list(scratch), {}
    moved_refs = len(lazy) + len(streamed)
    scratch += [pltpu.VMEM(inputs[i].shape, inputs[i].dtype) for i in lazy]
    scratch += [pltpu.VMEM(*outs[i]) for i in streamed]
    if moved_refs:
        scratch.append(pltpu.SemaphoreType.DMA((moved_refs,)))
        moved_refs += 1
    for cargo in cargos:
        for source, target in cargo.aliases.items():
            aliases[len(inputs) + source] = len(outs) + target
        inputs += cargo.inputs
        outs += cargo.outs
        scratch += cargo.scratch
        specs += [ANY] * len(cargo.inputs)
        out_specs += [ANY if cargo.any_outs else VMEM] * len(cargo.outs)

    def body(*refs):
        parts = [list(refs[: len(inputs)])]
        parts.append(list(refs[len(inputs) : len(inputs) + len(outs)]))
        parts.append(list(refs[len(inputs) + len(outs) :]))
        base = parts[0][:own_in] + parts[1][:own_out] + parts[2][:own_scratch]
        held = parts[2][own_scratch : own_scratch + moved_refs]
        bundle = Bundle(cargos)
        for k, i in enumerate(lazy):
            bundle.loads[i] = pltpu.make_async_copy(base[i], held[k], held[-1].at[k])
            base[i] = held[k]
        for k, i in enumerate(streamed, len(lazy)):
            bundle.stores[i] = pltpu.make_async_copy(held[k], base[own_in + i], held[-1].at[k])
            base[own_in + i] = held[k]
        at = [own_in, own_out, own_scratch + moved_refs]
        for cargo in cargos:
            held = []
            for i, items in enumerate((cargo.inputs, cargo.outs, cargo.scratch)):
                held.append(parts[i][at[i] : at[i] + len(items)])
                at[i] += len(items)
            cargo.bind(*held)
        kernel(*base, cargo=bundle)

    moved = sum(math.prod(one.shape) * one.dtype.itemsize for one in inputs)
    results = pl.pallas_call(
        body,
        out_shape=[jax.ShapeDtypeStruct(shape, dtype) for shape, dtype in outs],
        in_specs=specs,
        out_specs=out_specs,
        scratch_shapes=scratch,
        input_output_aliases=aliases,
        compiler_params=pltpu.CompilerParams(
            collective_id=number, has_side_effects=True, vmem_limit_bytes=56 * 2**20
        ),
        cost_estimate=pl.CostEstimate(flops=flops, bytes_accessed=moved, transcendentals=0),
    )(*inputs)
    at, carried = own_out, []
    for cargo in cargos:
        carried.append(results[at : at + len(cargo.outs)])
        at += len(cargo.outs)
    return results[:own_out], carried


def exchange_scratch(count, rows, length, width):
    return [
        pltpu.VMEM((count - 1, rows, length, width), BF16),
        pltpu.VMEM((count, rows, length, width), BF16),
        pltpu.VMEM((rows, length, width), BF16),
    ]


def semaphores(count):
    return [pltpu.SemaphoreType.DMA((2,))] + [
        pltpu.SemaphoreType.DMA((size,)) for size in (count, count, count - 1, count + 1)
    ]


class Shapes:
    def __init__(self, u, own, count):
        self.rows, self.length, self.width = u.shape
        self.count = count
        self.positions = self.length * count
        self.tokens = self.rows * self.positions
        self.heads_width = own["out"].shape[0]
        self.hidden = own["one"].shape[1]
        self.heads = self.heads_width // HEAD_WIDTH
        self.local = (self.rows, self.length, self.width)
        self.full = (self.rows, self.positions, self.width)
        self.wide = (self.rows, self.positions, self.heads * HEAD_LANES)
        self.own = own
        self.attend_outs = [
            (self.local, F32), (self.local, F32), (self.full, BF16),
            (self.wide, BF16), (self.wide, BF16), (self.wide, BF16),
            ((self.rows * self.heads, self.positions, self.positions), F32),
            ((self.rows, self.positions, self.heads_width), BF16),
        ]
        self.attend_scratch = [
            pltpu.VMEM(own["qkv"].shape, BF16),
            pltpu.VMEM(own["out"].shape, BF16),
            pltpu.VMEM(self.wide, BF16),
        ] + exchange_scratch(count, *self.local)
        self.spreads = pltpu.VMEM((3, 3 * self.heads_width, self.heads * HEAD_LANES), BF16)
        self.attend_scratch.append(self.spreads)
        self.mods = (3, MOD_ROWS, self.width)


def pairs(own, other, names):
    out = []
    for name in names:
        out += [own[name], other[name]]
    return out


def open_forward(sizes, u, cond, ada_w, ada_b, biases, segs, own, sections, cargos):
    count, width = sizes.count, sizes.width
    piece = ada_w.shape[0]
    inputs = [u, cond, ada_b, biases, *segs, ada_w] + [own[n] for n in ("qkv", "out", "one", "two")]
    plane = sections * count - 1
    results, carried = call(
        functools.partial(open_kernel, count, sections),
        0,
        inputs,
        5,
        [((sections, 6, MOD_ROWS, width), F32), ((sections,) + biases.shape, F32)]
        + [(own[n].shape, BF16) for n in ("qkv", "out", "one", "two")]
        + sizes.attend_outs,
        (2, 3, 4, 5),
        sizes.attend_scratch
        + [
            pltpu.VMEM(ada_w.shape, BF16),
            pltpu.VMEM((sections, MOD_ROWS, piece), F32),
            pltpu.VMEM((sections, count, MOD_ROWS, piece), F32),
            pltpu.VMEM((sections,) + biases.shape, F32),
        ]
        + semaphores(count)
        + [
            pltpu.SemaphoreType.DMA((plane + 1,)),
            pltpu.SemaphoreType.DMA((plane + 1,)),
            pltpu.SemaphoreType.DMA((4, 4)),
            pltpu.SemaphoreType.DMA((4, 4)),
            pltpu.SemaphoreType.DMA,
        ],
        2 * sizes.tokens * width * sizes.heads_width * 4,
        cargos,
        streamed=tuple(range(8, 14)),
    )
    other = dict(zip(("qkv", "out", "one", "two"), results[2:6]))
    return results[0], results[1], other, results[6:], carried


def attend_forward(sizes, block, u, mods, biases, segs, own, other, cargos):
    inputs = [u, mods, biases, *segs] + pairs(own, other, ("qkv", "out"))
    return call(
        functools.partial(attend_kernel, sizes.count, block),
        1,
        inputs,
        4,
        sizes.attend_outs,
        (),
        sizes.attend_scratch + semaphores(sizes.count),
        2 * sizes.tokens * sizes.width * sizes.heads_width * 4,
        cargos,
        streamed=tuple(range(2, 8)),
    )


def mlp_forward(sizes, block, middle, mods, biases, segs, own, other, cargos):
    inputs = [middle, mods, biases, segs[0]] + pairs(own, other, ("one", "two"))
    hidden = (sizes.rows, sizes.positions, sizes.hidden)
    return call(
        functools.partial(mlp_kernel, sizes.count, block),
        2 + block,
        inputs,
        4,
        [
            (sizes.local, BF16), (sizes.local, F32), (sizes.full, BF16),
            (hidden, F32), (hidden, BF16),
        ],
        (),
        [
            pltpu.VMEM(own["one"].shape, BF16),
            pltpu.VMEM(own["two"].shape, BF16),
        ]
        + exchange_scratch(sizes.count, *sizes.local)
        + semaphores(sizes.count),
        2 * sizes.tokens * sizes.width * sizes.hidden * 2,
        cargos,
        streamed=(2, 3, 4),
    )


def mlp_backward(sizes, block, grads, attend, mlp, mods, segs, own, other, cargos):
    out, branch, full, pre, act = mlp
    inputs = [*grads, attend[0], branch, mods, segs[0], full, pre, act]
    given = len(grads)
    inputs += pairs(own, other, ("one", "two"))
    return call(
        functools.partial(mlp_back_kernel, sizes.count, block, given),
        4 + block,
        inputs,
        4,
        [
            (sizes.local, F32), (sizes.mods, F32),
            ((2,) + quarter((sizes.width, sizes.hidden)), BF16),
            ((2,) + quarter((sizes.width, sizes.hidden)), BF16),
            ((1, sizes.hidden), F32), ((1, sizes.width), F32),
        ],
        (),
        [
            pltpu.VMEM(sizes.full, BF16),
            pltpu.VMEM((sizes.rows, sizes.positions, sizes.hidden), BF16),
            pltpu.VMEM(own["one"].shape, BF16),
            pltpu.VMEM(own["two"].shape, BF16),
        ]
        + exchange_scratch(sizes.count, *sizes.local)
        + semaphores(sizes.count)
        + core_sum_scratch((sizes.width, sizes.hidden)) * 2
        + [
            pltpu.VMEM((sizes.rows * sizes.length, sizes.width), F32),
            pltpu.VMEM((sizes.rows * sizes.length, sizes.width), F32),
        ],
        2 * sizes.tokens * sizes.width * sizes.hidden * 4,
        cargos,
        lazy=(given + 4, given + 5, given + 6),
    )


def attend_backward(sizes, block, d_middle, u, attend, mods, segs, own, other, cargos):
    middle, branch, full, q, k, v, probs, mixed = attend
    inputs = [d_middle, u, branch, mods, segs[0], full, q, k, v, probs, mixed]
    inputs += pairs(own, other, ("qkv", "out"))
    return call(
        functools.partial(attend_back_kernel, sizes.count, block),
        6 + block,
        inputs,
        4,
        [
            (sizes.local, F32), (sizes.mods, F32),
            ((2,) + quarter((sizes.width, 3 * sizes.heads_width)), BF16),
            ((2,) + quarter((sizes.width, sizes.heads_width)), BF16),
            ((1, 3 * sizes.heads_width), F32), ((1, sizes.width), F32),
        ],
        (),
        [
            pltpu.VMEM(sizes.full, BF16),
            pltpu.VMEM((4,) + sizes.wide, BF16),
            pltpu.VMEM((sizes.rows, sizes.positions, 3 * sizes.heads_width), BF16),
            pltpu.VMEM(own["qkv"].shape, BF16),
            pltpu.VMEM(own["out"].shape, BF16),
        ]
        + exchange_scratch(sizes.count, *sizes.local)
        + semaphores(sizes.count)
        + core_sum_scratch((sizes.width, 3 * sizes.heads_width))
        + core_sum_scratch((sizes.width, sizes.heads_width))
        + [
            sizes.spreads,
            pltpu.VMEM((sizes.rows * sizes.length, sizes.width), F32),
        ],
        2 * sizes.tokens * sizes.width * sizes.heads_width * 8,
        cargos,
        lazy=(5, 6, 7, 8, 9, 10),
    )


def project(sizes, sent, weights, targets, biases, p2_b, token_count):
    tokens = sizes.rows * sizes.length
    p1, p2, p3 = weights
    lane, hidden = p1.shape[2], p2.shape[2]
    inputs = [sent, targets, biases, p2_b, p1, p2, p3]
    results, unused = call(
        functools.partial(project_kernel, token_count),
        9,
        inputs,
        3,
        [
            (sizes.local, F32), (p1.shape, BF16), (p2.shape, BF16), (p3.shape, BF16),
            ((sizes.count, MOD_ROWS, lane), F32),
        ],
        (),
        [
            pltpu.VMEM(p1.shape, BF16),
            pltpu.VMEM(p2.shape, BF16),
            pltpu.VMEM(p3.shape, BF16),
            pltpu.VMEM((2, tokens, sizes.width), BF16),
            pltpu.VMEM((2, 2 * tokens, lane), F32),
            pltpu.VMEM((2, 2 * tokens, lane), BF16),
            pltpu.VMEM((tokens, hidden), F32),
            pltpu.VMEM((2, tokens, hidden), BF16),
            pltpu.VMEM((2, tokens, hidden), BF16),
            pltpu.VMEM((2, 2 * tokens, HEAD_LANES), F32),
            pltpu.VMEM((2, tokens, hidden), BF16),
            pltpu.VMEM((2, tokens, hidden), BF16),
            pltpu.VMEM((2, tokens, sizes.width), BF16),
            pltpu.VMEM((2, 2 * tokens, lane), BF16),
            pltpu.SemaphoreType.DMA((3,)),
            pltpu.SemaphoreType.DMA((7,)),
            pltpu.SemaphoreType.DMA((7,)),
        ],
        12 * tokens * sum(math.prod(one.shape) for one in weights),
    )
    return results


def close_backward(sizes, grads, mod_grads, small, proj_small, cond, sections, replicas, cargos):
    count, width = sizes.count, sizes.width
    piece = 6 * width // count
    share = width // replicas
    inputs = [*grads, *mod_grads, *small, proj_small, cond]
    copies = 2 * count + 4 * (sections * replicas - 1)
    both = (sections * sizes.rows,) + sizes.local[1:]
    return call(
        functools.partial(close_kernel, count, sections, replicas),
        8,
        inputs,
        0,
        [
            (both, F32), ((share, piece), F32), ((1, piece), F32),
            ((MOD_ROWS, width), F32), (proj_small.shape[1:], F32),
        ],
        (),
        [
            pltpu.VMEM((count, sections, MOD_ROWS, piece), F32),
            pltpu.VMEM((count - 1, sections, MOD_ROWS, piece), F32),
            pltpu.VMEM((sections, MOD_ROWS, piece), F32),
            pltpu.VMEM((sections, replicas, MOD_ROWS, piece), F32),
            pltpu.VMEM((sections, MOD_ROWS, width), F32),
            pltpu.VMEM((sections, replicas, MOD_ROWS, width), F32),
            pltpu.VMEM((sections, replicas, MOD_ROWS, share), F32),
            pltpu.VMEM(sizes.local, BF16),
            pltpu.VMEM(sizes.local, BF16),
            pltpu.VMEM((count - 1,) + proj_small.shape[1:], F32),
            pltpu.VMEM(proj_small.shape[1:], F32),
            pltpu.VMEM((sections, replicas) + proj_small.shape[1:], F32),
            pltpu.SemaphoreType.DMA((copies,)),
            pltpu.SemaphoreType.DMA((copies,)),
        ],
        2 * sections * replicas * MOD_ROWS * share * piece,
        cargos,
    )


def assemble_kernel(heads_width, *refs):
    fc1, fc2 = refs[0:2], refs[2:4]
    alone, (qkv, wo) = refs[4:9], (refs[9:11], refs[11:13])
    grad_ref, small, proj = refs[13:16]
    outs, sems = refs[16:-1], refs[-1]
    is_first = lax.axis_index("section") == 0
    waits = []
    for i, pair in enumerate((fc1, fc2)):
        waits.append(pltpu.make_async_copy(pair[0], outs[i], sems.at[i]))

        @pl.when(is_first)
        def take_one(pair=pair, i=i):
            pltpu.make_async_copy(pair[0], outs[i], sems.at[i]).start()

        @pl.when(jnp.logical_not(is_first))
        def take_two(pair=pair, i=i):
            pltpu.make_async_copy(pair[1], outs[i], sems.at[i]).start()

    for i, one in enumerate(alone):
        waits.append(local(one, outs[2 + i], sems.at[2 + i]))
    grad_out, qkv_out, wo_out, qv_b, out_b, fc1_b, fc2_b, p1_b, p2_b, p3_b, loss = outs[7:]
    for row in range(grad_ref.shape[0]):
        grad_out[:, row, :] = grad_ref[row]
    qkv_own = jnp.where(is_first, qkv[0][...], qkv[1][...])
    for which in range(3):
        qkv_out[which] = qkv_own[:, which * heads_width : (which + 1) * heads_width]
    wo_out[...] = jnp.where(is_first, wo[0][...], wo[1][...]).T
    qv_b[0:1, :] = small[0:1, :heads_width]
    qv_b[1:2, :] = small[0:1, 2 * heads_width : 3 * heads_width]
    out_b[...] = small[2:3, :]
    fc1_b[...] = small[3:4, :]
    fc2_b[...] = small[4:5, :]
    p1_b[...] = proj[0:1, :]
    p2_b[...] = jnp.concatenate([proj[2 + row : 3 + row, :] for row in range(4)], axis=1)
    p3_b[...] = proj[1:2, : p3_b.shape[1]]
    loss[...] = proj[6:7, :HEAD_LANES]
    wait_all(waits)


def assemble(choices, alone, section_grad, small, proj_small, heads_width):
    (fc1, fc2, qkv, wo) = choices
    inputs = [*fc1, *fc2, *alone, *qkv, *wo, section_grad, small, proj_small]
    both, length, width = section_grad.shape
    share, lane = fc1[0].shape[0], proj_small.shape[1]
    third = alone[4].shape[0]
    shapes = [fc1[0].shape, fc2[0].shape] + [one.shape for one in alone] + [
        (length, both, width), (3, share, heads_width), wo[0].shape[::-1], (2, heads_width),
        (1, width), (1, width), (1, width), (1, lane), (1, 4 * lane), (1, third), (1, HEAD_LANES),
    ]
    return pl.pallas_call(
        functools.partial(assemble_kernel, heads_width),
        out_shape=[jax.ShapeDtypeStruct(shape, F32) for shape in shapes],
        in_specs=[ANY] * 9 + [VMEM] * 7,
        out_specs=[VMEM] * 18,
        scratch_shapes=[pltpu.SemaphoreType.DMA((7,))],
        compiler_params=pltpu.CompilerParams(vmem_limit_bytes=62 * 2**20),
        cost_estimate=pl.CostEstimate(flops=1000, bytes_accessed=2**24, transcendentals=0),
    )(*inputs)


def halve(value, axis, bit, position):
    size = lax.axis_size(axis)
    mine = (lax.axis_index(axis) & bit) // bit
    keep = lax.dynamic_index_in_dim(value, mine, position, keepdims=False)
    give = lax.dynamic_index_in_dim(value, 1 - mine, position, keepdims=False)
    return keep + lax.ppermute(give, axis, [(i, i ^ bit) for i in range(size)])


def sum_beyond_quads(value):
    size = lax.axis_size("dp")
    if size == 4:
        return value
    quads = size // 4
    bits = quads.bit_length() - 1
    lead = value.ndim - 2
    shape = value.shape
    value = value.reshape(shape[:lead] + (2,) * bits + (shape[-2] // quads, shape[-1]))
    for bit in range(bits):
        value = halve(value, "dp", 4 << bit, lead + bits - 1 - bit)
    route = [(high * 4 + low, low * quads + high) for high in range(quads) for low in range(4)]
    return lax.ppermute(value, "dp", route)


def per_device(
    block_eight_input,
    cond,
    image_slot_index,
    targets,
    cot,
    ada_w,
    ada_b,
    query_key_value_weight,
    query_value_bias,
    attention_output_weight,
    attention_output_bias,
    hidden_weight,
    hidden_bias,
    output_weight_mlp,
    output_bias_mlp,
    p1_w,
    p1_b,
    p2_w,
    p2_b,
    p3_w,
    p3_b,
):
    section = lax.axis_index("section")
    tensor = lax.axis_index("tensor")
    is_first = section == 0
    count = lax.axis_size("tensor")
    sections = lax.axis_size("section")
    replicas = lax.axis_size("dp")
    length, replica_rows, width = block_eight_input.shape
    positions = length * count
    rows = replica_rows // sections
    total_token_count = positions * replica_rows * replicas
    heads_width = attention_output_weight.shape[1]
    hidden = hidden_weight.shape[2]

    def my_rows(value, axis):
        return lax.dynamic_slice_in_dim(value, section * rows, rows, axis)

    def to_rows(value):
        return jnp.transpose(my_rows(value, 1), (1, 0, 2))

    own = {
        "qkv": query_key_value_weight[0].reshape(width, 3 * heads_width),
        "out": attention_output_weight[0],
        "one": hidden_weight[0],
        "two": output_weight_mlp[0],
    }

    def padded(value):
        return jnp.pad(value.astype(F32), ((0, 0), (0, width - value.shape[-1])))

    biases = jnp.concatenate(
        [
            padded(
                jnp.concatenate(
                    [
                        query_value_bias[0, 0:1], jnp.zeros((1, heads_width), BF16),
                        query_value_bias[0, 1:2],
                    ],
                    axis=1,
                )
            ),
            jnp.zeros((1, width), F32), padded(attention_output_bias), padded(hidden_bias),
            padded(output_bias_mlp), jnp.zeros((MOD_ROWS - 5, width), F32),
        ],
        axis=0,
    )
    used = rows * IMAGES_PER_ROW
    cond_pad = jnp.pad(
        cond.reshape(sections, used, width), ((0, 0), (0, MOD_ROWS - used), (0, 0))
    )
    segs_full = my_rows(image_slot_index, 0)
    seg_own = lax.dynamic_slice_in_dim(segs_full, tensor * length, length, 1)
    segs = (seg_own[:, :, None], segs_full[:, :, None], segs_full[:, None, :])

    target_parts = my_rows(targets, 1).reshape(count, length, rows, targets.shape[2])
    target_parts = jnp.transpose(target_parts, (0, 2, 1, 3))
    lane = p1_b.shape[0]
    proj_biases = jnp.concatenate(
        [
            p1_b.astype(F32)[None],
            jnp.pad(p3_b.astype(F32), (0, lane - p3_b.shape[0]))[None],
            jnp.zeros((MOD_ROWS - 2, lane), F32),
        ],
        axis=0,
    )
    gather = ColumnGather((p1_w, p2_w, p3_w.T), PROJECTOR_AXES, target_parts, proj_biases)

    u = to_rows(block_eight_input)
    sizes = Shapes(u, own, count)
    mods, bias_all, other, attend_one, carried = open_forward(
        sizes, u, cond_pad.reshape(-1, width), ada_w[0].T, ada_b, biases, segs, own, sections,
        (gather,),
    )
    *proj_weights, target_all, proj_bias_all = carried[0]
    mlp_one, carried = mlp_forward(
        sizes, 0, attend_one[0], mods, bias_all, segs, own, other,
        (ShareAlong(proj_weights, PROJECTOR_AXES, 0),),
    )
    proj_weights = carried[0]
    first_out = mlp_one[0]
    attend_two, carried = attend_forward(
        sizes, 1, first_out, mods, bias_all, segs, own, other, (ShareAlong(proj_weights, PROJECTOR_AXES, 1),)
    )
    proj_weights = carried[0]
    mlp_two, carried = mlp_forward(
        sizes, 1, attend_two[0], mods, bias_all, segs, own, other, (ShareAlong(proj_weights, PROJECTOR_AXES, 2),)
    )
    proj_weights = carried[0]
    second_out = mlp_two[0]

    grad_sent, grad_p1, grad_p2, grad_p3, proj_small = project(
        sizes, first_out, proj_weights, target_all, proj_bias_all, p2_b[None], total_token_count
    )

    back = (mods, segs, own, other)
    (d_middle_two, mod_mlp_two, *mlp_grads_two), carried = mlp_backward(
        sizes, 1, [to_rows(cot)], attend_two, mlp_two, *back,
        [
            Swap(first_out, second_out), HalfSum(grad_p1, 0, "x"),
            HalfSum(grad_p3, 1, "x", (0, 1)),
        ],
    )
    (other_out,), (grad_p1,), (grad_p3_a,) = carried
    (second_grad, mod_attend_two, *attend_grads_two), carried = attend_backward(
        sizes, 1, d_middle_two, first_out, attend_two, *back,
        [YSum(grad, BF16) for grad in mlp_grads_two[:2]]
        + [HalfSum(grad_p2, 1, "x", (0, 1)), HalfSum(grad_p3, 1, "x", (1, 1))]
        + [HalfSum(grad_p1, 0, "y", (0, 1))],
    )
    (mlp_part_a,), (mlp_part_b,), (grad_p2_a,), (grad_p3_b,), (grad_p1_a,) = carried
    (d_middle_one, mod_mlp_one, *mlp_grads_one), carried = mlp_backward(
        sizes, 0, [second_grad, grad_sent], attend_one, mlp_one, *back,
        [YSum(grad, BF16) for grad in attend_grads_two[:2]]
        + [SectionSum(mlp_part_a, 1), HalfSum(grad_p2, 1, "x", (1, 1))]
        + [HalfSum(grad_p1, 0, "y", (1, 1)), HalfSum(grad_p2_a, 1, "y")],
    )
    attend_parts_two, sum_mlp_a = carried[:2], carried[2]
    (grad_p2_b,), (grad_p1_b,), (grad_p2_a,) = carried[3:]
    (first_grad, mod_attend_one, *attend_grads_one), carried = attend_backward(
        sizes, 0, d_middle_one, u, attend_one, *back,
        [LastSum(mlp_grads_one[0], 0), SectionSum(mlp_grads_one[1], 0, BF16)]
        + [SectionSum(part, 1) for part, in attend_parts_two]
        + [SectionSum(mlp_part_b, 1), HalfSum(grad_p2_b, 1, "y")]
        + [HalfSum(grad_p3_a, 1, "y"), HalfSum(grad_p3_b, 1, "y")]
        + [ColumnSum((grad_p1_a, grad_p1_b), 0)],
    )
    sum_mlp_c, (mlp_part_two,), sums_attend_two = carried[0], carried[1], carried[2:4]
    sums_mlp_two = (sum_mlp_a, carried[4])
    (grad_p2_b,), (grad_p3_a,), (grad_p3_b,), (red_p1_w,) = carried[5:]

    cond_act = silu(my_rows(cond, 0).astype(F32)).astype(BF16).astype(F32)
    share = width // replicas
    cond_cols = jnp.pad(cond_act.reshape(used, width), ((0, MOD_ROWS - used), (0, 0)))
    cond_cols = jnp.transpose(cond_cols.reshape(MOD_ROWS, replicas, share), (1, 0, 2))
    small = [
        attend_grads_one[2], attend_grads_one[3], mlp_grads_one[2], mlp_grads_one[3],
        attend_grads_two[2], attend_grads_two[3], mlp_grads_two[2], mlp_grads_two[3],
    ]
    (section_grad, grad_ada_w, grad_ada_b, small, proj_small), carried = close_backward(
        sizes, (first_grad, second_grad),
        (mod_attend_one, mod_mlp_one, mod_attend_two, mod_mlp_two),
        small, proj_small, cond_cols, sections, replicas,
        [LastSum(grad, 0) for grad in attend_grads_one[:2]]
        + [YSum(mlp_part_two, F32)]
        + [ColumnSum((grad_p2_a, grad_p2_b), 1), ColumnSum((grad_p3_a, grad_p3_b), 1)],
    )
    sums_attend_one, sums_mlp_one = carried[:2], (sum_mlp_c, carried[2])
    (red_p2_w,), (red_p3_w,) = carried[3:]

    own_out = jnp.where(is_first, first_out, second_out)
    section_out = jnp.where(
        is_first,
        jnp.concatenate([own_out, other_out], axis=0),
        jnp.concatenate([other_out, own_out], axis=0),
    )
    section_out = jnp.transpose(section_out, (1, 0, 2))[None]
    choices = [
        (one[0], two[0])
        for one, two in zip(
            list(sums_mlp_one) + list(sums_attend_one), list(sums_mlp_two) + list(sums_attend_two)
        )
    ]
    if replicas == 4:
        alone = [grad_ada_w, grad_ada_b, red_p1_w, red_p2_w, red_p3_w]
        final = assemble(choices, alone, section_grad, small, proj_small, heads_width)
        red_fc1, red_fc2, grad_ada_w, grad_ada_b, red_p1_w, red_p2_w, red_p3_w = final[:7]
        section_grad, red_qkv, red_out, qv_b, out_b, fc1_b, fc2_b, p1_sum, p2_sum, p3_sum, loss = (
            final[7:]
        )
        red_p1_b, red_p2_b, red_p3_b = p1_sum[0], p2_sum[0], p3_sum[0]
        loss_total = loss[0, 0]
    else:
        red_fc1, red_fc2, red_qkv, red_out = [
            sum_beyond_quads(jnp.where(is_first, one, two)) for one, two in choices
        ]
        red_qkv = jnp.transpose(red_qkv.reshape(-1, 3, heads_width), (1, 0, 2))
        red_out = red_out.T
        red_p1_w = sum_beyond_quads(red_p1_w)
        red_p2_w, red_p3_w = sum_beyond_quads(red_p2_w.T).T, sum_beyond_quads(red_p3_w.T).T
        section_grad = jnp.transpose(section_grad, (1, 0, 2))
        qv_b = jnp.stack([small[0, :heads_width], small[0, 2 * heads_width : 3 * heads_width]])
        out_b, fc1_b, fc2_b = small[2:3], small[3:4], small[4:5]
        red_p1_b, red_p2_b = proj_small[0], proj_small[2:6].reshape(-1)
        red_p3_b, loss_total = proj_small[1, : p3_b.shape[0]], proj_small[6, 0]
    align_loss = -0.5 * loss_total / total_token_count
    return (
        section_out,
        section_grad[None],
        align_loss,
        grad_ada_w[None],
        grad_ada_b,
        jnp.transpose(red_qkv, (1, 0, 2))[None],
        qv_b[None],
        red_out[None],
        out_b,
        red_fc1[None],
        fc1_b[:, :hidden],
        red_fc2.T[None],
        fc2_b,
        red_p1_w,
        red_p1_b,
        red_p2_w,
        red_p2_b[: p2_b.shape[0]],
        red_p3_w.T,
        red_p3_b,
    )


def solution(mesh):
    in_specs = (
        P("tensor", "dp", None),
        P("dp", None, None),
        P("dp", None),
        P(None, "dp", "tensor"),
        P("tensor", "dp", None),
        P("section", None, "tensor"),
        P("section", "tensor"),
        P("section", None, None, "tensor"),
        P("section", None, "tensor"),
        P("section", "tensor", None),
        P("section", None),
        P("section", None, "tensor"),
        P("section", "tensor"),
        P("section", "tensor", None),
        P("section", None),
        P(None, "tensor"),
        P("tensor"),
        P("tensor", None),
        P(),
        P(None, "tensor"),
        P("tensor"),
    )
    out_specs = (
        P("section", "tensor", "dp", None),
        P("section", "tensor", "dp", None),
        P(),
        P("section", "dp", "tensor"),
        P("section", "tensor"),
        P("section", "dp", None, "tensor"),
        P("section", None, "tensor"),
        P("section", "tensor", "dp"),
        P("section", None),
        P("section", "dp", "tensor"),
        P("section", "tensor"),
        P("section", "tensor", "dp"),
        P("section", None),
        P(("section", "dp"), "tensor"),
        P("tensor"),
        P("tensor", ("section", "dp")),
        P(),
        P(("section", "dp"), "tensor"),
        P("tensor"),
    )
    return jax.shard_map(
        per_device, mesh=mesh, in_specs=in_specs, out_specs=out_specs, check_vma=False
    )
```
